32 devices in a mesh: dp: 4 (over z), seq: 2 (over core), lvl: 4 (over y, x).
Axes of the slice: x: 2, y: 2, z: 4, core: 2. Of those that a mesh axis runs over, the one named last changes fastest.
Arguments:
- tokens: float32 [4, 4096, 768], P('dp', 'seq'), may hold values from -6 to 6
- cotangent: float32 [4, 4096, 768], P('dp', 'seq'), may hold values from -6 to 6
- lengths: int32 [4], P('dp'), may hold values from 2308 to 4096, as said below
- qkv_weight: float32 [3, 768, 768], P(None, None, 'lvl'), may hold values from -0.21875 to 0.21875
- out_weight: float32 [768, 768], P('lvl'), may hold values from -1.75 to 1.75
- ffn_in_weight: float32 [3072, 768], P('lvl'), may hold values from -0.21875 to 0.21875
- ffn_out_weight: float32 [3072, 768], P('lvl'), may hold values from -0.109375 to 0.109375
- vectors: float32 [8, 768], replicated, may hold values from -1.2 to 1.25, as said below
- ffn_bias: float32 [3072], replicated, may hold values from -1.2 to 1.2
- pool_kernel: float32 [2, 5, 6], replicated, may hold values from 0.05 to 0.4
- qkv_moments: float32 [2, 3, 768, 768], P(None, None, ('dp', 'seq'), 'lvl'), may hold values from -0.4 to 0.4, as said below
- out_moments: float32 [2, 768, 768], P(None, 'lvl', ('dp', 'seq')), may hold values from -0.4 to 0.4, as said below
- ffn_in_moments: float32 [2, 3072, 768], P(None, 'lvl', ('dp', 'seq')), may hold values from -0.4 to 0.4, as said below
- ffn_out_moments: float32 [2, 3072, 768], P(None, 'lvl', ('dp', 'seq')), may hold values from -0.4 to 0.4, as said below
- vector_moments: float32 [2, 8, 768], replicated, may hold values from -0.4 to 0.4, as said below
- bias_moments: float32 [2, 3072], replicated, may hold values from -0.4 to 0.4, as said below
- pool_moments: float32 [2, 2, 5, 6], replicated, may hold values from -0.4 to 0.4, as said below
Outputs:
- block_out: float32 [4, 4096, 768], P('dp', 'seq')
- input_grad: float32 [4, 4096, 768], P('dp', 'seq')
- qkv_grad: float32 [3, 768, 768], P(None, ('dp', 'seq'), 'lvl')
- qkv_step: float32 [3, 768, 768], P(None, ('dp', 'seq'), 'lvl')
- qkv_moments_new: float32 [2, 3, 768, 768], P(None, None, ('dp', 'seq'), 'lvl')
- out_grad: float32 [768, 768], P('lvl', ('dp', 'seq'))
- out_step: float32 [768, 768], P('lvl', ('dp', 'seq'))
- out_moments_new: float32 [2, 768, 768], P(None, 'lvl', ('dp', 'seq'))
- ffn_in_grad: float32 [3072, 768], P('lvl', ('dp', 'seq'))
- ffn_in_step: float32 [3072, 768], P('lvl', ('dp', 'seq'))
- ffn_in_moments_new: float32 [2, 3072, 768], P(None, 'lvl', ('dp', 'seq'))
- ffn_out_grad: float32 [3072, 768], P('lvl', ('dp', 'seq'))
- ffn_out_step: float32 [3072, 768], P('lvl', ('dp', 'seq'))
- ffn_out_moments_new: float32 [2, 3072, 768], P(None, 'lvl', ('dp', 'seq'))
- vectors_grad: float32 [8, 768], replicated
- vectors_step: float32 [8, 768], replicated
- vector_moments_new: float32 [2, 8, 768], replicated
- bias_grad: float32 [3072], replicated
- bias_step: float32 [3072], replicated
- bias_moments_new: float32 [2, 3072], replicated
- pool_grad: float32 [2, 5, 6], replicated
- pool_step: float32 [2, 5, 6], replicated
- pool_moments_new: float32 [2, 2, 5, 6], replicated
- clip_factor: float32 [], replicated
- group_norms: float32 [4], replicated
The draws below stay inside these ranges and needn't reach their ends.
Inputs may be any that keep to these rules, and one draw needn't show every extreme that they name: `lengths`: each length is a multiple of 4 and at least 2308; in every draw some sequence is full. `vectors`: rows 4 and 6 lie near 1. `qkv_moments`: second moments are positive. `out_moments`: second moments are positive. `ffn_in_moments`: second moments are positive. `ffn_out_moments`: second moments are positive. `vector_moments`: second moments are positive. `bias_moments`: second moments are positive. `pool_moments`: second moments are positive.
All inputs are finite; a program needn't handle non-finite values.
Results may differ from the reference program's by a relative error of at most 0.015.
The reference program's roundings to bfloat16 on the way count: a program that leaves them out, or rounds other values in their place, can miss the bound.
Values may be sent and summed in bfloat16 or wider, within the bound.
No kernel may reach another device: no remote copies, remote signals or barrier semaphores. Data moves between devices by JAX's collectives and lax.ppermute only.
A program may use at most 192 MiB of HBM per device.

```python
import math
import jax
import jax.numpy as jnp
from jax import lax

D = 768
HEADS = 12
FF = 3072
W1 = 128
W2 = 512
QB = 512
HP = 6
SEQ_LEN = 4096
SEQS = 4


def moment_pair(key, shape):
    first = 0.1 * jnp.clip(jax.random.normal(jax.random.fold_in(key, 11), shape, jnp.float32), -4.0, 4.0)
    second = jnp.exp(jax.random.uniform(jax.random.fold_in(key, 12), shape, jnp.float32, math.log(0.001), math.log(0.1)))
    return jnp.stack([first, second]).astype(jnp.float32)


def draw_lengths(key, part):
    key = jax.random.fold_in(key, 1)
    lowest = (SEQ_LEN // 2 + W2 // 2 + 4 + 3) // 4
    units = jax.random.randint(jax.random.fold_in(key, 1), (SEQS,), lowest, SEQ_LEN // 4 + 1)
    chosen = jax.random.randint(jax.random.fold_in(key, 2), (), 0, SEQS)
    return jnp.where(jnp.arange(SEQS) == chosen, SEQ_LEN, 4 * units).astype(jnp.int32)


def draw_vectors(key, part):
    key = jax.random.fold_in(key, 2)
    biases = 0.3 * jnp.clip(jax.random.normal(jax.random.fold_in(key, 1), (8, D), jnp.float32), -4.0, 4.0)
    gains = 1.0 + 0.25 * jax.random.uniform(jax.random.fold_in(key, 2), (8, D), jnp.float32, -1.0, 1.0)
    row_index = jnp.arange(8)[:, None]
    is_gain = (row_index == 4) | (row_index == 6)
    return jnp.where(is_gain, gains, biases).astype(jnp.float32)


def draw_qkv_moments(key, part):
    key = jax.random.fold_in(key, 3)
    return moment_pair(key, (3, D, D))


def draw_out_moments(key, part):
    key = jax.random.fold_in(key, 4)
    return moment_pair(key, (D, D))


def draw_ffn_in_moments(key, part):
    key = jax.random.fold_in(key, 5)
    return moment_pair(key, (FF, D))


def draw_ffn_out_moments(key, part):
    key = jax.random.fold_in(key, 6)
    return moment_pair(key, (FF, D))


def draw_vector_moments(key, part):
    key = jax.random.fold_in(key, 8)
    return moment_pair(key, (8, D))


def draw_bias_moments(key, part):
    key = jax.random.fold_in(key, 9)
    return moment_pair(key, (FF,))


def draw_pool_moments(key, part):
    key = jax.random.fold_in(key, 10)
    return moment_pair(key, (2, 5, HP))


def with_spikes(values, rng, source, target, shards_of, factor):
    owner, partner = [(jnp.arange(values.shape[position]) // (values.shape[position] // shards_of)).reshape([-1 if axis == position else 1 for axis in range(values.ndim)]) for position in (source, target)]
    chosen = jax.random.permutation(rng, shards_of)[partner]
    strong = (owner == chosen) | (owner == (partner + shards_of // 2) % shards_of)
    return jnp.where(strong, factor * values, values)


def block_scale(rng, dims, split, low, high):
    level = 1.0
    for axis_at, blocks in split:
        draws = jax.random.uniform(jax.random.fold_in(jax.random.fold_in(rng, 6), axis_at), (blocks,), jnp.float32, low / len(split), high / len(split))
        level = level * jnp.repeat(jnp.exp(draws), dims[axis_at] // blocks).reshape((-1,) + (1,) * (len(dims) - 1 - axis_at))
    return level


def centred(key, dims, width, bound, cuts=(), kind=jnp.bfloat16):
    level = block_scale(key, dims, cuts, -0.22, 0.18) if cuts else 1.0
    values = jax.random.normal(key, dims, jnp.float32) * width * level
    return jnp.minimum(jnp.maximum(values, -bound), bound).astype(kind)


def noise_with(own_key, shape, spread, most, split, heavy, kind=jnp.bfloat16):
    entries = spread * jax.random.normal(own_key, shape, jnp.float32)
    if split:
        entries = entries * block_scale(own_key, shape, split, -0.22, 0.18)
    return jnp.clip(with_spikes(entries, jax.random.fold_in(own_key, 3), *heavy), -most, most).astype(kind)


def setup_inputs(seed: int = 0) -> dict:
    streams_of = jax.random.split(jax.random.key(seed), 18)
    return {
        "tokens": centred(streams_of[0], (SEQS, SEQ_LEN, D), 1.0, 6.0, ((0, 4), (1, 2)), jnp.float32),
        "cotangent": noise_with(streams_of[1], (SEQS, SEQ_LEN, D), 1.0, 6.0, ((0, 4), (1, 2)), (0, 2, 4, 2.0), jnp.float32),
        "lengths": draw_lengths(jax.random.fold_in(streams_of[17], 71), 0),
        "qkv_weight": centred(streams_of[3], (3, D, D), D ** -0.5, 0.21875, ((2, 4),), jnp.float32),
        "out_weight": centred(streams_of[4], (D, D), (D // 64) ** -0.5, 1.75, ((0, 4),), jnp.float32),
        "ffn_in_weight": centred(streams_of[5], (FF, D), D ** -0.5, 0.21875, ((0, 4),), jnp.float32),
        "ffn_out_weight": centred(streams_of[6], (FF, D), FF ** -0.5, 0.109375, ((0, 4),), jnp.float32),
        "vectors": draw_vectors(jax.random.fold_in(streams_of[17], 71), 0),
        "ffn_bias": centred(streams_of[8], (FF,), 0.3, 1.2, (), jnp.float32),
        "pool_kernel": jnp.clip(jax.random.uniform(streams_of[9], (2, 5, HP), jnp.float32, 0.05, 0.4), 0.05, 0.4),
        "qkv_moments": draw_qkv_moments(jax.random.fold_in(streams_of[17], 71), 0),
        "out_moments": draw_out_moments(jax.random.fold_in(streams_of[17], 71), 0),
        "ffn_in_moments": draw_ffn_in_moments(jax.random.fold_in(streams_of[17], 71), 0),
        "ffn_out_moments": draw_ffn_out_moments(jax.random.fold_in(streams_of[17], 71), 0),
        "vector_moments": draw_vector_moments(jax.random.fold_in(streams_of[17], 71), 0),
        "bias_moments": draw_bias_moments(jax.random.fold_in(streams_of[17], 71), 0),
        "pool_moments": draw_pool_moments(jax.random.fold_in(streams_of[17], 71), 0),
    }


@jax.custom_vjp
def low(v):
    return lax.optimization_barrier(v.astype(jnp.bfloat16)).astype(jnp.float32)

@jax.custom_vjp
def low_back(v):
    return v

def low_keep(v):
    return (low(v), None)

def low_pass(kept, grad):
    return (grad,)

def back_keep(v):
    return (v, None)

def back_low(kept, grad):
    return (low(grad),)
low.defvjp(low_keep, low_pass)
low_back.defvjp(back_keep, back_low)
norm_eps = 1e-05
beta_first = 0.9
beta_second = 0.999
adam_eps = 1e-08
decay_rate = 0.01
adam_step = 10.0
max_rms = 1.0
masked_score = -1e+30
highest = lax.Precision.HIGHEST

def layer_norm(value, gain, shift):
    mean = lax.optimization_barrier(jnp.mean(value, axis=-1, keepdims=True))
    centered = value - mean
    inverse = lax.rsqrt(lax.optimization_barrier(jnp.mean(centered * centered, axis=-1, keepdims=True)) + norm_eps)
    return centered * inverse * gain + shift

def attend(query, keys, values, visible):
    scale = 1.0 / math.sqrt(query.shape[-1])
    scores = low_back(jnp.einsum('hqe,hke->hqk', query, keys, precision=highest) * scale)
    scores = jnp.where(visible[None], scores, masked_score)
    top = lax.optimization_barrier(jnp.max(scores, axis=-1, keepdims=True))
    raised = jnp.exp(scores - top)
    chance = low(raised / lax.optimization_barrier(jnp.sum(raised, axis=-1, keepdims=True)))
    return jnp.einsum('hqk,hke->hqe', chance, values, precision=highest)

def visibility(rows, cols, reach, length):
    same_side = (rows < length)[:, None] == (cols < length)[None, :]
    return (jnp.abs(rows[:, None] - cols[None, :]) <= reach) & same_side

def sequence_layer(params, sequence, length):
    qkv_weight, out_weight, ffn_in_weight, ffn_out_weight, vectors, ffn_bias, pool_kernel = params
    head_dim = D // HEADS
    half = HEADS // 2
    inputs = low(sequence)
    projected = jnp.einsum('td,cde->cte', inputs, low(qkv_weight), precision=highest)
    query = low(low_back(projected[0]) + vectors[0])
    keys = low(low_back(projected[1]))
    values = low(low_back(projected[2]) + vectors[1])

    def split_heads(value):
        return value.reshape(SEQ_LEN, HEADS, head_dim).transpose(1, 0, 2)
    query = split_heads(query)
    keys = split_heads(keys)
    values = split_heads(values)
    padded = jnp.pad(jnp.stack([keys[half:], values[half:]]), ((0, 0), (0, 0), (2, 2), (0, 0)))
    pooled = jnp.zeros((2, half, SEQ_LEN // 4, head_dim), jnp.float32)
    for tap in range(5):
        pooled = pooled + pool_kernel[:, tap][:, :, None, None] * padded[:, :, tap:tap + SEQ_LEN:4]
    pooled = low(pooled)
    positions = jnp.arange(SEQ_LEN, dtype=jnp.int32)
    centers = 4 * jnp.arange(SEQ_LEN // 4, dtype=jnp.int32)

    def block(start):
        rows = start + jnp.arange(QB, dtype=jnp.int32)
        near = visibility(rows, positions, W1 // 2, length)
        far = visibility(rows, centers, W2 // 2, length)
        query_block = lax.dynamic_slice_in_dim(query, start, QB, 1)
        first_level = attend(query_block[:half], keys[:half], values[:half], near)
        second_level = attend(query_block[half:], pooled[0], pooled[1], far)
        return jnp.concatenate([first_level, second_level], axis=0)
    starts = QB * jnp.arange(SEQ_LEN // QB, dtype=jnp.int32)
    blocks = lax.map(jax.checkpoint(block), starts)
    mixed = low(low_back(blocks.transpose(0, 2, 1, 3).reshape(SEQ_LEN, D)))
    attention = low_back(jnp.dot(mixed, low(out_weight), precision=highest, preferred_element_type=jnp.float32)) + vectors[2]
    first = layer_norm(sequence + attention, vectors[4], vectors[5])
    first_low = low(first)
    pre = low_back(jnp.dot(first_low, low(ffn_in_weight).T, precision=highest, preferred_element_type=jnp.float32)) + ffn_bias
    activation = low(jax.nn.gelu(pre, approximate=False))
    branch = low_back(jnp.dot(activation, low(ffn_out_weight), precision=highest, preferred_element_type=jnp.float32)) + vectors[3]
    return layer_norm(first + branch, vectors[6], vectors[7])

def adamw(weight, grad, moments, decay, clip):
    clipped = clip * grad
    first_moment = beta_first * moments[0] + (1.0 - beta_first) * clipped
    second_moment = beta_second * moments[1] + (1.0 - beta_second) * clipped * clipped
    corrected_first = first_moment / (1.0 - beta_first ** adam_step)
    corrected_second = second_moment / (1.0 - beta_second ** adam_step)
    update = corrected_first / (jnp.sqrt(corrected_second) + adam_eps) + decay * weight
    return (update, jnp.stack([first_moment, second_moment]))

def reference(tokens, cotangent, lengths, qkv_weight, out_weight, ffn_in_weight, ffn_out_weight, vectors, ffn_bias, pool_kernel, qkv_moments, out_moments, ffn_in_moments, ffn_out_moments, vector_moments, bias_moments, pool_moments):
    params = (qkv_weight, out_weight, ffn_in_weight, ffn_out_weight, vectors, ffn_bias, pool_kernel)
    zeros = jax.tree.map(jnp.zeros_like, params)

    def per_sequence(carry, item):
        sequence, tangent, length = item

        def layer_of(weights, values):
            return sequence_layer(weights, values, length)
        output, pullback = jax.vjp(layer_of, params, sequence)
        weight_grads, sequence_grad = pullback(tangent)
        return (jax.tree.map(jnp.add, carry, weight_grads), (output, sequence_grad))
    totals, (outputs, input_grads) = lax.scan(per_sequence, zeros, (tokens, cotangent, lengths))
    qkv_grad, out_grad, ffn_in_grad, ffn_out_grad, vectors_grad, bias_grad, pool_grad = totals
    squares = jnp.stack([jnp.sum(qkv_grad * qkv_grad) + jnp.sum(out_grad * out_grad), jnp.sum(ffn_in_grad * ffn_in_grad) + jnp.sum(ffn_out_grad * ffn_out_grad), jnp.sum(vectors_grad * vectors_grad) + jnp.sum(bias_grad * bias_grad), jnp.sum(pool_grad * pool_grad)])
    group_norms = jnp.sqrt(squares)
    total = jnp.sqrt(jnp.sum(squares))
    param_count = 4 * D * D + 2 * FF * D + 8 * D + FF + 10 * (HEADS // 2)
    clip = jnp.minimum(1.0, max_rms * math.sqrt(param_count) / (total + 1e-06))
    qkv_step, qkv_moments_new = adamw(qkv_weight, qkv_grad, qkv_moments, decay_rate, clip)
    out_step, out_moments_new = adamw(out_weight, out_grad, out_moments, decay_rate, clip)
    ffn_in_step, ffn_in_moments_new = adamw(ffn_in_weight, ffn_in_grad, ffn_in_moments, decay_rate, clip)
    ffn_out_step, ffn_out_moments_new = adamw(ffn_out_weight, ffn_out_grad, ffn_out_moments, decay_rate, clip)
    vectors_step, vector_moments_new = adamw(vectors, vectors_grad, vector_moments, 0.0, clip)
    bias_step, bias_moments_new = adamw(ffn_bias, bias_grad, bias_moments, 0.0, clip)
    pool_step, pool_moments_new = adamw(pool_kernel, pool_grad, pool_moments, 0.0, clip)
    return (outputs, input_grads, qkv_grad, qkv_step, qkv_moments_new, out_grad, out_step, out_moments_new, ffn_in_grad, ffn_in_step, ffn_in_moments_new, ffn_out_grad, ffn_out_step, ffn_out_moments_new, vectors_grad, vectors_step, vector_moments_new, bias_grad, bias_step, bias_moments_new, pool_grad, pool_step, pool_moments_new, clip, group_norms)
```

```python
import math

import jax
import jax.numpy as jnp
from jax import lax
from jax.sharding import PartitionSpec as P

D = 768
HEADS = 12
HEAD = 64
FF = 3072
REACH1 = 64
REACH2 = 256
LEFT = 272
RIGHT = 256
NEARB = 128

norm_eps = 1e-05
beta_first = 0.9
beta_second = 0.999
adam_eps = 1e-08
decay_rate = 0.01
adam_step = 10.0
max_rms = 1.0
masked_score = -1e30

f32 = jnp.float32
bf16 = jnp.bfloat16
SWAP = [(0, 1), (1, 0)]
MINE = [(i, i ^ 1) for i in range(4)] + [(4 + i, 4 + (i ^ 2)) for i in range(4)]
CROSS = [(i, i ^ 2) for i in range(4)] + [(4 + i, 4 + (i ^ 1)) for i in range(4)]
PATH = [0, 1, 3, 2, 6, 7, 5, 4]
RIGHTWARD = list(zip(PATH[:-1], PATH[1:]))
LEFTWARD = [(b, a) for a, b in RIGHTWARD]
PLACE = ("seq", "lvl")


def bfloat(value):
    return value.astype(bf16)


def normalize(value):
    mean = jnp.mean(value, axis=-1, keepdims=True)
    centered = value - mean
    inverse = lax.rsqrt(jnp.mean(centered * centered, axis=-1, keepdims=True) + norm_eps)
    return (centered * inverse, inverse)


def norm_back(incoming, normed, inverse, gain):
    scaled = incoming * gain
    return inverse * (
        scaled
        - jnp.mean(scaled, axis=-1, keepdims=True)
        - normed * jnp.mean(scaled * normed, axis=-1, keepdims=True)
    )


def adamw(weight, grad, moments, decay, clip):
    clipped = clip * grad
    first_moment = beta_first * moments[0] + (1.0 - beta_first) * clipped
    second_moment = beta_second * moments[1] + (1.0 - beta_second) * clipped * clipped
    corrected_first = first_moment / (1.0 - beta_first**adam_step)
    corrected_second = second_moment / (1.0 - beta_second**adam_step)
    update = corrected_first / (jnp.sqrt(corrected_second) + adam_eps) + decay * weight
    return (update, jnp.stack([first_moment, second_moment]))


def gather_shards(own, core):
    half = own.shape[0] // 2
    mine = lax.ppermute(own, PLACE, MINE)
    part = lax.dynamic_slice_in_dim(mine, core * half, half, 0)
    diag_mine = lax.ppermute(part, PLACE, CROSS)
    other = lax.ppermute(mine, "seq", SWAP)
    diag_other = lax.ppermute(diag_mine, "seq", SWAP)
    low = jnp.where(core == 0, diag_mine, diag_other)
    high = jnp.where(core == 0, diag_other, diag_mine)
    return [own, mine, other, jnp.concatenate([low, high], axis=0)]


def reduce_grads(mine, sent, dp, dp_index):
    got = lax.ppermute(sent, "seq", SWAP)[:, :, jnp.array([0, 2, 1, 3])]
    total = mine.astype(f32) + got.astype(f32)
    first = lax.ppermute(bfloat(total[:, :, 1::2]), PLACE, MINE)
    kept = total[:, :, 0] + first[:, :, 0].astype(f32)
    passed = total[:, :, 2] + first[:, :, 1].astype(f32)
    second = lax.ppermute(bfloat(passed), PLACE, CROSS)
    total = kept + second.astype(f32)
    step = 1
    while step < dp:
        w, c = total.shape[-2:]
        split = total.reshape(-1, 2, w, c)
        bit = (dp_index // step) % 2
        keep = lax.dynamic_index_in_dim(split, bit, 1, False)
        send = lax.dynamic_index_in_dim(split, 1 - bit, 1, False)
        got = lax.ppermute(bfloat(send), "dp", [(i, i ^ step) for i in range(dp)])
        total = keep + got.astype(f32)
        step *= 2
    return total[0]


def sum_everywhere(value, dp):
    value = value + lax.ppermute(value, "seq", SWAP)
    for step in (1, 2):
        value = value + lax.ppermute(value, "lvl", [(i, i ^ step) for i in range(4)])
    step = 1
    while step < dp:
        value = value + lax.ppermute(value, "dp", [(i, i ^ step) for i in range(dp)])
        step *= 2
    return value


def gather_rows(own, count, core, level, chunk_of):
    mine = lax.ppermute(own, PLACE, MINE)
    both = lax.ppermute(jnp.concatenate([own, mine], axis=0), PLACE, CROSS)
    size = own.shape[0]
    along = jnp.where(core == 0, 1, 2)
    result = jnp.zeros((count, own.shape[1]), f32)
    pieces = ((own, level), (mine, level ^ along), (both[:size], level ^ (3 - along)), (both[size:], level ^ 3))
    for piece, owner in pieces:
        result = lax.dynamic_update_slice_in_dim(result, piece.astype(f32), chunk_of(owner) * size, 0)
    return result


def visibility(rows, cols, reach, length, limit):
    same_side = (rows < length)[:, None] == (cols < length)[None, :]
    inside = (cols >= 0) & (cols < limit)
    return (jnp.abs(rows[:, None] - cols[None, :]) <= reach) & same_side & inside[None, :]


def probabilities(query, keys, visible):
    scale = 1.0 / math.sqrt(HEAD)
    scores = jnp.einsum("qhe,khe->hqk", query, keys, preferred_element_type=f32) * scale
    scores = jnp.where(visible[None], scores, masked_score)
    raised = jnp.exp(scores - jnp.max(scores, axis=-1, keepdims=True))
    return raised / jnp.sum(raised, axis=-1, keepdims=True)


def attend(query, keys, values, visible):
    chance = bfloat(probabilities(query, keys, visible))
    return jnp.einsum("hqk,khe->qhe", chance, values, preferred_element_type=f32)


def attend_back(query, keys, values, visible, grad):
    scale = 1.0 / math.sqrt(HEAD)
    chance = probabilities(query, keys, visible)
    chance_grad = jnp.einsum("qhe,khe->hqk", grad, values, preferred_element_type=f32)
    score_grad = bfloat(chance * (chance_grad - jnp.sum(chance_grad * chance, axis=-1, keepdims=True)))
    query_grad = jnp.einsum("hqk,khe->qhe", score_grad, keys, preferred_element_type=f32) * scale
    key_grad = jnp.einsum("hqk,qhe->khe", score_grad, query, preferred_element_type=f32) * scale
    value_grad = jnp.einsum("hqk,qhe->khe", bfloat(chance), grad, preferred_element_type=f32)
    return (query_grad, key_grad, value_grad)


def on_device(
    tokens,
    cotangent,
    lengths,
    qkv_weight,
    out_weight,
    ffn_in_weight,
    ffn_out_weight,
    vectors,
    ffn_bias,
    pool_kernel,
    qkv_moments,
    out_moments,
    ffn_in_moments,
    ffn_out_moments,
    vector_moments,
    bias_moments,
    pool_moments,
):
    dp = lax.axis_size("dp")
    dp_index = lax.axis_index("dp")
    core = lax.axis_index("seq")
    level = lax.axis_index("lvl")
    length = lengths[0]
    count = tokens.shape[1]
    size = count // 4
    seq_len = 2 * count
    half = HEADS // 2
    wide = half * HEAD
    along = jnp.where(core == 0, 1, 2)
    slots = [level, level ^ along, level ^ (3 - along), level ^ 3]

    def chunk_of(owner):
        order = owner ^ (owner >> 1)
        return jnp.where(core == 0, order, 3 - order)

    chunk = chunk_of(level)
    base = core * count + chunk * size

    local = qkv_weight.shape[2]
    attn_own = jnp.concatenate(
        [bfloat(qkv_weight).transpose(0, 2, 1).reshape(3 * local, D), bfloat(out_weight)], axis=0
    )
    attn_slots = gather_shards(attn_own, core)
    in_slots = gather_shards(bfloat(ffn_in_weight), core)
    out_slots = gather_shards(bfloat(ffn_out_weight), core)
    attn_all = jnp.zeros((4, 4, local, D), bf16)
    for slot, owner in zip(attn_slots, slots):
        attn_all = lax.dynamic_update_slice(attn_all, slot.reshape(4, 1, local, D), (0, owner, 0, 0))
    attn_all = attn_all.reshape(4, D, D)
    in_all = jnp.concatenate(in_slots, axis=0)
    out_all = jnp.concatenate(out_slots, axis=0)
    hidden = ffn_in_weight.shape[0]
    bias_all = jnp.concatenate([lax.dynamic_slice_in_dim(ffn_bias, s * hidden, hidden) for s in slots])

    inputs = lax.dynamic_slice_in_dim(tokens[0], chunk * size, size, 0)
    incoming = lax.dynamic_slice_in_dim(cotangent[0], chunk * size, size, 0)
    edge = jnp.where(core == 0, tokens[0, count - LEFT :], tokens[0, :LEFT])
    edge = lax.ppermute(bfloat(edge), "seq", SWAP)
    before = jnp.where(core == 0, jnp.zeros_like(edge), edge)
    after = jnp.where(core == 0, edge, jnp.zeros_like(edge))[:RIGHT]
    extended = jnp.concatenate([before, bfloat(tokens[0]), after], axis=0)
    extended = lax.dynamic_slice_in_dim(extended, chunk * size, LEFT + size + RIGHT, 0)
    inputs_low = extended[LEFT : LEFT + size]
    ext_rows = base - LEFT + jnp.arange(LEFT + size + RIGHT)
    inside = ((ext_rows >= 0) & (ext_rows < seq_len))[:, None]

    query = bfloat(jnp.einsum("td,ed->te", inputs_low, attn_all[0], preferred_element_type=f32) + vectors[0])
    keys = bfloat(jnp.einsum("td,ed->te", extended, attn_all[1], preferred_element_type=f32))
    values = bfloat(jnp.einsum("td,ed->te", extended, attn_all[2], preferred_element_type=f32) + vectors[1])
    keys = jnp.where(inside, keys, 0)
    values = jnp.where(inside, values, 0)
    query = query.reshape(size, HEADS, HEAD)
    pooled_count = size // 4 + 2 * REACH2 // 4
    both = jnp.stack([keys[:, wide:], values[:, wide:]]).astype(f32)
    taps = [both[:, 14 + t : 14 + t + 4 * pooled_count - 3 : 4].reshape(2, pooled_count, half, HEAD) for t in range(5)]
    pooled = sum(pool_kernel[:, t][:, None, :, None] * taps[t] for t in range(5))
    pooled = bfloat(pooled)
    near_keys = keys[:, :wide].reshape(-1, half, HEAD)
    near_values = values[:, :wide].reshape(-1, half, HEAD)
    rows = base + jnp.arange(size)
    centers = base - REACH2 + 4 * jnp.arange(pooled_count)
    far = visibility(rows, centers, REACH2, length, seq_len)

    def near_block(q0):
        k0 = LEFT - REACH1 + q0
        cols = base + q0 - REACH1 + jnp.arange(NEARB + 2 * REACH1)
        mask = visibility(rows[q0 : q0 + NEARB], cols, REACH1, length, seq_len)
        window = slice(k0, k0 + NEARB + 2 * REACH1)
        return (query[q0 : q0 + NEARB, :half], near_keys[window], near_values[window], mask)

    starts = list(range(0, size, NEARB))
    near_out = jnp.concatenate([attend(*near_block(q0)) for q0 in starts], axis=0)
    far_out = attend(query[:, half:], pooled[0], pooled[1], far)
    mixed = bfloat(jnp.concatenate([near_out, far_out], axis=1).reshape(size, D))

    attention = jnp.dot(mixed, attn_all[3], preferred_element_type=f32)
    first_normed, first_inverse = normalize(inputs + attention + vectors[2])
    first = first_normed * vectors[4] + vectors[5]
    first_low = bfloat(first)
    pre = jnp.einsum("td,fd->tf", first_low, in_all, preferred_element_type=f32) + bias_all
    activation, gelu_back = jax.vjp(lambda v: jax.nn.gelu(v, approximate=False), pre)
    act_low = bfloat(activation)
    branch = jnp.dot(act_low, out_all, preferred_element_type=f32)
    second_normed, second_inverse = normalize(first + branch + vectors[3])
    block_low = bfloat(second_normed * vectors[6] + vectors[7])
    second_grad = norm_back(incoming, second_normed, second_inverse, vectors[6])
    branch_low = bfloat(second_grad)
    act_grad = jnp.einsum("td,fd->tf", branch_low, out_all, preferred_element_type=f32)
    pre_grad = gelu_back(act_grad)[0]
    pre_low = bfloat(pre_grad)
    first_grad = second_grad + jnp.dot(pre_low, in_all, preferred_element_type=f32)
    attn_grad = norm_back(first_grad, first_normed, first_inverse, vectors[4])
    attn_low = bfloat(attn_grad)
    mixed_grad = bfloat(jnp.einsum("td,ed->te", attn_low, attn_all[3], preferred_element_type=f32))

    block_out = gather_rows(block_low, count, core, level, chunk_of)

    def split_rows(grad):
        grad = bfloat(grad).reshape(dp, 2, D // (2 * dp), 4, -1)
        return (lax.dynamic_index_in_dim(grad, core, 1, False), lax.dynamic_index_in_dim(grad, 1 - core, 1, False))

    in_local = jnp.einsum("td,tf->df", first_low, pre_low, preferred_element_type=f32)
    out_local = jnp.einsum("td,tf->df", branch_low, act_low, preferred_element_type=f32)
    in_shard = reduce_grads(*split_rows(in_local), dp, dp_index)
    out_shard = reduce_grads(*split_rows(out_local), dp, dp_index)

    grad_heads = mixed_grad.reshape(size, HEADS, HEAD)
    query_parts = []
    near_grad = jnp.zeros((2, size + 2 * REACH1, half, HEAD), f32)
    for q0 in starts:
        block_query, block_keys, block_values, mask = near_block(q0)
        part = attend_back(block_query, block_keys, block_values, mask, grad_heads[q0 : q0 + NEARB, :half])
        query_parts.append(part[0])
        near_grad = near_grad.at[:, q0 : q0 + NEARB + 2 * REACH1].add(jnp.stack(part[1:]))
    far_part = attend_back(query[:, half:], pooled[0], pooled[1], far, grad_heads[:, half:])
    pooled_grad = jnp.stack(far_part[1:])
    query_grad = jnp.concatenate([jnp.concatenate(query_parts, axis=0), far_part[0]], axis=1).reshape(size, D)
    pool_local = jnp.stack([jnp.sum(pooled_grad * taps[t], axis=(1, 3)) for t in range(5)], axis=1)

    side = REACH2 // 4
    own_pool = size // 4
    near_flat = near_grad.reshape(2, -1, wide)
    pool_flat = pooled_grad.reshape(2, -1, wide)
    to_left = jnp.concatenate([near_flat[:, :REACH1], pool_flat[:, : side + 8]], axis=1)
    to_right = jnp.concatenate([near_flat[:, REACH1 + size :], pool_flat[:, side + own_pool :]], axis=1)
    from_right = lax.ppermute(bfloat(to_left), PLACE, LEFTWARD).astype(f32)
    from_left = lax.ppermute(bfloat(to_right), PLACE, RIGHTWARD).astype(f32)
    near_own = near_flat[:, REACH1 : REACH1 + size]
    near_own = near_own.at[:, :REACH1].add(from_left[:, :REACH1])
    near_own = near_own.at[:, size - REACH1 :].add(from_right[:, :REACH1])
    pool_own = pool_flat[:, side : side + own_pool + 8]
    pool_own = pool_own.at[:, :side].add(from_left[:, REACH1:])
    pool_own = pool_own.at[:, own_pool - side :].add(from_right[:, REACH1:])
    pool_own = pool_own[:, : own_pool + 1].reshape(2, own_pool + 1, half, HEAD)
    weighted = [pool_kernel[:, t][:, None, :, None] * pool_own for t in range(5)]
    columns = [
        weighted[2][:, :-1],
        weighted[3][:, :-1],
        weighted[4][:, :-1] + weighted[0][:, 1:],
        weighted[1][:, 1:],
    ]
    far_own = jnp.stack(columns, axis=2).reshape(2, size, wide)
    kv_grad = jnp.concatenate([near_own, far_own], axis=2)
    three_low = bfloat(jnp.stack([query_grad, kv_grad[0], kv_grad[1]]))
    input_own = attn_grad + jnp.einsum("cte,ced->td", three_low, attn_all[:3], preferred_element_type=f32)
    input_grad = gather_rows(bfloat(input_own), count, core, level, chunk_of)

    four = jnp.concatenate([three_low, mixed[None]], axis=0).reshape(4, size, 4, local)
    four = jnp.stack([lax.dynamic_index_in_dim(four, s, 2, False) for s in slots], axis=2)
    qkv_local = jnp.einsum("td,ctse->dsce", inputs_low, four[:3], preferred_element_type=f32)
    mix_local = jnp.einsum("td,tse->dse", attn_low, four[3], preferred_element_type=f32)
    attn_local = jnp.concatenate([qkv_local, mix_local[:, :, None]], axis=2).reshape(D, 4 * 4 * local)
    attn_shard = reduce_grads(*split_rows(attn_local), dp, dp_index)

    width = attn_shard.shape[0]
    attn_shard = attn_shard.reshape(width, 4, local)
    qkv_shard = attn_shard[:, :3].transpose(1, 0, 2)
    out_shard_w = attn_shard[:, 3].T
    ffn_in_shard = in_shard.T
    ffn_out_shard = out_shard.T

    vector_part = jnp.stack(
        [
            jnp.sum(query_grad, axis=0),
            jnp.sum(kv_grad[1], axis=0),
            jnp.sum(attn_grad, axis=0),
            jnp.sum(second_grad, axis=0),
            jnp.sum(first_grad * first_normed, axis=0),
            jnp.sum(first_grad, axis=0),
            jnp.sum(incoming * second_normed, axis=0),
            jnp.sum(incoming, axis=0),
        ]
    )
    bias_slots = jnp.sum(pre_grad, axis=0).reshape(4, hidden)
    bias_part = jnp.zeros((4, hidden), f32)
    for index, owner in enumerate(slots):
        bias_part = lax.dynamic_update_slice(bias_part, bias_slots[index : index + 1], (owner, 0))
    matrix_squares = jnp.stack(
        [
            jnp.sum(attn_shard * attn_shard),
            jnp.sum(in_shard * in_shard) + jnp.sum(out_shard * out_shard),
        ]
    )
    parts = [vector_part.reshape(-1), bias_part.reshape(-1), pool_local.reshape(-1), matrix_squares]
    sizes = [p.shape[0] for p in parts]
    packed = jnp.concatenate(parts)
    packed = jnp.pad(packed, (0, -packed.shape[0] % 1024)).reshape(-1, 128)
    packed = sum_everywhere(packed, dp).reshape(-1)
    pieces = []
    at = 0
    for n in sizes:
        pieces.append(packed[at : at + n])
        at += n
    vectors_grad = pieces[0].reshape(8, D)
    bias_grad = pieces[1]
    pool_grad = pieces[2].reshape(pool_kernel.shape)
    summed_squares = pieces[3]
    squares = jnp.stack(
        [
            summed_squares[0],
            summed_squares[1],
            jnp.sum(vectors_grad * vectors_grad) + jnp.sum(bias_grad * bias_grad),
            jnp.sum(pool_grad * pool_grad),
        ]
    )
    group_norms = jnp.sqrt(squares)
    total = jnp.sqrt(jnp.sum(squares))
    param_count = 4 * D * D + 2 * FF * D + 8 * D + FF + 10 * half
    clip = jnp.minimum(1.0, max_rms * math.sqrt(param_count) / (total + 1e-06))
    shard_index = dp_index * 2 + core

    def own_slice(weight):
        return lax.dynamic_slice_in_dim(weight, shard_index * width, width, 1)

    qkv_step, qkv_moments_new = adamw(own_slice(qkv_weight), qkv_shard, qkv_moments, decay_rate, clip)
    out_step, out_moments_new = adamw(own_slice(out_weight), out_shard_w, out_moments, decay_rate, clip)
    ffn_in_step, ffn_in_moments_new = adamw(
        own_slice(ffn_in_weight), ffn_in_shard, ffn_in_moments, decay_rate, clip
    )
    ffn_out_step, ffn_out_moments_new = adamw(
        own_slice(ffn_out_weight), ffn_out_shard, ffn_out_moments, decay_rate, clip
    )
    vectors_step, vector_moments_new = adamw(vectors, vectors_grad, vector_moments, 0.0, clip)
    bias_step, bias_moments_new = adamw(ffn_bias, bias_grad, bias_moments, 0.0, clip)
    pool_step, pool_moments_new = adamw(pool_kernel, pool_grad, pool_moments, 0.0, clip)
    return (
        block_out[None],
        input_grad[None],
        qkv_shard,
        qkv_step,
        qkv_moments_new,
        out_shard_w,
        out_step,
        out_moments_new,
        ffn_in_shard,
        ffn_in_step,
        ffn_in_moments_new,
        ffn_out_shard,
        ffn_out_step,
        ffn_out_moments_new,
        vectors_grad,
        vectors_step,
        vector_moments_new,
        bias_grad,
        bias_step,
        bias_moments_new,
        pool_grad,
        pool_step,
        pool_moments_new,
        clip,
        group_norms,
    )


def solution(mesh):
    in_specs = (
        P("dp", "seq", None),
        P("dp", "seq", None),
        P("dp"),
        P(None, None, "lvl"),
        P("lvl", None),
        P("lvl", None),
        P("lvl", None),
        P(),
        P(),
        P(),
        P(None, None, ("dp", "seq"), "lvl"),
        P(None, "lvl", ("dp", "seq")),
        P(None, "lvl", ("dp", "seq")),
        P(None, "lvl", ("dp", "seq")),
        P(),
        P(),
        P(),
    )
    out_specs = (
        P("dp", "seq", None),
        P("dp", "seq", None),
        P(None, ("dp", "seq"), "lvl"),
        P(None, ("dp", "seq"), "lvl"),
        P(None, None, ("dp", "seq"), "lvl"),
        P("lvl", ("dp", "seq")),
        P("lvl", ("dp", "seq")),
        P(None, "lvl", ("dp", "seq")),
        P("lvl", ("dp", "seq")),
        P("lvl", ("dp", "seq")),
        P(None, "lvl", ("dp", "seq")),
        P("lvl", ("dp", "seq")),
        P("lvl", ("dp", "seq")),
        P(None, "lvl", ("dp", "seq")),
        P(),
        P(),
        P(),
        P(),
        P(),
        P(),
        P(),
        P(),
        P(),
        P(),
        P(),
    )
    return jax.shard_map(
        on_device, mesh=mesh, in_specs=in_specs, out_specs=out_specs, check_vma=False
    )
```

```python
import functools
import math

import jax
import jax.numpy as jnp
from jax import lax
from jax.experimental import pallas as pl
from jax.experimental.pallas import tpu as pltpu
from jax.sharding import PartitionSpec as P

D = 768
HEADS = 12
HEAD = 64
FF = 3072
REACH1 = 64
REACH2 = 256
HALO = 320
ROWS = 512
EXT = ROWS + 2 * HALO
NEAR = ROWS + 2 * REACH1
NEAR0 = HALO - REACH1
FAR0 = 48
FAR = 1056
POOLED = 256
TAP0 = 14
BLOCK = 128
SUB = 384
PAIRS = HEADS // 4

norm_eps = 1e-05
beta_first = 0.9
beta_second = 0.999
adam_eps = 1e-08
decay_rate = 0.01
adam_step = 10.0
max_rms = 1.0
masked_score = -1e30
score_scale = 1.0 / math.sqrt(HEAD)

f32 = jnp.float32
bf16 = jnp.bfloat16
SWAP = [(0, 1), (1, 0)]
MINE = [(i, i ^ 1) for i in range(4)] + [(4 + i, 4 + (i ^ 2)) for i in range(4)]
CROSS = [(i, i ^ 2) for i in range(4)] + [(4 + i, 4 + (i ^ 1)) for i in range(4)]
PATH = [0, 1, 3, 2, 6, 7, 5, 4]
RIGHTWARD = list(zip(PATH[:-1], PATH[1:]))
LEFTWARD = [(b, a) for a, b in RIGHTWARD]
PLACE = ("seq", "lvl")

VM = pl.BlockSpec(memory_space=pltpu.VMEM)
SM = pl.BlockSpec(memory_space=pltpu.SMEM)
HB = pl.BlockSpec(memory_space=pl.ANY)


def bfloat(value):
    return value.astype(bf16)


def params(mib=56):
    return pltpu.CompilerParams(vmem_limit_bytes=mib * 1024 * 1024)


def cost(flops, moved, hard=0):
    return pl.CostEstimate(flops=int(flops), bytes_accessed=int(moved), transcendentals=int(hard))


def struct(shape, dtype):
    return jax.ShapeDtypeStruct(shape, dtype)


def dot(a, b):
    return jnp.dot(a, b, preferred_element_type=f32)


def dot_nt(a, b):
    return lax.dot_general(a, b, (((1,), (1,)), ((), ())), preferred_element_type=f32)


def turn(value):
    return jnp.transpose(value.astype(f32)).astype(bf16)


def row_mean(value):
    return jnp.mean(value, axis=-1, keepdims=True)


def col_sum(value):
    return jnp.sum(value, axis=0, keepdims=True)


def adamw(weight, grad, moments, decay, clip):
    clipped = clip * grad
    first_moment = beta_first * moments[0] + (1.0 - beta_first) * clipped
    second_moment = beta_second * moments[1] + (1.0 - beta_second) * clipped * clipped
    corrected_first = first_moment / (1.0 - beta_first**adam_step)
    corrected_second = second_moment / (1.0 - beta_second**adam_step)
    update = corrected_first / (jnp.sqrt(corrected_second) + adam_eps) + decay * weight
    return (update, jnp.stack([first_moment, second_moment]))


def attend_forward_kernel(
    place, own, mine, other, near_diag, far_diag, x, vectors, pool,
    weights, out_weight, mixed, query, near_keys, near_values, far_keys, far_values, pool_keys, pool_values, chance,
    key_rows, value_rows, near_mask, far_mask,
):
    level, slot1, slot2, slot3, core, base, length, seq_len = [place[i] for i in range(8)]
    local = own.shape[1]

    def rows_of(owner):
        return pl.ds(pl.multiple_of(owner * local, 64), local)

    for piece, owner in ((own, level), (mine, slot1), (other, slot2)):
        for c in range(3):
            weights[c, rows_of(owner)] = piece[c]
        out_weight[rows_of(owner)] = piece[3]

    def diagonal(low, high):
        weights[0, rows_of(slot3)] = low[0]
        weights[1, rows_of(slot3)] = low[1]
        weights[2, rows_of(slot3)] = high[0]
        out_weight[rows_of(slot3)] = high[1]

    @pl.when(core == 0)
    def _():
        diagonal(near_diag, far_diag)

    @pl.when(core != 0)
    def _():
        diagonal(far_diag, near_diag)

    wide = PAIRS * BLOCK
    lane = lax.broadcasted_iota(jnp.int32, (ROWS, BLOCK), 1)
    projected = (dot_nt(x[HALO : HALO + ROWS], weights[0]) + vectors[0:1]).astype(bf16).astype(f32) * score_scale
    for pair in range(2 * PAIRS):
        part = projected[:, pair * BLOCK : (pair + 1) * BLOCK]
        query[2 * pair] = jnp.where(lane < HEAD, part, 0.0).astype(bf16)
        query[2 * pair + 1] = jnp.where(lane >= HEAD, part, 0.0).astype(bf16)

    def inside(rows, first):
        index = first + lax.broadcasted_iota(jnp.int32, (rows, BLOCK), 0)
        return (index >= 0) & (index < seq_len)

    near_x = x[NEAR0 : NEAR0 + NEAR]
    near_inside = inside(NEAR, base - REACH1)
    far_x = x[FAR0 : FAR0 + FAR]
    far_inside = inside(FAR, base - HALO + FAR0)
    for c, near_ref, far_ref, rows_ref in ((1, near_keys, far_keys, key_rows), (2, near_values, far_values, value_rows)):
        near = dot_nt(near_x, weights[c, 0:wide])
        far = dot_nt(far_x, weights[c, wide:D])
        if c == 2:
            near = near + vectors[1:2, 0:wide]
            far = far + vectors[1:2, wide:D]
        for pair in range(PAIRS):
            lanes = slice(pair * BLOCK, (pair + 1) * BLOCK)
            near_ref[pair] = jnp.where(near_inside, near[:, lanes], 0.0).astype(bf16)
            low = jnp.where(far_inside, far[:, lanes], 0.0).astype(bf16)
            far_ref[pair] = low
            rows_ref[pair] = low.astype(f32)
    for at, rows_ref, pooled_ref in ((0, key_rows, pool_keys), (5, value_rows, pool_values)):
        for pair in range(PAIRS):
            lanes = slice(pair * BLOCK, (pair + 1) * BLOCK)
            total = None
            for tap in range(5):
                part = pool[at + tap : at + tap + 1, lanes] * rows_ref[pair, pl.ds(TAP0 + tap, POOLED, stride=4), :]
                total = part if total is None else total + part
            pooled_ref[pair] = total.astype(bf16)

    key_at = lax.broadcasted_iota(jnp.int32, (2 * BLOCK, BLOCK), 0)
    row_at = lax.broadcasted_iota(jnp.int32, (2 * BLOCK, BLOCK), 1)

    def bias(rows, cols, reach):
        same = jnp.where(rows < length, 1, 0) == jnp.where(cols < length, 1, 0)
        seen = (jnp.abs(rows - cols) <= reach) & same & (cols >= 0) & (cols < seq_len)
        return jnp.where(seen, 0.0, masked_score)

    blocks = ROWS // BLOCK
    for block in range(blocks):
        rows = base + block * BLOCK + row_at
        near_mask[block] = bias(rows, base + block * BLOCK - REACH1 + key_at, REACH1)
        far_mask[block] = bias(rows, base - REACH2 + 4 * key_at, REACH2)

    def attend(keys, head, block, mask):
        rows = slice(block * BLOCK, (block + 1) * BLOCK)
        scores = dot_nt(keys, query[head, rows]) + mask[block]
        raised = jnp.exp(scores - jnp.max(scores, axis=0, keepdims=True))
        low = (raised * (1.0 / jnp.sum(raised, axis=0, keepdims=True))).astype(bf16)
        chance[head, block] = low
        return low

    def near_pair(pair, carry):
        turned = turn(near_values[pair])
        lanes = pl.ds(pl.multiple_of(pair * BLOCK, BLOCK), BLOCK)
        for block in range(blocks):
            window = slice(block * BLOCK, (block + 2) * BLOCK)
            parts = []
            for e in range(2):
                low = attend(near_keys[pair, window], 2 * pair + e, block, near_mask)
                parts.append(dot(turned[e * HEAD : (e + 1) * HEAD, window], low))
            rows = slice(block * BLOCK, (block + 1) * BLOCK)
            mixed[rows, lanes] = turn(jnp.concatenate(parts, axis=0))
        return carry

    def far_pair(pair, carry):
        turned = turn(pool_values[pair])
        lanes = pl.ds(pl.multiple_of((pair + PAIRS) * BLOCK, BLOCK), BLOCK)
        for block in range(blocks):
            parts = []
            for e in range(2):
                low = attend(pool_keys[pair], 2 * PAIRS + 2 * pair + e, block, far_mask)
                parts.append(dot(turned[e * HEAD : (e + 1) * HEAD], low))
            rows = slice(block * BLOCK, (block + 1) * BLOCK)
            mixed[rows, lanes] = turn(jnp.concatenate(parts, axis=0))
        return carry

    lax.fori_loop(0, PAIRS, near_pair, 0)
    lax.fori_loop(0, PAIRS, far_pair, 0)


def attend_forward(place, slots, x, vectors, pool):
    own, mine, other, near_diag, far_diag = slots
    shapes = (
        struct((3, D, D), bf16),
        struct((D, D), bf16),
        struct((ROWS, D), bf16),
        struct((HEADS, ROWS, BLOCK), bf16),
        struct((PAIRS, NEAR, BLOCK), bf16),
        struct((PAIRS, NEAR, BLOCK), bf16),
        struct((PAIRS, FAR, BLOCK), bf16),
        struct((PAIRS, FAR, BLOCK), bf16),
        struct((PAIRS, POOLED, BLOCK), bf16),
        struct((PAIRS, POOLED, BLOCK), bf16),
        struct((HEADS, ROWS // BLOCK, 2 * BLOCK, BLOCK), bf16),
    )
    return pl.pallas_call(
        attend_forward_kernel,
        out_shape=shapes,
        in_specs=[SM] + [VM] * 8,
        out_specs=tuple([VM] * len(shapes)),
        scratch_shapes=[
            pltpu.VMEM((PAIRS, FAR, BLOCK), f32),
            pltpu.VMEM((PAIRS, FAR, BLOCK), f32),
            pltpu.VMEM((ROWS // BLOCK, 2 * BLOCK, BLOCK), f32),
            pltpu.VMEM((ROWS // BLOCK, 2 * BLOCK, BLOCK), f32),
        ],
        compiler_params=params(),
        cost_estimate=cost(5e9, 20e6, 2e6),
        name="attend_forward",
    )(place, own, mine, other, near_diag, far_diag, x, vectors, pool)


def attend_backward_kernel(
    grad, query, near_keys, near_values, far_keys, far_values, pool_keys, pool_values, chance, pool,
    query_grad, near_low, far_low, near_own, pool_own, to_left, to_right, query_sum, pool_sum,
    near_total, pool_total, far_rows, shifted,
):
    blocks = ROWS // BLOCK
    near_total[...] = jnp.zeros_like(near_total)
    pool_total[...] = jnp.zeros_like(pool_total)
    query_grad[0:REACH1] = jnp.zeros((REACH1, D), bf16)
    query_grad[NEAR - REACH1 : NEAR] = jnp.zeros((REACH1, D), bf16)

    def back(values, turned, head, block, window):
        rows = slice(block * BLOCK, (block + 1) * BLOCK)
        part = grad[head, rows]
        low = chance[head, block]
        wide = low.astype(f32)
        chance_grad = dot_nt(values, part)
        mean = jnp.sum(wide * chance_grad, axis=0, keepdims=True)
        score_grad = (wide * (chance_grad - mean)).astype(bf16)
        key_grad = dot(score_grad, query[head, rows])
        value_grad = dot(low, part)
        return (dot(turned, score_grad), key_grad, value_grad)

    def put_query(parts, pair, block):
        turned = jnp.transpose(jnp.concatenate(parts, axis=0)) * score_scale
        lanes = pl.ds(pl.multiple_of(pair * BLOCK, BLOCK), BLOCK)
        query_grad[REACH1 + block * BLOCK : REACH1 + (block + 1) * BLOCK, lanes] = turned.astype(bf16)
        return col_sum(turned)

    def near_pair(pair, carry):
        turned = turn(near_keys[pair])
        sums = jnp.zeros((1, BLOCK), f32)
        for block in range(blocks):
            window = slice(block * BLOCK, (block + 2) * BLOCK)
            parts = []
            keys = None
            values = None
            for e in range(2):
                results = back(
                    near_values[pair, window], turned[e * HEAD : (e + 1) * HEAD, window], 2 * pair + e, block, window
                )
                parts.append(results[0])
                keys = results[1] if keys is None else keys + results[1]
                values = results[2] if values is None else values + results[2]
            near_total[0, pair, window] += keys
            near_total[1, pair, window] += values
            sums = sums + put_query(parts, pair, block)
        query_sum[pair] = sums
        return carry

    def far_pair(pair, carry):
        turned = turn(pool_keys[pair])
        sums = jnp.zeros((1, BLOCK), f32)
        for block in range(blocks):
            parts = []
            keys = None
            values = None
            for e in range(2):
                results = back(
                    pool_values[pair], turned[e * HEAD : (e + 1) * HEAD], 2 * PAIRS + 2 * pair + e, block, None
                )
                parts.append(results[0])
                keys = results[1] if keys is None else keys + results[1]
                values = results[2] if values is None else values + results[2]
            pool_total[0, pair] += keys
            pool_total[1, pair] += values
            sums = sums + put_query(parts, PAIRS + pair, block)
        query_sum[PAIRS + pair] = sums
        return carry

    lax.fori_loop(0, PAIRS, near_pair, 0)
    lax.fori_loop(0, PAIRS, far_pair, 0)

    side = REACH2 // 4
    own_pool = ROWS // 4
    for kind in range(2):
        near_low[kind] = near_total[kind].astype(bf16)
        near_own[kind] = near_total[kind, :, REACH1 : REACH1 + ROWS]
        pool_own[kind] = pool_total[kind, :, side : side + own_pool + 8]
        to_left[kind, :, 0:REACH1] = near_total[kind, :, 0:REACH1].astype(bf16)
        to_left[kind, :, REACH1 : REACH1 + side + 16] = pool_total[kind, :, 0 : side + 16].astype(bf16)
        to_right[kind, :, 0:REACH1] = near_total[kind, :, NEAR - REACH1 : NEAR].astype(bf16)
        to_right[kind, :, REACH1 : REACH1 + side] = pool_total[kind, :, side + own_pool :].astype(bf16)

    for kind, rows_ref in ((0, far_keys), (1, far_values)):
        for pair in range(PAIRS):
            lanes = slice(pair * BLOCK, (pair + 1) * BLOCK)
            far_rows[0:FAR] = rows_ref[pair].astype(f32)
            pooled = pool_total[kind, pair]
            for tap in range(5):
                pool_sum[5 * kind + tap : 5 * kind + tap + 1, lanes] = col_sum(
                    pooled * far_rows[pl.ds(TAP0 + tap, POOLED, stride=4), :]
                )
            shifted[0:8] = jnp.zeros((8, BLOCK), f32)
            shifted[8 : 8 + POOLED] = pooled
            weight = [pool[5 * kind + tap : 5 * kind + tap + 1, lanes] for tap in range(5)]
            first = FAR0 + TAP0
            far_rows[0 : first + 2] = jnp.zeros((first + 2, BLOCK), f32)
            far_rows[EXT - 72 : EXT] = jnp.zeros((72, BLOCK), f32)
            far_rows[pl.ds(first, POOLED, stride=4), :] = weight[0] * pooled + weight[4] * shifted[7 : 7 + POOLED]
            for tap in range(1, 4):
                far_rows[pl.ds(first + tap, POOLED, stride=4), :] = weight[tap] * pooled
            far_rows[first + 4 * POOLED : first + 4 * POOLED + 1] = weight[4] * pooled[POOLED - 1 : POOLED]
            far_low[kind, pair] = far_rows[...].astype(bf16)


def attend_backward(grad, query, near_keys, near_values, far_keys, far_values, pool_keys, pool_values, chance, pool):
    side = REACH2 // 4
    shapes = (
        struct((NEAR, D), bf16),
        struct((2, PAIRS, NEAR, BLOCK), bf16),
        struct((2, PAIRS, EXT, BLOCK), bf16),
        struct((2, PAIRS, ROWS, BLOCK), f32),
        struct((2, PAIRS, ROWS // 4 + 8, BLOCK), f32),
        struct((2, PAIRS, REACH1 + side + 16, BLOCK), bf16),
        struct((2, PAIRS, REACH1 + side, BLOCK), bf16),
        struct((2 * PAIRS, 1, BLOCK), f32),
        struct((10, PAIRS * BLOCK), f32),
    )
    return pl.pallas_call(
        attend_backward_kernel,
        out_shape=shapes,
        in_specs=[VM] * 10,
        out_specs=tuple([VM] * len(shapes)),
        scratch_shapes=[
            pltpu.VMEM((2, PAIRS, NEAR, BLOCK), f32),
            pltpu.VMEM((2, PAIRS, POOLED, BLOCK), f32),
            pltpu.VMEM((EXT, BLOCK), f32),
            pltpu.VMEM((POOLED + 8, BLOCK), f32),
        ],
        compiler_params=params(),
        cost_estimate=cost(5e9, 20e6, 0),
        name="attend_backward",
    )(grad, query, near_keys, near_values, far_keys, far_values, pool_keys, pool_values, chance, pool)


def start_pieces(pieces, held, sems):
    own, mine, other, near_diag, far_diag = pieces
    copies = []
    for at, ref, part in ((0, own, 0), (1, own, 1), (2, mine, 0), (3, mine, 1), (4, other, 0), (5, other, 1)):
        copies.append(pltpu.make_async_copy(ref.at[pl.ds(part * SUB, SUB)], held.at[at], sems.at[at]))
    copies.append(pltpu.make_async_copy(near_diag, held.at[6], sems.at[6]))
    copies.append(pltpu.make_async_copy(far_diag, held.at[7], sems.at[7]))
    for copy in copies:
        copy.start()
    return copies


def feed_forward_kernel(
    mixed, out_weight, inputs, vectors, bias, own, mine, other, near_diag, far_diag,
    normed, inverse, first_low, act, slope,
    held, total, sems,
):
    copies = start_pieces((own, mine, other, near_diag, far_diag), held, sems)
    total[...] = dot(mixed[...], out_weight[...])

    def rows_step(i, carry):
        rows = pl.ds(pl.multiple_of(i * BLOCK, BLOCK), BLOCK)
        value = inputs[rows] + total[rows] + vectors[2:3]
        centered = value - row_mean(value)
        inv = lax.rsqrt(row_mean(centered * centered) + norm_eps)
        z = centered * inv
        normed[rows] = z
        inverse[rows] = inv
        first_low[rows] = (z * vectors[4:5] + vectors[5:6]).astype(bf16)
        return carry

    lax.fori_loop(0, ROWS // BLOCK, rows_step, 0)
    for copy in copies:
        copy.wait()

    def hidden_step(j, carry):
        for half in range(2):
            rows = slice(half * (ROWS // 2), (half + 1) * (ROWS // 2))
            pre = dot_nt(first_low[rows], held[j]) + bias[j]
            gate = 0.5 + 0.5 * lax.erf(pre * math.sqrt(0.5))
            act[j, rows] = (pre * gate).astype(bf16)
            slope[j, rows] = (gate + pre * (jnp.exp(-0.5 * pre * pre) * (1.0 / math.sqrt(2.0 * math.pi)))).astype(bf16)
        return carry

    lax.fori_loop(0, 8, hidden_step, 0)


def feed_forward(mixed, out_weight, inputs, vectors, bias, pieces):
    shapes = (
        struct((ROWS, D), f32),
        struct((ROWS, 1), f32),
        struct((ROWS, D), bf16),
        struct((8, ROWS, SUB), bf16),
        struct((8, ROWS, SUB), bf16),
    )
    return pl.pallas_call(
        feed_forward_kernel,
        out_shape=shapes,
        in_specs=[VM] * 5 + [HB] * 5,
        out_specs=tuple([VM] * len(shapes)),
        scratch_shapes=[
            pltpu.VMEM((8, SUB, D), bf16),
            pltpu.VMEM((ROWS, D), f32),
            pltpu.SemaphoreType.DMA((8,)),
        ],
        compiler_params=params(),
        cost_estimate=cost(3e9, 16e6, 3e6),
        name="feed_forward",
    )(mixed, out_weight, inputs, vectors, bias, *pieces)


def feed_back_kernel(
    act, slope, normed, inverse, incoming, vectors, out_weight,
    in_own, in_mine, in_other, in_near, in_far, out_own, out_mine, out_other, out_near, out_far,
    block_low, branch_low, pre_low, attn_low, attn_grad, heads_grad, sums, bias_sum,
    in_held, out_held, total, second, in_sems, out_sems,
):
    out_copies = start_pieces((out_own, out_mine, out_other, out_near, out_far), out_held, out_sems)
    in_copies = start_pieces((in_own, in_mine, in_other, in_near, in_far), in_held, in_sems)
    sums[...] = jnp.zeros_like(sums)
    total[...] = jnp.zeros_like(total)
    for copy in out_copies:
        copy.wait()

    def branch_step(j, carry):
        total[...] += dot(act[j], out_held[j])
        return carry

    lax.fori_loop(0, 8, branch_step, 0)

    def second_step(i, carry):
        rows = pl.ds(pl.multiple_of(i * BLOCK, BLOCK), BLOCK)
        first = normed[rows] * vectors[4:5] + vectors[5:6]
        value = first + total[rows] + vectors[3:4]
        centered = value - row_mean(value)
        inv = lax.rsqrt(row_mean(centered * centered) + norm_eps)
        z = centered * inv
        block_low[rows] = (z * vectors[6:7] + vectors[7:8]).astype(bf16)
        upper = incoming[rows]
        scaled = upper * vectors[6:7]
        grad = inv * (scaled - row_mean(scaled) - z * row_mean(scaled * z))
        second[rows] = grad
        branch_low[rows] = grad.astype(bf16)
        sums[3:4] += col_sum(grad)
        sums[6:7] += col_sum(upper * z)
        sums[7:8] += col_sum(upper)
        return carry

    lax.fori_loop(0, ROWS // BLOCK, second_step, 0)
    total[...] = second[...]
    for copy in in_copies:
        copy.wait()

    def hidden_step(j, carry):
        act_grad = dot_nt(branch_low[...], out_held[j])
        pre_grad = act_grad * slope[j].astype(f32)
        low = pre_grad.astype(bf16)
        pre_low[j] = low
        bias_sum[j] = col_sum(pre_grad)
        total[...] += dot(low, in_held[j])
        return carry

    lax.fori_loop(0, 8, hidden_step, 0)

    def first_step(i, carry):
        rows = pl.ds(pl.multiple_of(i * BLOCK, BLOCK), BLOCK)
        z = normed[rows]
        first_grad = total[rows]
        scaled = first_grad * vectors[4:5]
        grad = inverse[rows] * (scaled - row_mean(scaled) - z * row_mean(scaled * z))
        attn_grad[rows] = grad
        attn_low[rows] = grad.astype(bf16)
        sums[2:3] += col_sum(grad)
        sums[4:5] += col_sum(first_grad * z)
        sums[5:6] += col_sum(first_grad)
        return carry

    lax.fori_loop(0, ROWS // BLOCK, first_step, 0)
    total[...] = dot_nt(attn_low[...], out_weight[...])
    lane = lax.broadcasted_iota(jnp.int32, (ROWS, BLOCK), 1)
    for pair in range(2 * PAIRS):
        part = total[:, pair * BLOCK : (pair + 1) * BLOCK]
        heads_grad[2 * pair] = jnp.where(lane < HEAD, part, 0.0).astype(bf16)
        heads_grad[2 * pair + 1] = jnp.where(lane >= HEAD, part, 0.0).astype(bf16)


def feed_back(act, slope, normed, inverse, incoming, vectors, out_weight, in_pieces, out_pieces):
    shapes = (
        struct((ROWS, D), bf16),
        struct((ROWS, D), bf16),
        struct((8, ROWS, SUB), bf16),
        struct((ROWS, D), bf16),
        struct((ROWS, D), f32),
        struct((HEADS, ROWS, BLOCK), bf16),
        struct((8, D), f32),
        struct((8, 1, SUB), f32),
    )
    return pl.pallas_call(
        feed_back_kernel,
        out_shape=shapes,
        in_specs=[VM] * 7 + [HB] * 10,
        out_specs=tuple([VM] * len(shapes)),
        scratch_shapes=[
            pltpu.VMEM((8, SUB, D), bf16),
            pltpu.VMEM((8, SUB, D), bf16),
            pltpu.VMEM((ROWS, D), f32),
            pltpu.VMEM((ROWS, D), f32),
            pltpu.SemaphoreType.DMA((8,)),
            pltpu.SemaphoreType.DMA((8,)),
        ],
        compiler_params=params(),
        cost_estimate=cost(8e9, 30e6, 0),
        name="feed_back",
    )(act, slope, normed, inverse, incoming, vectors, out_weight, *in_pieces, *out_pieces)


def ffn_grad_kernel(order, rows, cols, own, sent, turned):
    @pl.when(pl.program_id(0) == 0)
    def _():
        turned[...] = dot_nt(order[...], rows[...]).astype(bf16)

    result = dot(turned[...], cols[0]).astype(bf16)
    own[0] = result[: D // 2]
    sent[0] = result[D // 2 :]


def ffn_grad(order, rows, cols):
    block = pl.BlockSpec((1, D // 2, SUB), lambda j: (j, 0, 0))
    return pl.pallas_call(
        ffn_grad_kernel,
        out_shape=(struct((8, D // 2, SUB), bf16),) * 2,
        grid=(8,),
        in_specs=[
            pl.BlockSpec((D, D), lambda j: (0, 0)),
            pl.BlockSpec((ROWS, D), lambda j: (0, 0)),
            pl.BlockSpec((1, ROWS, SUB), lambda j: (j, 0, 0)),
        ],
        out_specs=(block, block),
        scratch_shapes=[pltpu.VMEM((D, ROWS), bf16)],
        compiler_params=params(32),
        cost_estimate=cost(3e9, 10e6),
        name="ffn_grad",
    )(order, rows, cols)


def attn_weight_grad_kernel(order, x, attn_low, mixed, query_grad, near_low, far_low, own, sent, turned, held):
    turned[...] = dot_nt(order[...], x[...]).astype(bf16)
    near_x = turned[:, NEAR0 : NEAR0 + NEAR]
    held[0] = dot(near_x, query_grad[...])
    for kind in range(2):
        near = jnp.concatenate([near_low[kind, pair] for pair in range(PAIRS)], axis=1)
        far = jnp.concatenate([far_low[kind, pair] for pair in range(PAIRS)], axis=1)
        held[1 + kind, :, 0 : D // 2] = dot(near_x, near)
        held[1 + kind, :, D // 2 : D] = dot(turned[...], far)
    held[3] = dot(dot_nt(order[...], attn_low[...]).astype(bf16), mixed[...])

    rows = D // 4
    lane = lax.broadcasted_iota(jnp.int32, (rows, BLOCK), 1)

    def step(i, carry):
        here = pl.ds(pl.multiple_of(i * rows, rows), rows)
        for pair in range(2):
            even, odd = 2 * pair, 2 * pair + 1
            tiles = [[held[c, here, (3 * pair + t) * BLOCK : (3 * pair + t + 1) * BLOCK] for t in range(3)] for c in range(4)]
            for lvl, whole in ((even, 0), (odd, 2)):
                parts = [tiles[c][whole] for c in range(4)]
                for c in (0, 2):
                    a, b = (tiles[c][1], tiles[c + 1][1])
                    if lvl == even:
                        parts.append(jnp.where(lane < HEAD, a, pltpu.roll(b, HEAD, 1)))
                    else:
                        parts.append(jnp.where(lane < HEAD, pltpu.roll(a, HEAD, 1), b))
                for t, part in enumerate(parts):
                    own_or_sent(lvl, i, t, part.astype(bf16))
        return carry

    def own_or_sent(lvl, i, t, part):
        lanes = slice(t * BLOCK, (t + 1) * BLOCK)

        @pl.when(i < 2)
        def _():
            own[lvl, pl.ds(pl.multiple_of(i * rows, rows), rows), lanes] = part

        @pl.when(i >= 2)
        def _():
            sent[lvl, pl.ds(pl.multiple_of((i - 2) * rows, rows), rows), lanes] = part

    lax.fori_loop(0, 4, step, 0)


def attn_weight_grad(order, x, attn_low, mixed, query_grad, near_low, far_low):
    return pl.pallas_call(
        attn_weight_grad_kernel,
        out_shape=(struct((4, D // 2, D), bf16),) * 2,
        in_specs=[VM] * 7,
        out_specs=(VM, VM),
        scratch_shapes=[pltpu.VMEM((D, EXT), bf16), pltpu.VMEM((4, D, D), f32)],
        compiler_params=params(),
        cost_estimate=cost(7e9, 16e6),
        name="attn_weight_grad",
    )(order, x, attn_low, mixed, query_grad, near_low, far_low)


def merge_kernel(n, at_own, at_got, own, got, send, keep):
    total = own[...].astype(f32) + got[...].astype(f32)
    step = pl.program_id(0)

    @pl.when(step < n // 2)
    def _():
        send[...] = total.astype(bf16)

    @pl.when(step >= n // 2)
    def _():
        keep[...] = total


def merge(own, got, at_own, at_got):
    n, rows, cols = own.shape
    block = (1, rows, cols)
    return pl.pallas_call(
        functools.partial(merge_kernel, n),
        out_shape=(struct((n // 2, rows, cols), bf16), struct((n // 2, rows, cols), f32)),
        grid_spec=pltpu.PrefetchScalarGridSpec(
            num_scalar_prefetch=2,
            grid=(n,),
            in_specs=[
                pl.BlockSpec(block, lambda i, a, b: (a[i], 0, 0)),
                pl.BlockSpec(block, lambda i, a, b: (b[i], 0, 0)),
            ],
            out_specs=(
                pl.BlockSpec(block, lambda i, a, b: (jnp.minimum(i, n // 2 - 1), 0, 0)),
                pl.BlockSpec(block, lambda i, a, b: (jnp.maximum(i - n // 2, 0), 0, 0)),
            ),
        ),
        compiler_params=params(32),
        cost_estimate=cost(1e6, 9e6),
        name="merge",
    )(at_own, at_got, own, got)


def input_grad_kernel(
    query_grad, near_own, pool_own, from_left, from_right, weights, attn_grad, pool,
    low, value_sum,
    pooled, rows_held, grads,
):
    side = REACH2 // 4
    own_pool = ROWS // 4
    wide = PAIRS * BLOCK
    for kind in range(2):
        for pair in range(PAIRS):
            lanes = slice(pair * BLOCK, (pair + 1) * BLOCK)
            rows_held[...] = near_own[kind, pair]
            rows_held[0:REACH1] += from_left[kind, pair, 0:REACH1].astype(f32)
            rows_held[ROWS - REACH1 : ROWS] += from_right[kind, pair, 0:REACH1].astype(f32)
            if kind:
                value_sum[:, lanes] = col_sum(rows_held[...])
            grads[kind, :, lanes] = rows_held[...].astype(bf16)

            pooled[...] = pool_own[kind, pair]
            pooled[0:side] += from_left[kind, pair, REACH1 : REACH1 + side].astype(f32)
            pooled[side : own_pool + 8] += from_right[kind, pair, REACH1 : REACH1 + side + 8].astype(f32)
            here, following = pooled[0:own_pool], pooled[1 : own_pool + 1]
            weight = [pool[5 * kind + tap : 5 * kind + tap + 1, lanes] for tap in range(5)]
            rows_held[pl.ds(0, own_pool, stride=4), :] = weight[2] * here
            rows_held[pl.ds(1, own_pool, stride=4), :] = weight[3] * here
            rows_held[pl.ds(2, own_pool, stride=4), :] = weight[4] * here + weight[0] * following
            rows_held[pl.ds(3, own_pool, stride=4), :] = weight[1] * following
            lanes = slice(wide + pair * BLOCK, wide + (pair + 1) * BLOCK)
            if kind:
                value_sum[:, lanes] = col_sum(rows_held[...])
            grads[kind, :, lanes] = rows_held[...].astype(bf16)
    total = attn_grad[...] + dot(query_grad[REACH1 : REACH1 + ROWS], weights[0])
    total = total + dot(grads[0], weights[1])
    low[...] = (total + dot(grads[1], weights[2])).astype(bf16)


def input_grad_of(query_grad, near_own, pool_own, from_left, from_right, weights, attn_grad, pool):
    return pl.pallas_call(
        input_grad_kernel,
        out_shape=(struct((ROWS, D), bf16), struct((1, D), f32)),
        in_specs=[VM] * 8,
        out_specs=(VM, VM),
        scratch_shapes=[
            pltpu.VMEM((ROWS // 4 + 8, BLOCK), f32),
            pltpu.VMEM((ROWS, BLOCK), f32),
            pltpu.VMEM((2, ROWS, D), bf16),
        ],
        compiler_params=params(32),
        cost_estimate=cost(2e9, 9e6),
        name="input_grad",
    )(query_grad, near_own, pool_own, from_left, from_right, weights, attn_grad, pool)


def gather_shards(own, core):
    half = own.shape[0] // 2
    mine = lax.ppermute(own, PLACE, MINE)
    part = lax.dynamic_slice_in_dim(mine, core * half, half, 0)
    near_diag = lax.ppermute(part, PLACE, CROSS)
    other = lax.ppermute(mine, "seq", SWAP)
    far_diag = lax.ppermute(near_diag, "seq", SWAP)
    return (own, mine, other, near_diag, far_diag)


def reduce_grads(own, sent, at_own, at_got, dp, dp_index):
    n, rows, cols = own.shape
    got = lax.ppermute(sent, "seq", SWAP)
    send, keep = merge(own, got, at_own, at_got)
    quarter = n // 4
    first = lax.ppermute(send, PLACE, MINE)
    passed = bfloat(keep[quarter:] + first[quarter:].astype(f32))
    second = lax.ppermute(passed, PLACE, CROSS)
    total = keep[:quarter] + first[:quarter].astype(f32) + second.astype(f32)
    width = rows // dp
    total = total.reshape(quarter, dp, width, cols)
    step = 1
    while step < dp:
        split = total.reshape(quarter, -1, 2, width, cols)
        bit = (dp_index // step) % 2
        keep = lax.dynamic_index_in_dim(split, bit, 2, False)
        send = lax.dynamic_index_in_dim(split, 1 - bit, 2, False)
        got = lax.ppermute(bfloat(send), "dp", [(i, i ^ step) for i in range(dp)])
        total = keep + got.astype(f32)
        step *= 2
    return total[:, 0]


def sum_everywhere(value, dp):
    value = value + lax.ppermute(value, "seq", SWAP)
    for step in (1, 2):
        value = value + lax.ppermute(value, "lvl", [(i, i ^ step) for i in range(4)])
    step = 1
    while step < dp:
        value = value + lax.ppermute(value, "dp", [(i, i ^ step) for i in range(dp)])
        step *= 2
    return value


def gather_rows(own, count, core, level, chunk_of):
    mine = lax.ppermute(own, PLACE, MINE)
    both = lax.ppermute(jnp.concatenate([own, mine], axis=0), PLACE, CROSS)
    size = own.shape[0]
    along = jnp.where(core == 0, 1, 2)
    result = jnp.zeros((count, own.shape[1]), f32)
    pieces = ((own, level), (mine, level ^ along), (both[:size], level ^ (3 - along)), (both[size:], level ^ 3))
    for piece, owner in pieces:
        result = lax.dynamic_update_slice_in_dim(result, piece.astype(f32), chunk_of(owner) * size, 0)
    return result


def on_device(
    tokens,
    cotangent,
    lengths,
    qkv_weight,
    out_weight,
    ffn_in_weight,
    ffn_out_weight,
    vectors,
    ffn_bias,
    pool_kernel,
    qkv_moments,
    out_moments,
    ffn_in_moments,
    ffn_out_moments,
    vector_moments,
    bias_moments,
    pool_moments,
):
    dp = lax.axis_size("dp")
    dp_index = lax.axis_index("dp")
    core = lax.axis_index("seq")
    level = lax.axis_index("lvl")
    length = lengths[0]
    count = tokens.shape[1]
    size = count // 4
    seq_len = 2 * count
    half = HEADS // 2
    along = jnp.where(core == 0, 1, 2)
    slots = [level, level ^ along, level ^ (3 - along), level ^ 3]

    def chunk_of(owner):
        order = owner ^ (owner >> 1)
        return jnp.where(core == 0, order, 3 - order)

    chunk = chunk_of(level)
    base = core * count + chunk * size
    width = D // (2 * dp)

    local = qkv_weight.shape[2]
    attn_own = jnp.concatenate(
        [bfloat(qkv_weight).transpose(0, 2, 1).reshape(3 * local, D), bfloat(out_weight)], axis=0
    )
    attn_pieces = [p.reshape(-1, local, D) for p in gather_shards(attn_own, core)]
    in_pieces = gather_shards(bfloat(ffn_in_weight), core)
    out_pieces = gather_shards(bfloat(ffn_out_weight), core)
    hidden = ffn_in_weight.shape[0]
    bias_parts = [lax.dynamic_slice_in_dim(ffn_bias, s * hidden, hidden) for s in slots[:3]]
    bias_parts += [lax.dynamic_slice_in_dim(ffn_bias, slots[3] * hidden + c * SUB, SUB) for c in (core, 1 - core)]
    bias = jnp.concatenate(bias_parts).reshape(8, 1, SUB)

    inputs = lax.dynamic_slice_in_dim(tokens[0], chunk * size, size, 0)
    incoming = lax.dynamic_slice_in_dim(cotangent[0], chunk * size, size, 0)
    edge = jnp.where(core == 0, tokens[0, count - HALO :], tokens[0, :HALO])
    edge = lax.ppermute(bfloat(edge), "seq", SWAP)
    before = jnp.where(core == 0, jnp.zeros_like(edge), edge)
    after = jnp.where(core == 0, edge, jnp.zeros_like(edge))
    extended = jnp.concatenate([before, bfloat(tokens[0]), after], axis=0)
    extended = lax.dynamic_slice_in_dim(extended, chunk * size, EXT, 0)

    pool_lanes = jnp.repeat(pool_kernel.reshape(10, half), HEAD, axis=1)
    place = jnp.stack([*slots, core, base, length, seq_len]).astype(jnp.int32)
    row = jnp.arange(D)
    side, rest = (row // (D // 2), row % (D // 2))
    feature = (rest // width) * (2 * width) + jnp.where(side == 0, core, 1 - core) * width + rest % width
    order = (feature[:, None] == row[None, :]).astype(bf16)

    (weights, out_all, mixed, query, near_keys, near_values, far_keys, far_values, pool_keys, pool_values, chance) = (
        attend_forward(place, attn_pieces, extended, vectors, pool_lanes)
    )
    normed, inverse, first_low, act, slope = feed_forward(mixed, out_all, inputs, vectors, bias, in_pieces)
    block_low, branch_low, pre_low, attn_low, attn_grad, heads_grad, sums, bias_sum = feed_back(
        act, slope, normed, inverse, incoming, vectors, out_all, in_pieces, out_pieces
    )
    block_out = gather_rows(block_low, count, core, level, chunk_of)

    ffn_own = jnp.stack([2, 3, 6 + core, 7 - core, 0, 1, 4, 5]).astype(jnp.int32)
    ffn_got = jnp.stack([4, 5, 7 - core, 6 + core, 0, 1, 2, 3]).astype(jnp.int32)
    attn_at = jnp.stack([slots[1], slots[3], slots[0], slots[2]]).astype(jnp.int32)
    out_shard = reduce_grads(*ffn_grad(order, branch_low, act), ffn_own, ffn_got, dp, dp_index)
    in_shard = reduce_grads(*ffn_grad(order, first_low, pre_low), ffn_own, ffn_got, dp, dp_index)

    (query_grad, near_low, far_low, near_own, pool_own, to_left, to_right, query_sum, pool_sum) = attend_backward(
        heads_grad, query, near_keys, near_values, far_keys, far_values, pool_keys, pool_values, chance, pool_lanes
    )
    from_right = lax.ppermute(to_left, PLACE, LEFTWARD)
    from_left = lax.ppermute(to_right, PLACE, RIGHTWARD)
    attn_shard = reduce_grads(
        *attn_weight_grad(order, extended, attn_low, mixed, query_grad, near_low, far_low), attn_at, attn_at, dp, dp_index
    )[0]
    input_low, value_sum = input_grad_of(
        query_grad, near_own, pool_own, from_left, from_right, weights, attn_grad, pool_lanes
    )
    input_grad = gather_rows(input_low, count, core, level, chunk_of)

    def columns(c):
        whole = attn_shard[:, c * BLOCK : (c + 1) * BLOCK]
        at = 4 * BLOCK + c * HEAD
        rest = attn_shard[:, at : at + HEAD]
        even = jnp.concatenate([whole, rest], axis=1)
        return jnp.where(level % 2 == 0, even, jnp.concatenate([rest, whole], axis=1))

    qkv_shard = jnp.stack([columns(c) for c in range(3)])
    out_shard_w = columns(3).T
    ffn_in_shard = in_shard.transpose(0, 2, 1).reshape(hidden, width)
    ffn_out_shard = out_shard.transpose(0, 2, 1).reshape(hidden, width)

    vector_part = jnp.concatenate([query_sum.reshape(1, D), value_sum, sums[2:]], axis=0)
    bias_part = jnp.zeros((FF,), f32)
    bias_flat = bias_sum.reshape(-1)
    for index in range(3):
        bias_part = lax.dynamic_update_slice(
            bias_part, bias_flat[index * hidden : (index + 1) * hidden], (slots[index] * hidden,)
        )
    for index, c in ((6, core), (7, 1 - core)):
        bias_part = lax.dynamic_update_slice(
            bias_part, bias_flat[index * SUB : (index + 1) * SUB], (slots[3] * hidden + c * SUB,)
        )
    pool_local = jnp.sum(pool_sum.reshape(10, half, HEAD), axis=-1)
    matrix_squares = jnp.stack(
        [
            jnp.sum(attn_shard * attn_shard),
            jnp.sum(in_shard * in_shard) + jnp.sum(out_shard * out_shard),
        ]
    )
    parts = [vector_part.reshape(-1), bias_part, pool_local.reshape(-1), matrix_squares]
    sizes = [p.shape[0] for p in parts]
    packed = jnp.concatenate(parts)
    packed = jnp.pad(packed, (0, -packed.shape[0] % 1024)).reshape(-1, 128)
    packed = sum_everywhere(packed, dp).reshape(-1)
    pieces = []
    at = 0
    for n in sizes:
        pieces.append(packed[at : at + n])
        at += n
    vectors_grad = pieces[0].reshape(8, D)
    bias_grad = pieces[1]
    pool_grad = pieces[2].reshape(pool_kernel.shape)
    summed_squares = pieces[3]
    squares = jnp.stack(
        [
            summed_squares[0],
            summed_squares[1],
            jnp.sum(vectors_grad * vectors_grad) + jnp.sum(bias_grad * bias_grad),
            jnp.sum(pool_grad * pool_grad),
        ]
    )
    group_norms = jnp.sqrt(squares)
    total = jnp.sqrt(jnp.sum(squares))
    param_count = 4 * D * D + 2 * FF * D + 8 * D + FF + 10 * half
    clip = jnp.minimum(1.0, max_rms * math.sqrt(param_count) / (total + 1e-06))
    shard_index = dp_index * 2 + core

    def own_slice(weight):
        return lax.dynamic_slice_in_dim(weight, shard_index * width, width, 1)

    qkv_step, qkv_moments_new = adamw(own_slice(qkv_weight), qkv_shard, qkv_moments, decay_rate, clip)
    out_step, out_moments_new = adamw(own_slice(out_weight), out_shard_w, out_moments, decay_rate, clip)
    ffn_in_step, ffn_in_moments_new = adamw(
        own_slice(ffn_in_weight), ffn_in_shard, ffn_in_moments, decay_rate, clip
    )
    ffn_out_step, ffn_out_moments_new = adamw(
        own_slice(ffn_out_weight), ffn_out_shard, ffn_out_moments, decay_rate, clip
    )
    vectors_step, vector_moments_new = adamw(vectors, vectors_grad, vector_moments, 0.0, clip)
    bias_step, bias_moments_new = adamw(ffn_bias, bias_grad, bias_moments, 0.0, clip)
    pool_step, pool_moments_new = adamw(pool_kernel, pool_grad, pool_moments, 0.0, clip)
    return (
        block_out[None],
        input_grad[None],
        qkv_shard,
        qkv_step,
        qkv_moments_new,
        out_shard_w,
        out_step,
        out_moments_new,
        ffn_in_shard,
        ffn_in_step,
        ffn_in_moments_new,
        ffn_out_shard,
        ffn_out_step,
        ffn_out_moments_new,
        vectors_grad,
        vectors_step,
        vector_moments_new,
        bias_grad,
        bias_step,
        bias_moments_new,
        pool_grad,
        pool_step,
        pool_moments_new,
        clip,
        group_norms,
    )


def solution(mesh):
    in_specs = (
        P("dp", "seq", None),
        P("dp", "seq", None),
        P("dp"),
        P(None, None, "lvl"),
        P("lvl", None),
        P("lvl", None),
        P("lvl", None),
        P(),
        P(),
        P(),
        P(None, None, ("dp", "seq"), "lvl"),
        P(None, "lvl", ("dp", "seq")),
        P(None, "lvl", ("dp", "seq")),
        P(None, "lvl", ("dp", "seq")),
        P(),
        P(),
        P(),
    )
    out_specs = (
        P("dp", "seq", None),
        P("dp", "seq", None),
        P(None, ("dp", "seq"), "lvl"),
        P(None, ("dp", "seq"), "lvl"),
        P(None, None, ("dp", "seq"), "lvl"),
        P("lvl", ("dp", "seq")),
        P("lvl", ("dp", "seq")),
        P(None, "lvl", ("dp", "seq")),
        P("lvl", ("dp", "seq")),
        P("lvl", ("dp", "seq")),
        P(None, "lvl", ("dp", "seq")),
        P("lvl", ("dp", "seq")),
        P("lvl", ("dp", "seq")),
        P(None, "lvl", ("dp", "seq")),
        P(),
        P(),
        P(),
        P(),
        P(),
        P(),
        P(),
        P(),
        P(),
        P(),
        P(),
    )
    return jax.shard_map(
        on_device, mesh=mesh, in_specs=in_specs, out_specs=out_specs, check_vma=False
    )
```

```python
import functools
import math

import jax
import jax.numpy as jnp
from jax import lax
from jax.experimental import pallas as pl
from jax.experimental.pallas import tpu as pltpu
from jax.sharding import PartitionSpec as P

D = 768
HEADS = 12
HEAD = 64
FF = 3072
REACH1 = 64
REACH2 = 256
HALO = 320
ROWS = 512
EXT = ROWS + 2 * HALO
NEAR = ROWS + 2 * REACH1
NEAR0 = HALO - REACH1
FAR0 = 48
FAR = 1056
POOLED = 256
TAP0 = 14
BLOCK = 128
BLOCKS = ROWS // BLOCK
PAIRS = HEADS // 4

norm_eps = 1e-05
beta_first = 0.9
beta_second = 0.999
adam_eps = 1e-08
decay_rate = 0.01
adam_step = 10.0
max_rms = 1.0
masked_score = -1e30
score_scale = 1.0 / math.sqrt(HEAD)

f32 = jnp.float32
bf16 = jnp.bfloat16
SWAP = [(0, 1), (1, 0)]
MINE = [(i, i ^ 1) for i in range(4)] + [(4 + i, 4 + (i ^ 2)) for i in range(4)]
CROSS = [(i, i ^ 2) for i in range(4)] + [(4 + i, 4 + (i ^ 1)) for i in range(4)]
PATH = [0, 1, 3, 2, 6, 7, 5, 4]
RIGHTWARD = list(zip(PATH[:-1], PATH[1:]))
LEFTWARD = [(b, a) for a, b in RIGHTWARD]
PLACE = ("seq", "lvl")

SM = pl.BlockSpec(memory_space=pltpu.SMEM)
HB = pl.BlockSpec(memory_space=pltpu.HBM)


def bfloat(value):
    return value.astype(bf16)


def params(mib=56):
    return pltpu.CompilerParams(vmem_limit_bytes=mib * 1024 * 1024)


def struct(shape, dtype):
    return jax.ShapeDtypeStruct(shape, dtype)


def dot(a, b):
    return jnp.dot(a, b, preferred_element_type=f32)


def dot_nt(a, b):
    return lax.dot_general(a, b, (((1,), (1,)), ((), ())), preferred_element_type=f32)


def turn(value):
    return jnp.transpose(value.astype(f32)).astype(bf16)


def row_mean(value):
    return jnp.mean(value, axis=-1, keepdims=True)


def col_sum(value):
    return jnp.sum(value, axis=0, keepdims=True)


def whole(shape):
    return pl.BlockSpec(shape, lambda *_: (0,) * len(shape), pipeline_mode=pl.Buffered(1))


def wholes(operands):
    return [whole(operand.shape) for operand in operands]


def copy_when(condition, source, target, sem):
    @pl.when(condition)
    def _():
        pltpu.make_async_copy(source, target, sem).start()


def wait_when(condition, target, sem):
    @pl.when(condition)
    def _():
        pltpu.make_async_copy(target, target, sem).wait()


def fetch_attention(place, pieces, weights, out_weight, sems):
    own, mine, other, near_diag, far_diag = pieces
    core = place[4]
    local = own.shape[1]
    copies = []

    def rows_of(owner):
        return pl.ds(pl.multiple_of(owner * local, 64), local)

    for at, piece in enumerate((own, mine, other)):
        rows = rows_of(place[at])
        copies.append(pltpu.make_async_copy(piece.at[pl.ds(0, 3)], weights.at[:, rows], sems.at[at]))
        if out_weight is not None:
            copies.append(pltpu.make_async_copy(piece.at[3], out_weight.at[rows], sems.at[3 + at]))
    for copy in copies:
        copy.start()
    rows = rows_of(place[3])
    targets = [weights.at[pl.ds(0, 2), rows], weights.at[2, rows]]
    if out_weight is not None:
        targets.append(out_weight.at[rows])
    for condition, low, high in ((core == 0, near_diag, far_diag), (core != 0, far_diag, near_diag)):
        for at, source in enumerate((low, high.at[0], high.at[1])[: len(targets)]):
            copy_when(condition, source, targets[at], sems.at[6 + at])

    def wait():
        for copy in copies:
            copy.wait()
        for at, target in enumerate(targets):
            pltpu.make_async_copy(target, target, sems.at[6 + at]).wait()

    return wait


def prepare_kernel(place, edge, tokens, cotangent, low, inputs, incoming, near_mask, far_mask, x, sems):
    core, base, length, seq_len, chunk = [place[i] for i in range(4, 9)]
    first = pl.multiple_of(chunk * ROWS, ROWS)
    left, right = x.at[pl.ds(0, HALO)], x.at[pl.ds(HALO + ROWS, HALO)]
    middle = pltpu.make_async_copy(tokens.at[0, pl.ds(first, ROWS)], inputs, sems.at[0])
    upper = pltpu.make_async_copy(cotangent.at[0, pl.ds(first, ROWS)], incoming, sems.at[3])
    middle.start()
    upper.start()
    starts, ends = chunk == 0, chunk == 3
    left_at = pl.multiple_of(jnp.maximum(first - HALO, 0), 64)
    right_at = pl.multiple_of(jnp.minimum(first + ROWS, 4 * ROWS - HALO), 64)
    copy_when(jnp.logical_not(starts), tokens.at[0, pl.ds(left_at, HALO)], left, sems.at[1])
    copy_when(jnp.logical_and(starts, core == 1), edge, left, sems.at[1])
    copy_when(jnp.logical_not(ends), tokens.at[0, pl.ds(right_at, HALO)], right, sems.at[2])
    copy_when(jnp.logical_and(ends, core == 0), edge, right, sems.at[2])
    no_left = jnp.logical_and(starts, core == 0)
    no_right = jnp.logical_and(ends, core == 1)

    @pl.when(no_left)
    def _():
        x[0:HALO] = jnp.zeros((HALO, D), f32)

    @pl.when(no_right)
    def _():
        x[HALO + ROWS : EXT] = jnp.zeros((HALO, D), f32)

    key_at = lax.broadcasted_iota(jnp.int32, (2 * BLOCK, BLOCK), 0)
    row_at = lax.broadcasted_iota(jnp.int32, (2 * BLOCK, BLOCK), 1)

    def bias(rows, cols, reach):
        same = jnp.where(rows < length, 1, 0) == jnp.where(cols < length, 1, 0)
        seen = (jnp.abs(rows - cols) <= reach) & same & (cols >= 0) & (cols < seq_len)
        return jnp.where(seen, 0.0, masked_score)

    for block in range(BLOCKS):
        rows = base + block * BLOCK + row_at
        near_mask[block] = bias(rows, base + block * BLOCK - REACH1 + key_at, REACH1)
        far_mask[block] = bias(rows, base - REACH2 + 4 * key_at, REACH2)

    middle.wait()
    upper.wait()
    wait_when(jnp.logical_not(no_left), left, sems.at[1])
    wait_when(jnp.logical_not(no_right), right, sems.at[2])
    low[0:HALO] = x[0:HALO].astype(bf16)
    low[HALO : HALO + ROWS] = inputs[...].astype(bf16)
    low[HALO + ROWS : EXT] = x[HALO + ROWS : EXT].astype(bf16)


def prepare(place, edge, tokens, cotangent):
    shapes = (
        struct((EXT, D), bf16),
        struct((ROWS, D), f32),
        struct((ROWS, D), f32),
        struct((BLOCKS, 2 * BLOCK, BLOCK), f32),
        struct((BLOCKS, 2 * BLOCK, BLOCK), f32),
    )
    return pl.pallas_call(
        prepare_kernel,
        out_shape=shapes,
        grid=(1,),
        in_specs=[SM] + [HB] * 3,
        out_specs=tuple(wholes(shapes)),
        scratch_shapes=[pltpu.VMEM((EXT, D), f32), pltpu.SemaphoreType.DMA((4,))],
        compiler_params=params(18),
        name="prepare",
    )(place, edge, tokens, cotangent)


def project_kernel(
    place, low, own, mine, other, near_diag, far_diag, vectors, pool,
    out_weight, query, near_keys, near_values, far_keys, far_values, pool_keys, pool_values,
    weights, key_rows, value_rows, sems,
):
    base, seq_len = place[5], place[7]
    fetch_attention(place, (own, mine, other, near_diag, far_diag), weights, out_weight, sems)()
    wide = PAIRS * BLOCK
    lane = lax.broadcasted_iota(jnp.int32, (ROWS, BLOCK), 1)
    projected = (dot_nt(low[HALO : HALO + ROWS], weights[0]) + vectors[0:1]).astype(bf16).astype(f32) * score_scale
    put_heads(query, projected, lane)

    def inside(rows, start):
        index = start + lax.broadcasted_iota(jnp.int32, (rows, BLOCK), 0)
        return (index >= 0) & (index < seq_len)

    near_inside = inside(NEAR, base - REACH1)
    far_inside = inside(FAR, base - HALO + FAR0)
    for c, near_ref, far_ref, rows_ref in ((1, near_keys, far_keys, key_rows), (2, near_values, far_values, value_rows)):
        near = dot_nt(low[NEAR0 : NEAR0 + NEAR], weights[c, 0:wide])
        far = dot_nt(low[FAR0 : FAR0 + FAR], weights[c, wide:D])
        if c == 2:
            near = near + vectors[1:2, 0:wide]
            far = far + vectors[1:2, wide:D]
        for pair in range(PAIRS):
            lanes = slice(pair * BLOCK, (pair + 1) * BLOCK)
            near_ref[pair] = jnp.where(near_inside, near[:, lanes], 0.0).astype(bf16)
            part = jnp.where(far_inside, far[:, lanes], 0.0).astype(bf16)
            far_ref[pair] = part
            rows_ref[pair] = part.astype(f32)
    for at, rows_ref, pooled_ref in ((0, key_rows, pool_keys), (5, value_rows, pool_values)):
        for pair in range(PAIRS):
            lanes = slice(pair * BLOCK, (pair + 1) * BLOCK)
            total = None
            for tap in range(5):
                part = pool[at + tap : at + tap + 1, lanes] * rows_ref[pair, pl.ds(TAP0 + tap, POOLED, stride=4), :]
                total = part if total is None else total + part
            pooled_ref[pair] = total.astype(bf16)


def put_heads(target, value, lane):
    for pair in range(2 * PAIRS):
        part = value[:, pair * BLOCK : (pair + 1) * BLOCK]
        first = jnp.where(lane < HEAD, part, 0.0).astype(bf16)
        second = jnp.where(lane >= HEAD, part, 0.0).astype(bf16)
        for block in range(BLOCKS):
            rows = slice(block * BLOCK, (block + 1) * BLOCK)
            target[pair, block, 0:BLOCK] = first[rows]
            target[pair, block, BLOCK : 2 * BLOCK] = second[rows]


def project(place, low, pieces, vectors, pool):
    shapes = (
        struct((D, D), bf16),
        struct((2 * PAIRS, BLOCKS, 2 * BLOCK, BLOCK), bf16),
        struct((PAIRS, NEAR, BLOCK), bf16),
        struct((PAIRS, NEAR, BLOCK), bf16),
        struct((PAIRS, FAR, BLOCK), bf16),
        struct((PAIRS, FAR, BLOCK), bf16),
        struct((PAIRS, POOLED, BLOCK), bf16),
        struct((PAIRS, POOLED, BLOCK), bf16),
    )
    return pl.pallas_call(
        project_kernel,
        out_shape=shapes,
        grid=(1,),
        in_specs=[SM, whole((EXT, D))] + [HB] * 5 + wholes((vectors, pool)),
        out_specs=tuple(wholes(shapes)),
        scratch_shapes=[
            pltpu.VMEM((3, D, D), bf16),
            pltpu.VMEM((PAIRS, FAR, BLOCK), f32),
            pltpu.VMEM((PAIRS, FAR, BLOCK), f32),
            pltpu.SemaphoreType.DMA((9,)),
        ],
        compiler_params=params(24),
        name="project",
    )(place, low, *pieces, vectors, pool)


def attend_forward_kernel(
    query, near_keys, near_values, pool_keys, pool_values, near_mask, far_mask,
    mixed, log_total,
):
    def attend(keys, turned, pair, block, mask):
        scores = dot_nt(keys, query[pair, block])
        parts = []
        for e in range(2):
            lanes = slice(e * BLOCK, (e + 1) * BLOCK)
            masked = scores[:, lanes] + mask[block]
            top = jnp.max(masked, axis=0, keepdims=True)
            raised = jnp.exp(masked - top)
            total = jnp.sum(raised, axis=0, keepdims=True)
            log_total[pair, block, :, lanes] = top + jnp.log(total)
            parts.append((raised * (1.0 / total)).astype(bf16))
        both = dot(turned, jnp.concatenate(parts, axis=1))
        output = jnp.concatenate([both[0:HEAD, 0:BLOCK], both[HEAD:BLOCK, BLOCK : 2 * BLOCK]], axis=0)
        lanes = pl.ds(pl.multiple_of(pair * BLOCK, BLOCK), BLOCK)
        mixed[block * BLOCK : (block + 1) * BLOCK, lanes] = turn(output)

    def near_pair(pair, carry):
        turned = turn(near_values[pair])
        for block in range(BLOCKS):
            window = slice(block * BLOCK, (block + 2) * BLOCK)
            attend(near_keys[pair, window], turned[:, window], pair, block, near_mask)
        return carry

    def far_pair(pair, carry):
        turned = turn(pool_values[pair])
        for block in range(BLOCKS):
            attend(pool_keys[pair], turned, PAIRS + pair, block, far_mask)
        return carry

    lax.fori_loop(0, PAIRS, near_pair, 0)
    lax.fori_loop(0, PAIRS, far_pair, 0)


def attend_forward(*operands):
    shapes = (struct((ROWS, D), bf16), struct((2 * PAIRS, BLOCKS, 1, 2 * BLOCK), f32))
    return pl.pallas_call(
        attend_forward_kernel,
        out_shape=shapes,
        grid=(1,),
        in_specs=wholes(operands),
        out_specs=tuple(wholes(shapes)),
        compiler_params=params(14),
        name="attend_forward",
    )(*operands)


def attend_backward_kernel(
    grad, query, near_keys, near_values, far_keys, far_values, pool_keys, pool_values, near_mask, far_mask, log_total,
    pool,
    query_grad, near_low, far_low, near_own, pool_own, to_left, to_right, query_sum, pool_sum,
    near_total, pool_total, far_rows, shifted,
):
    near_total[...] = jnp.zeros_like(near_total)
    pool_total[...] = jnp.zeros_like(pool_total)
    query_grad[0:REACH1] = jnp.zeros((REACH1, D), bf16)
    query_grad[NEAR - REACH1 : NEAR] = jnp.zeros((REACH1, D), bf16)

    def back(keys, values, turned, pair, block, mask):
        part = grad[pair, block]
        asked = query[pair, block]
        scores = dot_nt(keys, asked)
        chance_grads = dot_nt(values, part)
        chances = []
        score_grads = []
        for e in range(2):
            lanes = slice(e * BLOCK, (e + 1) * BLOCK)
            chance = jnp.exp(scores[:, lanes] + mask[block] - log_total[pair, block, :, lanes])
            chance_grad = chance_grads[:, lanes]
            mean = jnp.sum(chance * chance_grad, axis=0, keepdims=True)
            score_grads.append((chance * (chance_grad - mean)).astype(bf16))
            chances.append(chance.astype(bf16))
        score_grad = jnp.concatenate(score_grads, axis=1)
        both = dot(turned, score_grad)
        output = jnp.concatenate([both[0:HEAD, 0:BLOCK], both[HEAD:BLOCK, BLOCK : 2 * BLOCK]], axis=0)
        output = jnp.transpose(output) * score_scale
        lanes = pl.ds(pl.multiple_of(pair * BLOCK, BLOCK), BLOCK)
        query_grad[REACH1 + block * BLOCK : REACH1 + (block + 1) * BLOCK, lanes] = output.astype(bf16)
        return (col_sum(output), dot(score_grad, asked), dot(jnp.concatenate(chances, axis=1), part))

    def near_pair(pair, carry):
        turned = turn(near_keys[pair])
        sums = jnp.zeros((1, BLOCK), f32)
        for block in range(BLOCKS):
            window = slice(block * BLOCK, (block + 2) * BLOCK)
            part, keys, values = back(
                near_keys[pair, window], near_values[pair, window], turned[:, window], pair, block, near_mask
            )
            near_total[0, pair, window] += keys
            near_total[1, pair, window] += values
            sums = sums + part
        query_sum[pair] = sums
        return carry

    def far_pair(pair, carry):
        turned = turn(pool_keys[pair])
        sums = jnp.zeros((1, BLOCK), f32)
        for block in range(BLOCKS):
            part, keys, values = back(pool_keys[pair], pool_values[pair], turned, PAIRS + pair, block, far_mask)
            pool_total[0, pair] += keys
            pool_total[1, pair] += values
            sums = sums + part
        query_sum[PAIRS + pair] = sums
        return carry

    lax.fori_loop(0, PAIRS, near_pair, 0)
    lax.fori_loop(0, PAIRS, far_pair, 0)

    side = REACH2 // 4
    own_pool = ROWS // 4
    for kind in range(2):
        near_low[kind] = near_total[kind].astype(bf16)
        near_own[kind] = near_total[kind, :, REACH1 : REACH1 + ROWS]
        pool_own[kind] = pool_total[kind, :, side : side + own_pool + 8]
        to_left[kind, :, 0:REACH1] = near_total[kind, :, 0:REACH1].astype(bf16)
        to_left[kind, :, REACH1 : REACH1 + side + 16] = pool_total[kind, :, 0 : side + 16].astype(bf16)
        to_right[kind, :, 0:REACH1] = near_total[kind, :, NEAR - REACH1 : NEAR].astype(bf16)
        to_right[kind, :, REACH1 : REACH1 + side] = pool_total[kind, :, side + own_pool :].astype(bf16)

    for kind, rows_ref in ((0, far_keys), (1, far_values)):
        for pair in range(PAIRS):
            lanes = slice(pair * BLOCK, (pair + 1) * BLOCK)
            far_rows[0:FAR] = rows_ref[pair].astype(f32)
            pooled = pool_total[kind, pair]
            for tap in range(5):
                pool_sum[5 * kind + tap : 5 * kind + tap + 1, lanes] = col_sum(
                    pooled * far_rows[pl.ds(TAP0 + tap, POOLED, stride=4), :]
                )
            shifted[0:8] = jnp.zeros((8, BLOCK), f32)
            shifted[8 : 8 + POOLED] = pooled
            weight = [pool[5 * kind + tap : 5 * kind + tap + 1, lanes] for tap in range(5)]
            first = FAR0 + TAP0
            far_rows[0 : first + 2] = jnp.zeros((first + 2, BLOCK), f32)
            far_rows[EXT - 72 : EXT] = jnp.zeros((72, BLOCK), f32)
            far_rows[pl.ds(first, POOLED, stride=4), :] = weight[0] * pooled + weight[4] * shifted[7 : 7 + POOLED]
            for tap in range(1, 4):
                far_rows[pl.ds(first + tap, POOLED, stride=4), :] = weight[tap] * pooled
            far_rows[first + 4 * POOLED : first + 4 * POOLED + 1] = weight[4] * pooled[POOLED - 1 : POOLED]
            far_low[kind, pair] = far_rows[...].astype(bf16)


def attend_backward(*operands):
    side = REACH2 // 4
    shapes = (
        struct((NEAR, D), bf16),
        struct((2, PAIRS, NEAR, BLOCK), bf16),
        struct((2, PAIRS, EXT, BLOCK), bf16),
        struct((2, PAIRS, ROWS, BLOCK), f32),
        struct((2, PAIRS, ROWS // 4 + 8, BLOCK), f32),
        struct((2, PAIRS, REACH1 + side + 16, BLOCK), bf16),
        struct((2, PAIRS, REACH1 + side, BLOCK), bf16),
        struct((2 * PAIRS, 1, BLOCK), f32),
        struct((10, PAIRS * BLOCK), f32),
    )
    return pl.pallas_call(
        attend_backward_kernel,
        out_shape=shapes,
        grid=(1,),
        in_specs=wholes(operands),
        out_specs=tuple(wholes(shapes)),
        scratch_shapes=[
            pltpu.VMEM((2, PAIRS, NEAR, BLOCK), f32),
            pltpu.VMEM((2, PAIRS, POOLED, BLOCK), f32),
            pltpu.VMEM((EXT, BLOCK), f32),
            pltpu.VMEM((POOLED + 8, BLOCK), f32),
        ],
        compiler_params=params(24),
        name="attend_backward",
    )(*operands)


def fetch_hidden(place, pieces, held, sems):
    own, mine, other, near_diag, far_diag = pieces
    core = place[4]
    half = D // 2
    copies = [pltpu.make_async_copy(piece, held.at[at], sems.at[at]) for at, piece in enumerate((own, mine, other))]
    for at, (piece, where) in enumerate(((near_diag, core), (far_diag, 1 - core))):
        target = held.at[3, pl.ds(pl.multiple_of(where * half, half), half)]
        copies.append(pltpu.make_async_copy(piece, target, sems.at[3 + at]))
    for copy in copies:
        copy.start()


def wait_hidden(j, held, sems):
    @pl.when(j < 3)
    def _():
        pltpu.make_async_copy(held.at[j], held.at[j], sems.at[j]).wait()

    @pl.when(j == 3)
    def _():
        for at in range(2):
            target = held.at[3, pl.ds(at * (D // 2), D // 2)]
            pltpu.make_async_copy(target, target, sems.at[3 + at]).wait()


def gelu_block(first_low, held, bias, act, slope, j):
    for block in range(BLOCKS):
        rows = slice(block * BLOCK, (block + 1) * BLOCK)
        pre = dot_nt(first_low[rows], held) + bias
        gate = 0.5 + 0.5 * lax.erf(pre * math.sqrt(0.5))
        act[0, rows] = (pre * gate).astype(bf16)
        slope[0, rows] = gate + pre * (jnp.exp(-0.5 * pre * pre) * (1.0 / math.sqrt(2.0 * math.pi)))


def feed_forward_kernel(
    mixed, out_weight, inputs, vectors, bias, own, mine,
    normed, inverse, first_low, act, slope,
    held, total, sems,
):
    j = pl.program_id(0)

    @pl.when(j == 0)
    def _():
        copies = [pltpu.make_async_copy(piece, held.at[at], sems.at[at]) for at, piece in enumerate((own, mine))]
        for copy in copies:
            copy.start()
        total[...] = dot(mixed[...], out_weight[...])

        def rows_step(i, carry):
            rows = pl.ds(pl.multiple_of(i * BLOCK, BLOCK), BLOCK)
            value = inputs[rows] + total[rows] + vectors[2:3]
            centered = value - row_mean(value)
            inv = lax.rsqrt(row_mean(centered * centered) + norm_eps)
            z = centered * inv
            normed[rows] = z
            inverse[rows] = inv
            first_low[rows] = (z * vectors[4:5] + vectors[5:6]).astype(bf16)
            return carry

        lax.fori_loop(0, BLOCKS, rows_step, 0)

    pltpu.make_async_copy(held.at[j], held.at[j], sems.at[j]).wait()
    gelu_block(first_low, held[j], bias[j], act, slope, j)


def feed_forward(mixed, out_weight, inputs, vectors, bias, pieces):
    shapes = (
        struct((ROWS, D), f32),
        struct((ROWS, 1), f32),
        struct((ROWS, D), bf16),
        struct((2, ROWS, D), bf16),
        struct((2, ROWS, D), f32),
    )
    block = pl.BlockSpec((1, ROWS, D), lambda j: (j, 0, 0))
    return pl.pallas_call(
        feed_forward_kernel,
        out_shape=shapes,
        grid=(2,),
        in_specs=wholes((mixed, out_weight, inputs, vectors, bias)) + [HB] * 2,
        out_specs=(*wholes(shapes[:3]), block, block),
        scratch_shapes=[
            pltpu.VMEM((2, D, D), bf16),
            pltpu.VMEM((ROWS, D), f32),
            pltpu.SemaphoreType.DMA((2,)),
        ],
        compiler_params=params(22),
        name="feed_forward",
    )(mixed, out_weight, inputs, vectors, bias, *pieces)


def feed_forward_rest_kernel(
    place, first_low, bias, other, near_diag, far_diag,
    act, slope,
    held, sems,
):
    j = pl.program_id(0)

    @pl.when(j == 0)
    def _():
        half = D // 2
        core = place[4]
        pltpu.make_async_copy(other, held.at[0], sems.at[0]).start()
        for at, (piece, where) in enumerate(((near_diag, core), (far_diag, 1 - core))):
            target = held.at[1, pl.ds(pl.multiple_of(where * half, half), half)]
            pltpu.make_async_copy(piece, target, sems.at[1 + at]).start()
        pltpu.make_async_copy(held.at[0], held.at[0], sems.at[0]).wait()

    @pl.when(j == 1)
    def _():
        for at in range(2):
            target = held.at[1, pl.ds(at * (D // 2), D // 2)]
            pltpu.make_async_copy(target, target, sems.at[1 + at]).wait()

    gelu_block(first_low, held[j], bias[2 + j], act, slope, j)


def feed_forward_rest(place, first_low, bias, pieces):
    block = pl.BlockSpec((1, ROWS, D), lambda j: (j, 0, 0))
    return pl.pallas_call(
        feed_forward_rest_kernel,
        out_shape=(struct((2, ROWS, D), bf16), struct((2, ROWS, D), f32)),
        grid=(2,),
        in_specs=[SM, *wholes((first_low, bias))] + [HB] * 3,
        out_specs=(block, block),
        scratch_shapes=[pltpu.VMEM((2, D, D), bf16), pltpu.SemaphoreType.DMA((3,))],
        compiler_params=params(14),
        name="feed_forward_rest",
    )(place, first_low, bias, *pieces)


def two_halves(rows, cols):
    return [
        pl.BlockSpec((1, rows, cols), lambda j: (jnp.minimum(j, 1), 0, 0)),
        pl.BlockSpec((1, rows, cols), lambda j: (jnp.maximum(j - 2, 0), 0, 0)),
    ]


def with_half(j, first, second, use):
    @pl.when(j < 2)
    def _():
        use(first)

    @pl.when(j >= 2)
    def _():
        use(second)


def branch_kernel(
    place, act, act_rest, normed, incoming, vectors, own, mine, other, near_diag, far_diag,
    block_low, branch_low, second, sums,
    held, total, sems,
):
    j = pl.program_id(0)

    @pl.when(j == 0)
    def _():
        fetch_hidden(place, (own, mine, other, near_diag, far_diag), held, sems)
        sums[...] = jnp.zeros_like(sums)
        total[...] = jnp.zeros_like(total)

    wait_hidden(j, held, sems)

    def add(part):
        total[...] += dot(part[0], held[j])

    with_half(j, act, act_rest, add)

    @pl.when(j == 3)
    def _():

        def second_step(i, carry):
            rows = pl.ds(pl.multiple_of(i * BLOCK, BLOCK), BLOCK)
            first = normed[rows] * vectors[4:5] + vectors[5:6]
            value = first + total[rows] + vectors[3:4]
            centered = value - row_mean(value)
            inv = lax.rsqrt(row_mean(centered * centered) + norm_eps)
            z = centered * inv
            block_low[rows] = (z * vectors[6:7] + vectors[7:8]).astype(bf16)
            upper = incoming[rows]
            scaled = upper * vectors[6:7]
            grad = inv * (scaled - row_mean(scaled) - z * row_mean(scaled * z))
            second[rows] = grad
            branch_low[rows] = grad.astype(bf16)
            sums[0:1] += col_sum(grad)
            sums[1:2] += col_sum(upper * z)
            sums[2:3] += col_sum(upper)
            return carry

        lax.fori_loop(0, BLOCKS, second_step, 0)


def branch_of(place, act, act_rest, normed, incoming, vectors, pieces):
    shapes = (
        struct((ROWS, D), bf16),
        struct((ROWS, D), bf16),
        struct((ROWS, D), f32),
        struct((8, D), f32),
    )
    return pl.pallas_call(
        branch_kernel,
        out_shape=shapes,
        grid=(4,),
        in_specs=[SM, *two_halves(ROWS, D), *wholes((normed, incoming, vectors))] + [HB] * 5,
        out_specs=tuple(wholes(shapes)),
        scratch_shapes=[
            pltpu.VMEM((4, D, D), bf16),
            pltpu.VMEM((ROWS, D), f32),
            pltpu.SemaphoreType.DMA((5,)),
        ],
        compiler_params=params(22),
        name="branch",
    )(place, act, act_rest, normed, incoming, vectors, *pieces)


def feed_back_kernel(
    place, slope, slope_rest, branch_low, second, normed, inverse, vectors, out_weight,
    in_own, in_mine, in_other, in_near, in_far, out_own, out_mine, out_other, out_near, out_far,
    pre_low, attn_low, attn_grad, heads_grad, sums, bias_sum,
    in_held, out_held, total, in_sems, out_sems,
):
    j = pl.program_id(0)

    @pl.when(j == 0)
    def _():
        fetch_hidden(place, (out_own, out_mine, out_other, out_near, out_far), out_held, out_sems)
        fetch_hidden(place, (in_own, in_mine, in_other, in_near, in_far), in_held, in_sems)
        sums[...] = jnp.zeros_like(sums)
        total[...] = second[...]

    wait_hidden(j, out_held, out_sems)
    wait_hidden(j, in_held, in_sems)

    def back(part):
        pre_grad = dot_nt(branch_low[...], out_held[j]) * part[0]
        pre_low[0] = pre_grad.astype(bf16)
        bias_sum[0] = col_sum(pre_grad)

    with_half(j, slope, slope_rest, back)
    total[...] += dot(pre_low[0], in_held[j])

    @pl.when(j == 3)
    def _():
        def first_step(i, carry):
            rows = pl.ds(pl.multiple_of(i * BLOCK, BLOCK), BLOCK)
            z = normed[rows]
            first_grad = total[rows]
            scaled = first_grad * vectors[4:5]
            grad = inverse[rows] * (scaled - row_mean(scaled) - z * row_mean(scaled * z))
            attn_grad[rows] = grad
            attn_low[rows] = grad.astype(bf16)
            sums[0:1] += col_sum(grad)
            sums[1:2] += col_sum(first_grad * z)
            sums[2:3] += col_sum(first_grad)
            return carry

        lax.fori_loop(0, BLOCKS, first_step, 0)
        total[...] = dot_nt(attn_low[...], out_weight[...])
        put_heads(heads_grad, total, lax.broadcasted_iota(jnp.int32, (ROWS, BLOCK), 1))


def feed_back(place, slope, slope_rest, branch_low, second, normed, inverse, vectors, out_weight, in_pieces, out_pieces):
    shapes = (
        struct((4, ROWS, D), bf16),
        struct((ROWS, D), bf16),
        struct((ROWS, D), f32),
        struct((2 * PAIRS, BLOCKS, 2 * BLOCK, BLOCK), bf16),
        struct((8, D), f32),
        struct((4, 1, D), f32),
    )
    block = pl.BlockSpec((1, ROWS, D), lambda j: (j, 0, 0))
    return pl.pallas_call(
        feed_back_kernel,
        out_shape=shapes,
        grid=(4,),
        in_specs=[
            SM,
            *two_halves(ROWS, D),
            whole((ROWS, D)),
            whole((ROWS, D)),
            whole((ROWS, D)),
            whole((ROWS, 1)),
            whole((8, D)),
            whole((D, D)),
        ]
        + [HB] * 10,
        out_specs=(
            block,
            whole((ROWS, D)),
            whole((ROWS, D)),
            whole(shapes[3].shape),
            whole((8, D)),
            pl.BlockSpec((1, 1, D), lambda j: (j, 0, 0)),
        ),
        scratch_shapes=[
            pltpu.VMEM((4, D, D), bf16),
            pltpu.VMEM((4, D, D), bf16),
            pltpu.VMEM((ROWS, D), f32),
            pltpu.SemaphoreType.DMA((5,)),
            pltpu.SemaphoreType.DMA((5,)),
        ],
        compiler_params=params(34),
        name="feed_back",
    )(place, slope, slope_rest, branch_low, second, normed, inverse, vectors, out_weight, *in_pieces, *out_pieces)


def ffn_grad_kernel(order, rows, *refs):
    cols, (own, sent, turned) = refs[:-3], refs[-3:]
    j = pl.program_id(0)

    @pl.when(j == 0)
    def _():
        turned[...] = dot_nt(order[...], rows[...]).astype(bf16)

    def product(part):
        result = dot(turned[...], part[0]).astype(bf16)
        own[0] = result[: D // 2]
        sent[0] = result[D // 2 :]

    if len(cols) == 1:
        product(cols[0])
    else:
        with_half(j, *cols, product)


def ffn_grad(order, rows, *cols):
    block = pl.BlockSpec((1, D // 2, D), lambda j: (j, 0, 0))
    one = [pl.BlockSpec((1, ROWS, D), lambda j: (j, 0, 0))]
    return pl.pallas_call(
        ffn_grad_kernel,
        out_shape=(struct((4, D // 2, D), bf16),) * 2,
        grid=(4,),
        in_specs=wholes((order, rows)) + (one if len(cols) == 1 else two_halves(ROWS, D)),
        out_specs=(block, block),
        scratch_shapes=[pltpu.VMEM((D, ROWS), bf16)],
        compiler_params=params(16),
        name="ffn_grad",
    )(order, rows, *cols)


def turn_kernel(order, x, turned):
    turned[...] = dot_nt(order[...], x[...]).astype(bf16)


def turn_rows(order, x):
    return pl.pallas_call(
        turn_kernel,
        out_shape=struct((D, EXT), bf16),
        grid=(1,),
        in_specs=wholes((order, x)),
        out_specs=whole((D, EXT)),
        compiler_params=params(12),
        name="turn_rows",
    )(order, x)


def attn_weight_grad_kernel(order, turned, attn_low, mixed, query_grad, near_low, far_low, target, held):
    near_x = turned[:, NEAR0 : NEAR0 + NEAR]
    held[0] = dot(near_x, query_grad[...])
    for kind in range(2):
        near = jnp.concatenate([near_low[kind, pair] for pair in range(PAIRS)], axis=1)
        far = jnp.concatenate([far_low[kind, pair] for pair in range(PAIRS)], axis=1)
        held[1 + kind, :, 0 : D // 2] = dot(near_x, near)
        held[1 + kind, :, D // 2 : D] = dot(turned[...], far)
    held[3] = dot(dot_nt(order[...], attn_low[...]).astype(bf16), mixed[...])

    rows = D // 8
    lane = lax.broadcasted_iota(jnp.int32, (rows, BLOCK), 1)

    def step(i, carry):
        here = pl.ds(pl.multiple_of(i * rows, rows), rows)
        for pair in range(2):
            tiles = [
                [held[c, here, (3 * pair + t) * BLOCK : (3 * pair + t + 1) * BLOCK] for t in range(3)] for c in range(4)
            ]
            for odd in range(2):
                parts = [tiles[c][2 * odd] for c in range(4)]
                for c in (0, 2):
                    a, b = (tiles[c][1], tiles[c + 1][1])
                    if odd:
                        parts.append(jnp.where(lane < HEAD, pltpu.roll(a, HEAD, 1), b))
                    else:
                        parts.append(jnp.where(lane < HEAD, a, pltpu.roll(b, HEAD, 1)))
                for t, part in enumerate(parts):
                    target[2 * pair + odd, here, t * BLOCK : (t + 1) * BLOCK] = part.astype(bf16)
        return carry

    lax.fori_loop(0, 4, step, 0)


def attn_weight_grad(half, order, turned, attn_low, mixed, query_grad, near_low, far_low):
    return pl.pallas_call(
        attn_weight_grad_kernel,
        out_shape=struct((4, D // 2, D), bf16),
        grid=(1,),
        in_specs=[
            pl.BlockSpec((D // 2, D), lambda i: (half, 0)),
            pl.BlockSpec((D // 2, EXT), lambda i: (half, 0)),
        ]
        + [whole(a.shape) for a in (attn_low, mixed, query_grad, near_low, far_low)],
        out_specs=whole((4, D // 2, D)),
        scratch_shapes=[pltpu.VMEM((4, D // 2, D), f32)],
        compiler_params=params(24),
        name="attn_weight_grad",
    )(order, turned, attn_low, mixed, query_grad, near_low, far_low)


def add_kernel(count, *refs):
    operands, target = refs[count : 2 * count], refs[2 * count]
    total = operands[0][...].astype(f32)
    for operand in operands[1:]:
        total = total + operand[...].astype(f32)
    target[...] = total.astype(target.dtype)


def add_blocks(dtype, *terms):
    m = terms[0][1].shape[0]
    rows, cols = terms[0][0].shape[1:]
    block = (1, rows, cols)
    count = len(terms)

    def spec(k):
        return pl.BlockSpec(block, lambda i, *at: (at[k][i], 0, 0))

    return pl.pallas_call(
        functools.partial(add_kernel, count),
        out_shape=struct((m, rows, cols), dtype),
        grid_spec=pltpu.PrefetchScalarGridSpec(
            num_scalar_prefetch=count,
            grid=(m,),
            in_specs=[spec(k) for k in range(count)],
            out_specs=pl.BlockSpec(block, lambda i, *at: (i, 0, 0)),
        ),
        compiler_params=params(10),
        name="add_blocks",
    )(*[at for _, at in terms], *[array for array, _ in terms])


def input_grad_kernel(
    place, query_grad, near_own, pool_own, from_left, from_right, attn_grad, pool, own, mine, other, near_diag, far_diag,
    low, value_sum,
    pooled, rows_held, grads, weights, sems,
):
    wait_weights = fetch_attention(place, (own, mine, other, near_diag, far_diag), weights, None, sems)
    side = REACH2 // 4
    own_pool = ROWS // 4
    wide = PAIRS * BLOCK
    for kind in range(2):
        for pair in range(PAIRS):
            lanes = slice(pair * BLOCK, (pair + 1) * BLOCK)
            rows_held[...] = near_own[kind, pair]
            rows_held[0:REACH1] += from_left[kind, pair, 0:REACH1].astype(f32)
            rows_held[ROWS - REACH1 : ROWS] += from_right[kind, pair, 0:REACH1].astype(f32)
            if kind:
                value_sum[:, lanes] = col_sum(rows_held[...])
            grads[kind, :, lanes] = rows_held[...].astype(bf16)

            pooled[...] = pool_own[kind, pair]
            pooled[0:side] += from_left[kind, pair, REACH1 : REACH1 + side].astype(f32)
            pooled[side : own_pool + 8] += from_right[kind, pair, REACH1 : REACH1 + side + 8].astype(f32)
            here, following = pooled[0:own_pool], pooled[1 : own_pool + 1]
            weight = [pool[5 * kind + tap : 5 * kind + tap + 1, lanes] for tap in range(5)]
            rows_held[pl.ds(0, own_pool, stride=4), :] = weight[2] * here
            rows_held[pl.ds(1, own_pool, stride=4), :] = weight[3] * here
            rows_held[pl.ds(2, own_pool, stride=4), :] = weight[4] * here + weight[0] * following
            rows_held[pl.ds(3, own_pool, stride=4), :] = weight[1] * following
            lanes = slice(wide + pair * BLOCK, wide + (pair + 1) * BLOCK)
            if kind:
                value_sum[:, lanes] = col_sum(rows_held[...])
            grads[kind, :, lanes] = rows_held[...].astype(bf16)
    wait_weights()
    total = attn_grad[...] + dot(query_grad[REACH1 : REACH1 + ROWS], weights[0])
    total = total + dot(grads[0], weights[1])
    low[...] = (total + dot(grads[1], weights[2])).astype(bf16)


def input_grad_of(place, query_grad, near_own, pool_own, from_left, from_right, attn_grad, pool, pieces):
    return pl.pallas_call(
        input_grad_kernel,
        out_shape=(struct((ROWS, D), bf16), struct((1, D), f32)),
        grid=(1,),
        in_specs=[SM, *wholes((query_grad, near_own, pool_own, from_left, from_right, attn_grad, pool))] + [HB] * 5,
        out_specs=(whole((ROWS, D)), whole((1, D))),
        scratch_shapes=[
            pltpu.VMEM((ROWS // 4 + 8, BLOCK), f32),
            pltpu.VMEM((ROWS, BLOCK), f32),
            pltpu.VMEM((2, ROWS, D), bf16),
            pltpu.VMEM((3, D, D), bf16),
            pltpu.SemaphoreType.DMA((9,)),
        ],
        compiler_params=params(18),
        name="input_grad",
    )(place, query_grad, near_own, pool_own, from_left, from_right, attn_grad, pool, *pieces)


def place_kernel(at, own, mine, other, diag, target):
    step = pl.program_id(0)
    for k, piece in enumerate((own, mine, other, diag)):

        @pl.when(step == k)
        def _(piece=piece):
            target[...] = piece[...].astype(f32)


def place_rows(at, *pieces):
    return pl.pallas_call(
        place_kernel,
        out_shape=struct((4 * ROWS, D), f32),
        grid_spec=pltpu.PrefetchScalarGridSpec(
            num_scalar_prefetch=1,
            grid=(4,),
            in_specs=[whole((ROWS, D))] * 4,
            out_specs=pl.BlockSpec((ROWS, D), lambda i, at: (at[i], 0)),
        ),
        compiler_params=params(14),
        name="place_rows",
    )(at, *pieces)


def square_sum(value):
    return jnp.sum(value * value)


def pack_kernel(place, query_sum, value_sum, first_sums, second_sums, bias_sum, pool_sum, attn, hidden_in, hidden_out, packed):
    packed[...] = jnp.zeros_like(packed)
    for pair in range(2 * PAIRS):
        packed[0:1, pair * BLOCK : (pair + 1) * BLOCK] = query_sum[pair]
    packed[1:2] = value_sum[...]
    packed[2:3] = first_sums[0:1]
    packed[3:4] = second_sums[0:1]
    packed[4:6] = first_sums[1:3]
    packed[6:8] = second_sums[1:3]
    for at in range(4):
        packed[pl.ds(8 + place[at], 1), :] = bias_sum[at]
    lane = lax.broadcasted_iota(jnp.int32, (1, BLOCK), 1)
    wide = lax.broadcasted_iota(jnp.int32, (1, PAIRS * BLOCK), 1)
    for tap in range(10):
        row = jnp.zeros((1, BLOCK), f32)
        taps = pool_sum[tap : tap + 1, :]
        for head in range(HEADS // 2):
            mine = (wide >= head * HEAD) & (wide < (head + 1) * HEAD)
            row = row + jnp.where(lane == head, jnp.sum(jnp.where(mine, taps, 0.0), axis=1, keepdims=True), 0.0)
        at = 12 + tap // 5
        packed[at : at + 1, (tap % 5) * BLOCK : (tap % 5 + 1) * BLOCK] = row
    first = square_sum(attn[...])
    second = square_sum(hidden_in[...]) + square_sum(hidden_out[...])
    packed[14:15, 0:BLOCK] = jnp.where(lane == 0, first, jnp.where(lane == 1, second, 0.0))


def pack(*operands):
    return pl.pallas_call(
        pack_kernel,
        out_shape=struct((16, D), f32),
        grid=(1,),
        in_specs=[SM, *wholes(operands[1:])],
        out_specs=whole((16, D)),
        compiler_params=params(8),
        name="pack",
    )(*operands)


def update(weight, grad, moments, decay, clip, step, moments_new, at):
    clipped = clip * grad
    first_moment = beta_first * moments[0] + (1.0 - beta_first) * clipped
    second_moment = beta_second * moments[1] + (1.0 - beta_second) * clipped * clipped
    corrected_first = first_moment * (1.0 / (1.0 - beta_first**adam_step))
    corrected_second = second_moment * (1.0 / (1.0 - beta_second**adam_step))
    result = corrected_first / (jnp.sqrt(corrected_second) + adam_eps)
    step[at] = result + decay * weight if decay else result
    moments_new[(0, *at)] = first_moment
    moments_new[(1, *at)] = second_moment


def finish_kernel(
    place, packed, attn, hidden_in, hidden_out,
    qkv_weight, out_weight, in_weight, ff_out_weight,
    qkv_moments, out_moments, in_moments, ff_out_moments, vector_moments, bias_moments, pool_moments,
    qkv_grad, qkv_step, qkv_new, out_grad, out_step, out_new, in_grad, in_step, in_new,
    ff_out_grad, ff_out_step, ff_out_new, vector_grad, vector_step, vector_new,
    bias_grad, bias_step, bias_new, pool_grad, pool_step, pool_new, norms,
    held,
):
    lane = lax.broadcasted_iota(jnp.int32, (1, BLOCK), 1)
    squares = packed[14:15, 0:BLOCK]
    small = square_sum(packed[0:12])
    pooled = square_sum(packed[12:14])
    squares = jnp.where(lane == 2, small, jnp.where(lane == 3, pooled, squares))
    squares = jnp.where(lane < 4, squares, 0.0)
    total = jnp.sqrt(jnp.sum(squares, axis=1, keepdims=True))
    count = 4 * D * D + 2 * FF * D + 8 * D + FF + 10 * (HEADS // 2)
    clip = jnp.minimum(1.0, max_rms * math.sqrt(count) / (total + 1e-06))
    norms[0:1] = jnp.sqrt(squares)
    norms[1:2] = jnp.broadcast_to(clip, (1, BLOCK))

    width = attn.shape[0]
    even = place[0] % 2 == 0
    held[...] = jnp.zeros_like(held)
    everything = (slice(None), slice(None))
    for c in range(4):
        whole_part = attn[:, c * BLOCK : (c + 1) * BLOCK]
        tile = attn[:, (4 + c // 2) * BLOCK : (5 + c // 2) * BLOCK]
        moved = pltpu.roll(tile, HEAD, 1)
        low, high = (tile, moved) if c % 2 == 0 else (moved, tile)
        straight = jnp.concatenate([whole_part, low], axis=1)
        turned = pltpu.roll(jnp.concatenate([whole_part, high], axis=1), HEAD, 1)
        both = jnp.where(even, straight, turned)
        local = qkv_grad.shape[2]
        if c < 3:
            grad = both[:, 0:local]
            qkv_grad[c] = grad
            moments = (qkv_moments[0, c], qkv_moments[1, c])
            update(qkv_weight[c], grad, moments, decay_rate, clip, qkv_step, qkv_new, (c,))
        else:
            held[0:width] = both
            grad = jnp.transpose(held[...])[0:local, 0:width]
            out_grad[...] = grad
            update(out_weight[...], grad, out_moments, decay_rate, clip, out_step, out_new, everything)
    for shard, weight, moments, grad_ref, step, new in (
        (hidden_in, in_weight, in_moments, in_grad, in_step, in_new),
        (hidden_out, ff_out_weight, ff_out_moments, ff_out_grad, ff_out_step, ff_out_new),
    ):
        grad_ref[...] = shard[...]
        update(weight[...], shard[...], moments, decay_rate, clip, step, new, everything)
    vector_grad[...] = packed[0:8]
    update(None, packed[0:8], vector_moments, 0.0, clip, vector_step, vector_new, everything)
    bias_grad[...] = packed[8:12]
    update(None, packed[8:12], bias_moments, 0.0, clip, bias_step, bias_new, everything)
    pool_grad[...] = packed[12:14]
    update(None, packed[12:14], pool_moments, 0.0, clip, pool_step, pool_new, everything)


def finish(*operands):
    width = operands[2].shape[0]
    local = operands[5].shape[2]

    def three(*shape):
        return [struct(shape, f32), struct(shape, f32), struct((2, *shape), f32)]

    shapes = (
        three(3, width, local)
        + three(local, width)
        + three(width, D)
        + three(width, D)
        + three(8, D)
        + three(4, D)
        + three(2, D)
        + [struct((2, BLOCK), f32)]
    )
    return pl.pallas_call(
        finish_kernel,
        out_shape=tuple(shapes),
        grid=(1,),
        in_specs=[SM, *wholes(operands[1:])],
        out_specs=tuple(wholes(shapes)),
        scratch_shapes=[pltpu.VMEM((BLOCK, 2 * BLOCK), f32)],
        compiler_params=params(20),
        name="finish",
    )(*operands)


def cross_shards(own, mine, core):
    half = own.shape[0] // 2
    part = lax.dynamic_slice_in_dim(mine, core * half, half, 0)
    near_diag = lax.ppermute(part, PLACE, CROSS)
    other = lax.ppermute(mine, "seq", SWAP)
    far_diag = lax.ppermute(near_diag, "seq", SWAP)
    return (own, mine, other, near_diag, far_diag)


def after(value, *done):
    return lax.optimization_barrier((value, *done))[0]


def rows_by_dp(value, dp):
    n, rows, cols = value.shape
    return value.reshape(n * dp, rows // dp, cols)


def slots_by_dp(slot, dp):
    return (jnp.atleast_1d(slot)[:, None] * dp + jnp.arange(dp)).reshape(-1).astype(jnp.int32)


class DpSum:
    def __init__(self, dp, dp_index, *terms):
        self.dp, self.dp_index, self.step = dp, dp_index, 1
        self.terms = [(rows_by_dp(array, dp), slot * dp, 0) for array, slot in terms]

    def blocks(self, targets):
        return [
            (array, (first + (targets >> shift)).astype(jnp.int32)) for array, first, shift in self.terms
        ]

    def send(self):
        step = self.step
        free = jnp.arange(self.dp // (2 * step))
        targets = free * (2 * step) + (self.dp_index % (2 * step) ^ step)
        return add_blocks(bf16, *self.blocks(targets))

    def move(self, value):
        step = self.step
        got = lax.ppermute(value, "dp", [(i, i ^ step) for i in range(self.dp)])
        self.terms.append((got, 0, (2 * step).bit_length() - 1))
        self.step = 2 * step

    def done(self):
        return self.step >= self.dp

    def result(self):
        return add_blocks(f32, *self.blocks(self.dp_index + jnp.zeros((1,), jnp.int32)))[0]


def sum_everywhere(value, dp):
    value = value + lax.ppermute(value, "seq", SWAP)
    for step in (1, 2):
        value = value + lax.ppermute(value, "lvl", [(i, i ^ step) for i in range(4)])
    step = 1
    while step < dp:
        value = value + lax.ppermute(value, "dp", [(i, i ^ step) for i in range(dp)])
        step *= 2
    return value


def on_device(
    tokens,
    cotangent,
    lengths,
    qkv_weight,
    out_weight,
    ffn_in_weight,
    ffn_out_weight,
    vectors,
    ffn_bias,
    pool_kernel,
    qkv_moments,
    out_moments,
    ffn_in_moments,
    ffn_out_moments,
    vector_moments,
    bias_moments,
    pool_moments,
):
    dp = lax.axis_size("dp")
    dp_index = lax.axis_index("dp")
    core = lax.axis_index("seq")
    level = lax.axis_index("lvl")
    length = lengths[0]
    count = tokens.shape[1]
    size = count // 4
    seq_len = 2 * count
    half = HEADS // 2
    along = jnp.where(core == 0, 1, 2)
    slots = [level, level ^ along, level ^ (3 - along), level ^ 3]

    def chunk_of(owner):
        order = owner ^ (owner >> 1)
        return jnp.where(core == 0, order, 3 - order)

    chunk = chunk_of(level)
    base = core * count + chunk * size
    width = D // (2 * dp)

    local = qkv_weight.shape[2]
    attn_own = jnp.concatenate(
        [bfloat(qkv_weight).transpose(0, 2, 1).reshape(3 * local, D), bfloat(out_weight)], axis=0
    )
    hidden = ffn_in_weight.shape[0]
    bias = jnp.stack([lax.dynamic_slice_in_dim(ffn_bias, s * hidden, hidden) for s in slots]).reshape(4, 1, D)
    edge = jnp.where(core == 0, tokens[0, count - HALO :], tokens[0, :HALO])
    pool_lanes = jnp.repeat(pool_kernel.reshape(10, half), HEAD, axis=1)
    place = jnp.stack([*slots, core, base, length, seq_len, chunk]).astype(jnp.int32)
    row = jnp.arange(D)
    side, rest = (row // (D // 2), row % (D // 2))
    feature = (rest // width) * (2 * width) + jnp.where(side == 0, core, 1 - core) * width + rest % width
    order = (feature[:, None] == row[None, :]).astype(bf16)
    chunks = jnp.stack([chunk_of(s) for s in slots]).astype(jnp.int32)
    shard_index = dp_index * 2 + core

    def own_slice(weight):
        return lax.dynamic_slice_in_dim(weight, shard_index * width, width, 1)

    def index(*at):
        return jnp.stack([jnp.asarray(a) for a in at]).astype(jnp.int32)

    attn_mine = lax.ppermute(attn_own, PLACE, MINE)
    edge = lax.ppermute(after(edge, attn_own), "seq", SWAP)
    in_own = bfloat(ffn_in_weight)
    out_own = bfloat(ffn_out_weight)
    weight_slices = [own_slice(w) for w in (qkv_weight, out_weight)]
    weight_slices += [own_slice(w).T for w in (ffn_in_weight, ffn_out_weight)]
    extended, inputs, incoming, near_mask, far_mask = prepare(place, edge, tokens, cotangent)
    attn_mine = after(attn_mine, extended, in_own, out_own)
    part = lax.dynamic_slice_in_dim(attn_mine, core * (D // 2), D // 2, 0)
    attn_near = lax.ppermute(part, PLACE, CROSS)
    attn_other = lax.ppermute(attn_mine, "seq", SWAP)
    attn_near = after(attn_near, order, pool_lanes, place, bias, weight_slices)
    attn_far = lax.ppermute(attn_near, "seq", SWAP)
    attn_pieces = [
        p.reshape(-1, local, D) for p in (attn_own, attn_mine, attn_other, attn_near, attn_far)
    ]
    in_mine = lax.ppermute(after(in_own, attn_near), PLACE, MINE)
    out_all, *kept = project(place, extended, attn_pieces, vectors, pool_lanes)
    query, near_keys, near_values, far_keys, far_values, pool_keys, pool_values = kept
    in_mine = after(in_mine, query)
    part = lax.dynamic_slice_in_dim(in_mine, core * (D // 2), D // 2, 0)
    in_near = lax.ppermute(part, PLACE, CROSS)
    in_other = lax.ppermute(in_mine, "seq", SWAP)
    out_mine = lax.ppermute(after(out_own, part), PLACE, MINE)
    mixed, log_total = attend_forward(
        after(query, part), near_keys, near_values, pool_keys, pool_values, near_mask, far_mask
    )
    in_near = after(in_near, mixed)
    in_far = lax.ppermute(in_near, "seq", SWAP)
    normed, inverse, first_low, act, slope = feed_forward(mixed, out_all, inputs, vectors, bias, (in_own, in_mine))
    out_mine = after(out_mine, first_low)
    part = lax.dynamic_slice_in_dim(out_mine, core * (D // 2), D // 2, 0)
    out_near = lax.ppermute(part, PLACE, CROSS)
    out_other = lax.ppermute(out_mine, "seq", SWAP)
    act_rest, slope_rest = feed_forward_rest(
        place, after(first_low, part), bias, (after(in_other, first_low), in_near, after(in_far, first_low))
    )
    turned = turn_rows(order, after(extended, act_rest))
    out_near = after(out_near, turned)
    out_far = lax.ppermute(out_near, "seq", SWAP)
    in_pieces = (in_own, in_mine, in_other, in_near, in_far)
    out_pieces = (out_own, out_mine, out_other, out_near, out_far)
    block_low, branch_low, second, second_sums = branch_of(
        place, act, act_rest, normed, incoming, vectors, out_pieces
    )

    block_mine = lax.ppermute(block_low, PLACE, MINE)
    block_other = lax.ppermute(block_low, PLACE, CROSS)
    out_grad, grad_sent = ffn_grad(order, branch_low, act, act_rest)
    out_got = lax.ppermute(grad_sent, "seq", SWAP)
    pre_low, attn_low, attn_grad, heads_grad, first_sums, bias_sum = feed_back(
        place, slope, slope_rest, after(branch_low, out_grad), second, normed, inverse, vectors, out_all,
        in_pieces, out_pieces,
    )
    out_got = after(out_got, pre_low, block_mine, block_other)
    out_send = add_blocks(bf16, (out_grad, index(1, 3)), (out_got, index(2, 3)))
    out_first = lax.ppermute(out_send, PLACE, MINE)
    in_grad, grad_sent = ffn_grad(order, first_low, after(pre_low, out_send))
    in_got = lax.ppermute(grad_sent, "seq", SWAP)
    in_send = add_blocks(bf16, (in_grad, index(1, 3)), (in_got, index(2, 3)))
    in_first = lax.ppermute(in_send, PLACE, MINE)

    (query_grad, near_low, far_low, near_own, pool_own, to_left, to_right, query_sum, pool_sum) = attend_backward(
        after(heads_grad, in_send), *kept, near_mask, far_mask, log_total, pool_lanes
    )
    from_right = lax.ppermute(to_left, PLACE, LEFTWARD)
    from_left = lax.ppermute(to_right, PLACE, RIGHTWARD)
    out_first = after(out_first, query_grad)
    out_pass = add_blocks(bf16, (out_grad, index(2)), (out_got, index(1)), (out_first, index(1)))
    out_second = lax.ppermute(out_pass, PLACE, CROSS)
    grad_parts = (order, turned, attn_low, mixed, after(query_grad, out_pass), near_low, far_low)
    grad_sent = attn_weight_grad(1, *grad_parts)
    attn_got = lax.ppermute(grad_sent, "seq", SWAP)
    in_first = after(in_first, grad_sent)
    in_pass = add_blocks(bf16, (in_grad, index(2)), (in_got, index(1)), (in_first, index(1)))
    in_second = lax.ppermute(in_pass, PLACE, CROSS)
    query_grad = after(query_grad, in_pass)
    attn_wide = attn_weight_grad(0, *grad_parts[:4], query_grad, near_low, far_low)
    attn_got = after(attn_got, attn_wide, out_second, in_second, from_left, from_right)
    attn_at = index(slots[1], slots[3])
    attn_send = add_blocks(bf16, (attn_wide, attn_at), (attn_got, attn_at))
    attn_first = lax.ppermute(attn_send, PLACE, MINE)

    out_sum = DpSum(dp, dp_index, (out_grad, 0), (out_got, 0), (out_first, 0), (after(out_second, attn_send), 0))
    in_sum = DpSum(dp, dp_index, (in_grad, 0), (in_got, 0), (in_first, 0), (after(in_second, attn_send), 0))
    out_part = out_sum.send()
    out_sum.move(out_part)
    in_part = in_sum.send()
    in_sum.move(in_part)
    input_low, value_sum = input_grad_of(
        place, after(query_grad, out_part, in_part), near_own, pool_own, from_left, from_right, attn_grad, pool_lanes,
        attn_pieces,
    )
    attn_first = after(attn_first, input_low, out_sum.terms[-1][0], in_sum.terms[-1][0])
    attn_at = index(slots[2])
    attn_pass = add_blocks(bf16, (attn_wide, attn_at), (attn_got, attn_at), (attn_first, index(1)))
    attn_second = lax.ppermute(attn_pass, PLACE, CROSS)
    while not out_sum.done():
        out_part = out_sum.send()
        out_sum.move(out_part)
        in_part = in_sum.send()
        in_sum.move(in_part)
    attn_second = after(attn_second, out_sum.terms[-1][0], in_sum.terms[-1][0])
    attn_sum = DpSum(
        dp, dp_index, (attn_wide, slots[0]), (attn_got, slots[0]), (attn_first, 0), (attn_second, 0)
    )
    attn_part = attn_sum.send()
    attn_sum.move(attn_part)
    block_diag = lax.ppermute(after(block_mine, attn_part), PLACE, CROSS)
    input_mine = lax.ppermute(after(input_low, attn_part), PLACE, MINE)
    input_other = lax.ppermute(after(input_low, attn_part), PLACE, CROSS)
    out_shard = out_sum.result()
    in_shard = in_sum.result()
    while not attn_sum.done():
        attn_part = attn_sum.send()
        attn_sum.move(attn_part)
    attn_shard = attn_sum.result()
    input_diag = lax.ppermute(after(input_mine, attn_part), PLACE, CROSS)
    block_out = place_rows(chunks, block_low, block_mine, block_other, after(block_diag, attn_part))

    packed = pack(
        place, query_sum, value_sum, first_sums, second_sums, bias_sum, pool_sum, attn_shard, in_shard, out_shard
    )
    packed = sum_everywhere(packed, dp)
    bias_moments_rows = bias_moments.reshape(2, 4, D)
    pool_moments_rows = jnp.pad(
        pool_moments.reshape(2, 2, 5, half), ((0, 0), (0, 0), (0, 0), (0, BLOCK - half))
    ).reshape(2, 2, 5 * BLOCK)
    pool_moments_rows = jnp.pad(pool_moments_rows, ((0, 0), (0, 0), (0, D - 5 * BLOCK)))
    results = finish(
        place, packed, attn_shard, in_shard, out_shard, *weight_slices,
        qkv_moments, out_moments, ffn_in_moments.transpose(0, 2, 1), ffn_out_moments.transpose(0, 2, 1), vector_moments,
        bias_moments_rows, pool_moments_rows,
    )
    qkv_out, out_out, in_out, ff_out_out, vector_out = [results[3 * i : 3 * i + 3] for i in range(5)]
    *_, bias_grad, bias_step, bias_new, pool_grad, pool_step, pool_new, norms = results
    input_grad = place_rows(chunks, input_low, input_mine, input_other, input_diag)

    def pool_of(rows):
        return rows[..., : 5 * BLOCK].reshape(*rows.shape[:-1], 5, BLOCK)[..., :half]

    return (
        block_out[None],
        input_grad[None],
        *qkv_out,
        *out_out,
        *[value.swapaxes(-1, -2) for value in (*in_out, *ff_out_out)],
        *vector_out,
        bias_grad.reshape(FF),
        bias_step.reshape(FF),
        bias_new.reshape(2, FF),
        pool_of(pool_grad),
        pool_of(pool_step),
        pool_of(pool_new),
        norms[1, 0],
        norms[0, :4],
    )


def solution(mesh):
    in_specs = (
        P("dp", "seq", None),
        P("dp", "seq", None),
        P("dp"),
        P(None, None, "lvl"),
        P("lvl", None),
        P("lvl", None),
        P("lvl", None),
        P(),
        P(),
        P(),
        P(None, None, ("dp", "seq"), "lvl"),
        P(None, "lvl", ("dp", "seq")),
        P(None, "lvl", ("dp", "seq")),
        P(None, "lvl", ("dp", "seq")),
        P(),
        P(),
        P(),
    )
    out_specs = (
        P("dp", "seq", None),
        P("dp", "seq", None),
        P(None, ("dp", "seq"), "lvl"),
        P(None, ("dp", "seq"), "lvl"),
        P(None, None, ("dp", "seq"), "lvl"),
        P("lvl", ("dp", "seq")),
        P("lvl", ("dp", "seq")),
        P(None, "lvl", ("dp", "seq")),
        P("lvl", ("dp", "seq")),
        P("lvl", ("dp", "seq")),
        P(None, "lvl", ("dp", "seq")),
        P("lvl", ("dp", "seq")),
        P("lvl", ("dp", "seq")),
        P(None, "lvl", ("dp", "seq")),
        P(),
        P(),
        P(),
        P(),
        P(),
        P(),
        P(),
        P(),
        P(),
        P(),
        P(),
    )
    return jax.shard_map(
        on_device, mesh=mesh, in_specs=in_specs, out_specs=out_specs, check_vma=False
    )
```

```python
import functools
import math

import jax
import jax.numpy as jnp
from jax import lax
from jax.experimental import pallas as pl
from jax.experimental.pallas import tpu as pltpu
from jax.sharding import PartitionSpec as P

D = 768
HEADS = 12
HEAD = 64
FF = 3072
REACH1 = 64
REACH2 = 256
HALO = 320
ROWS = 512
EXT = ROWS + 2 * HALO
NEAR = ROWS + 2 * REACH1
NEAR0 = HALO - REACH1
FAR0 = 48
FAR = 1056
POOLED = 256
TAP0 = 14
BLOCK = 128
BLOCKS = ROWS // BLOCK
PAIRS = HEADS // 4

norm_eps = 1e-05
beta_first = 0.9
beta_second = 0.999
adam_eps = 1e-08
decay_rate = 0.01
adam_step = 10.0
max_rms = 1.0
masked_score = -1e30
score_scale = 1.0 / math.sqrt(HEAD)

f32 = jnp.float32
bf16 = jnp.bfloat16
SWAP = [(0, 1), (1, 0)]
MINE = [(i, i ^ 1) for i in range(4)] + [(4 + i, 4 + (i ^ 2)) for i in range(4)]
CROSS = [(i, i ^ 2) for i in range(4)] + [(4 + i, 4 + (i ^ 1)) for i in range(4)]
PATH = [0, 1, 3, 2, 6, 7, 5, 4]
RIGHTWARD = list(zip(PATH, PATH[1:] + PATH[:1]))
LEFTWARD = [(b, a) for a, b in RIGHTWARD]
PLACE = ("seq", "lvl")

SM = pl.BlockSpec(memory_space=pltpu.SMEM)
HB = pl.BlockSpec(memory_space=pltpu.HBM)


def bfloat(value):
    return value.astype(bf16)


def params(mib=56):
    return pltpu.CompilerParams(vmem_limit_bytes=mib * 1024 * 1024)


def struct(shape, dtype):
    return jax.ShapeDtypeStruct(shape, dtype)


def dot(a, b):
    return jnp.dot(a, b, preferred_element_type=f32)


def dot_nt(a, b):
    return lax.dot_general(a, b, (((1,), (1,)), ((), ())), preferred_element_type=f32)


def turn(value):
    return jnp.transpose(value.astype(f32)).astype(bf16)


def row_mean(value):
    return jnp.mean(value, axis=-1, keepdims=True)


def col_sum(value):
    return jnp.sum(value, axis=0, keepdims=True)


def whole(shape):
    return pl.BlockSpec(shape, lambda *_: (0,) * len(shape), pipeline_mode=pl.Buffered(1))


def wholes(operands):
    return [whole(operand.shape) for operand in operands]


def copy_when(condition, source, target, sem):
    @pl.when(condition)
    def _():
        pltpu.make_async_copy(source, target, sem).start()


def wait_when(condition, target, sem):
    @pl.when(condition)
    def _():
        pltpu.make_async_copy(target, target, sem).wait()


def fetch_attention(place, pieces, weights, out_weight, sems):
    own, mine, other, near_diag, far_diag = pieces
    core = place[4]
    local = own.shape[1]
    copies = []

    def rows_of(owner):
        return pl.ds(pl.multiple_of(owner * local, 64), local)

    for at, piece in enumerate((own, mine, other)):
        rows = rows_of(place[at])
        copies.append(pltpu.make_async_copy(piece.at[pl.ds(0, 3)], weights.at[:, rows], sems.at[at]))
        if out_weight is not None:
            copies.append(pltpu.make_async_copy(piece.at[3], out_weight.at[rows], sems.at[3 + at]))
    for copy in copies:
        copy.start()
    rows = rows_of(place[3])
    targets = [weights.at[pl.ds(0, 2), rows], weights.at[2, rows]]
    if out_weight is not None:
        targets.append(out_weight.at[rows])
    for condition, low, high in ((core == 0, near_diag, far_diag), (core != 0, far_diag, near_diag)):
        for at, source in enumerate((low, high.at[0], high.at[1])[: len(targets)]):
            copy_when(condition, source, targets[at], sems.at[6 + at])

    def wait():
        for copy in copies:
            copy.wait()
        for at, target in enumerate(targets):
            pltpu.make_async_copy(target, target, sems.at[6 + at]).wait()

    return wait


def prepare_kernel(place, edge, tokens, cotangent, low, inputs, incoming, near_mask, far_mask, x, sems):
    core, base, length, seq_len, chunk = [place[i] for i in range(4, 9)]
    first = pl.multiple_of(chunk * ROWS, ROWS)
    left, right = x.at[pl.ds(0, HALO)], x.at[pl.ds(HALO + ROWS, HALO)]
    middle = pltpu.make_async_copy(tokens.at[0, pl.ds(first, ROWS)], inputs, sems.at[0])
    upper = pltpu.make_async_copy(cotangent.at[0, pl.ds(first, ROWS)], incoming, sems.at[3])
    middle.start()
    upper.start()
    starts, ends = chunk == 0, chunk == 3
    left_at = pl.multiple_of(jnp.maximum(first - HALO, 0), 64)
    right_at = pl.multiple_of(jnp.minimum(first + ROWS, 4 * ROWS - HALO), 64)
    copy_when(jnp.logical_not(starts), tokens.at[0, pl.ds(left_at, HALO)], left, sems.at[1])
    copy_when(jnp.logical_and(starts, core == 1), edge, left, sems.at[1])
    copy_when(jnp.logical_not(ends), tokens.at[0, pl.ds(right_at, HALO)], right, sems.at[2])
    copy_when(jnp.logical_and(ends, core == 0), edge, right, sems.at[2])
    no_left = jnp.logical_and(starts, core == 0)
    no_right = jnp.logical_and(ends, core == 1)

    @pl.when(no_left)
    def _():
        x[0:HALO] = jnp.zeros((HALO, D), f32)

    @pl.when(no_right)
    def _():
        x[HALO + ROWS : EXT] = jnp.zeros((HALO, D), f32)

    key_at = lax.broadcasted_iota(jnp.int32, (2 * BLOCK, BLOCK), 0)
    row_at = lax.broadcasted_iota(jnp.int32, (2 * BLOCK, BLOCK), 1)

    def bias(rows, cols, reach):
        same = jnp.where(rows < length, 1, 0) == jnp.where(cols < length, 1, 0)
        seen = (jnp.abs(rows - cols) <= reach) & same & (cols >= 0) & (cols < seq_len)
        return jnp.where(seen, 0.0, masked_score)

    for block in range(BLOCKS):
        rows = base + block * BLOCK + row_at
        near_mask[block] = bias(rows, base + block * BLOCK - REACH1 + key_at, REACH1)
        far_mask[block] = bias(rows, base - REACH2 + 4 * key_at, REACH2)

    middle.wait()
    upper.wait()
    wait_when(jnp.logical_not(no_left), left, sems.at[1])
    wait_when(jnp.logical_not(no_right), right, sems.at[2])
    low[0:HALO] = x[0:HALO].astype(bf16)
    low[HALO : HALO + ROWS] = inputs[...].astype(bf16)
    low[HALO + ROWS : EXT] = x[HALO + ROWS : EXT].astype(bf16)


def prepare(place, edge, tokens, cotangent):
    shapes = (
        struct((EXT, D), bf16),
        struct((ROWS, D), f32),
        struct((ROWS, D), f32),
        struct((BLOCKS, 2 * BLOCK, BLOCK), f32),
        struct((BLOCKS, 2 * BLOCK, BLOCK), f32),
    )
    return pl.pallas_call(
        prepare_kernel,
        out_shape=shapes,
        grid=(1,),
        in_specs=[SM] + [HB] * 3,
        out_specs=tuple(wholes(shapes)),
        scratch_shapes=[pltpu.VMEM((EXT, D), f32), pltpu.SemaphoreType.DMA((4,))],
        compiler_params=params(56),
        name="prepare",
    )(place, edge, tokens, cotangent)


def project_kernel(
    place, low, own, mine, other, near_diag, far_diag, vectors, pool,
    out_weight, query, near_keys, near_values, far_keys, far_values, pool_keys, pool_values,
    weights, key_rows, value_rows, sems,
):
    base, seq_len = place[5], place[7]
    fetch_attention(place, (own, mine, other, near_diag, far_diag), weights, out_weight, sems)()
    wide = PAIRS * BLOCK
    lane = lax.broadcasted_iota(jnp.int32, (ROWS, BLOCK), 1)
    projected = (dot_nt(low[HALO : HALO + ROWS], weights[0]) + vectors[0:1]).astype(bf16).astype(f32) * score_scale
    put_heads(query, projected, lane)

    def inside(rows, start):
        index = start + lax.broadcasted_iota(jnp.int32, (rows, BLOCK), 0)
        return (index >= 0) & (index < seq_len)

    near_inside = inside(NEAR, base - REACH1)
    far_inside = inside(FAR, base - HALO + FAR0)
    for c, near_ref, far_ref, rows_ref in ((1, near_keys, far_keys, key_rows), (2, near_values, far_values, value_rows)):
        near = dot_nt(low[NEAR0 : NEAR0 + NEAR], weights[c, 0:wide])
        far = dot_nt(low[FAR0 : FAR0 + FAR], weights[c, wide:D])
        if c == 2:
            near = near + vectors[1:2, 0:wide]
            far = far + vectors[1:2, wide:D]
        for pair in range(PAIRS):
            lanes = slice(pair * BLOCK, (pair + 1) * BLOCK)
            near_ref[pair] = jnp.where(near_inside, near[:, lanes], 0.0).astype(bf16)
            part = jnp.where(far_inside, far[:, lanes], 0.0).astype(bf16)
            far_ref[pair] = part
            rows_ref[pair] = part.astype(f32)
    for at, rows_ref, pooled_ref in ((0, key_rows, pool_keys), (5, value_rows, pool_values)):
        for pair in range(PAIRS):
            lanes = slice(pair * BLOCK, (pair + 1) * BLOCK)
            total = None
            for tap in range(5):
                part = pool[at + tap : at + tap + 1, lanes] * rows_ref[pair, pl.ds(TAP0 + tap, POOLED, stride=4), :]
                total = part if total is None else total + part
            pooled_ref[pair] = total.astype(bf16)


def put_heads(target, value, lane):
    for pair in range(2 * PAIRS):
        part = value[:, pair * BLOCK : (pair + 1) * BLOCK]
        first = jnp.where(lane < HEAD, part, 0.0).astype(bf16)
        second = jnp.where(lane >= HEAD, part, 0.0).astype(bf16)
        for block in range(BLOCKS):
            rows = slice(block * BLOCK, (block + 1) * BLOCK)
            target[pair, block, 0:BLOCK] = first[rows]
            target[pair, block, BLOCK : 2 * BLOCK] = second[rows]


def project(place, low, pieces, vectors, pool):
    shapes = (
        struct((D, D), bf16),
        struct((2 * PAIRS, BLOCKS, 2 * BLOCK, BLOCK), bf16),
        struct((PAIRS, NEAR, BLOCK), bf16),
        struct((PAIRS, NEAR, BLOCK), bf16),
        struct((PAIRS, FAR, BLOCK), bf16),
        struct((PAIRS, FAR, BLOCK), bf16),
        struct((PAIRS, POOLED, BLOCK), bf16),
        struct((PAIRS, POOLED, BLOCK), bf16),
    )
    return pl.pallas_call(
        project_kernel,
        out_shape=shapes,
        grid=(1,),
        in_specs=[SM, whole((EXT, D))] + [HB] * 5 + wholes((vectors, pool)),
        out_specs=tuple(wholes(shapes)),
        scratch_shapes=[
            pltpu.VMEM((3, D, D), bf16),
            pltpu.VMEM((PAIRS, FAR, BLOCK), f32),
            pltpu.VMEM((PAIRS, FAR, BLOCK), f32),
            pltpu.SemaphoreType.DMA((9,)),
        ],
        compiler_params=params(24),
        name="project",
    )(place, low, *pieces, vectors, pool)


def attend_forward_kernel(
    query, near_keys, near_values, pool_keys, pool_values, near_mask, far_mask,
    mixed, log_total,
):
    def attend(keys, turned, pair, block, mask):
        scores = dot_nt(keys, query[pair, block])
        parts = []
        for e in range(2):
            lanes = slice(e * BLOCK, (e + 1) * BLOCK)
            masked = scores[:, lanes] + mask[block]
            top = jnp.max(masked, axis=0, keepdims=True)
            raised = jnp.exp(masked - top)
            total = jnp.sum(raised, axis=0, keepdims=True)
            log_total[pair, block, :, lanes] = top + jnp.log(total)
            parts.append((raised * (1.0 / total)).astype(bf16))
        both = dot(turned, jnp.concatenate(parts, axis=1))
        output = jnp.concatenate([both[0:HEAD, 0:BLOCK], both[HEAD:BLOCK, BLOCK : 2 * BLOCK]], axis=0)
        lanes = pl.ds(pl.multiple_of(pair * BLOCK, BLOCK), BLOCK)
        mixed[block * BLOCK : (block + 1) * BLOCK, lanes] = turn(output)

    def near_pair(pair, carry):
        turned = turn(near_values[pair])
        for block in range(BLOCKS):
            window = slice(block * BLOCK, (block + 2) * BLOCK)
            attend(near_keys[pair, window], turned[:, window], pair, block, near_mask)
        return carry

    def far_pair(pair, carry):
        turned = turn(pool_values[pair])
        for block in range(BLOCKS):
            attend(pool_keys[pair], turned, PAIRS + pair, block, far_mask)
        return carry

    lax.fori_loop(0, PAIRS, near_pair, 0)
    lax.fori_loop(0, PAIRS, far_pair, 0)


def attend_forward(*operands):
    shapes = (struct((ROWS, D), bf16), struct((2 * PAIRS, BLOCKS, 1, 2 * BLOCK), f32))
    return pl.pallas_call(
        attend_forward_kernel,
        out_shape=shapes,
        grid=(1,),
        in_specs=wholes(operands),
        out_specs=tuple(wholes(shapes)),
        compiler_params=params(14),
        name="attend_forward",
    )(*operands)


def attend_backward_kernel(
    grad, query, near_keys, near_values, far_keys, far_values, pool_keys, pool_values, near_mask, far_mask, log_total,
    pool,
    query_grad, near_low, far_low, near_own, pool_own, to_left, to_right, query_sum, pool_sum,
    near_total, pool_total, far_rows, shifted,
):
    near_total[...] = jnp.zeros_like(near_total)
    pool_total[...] = jnp.zeros_like(pool_total)
    query_grad[0:REACH1] = jnp.zeros((REACH1, D), bf16)
    query_grad[NEAR - REACH1 : NEAR] = jnp.zeros((REACH1, D), bf16)

    def back(keys, values, turned, pair, block, mask):
        part = grad[pair, block]
        asked = query[pair, block]
        scores = dot_nt(keys, asked)
        chance_grads = dot_nt(values, part)
        chances = []
        score_grads = []
        for e in range(2):
            lanes = slice(e * BLOCK, (e + 1) * BLOCK)
            chance = jnp.exp(scores[:, lanes] + mask[block] - log_total[pair, block, :, lanes])
            chance_grad = chance_grads[:, lanes]
            mean = jnp.sum(chance * chance_grad, axis=0, keepdims=True)
            score_grads.append((chance * (chance_grad - mean)).astype(bf16))
            chances.append(chance.astype(bf16))
        score_grad = jnp.concatenate(score_grads, axis=1)
        both = dot(turned, score_grad)
        output = jnp.concatenate([both[0:HEAD, 0:BLOCK], both[HEAD:BLOCK, BLOCK : 2 * BLOCK]], axis=0)
        output = jnp.transpose(output) * score_scale
        lanes = pl.ds(pl.multiple_of(pair * BLOCK, BLOCK), BLOCK)
        query_grad[REACH1 + block * BLOCK : REACH1 + (block + 1) * BLOCK, lanes] = output.astype(bf16)
        return (col_sum(output), dot(score_grad, asked), dot(jnp.concatenate(chances, axis=1), part))

    def near_pair(pair, carry):
        turned = turn(near_keys[pair])
        sums = jnp.zeros((1, BLOCK), f32)
        for block in range(BLOCKS):
            window = slice(block * BLOCK, (block + 2) * BLOCK)
            part, keys, values = back(
                near_keys[pair, window], near_values[pair, window], turned[:, window], pair, block, near_mask
            )
            near_total[0, pair, window] += keys
            near_total[1, pair, window] += values
            sums = sums + part
        query_sum[pair] = sums
        return carry

    def far_pair(pair, carry):
        turned = turn(pool_keys[pair])
        sums = jnp.zeros((1, BLOCK), f32)
        for block in range(BLOCKS):
            part, keys, values = back(pool_keys[pair], pool_values[pair], turned, PAIRS + pair, block, far_mask)
            pool_total[0, pair] += keys
            pool_total[1, pair] += values
            sums = sums + part
        query_sum[PAIRS + pair] = sums
        return carry

    lax.fori_loop(0, PAIRS, near_pair, 0)
    lax.fori_loop(0, PAIRS, far_pair, 0)

    side = REACH2 // 4
    own_pool = ROWS // 4
    for kind in range(2):
        near_low[kind] = near_total[kind].astype(bf16)
        near_own[kind] = near_total[kind, :, REACH1 : REACH1 + ROWS]
        pool_own[kind] = pool_total[kind, :, side : side + own_pool + 8]
        to_left[kind, :, 0:REACH1] = near_total[kind, :, 0:REACH1].astype(bf16)
        to_left[kind, :, REACH1 : REACH1 + side + 16] = pool_total[kind, :, 0 : side + 16].astype(bf16)
        to_right[kind, :, 0:REACH1] = near_total[kind, :, NEAR - REACH1 : NEAR].astype(bf16)
        to_right[kind, :, REACH1 : REACH1 + side] = pool_total[kind, :, side + own_pool :].astype(bf16)

    for kind, rows_ref in ((0, far_keys), (1, far_values)):
        for pair in range(PAIRS):
            lanes = slice(pair * BLOCK, (pair + 1) * BLOCK)
            far_rows[0:FAR] = rows_ref[pair].astype(f32)
            pooled = pool_total[kind, pair]
            for tap in range(5):
                pool_sum[5 * kind + tap : 5 * kind + tap + 1, lanes] = col_sum(
                    pooled * far_rows[pl.ds(TAP0 + tap, POOLED, stride=4), :]
                )
            shifted[0:8] = jnp.zeros((8, BLOCK), f32)
            shifted[8 : 8 + POOLED] = pooled
            weight = [pool[5 * kind + tap : 5 * kind + tap + 1, lanes] for tap in range(5)]
            first = FAR0 + TAP0
            far_rows[0 : first + 2] = jnp.zeros((first + 2, BLOCK), f32)
            far_rows[EXT - 72 : EXT] = jnp.zeros((72, BLOCK), f32)
            far_rows[pl.ds(first, POOLED, stride=4), :] = weight[0] * pooled + weight[4] * shifted[7 : 7 + POOLED]
            for tap in range(1, 4):
                far_rows[pl.ds(first + tap, POOLED, stride=4), :] = weight[tap] * pooled
            far_rows[first + 4 * POOLED : first + 4 * POOLED + 1] = weight[4] * pooled[POOLED - 1 : POOLED]
            far_low[kind, pair] = far_rows[...].astype(bf16)


def attend_backward(*operands):
    side = REACH2 // 4
    shapes = (
        struct((NEAR, D), bf16),
        struct((2, PAIRS, NEAR, BLOCK), bf16),
        struct((2, PAIRS, EXT, BLOCK), bf16),
        struct((2, PAIRS, ROWS, BLOCK), f32),
        struct((2, PAIRS, ROWS // 4 + 8, BLOCK), f32),
        struct((2, PAIRS, REACH1 + side + 16, BLOCK), bf16),
        struct((2, PAIRS, REACH1 + side, BLOCK), bf16),
        struct((2 * PAIRS, 1, BLOCK), f32),
        struct((10, PAIRS * BLOCK), f32),
    )
    return pl.pallas_call(
        attend_backward_kernel,
        out_shape=shapes,
        grid=(1,),
        in_specs=wholes(operands),
        out_specs=tuple(wholes(shapes)),
        scratch_shapes=[
            pltpu.VMEM((2, PAIRS, NEAR, BLOCK), f32),
            pltpu.VMEM((2, PAIRS, POOLED, BLOCK), f32),
            pltpu.VMEM((EXT, BLOCK), f32),
            pltpu.VMEM((POOLED + 8, BLOCK), f32),
        ],
        compiler_params=params(24),
        name="attend_backward",
    )(*operands)


def fetch_hidden(place, pieces, held, sems):
    own, mine, other, near_diag, far_diag = pieces
    core = place[4]
    half = D // 2
    copies = [pltpu.make_async_copy(piece, held.at[at], sems.at[at]) for at, piece in enumerate((own, mine, other))]
    for at, (piece, where) in enumerate(((near_diag, core), (far_diag, 1 - core))):
        target = held.at[3, pl.ds(pl.multiple_of(where * half, half), half)]
        copies.append(pltpu.make_async_copy(piece, target, sems.at[3 + at]))
    for copy in copies:
        copy.start()


def wait_hidden(j, held, sems):
    @pl.when(j < 3)
    def _():
        pltpu.make_async_copy(held.at[j], held.at[j], sems.at[j]).wait()

    @pl.when(j == 3)
    def _():
        for at in range(2):
            target = held.at[3, pl.ds(at * (D // 2), D // 2)]
            pltpu.make_async_copy(target, target, sems.at[3 + at]).wait()


def gelu_block(first_low, held, bias, act, slope, j):
    for block in range(BLOCKS):
        rows = slice(block * BLOCK, (block + 1) * BLOCK)
        pre = dot_nt(first_low[rows], held) + bias
        gate = 0.5 + 0.5 * lax.erf(pre * math.sqrt(0.5))
        act[0, rows] = (pre * gate).astype(bf16)
        slope[0, rows] = gate + pre * (jnp.exp(-0.5 * pre * pre) * (1.0 / math.sqrt(2.0 * math.pi)))


def feed_forward_kernel(
    mixed, out_weight, inputs, vectors, bias, own, mine,
    normed, inverse, first_low, act, slope,
    held, total, sems,
):
    j = pl.program_id(0)

    @pl.when(j == 0)
    def _():
        copies = [pltpu.make_async_copy(piece, held.at[at], sems.at[at]) for at, piece in enumerate((own, mine))]
        for copy in copies:
            copy.start()
        total[...] = dot(mixed[...], out_weight[...])

        def rows_step(i, carry):
            rows = pl.ds(pl.multiple_of(i * BLOCK, BLOCK), BLOCK)
            value = inputs[rows] + total[rows] + vectors[2:3]
            centered = value - row_mean(value)
            inv = lax.rsqrt(row_mean(centered * centered) + norm_eps)
            z = centered * inv
            normed[rows] = z
            inverse[rows] = inv
            first_low[rows] = (z * vectors[4:5] + vectors[5:6]).astype(bf16)
            return carry

        lax.fori_loop(0, BLOCKS, rows_step, 0)

    pltpu.make_async_copy(held.at[j], held.at[j], sems.at[j]).wait()
    gelu_block(first_low, held[j], bias[j], act, slope, j)


def feed_forward(mixed, out_weight, inputs, vectors, bias, pieces):
    shapes = (
        struct((ROWS, D), f32),
        struct((ROWS, 1), f32),
        struct((ROWS, D), bf16),
        struct((2, ROWS, D), bf16),
        struct((2, ROWS, D), f32),
    )
    block = pl.BlockSpec((1, ROWS, D), lambda j: (j, 0, 0))
    return pl.pallas_call(
        feed_forward_kernel,
        out_shape=shapes,
        grid=(2,),
        in_specs=wholes((mixed, out_weight, inputs, vectors, bias)) + [HB] * 2,
        out_specs=(*wholes(shapes[:3]), block, block),
        scratch_shapes=[
            pltpu.VMEM((2, D, D), bf16),
            pltpu.VMEM((ROWS, D), f32),
            pltpu.SemaphoreType.DMA((2,)),
        ],
        compiler_params=params(22),
        name="feed_forward",
    )(mixed, out_weight, inputs, vectors, bias, *pieces)


def fetch_rest(place, pieces, held, sems):
    other, near_diag, far_diag = pieces
    half = D // 2
    core = place[4]
    pltpu.make_async_copy(other, held.at[0], sems.at[0]).start()
    for at, (piece, where) in enumerate(((near_diag, core), (far_diag, 1 - core))):
        target = held.at[1, pl.ds(pl.multiple_of(where * half, half), half)]
        pltpu.make_async_copy(piece, target, sems.at[1 + at]).start()


def wait_rest(j, held, sems):
    @pl.when(j == 0)
    def _():
        pltpu.make_async_copy(held.at[0], held.at[0], sems.at[0]).wait()

    @pl.when(j == 1)
    def _():
        for at in range(2):
            target = held.at[1, pl.ds(at * (D // 2), D // 2)]
            pltpu.make_async_copy(target, target, sems.at[1 + at]).wait()


def feed_forward_rest_kernel(
    place, first_low, bias, other, near_diag, far_diag,
    act, slope,
    held, sems,
):
    j = pl.program_id(0)

    @pl.when(j == 0)
    def _():
        fetch_rest(place, (other, near_diag, far_diag), held, sems)

    wait_rest(j, held, sems)
    gelu_block(first_low, held[j], bias[2 + j], act, slope, j)


def feed_forward_rest(place, first_low, bias, pieces):
    block = pl.BlockSpec((1, ROWS, D), lambda j: (j, 0, 0))
    return pl.pallas_call(
        feed_forward_rest_kernel,
        out_shape=(struct((2, ROWS, D), bf16), struct((2, ROWS, D), f32)),
        grid=(2,),
        in_specs=[SM, *wholes((first_low, bias))] + [HB] * 3,
        out_specs=(block, block),
        scratch_shapes=[pltpu.VMEM((2, D, D), bf16), pltpu.SemaphoreType.DMA((3,))],
        compiler_params=params(14),
        name="feed_forward_rest",
    )(place, first_low, bias, *pieces)


def two_halves(rows, cols):
    return [
        pl.BlockSpec((1, rows, cols), lambda j: (jnp.minimum(j, 1), 0, 0)),
        pl.BlockSpec((1, rows, cols), lambda j: (jnp.maximum(j - 2, 0), 0, 0)),
    ]


def with_half(j, first, second, use):
    @pl.when(j < 2)
    def _():
        use(first)

    @pl.when(j >= 2)
    def _():
        use(second)


def branch_kernel(
    place, act, act_rest, normed, incoming, vectors, own, mine, other, near_diag, far_diag,
    block_low, branch_low, second, sums,
    held, total, sems,
):
    j = pl.program_id(0)

    @pl.when(j == 0)
    def _():
        fetch_hidden(place, (own, mine, other, near_diag, far_diag), held, sems)
        sums[...] = jnp.zeros_like(sums)
        total[...] = jnp.zeros_like(total)

    wait_hidden(j, held, sems)

    def add(part):
        total[...] += dot(part[0], held[j])

    with_half(j, act, act_rest, add)

    @pl.when(j == 3)
    def _():

        def second_step(i, carry):
            rows = pl.ds(pl.multiple_of(i * BLOCK, BLOCK), BLOCK)
            first = normed[rows] * vectors[4:5] + vectors[5:6]
            value = first + total[rows] + vectors[3:4]
            centered = value - row_mean(value)
            inv = lax.rsqrt(row_mean(centered * centered) + norm_eps)
            z = centered * inv
            block_low[rows] = (z * vectors[6:7] + vectors[7:8]).astype(bf16)
            upper = incoming[rows]
            scaled = upper * vectors[6:7]
            grad = inv * (scaled - row_mean(scaled) - z * row_mean(scaled * z))
            second[rows] = grad
            branch_low[rows] = grad.astype(bf16)
            sums[0:1] += col_sum(grad)
            sums[1:2] += col_sum(upper * z)
            sums[2:3] += col_sum(upper)
            return carry

        lax.fori_loop(0, BLOCKS, second_step, 0)


def branch_of(place, act, act_rest, normed, incoming, vectors, pieces):
    shapes = (
        struct((ROWS, D), bf16),
        struct((ROWS, D), bf16),
        struct((ROWS, D), f32),
        struct((8, D), f32),
    )
    return pl.pallas_call(
        branch_kernel,
        out_shape=shapes,
        grid=(4,),
        in_specs=[SM, *two_halves(ROWS, D), *wholes((normed, incoming, vectors))] + [HB] * 5,
        out_specs=tuple(wholes(shapes)),
        scratch_shapes=[
            pltpu.VMEM((4, D, D), bf16),
            pltpu.VMEM((ROWS, D), f32),
            pltpu.SemaphoreType.DMA((5,)),
        ],
        compiler_params=params(22),
        name="branch",
    )(place, act, act_rest, normed, incoming, vectors, *pieces)


def hidden_back(j, slope, branch_low, in_held, out_held, pre_low, bias_sum, total):
    pre_grad = dot_nt(branch_low[...], out_held[j]) * slope[0]
    pre_low[0] = pre_grad.astype(bf16)
    bias_sum[0] = col_sum(pre_grad)
    total[...] += dot(pre_low[0], in_held[j])


def feed_back_kernel(
    slope, branch_low, second, in_own, in_mine, out_own, out_mine,
    pre_low, bias_sum, total,
    in_held, out_held, sems,
):
    j = pl.program_id(0)

    @pl.when(j == 0)
    def _():
        for at, (piece, target) in enumerate(
            ((out_own, out_held.at[0]), (in_own, in_held.at[0]), (out_mine, out_held.at[1]), (in_mine, in_held.at[1]))
        ):
            pltpu.make_async_copy(piece, target, sems.at[at]).start()
        total[...] = second[...]

    for held, at in ((out_held, 0), (in_held, 1)):
        pltpu.make_async_copy(held.at[j], held.at[j], sems.at[2 * j + at]).wait()
    hidden_back(j, slope, branch_low, in_held, out_held, pre_low, bias_sum, total)


def feed_back(slope, branch_low, second, in_pieces, out_pieces):
    shapes = (struct((2, ROWS, D), bf16), struct((2, 1, D), f32), struct((ROWS, D), f32))
    block = pl.BlockSpec((1, ROWS, D), lambda j: (j, 0, 0))
    return pl.pallas_call(
        feed_back_kernel,
        out_shape=shapes,
        grid=(2,),
        in_specs=[block, *wholes((branch_low, second))] + [HB] * 4,
        out_specs=(block, pl.BlockSpec((1, 1, D), lambda j: (j, 0, 0)), whole((ROWS, D))),
        scratch_shapes=[
            pltpu.VMEM((2, D, D), bf16),
            pltpu.VMEM((2, D, D), bf16),
            pltpu.SemaphoreType.DMA((4,)),
        ],
        compiler_params=params(22),
        name="feed_back",
    )(slope, branch_low, second, *in_pieces, *out_pieces)


def feed_back_rest_kernel(
    place, slope, branch_low, partial, normed, inverse, vectors, out_weight,
    in_other, in_near, in_far, out_other, out_near, out_far,
    pre_low, bias_sum, attn_low, attn_grad, heads_grad, sums,
    in_held, out_held, total, in_sems, out_sems,
):
    j = pl.program_id(0)

    @pl.when(j == 0)
    def _():
        fetch_rest(place, (out_other, out_near, out_far), out_held, out_sems)
        fetch_rest(place, (in_other, in_near, in_far), in_held, in_sems)
        sums[...] = jnp.zeros_like(sums)
        total[...] = partial[...]

    wait_rest(j, out_held, out_sems)
    wait_rest(j, in_held, in_sems)
    hidden_back(j, slope, branch_low, in_held, out_held, pre_low, bias_sum, total)

    @pl.when(j == 1)
    def _():
        def first_step(i, carry):
            rows = pl.ds(pl.multiple_of(i * BLOCK, BLOCK), BLOCK)
            z = normed[rows]
            first_grad = total[rows]
            scaled = first_grad * vectors[4:5]
            grad = inverse[rows] * (scaled - row_mean(scaled) - z * row_mean(scaled * z))
            attn_grad[rows] = grad
            attn_low[rows] = grad.astype(bf16)
            sums[0:1] += col_sum(grad)
            sums[1:2] += col_sum(first_grad * z)
            sums[2:3] += col_sum(first_grad)
            return carry

        lax.fori_loop(0, BLOCKS, first_step, 0)
        total[...] = dot_nt(attn_low[...], out_weight[...])
        put_heads(heads_grad, total, lax.broadcasted_iota(jnp.int32, (ROWS, BLOCK), 1))


def feed_back_rest(place, slope, branch_low, partial, normed, inverse, vectors, out_weight, in_pieces, out_pieces):
    shapes = (
        struct((2, ROWS, D), bf16),
        struct((2, 1, D), f32),
        struct((ROWS, D), bf16),
        struct((ROWS, D), f32),
        struct((2 * PAIRS, BLOCKS, 2 * BLOCK, BLOCK), bf16),
        struct((8, D), f32),
    )
    block = pl.BlockSpec((1, ROWS, D), lambda j: (j, 0, 0))
    return pl.pallas_call(
        feed_back_rest_kernel,
        out_shape=shapes,
        grid=(2,),
        in_specs=[SM, block, *wholes((branch_low, partial, normed, inverse, vectors, out_weight))] + [HB] * 6,
        out_specs=(block, pl.BlockSpec((1, 1, D), lambda j: (j, 0, 0)), *wholes(shapes[2:])),
        scratch_shapes=[
            pltpu.VMEM((2, D, D), bf16),
            pltpu.VMEM((2, D, D), bf16),
            pltpu.VMEM((ROWS, D), f32),
            pltpu.SemaphoreType.DMA((3,)),
            pltpu.SemaphoreType.DMA((3,)),
        ],
        compiler_params=params(28),
        name="feed_back_rest",
    )(place, slope, branch_low, partial, normed, inverse, vectors, out_weight, *in_pieces, *out_pieces)


def ffn_grad_kernel(order, rows, *refs):
    cols, (own, sent, turned) = refs[:-3], refs[-3:]
    j = pl.program_id(0)

    @pl.when(j == 0)
    def _():
        turned[...] = dot_nt(order[...], rows[...]).astype(bf16)

    def product(part):
        result = dot(turned[...], part[0]).astype(bf16)
        own[0] = result[: D // 2]
        sent[0] = result[D // 2 :]

    if len(cols) == 1:
        product(cols[0])
    else:
        with_half(j, *cols, product)


def ffn_grad(order, rows, *cols):
    block = pl.BlockSpec((1, D // 2, D), lambda j: (j, 0, 0))
    one = [pl.BlockSpec((1, ROWS, D), lambda j: (j, 0, 0))]
    return pl.pallas_call(
        ffn_grad_kernel,
        out_shape=(struct((4, D // 2, D), bf16),) * 2,
        grid=(4,),
        in_specs=wholes((order, rows)) + (one if len(cols) == 1 else two_halves(ROWS, D)),
        out_specs=(block, block),
        scratch_shapes=[pltpu.VMEM((D, ROWS), bf16)],
        compiler_params=params(16),
        name="ffn_grad",
    )(order, rows, *cols)


def turn_kernel(order, x, turned):
    turned[...] = dot_nt(order[...], x[...]).astype(bf16)


def turn_rows(order, x):
    return pl.pallas_call(
        turn_kernel,
        out_shape=struct((D, EXT), bf16),
        grid=(1,),
        in_specs=wholes((order, x)),
        out_specs=whole((D, EXT)),
        compiler_params=params(12),
        name="turn_rows",
    )(order, x)


def attn_weight_grad_kernel(order, turned, attn_low, mixed, query_grad, near_low, far_low, target, held):
    near_x = turned[:, NEAR0 : NEAR0 + NEAR]
    held[0] = dot(near_x, query_grad[...])
    for kind in range(2):
        near = jnp.concatenate([near_low[kind, pair] for pair in range(PAIRS)], axis=1)
        far = jnp.concatenate([far_low[kind, pair] for pair in range(PAIRS)], axis=1)
        held[1 + kind, :, 0 : D // 2] = dot(near_x, near)
        held[1 + kind, :, D // 2 : D] = dot(turned[...], far)
    held[3] = dot(dot_nt(order[...], attn_low[...]).astype(bf16), mixed[...])

    rows = D // 8
    lane = lax.broadcasted_iota(jnp.int32, (rows, BLOCK), 1)

    def step(i, carry):
        here = pl.ds(pl.multiple_of(i * rows, rows), rows)
        for pair in range(2):
            tiles = [
                [held[c, here, (3 * pair + t) * BLOCK : (3 * pair + t + 1) * BLOCK] for t in range(3)] for c in range(4)
            ]
            for odd in range(2):
                parts = [tiles[c][2 * odd] for c in range(4)]
                for c in (0, 2):
                    a, b = (tiles[c][1], tiles[c + 1][1])
                    if odd:
                        parts.append(jnp.where(lane < HEAD, pltpu.roll(a, HEAD, 1), b))
                    else:
                        parts.append(jnp.where(lane < HEAD, a, pltpu.roll(b, HEAD, 1)))
                for t, part in enumerate(parts):
                    target[2 * pair + odd, here, t * BLOCK : (t + 1) * BLOCK] = part.astype(bf16)
        return carry

    lax.fori_loop(0, 4, step, 0)


def attn_weight_grad(half, order, turned, attn_low, mixed, query_grad, near_low, far_low):
    return pl.pallas_call(
        attn_weight_grad_kernel,
        out_shape=struct((4, D // 2, D), bf16),
        grid=(1,),
        in_specs=[
            pl.BlockSpec((D // 2, D), lambda i: (half, 0)),
            pl.BlockSpec((D // 2, EXT), lambda i: (half, 0)),
        ]
        + [whole(a.shape) for a in (attn_low, mixed, query_grad, near_low, far_low)],
        out_specs=whole((4, D // 2, D)),
        scratch_shapes=[pltpu.VMEM((4, D // 2, D), f32)],
        compiler_params=params(24),
        name="attn_weight_grad",
    )(order, turned, attn_low, mixed, query_grad, near_low, far_low)


def add_kernel(groups, steps, *refs):
    count = sum(groups)
    operands, target = refs[count : 2 * count], refs[2 * count]
    step = pl.program_id(0)
    at = 0
    for group, terms in enumerate(groups):
        mine = operands[at : at + terms]
        at += terms

        @pl.when((step >= group * steps) & (step < (group + 1) * steps))
        def _(mine=mine):
            total = mine[0][...].astype(f32)
            for operand in mine[1:]:
                total = total + operand[...].astype(f32)
            target[...] = total.astype(target.dtype)


def add_blocks(dtype, *groups, mib=16):
    steps = groups[0][0][1].shape[0]
    rows, cols = groups[0][0][0].shape[1:]
    block = (1, rows, cols)
    terms = [(array, at, group) for group, members in enumerate(groups) for array, at in members]
    count = len(terms)
    total = steps * len(groups)

    def spec(k, group):
        return pl.BlockSpec(block, lambda i, *at: (at[k][jnp.clip(i - group * steps, 0, steps - 1)], 0, 0))

    return pl.pallas_call(
        functools.partial(add_kernel, [len(members) for members in groups], steps),
        out_shape=struct((total, rows, cols), dtype),
        grid_spec=pltpu.PrefetchScalarGridSpec(
            num_scalar_prefetch=count,
            grid=(total,),
            in_specs=[spec(k, group) for k, (_, _, group) in enumerate(terms)],
            out_specs=pl.BlockSpec(block, lambda i, *at: (i, 0, 0)),
        ),
        compiler_params=params(mib),
        name="add_blocks",
    )(*[at for _, at, _ in terms], *[array for array, _, _ in terms])


def input_grad_kernel(
    place, query_grad, near_own, pool_own, from_left, from_right, attn_grad, pool, block_low,
    own, mine, other, near_diag, far_diag,
    low, value_sum,
    pooled, rows_held, grads, weights, sems,
):
    wait_weights = fetch_attention(place, (own, mine, other, near_diag, far_diag), weights, None, sems)
    left_on = jnp.where(place[5] > 0, 1.0, 0.0)
    right_on = jnp.where(place[5] + ROWS < place[7], 1.0, 0.0)
    side = REACH2 // 4
    own_pool = ROWS // 4
    wide = PAIRS * BLOCK
    for kind in range(2):
        for pair in range(PAIRS):
            lanes = slice(pair * BLOCK, (pair + 1) * BLOCK)
            rows_held[...] = near_own[kind, pair]
            rows_held[0:REACH1] += from_left[kind, pair, 0:REACH1].astype(f32) * left_on
            rows_held[ROWS - REACH1 : ROWS] += from_right[kind, pair, 0:REACH1].astype(f32) * right_on
            if kind:
                value_sum[:, lanes] = col_sum(rows_held[...])
            grads[kind, :, lanes] = rows_held[...].astype(bf16)

            pooled[...] = pool_own[kind, pair]
            pooled[0:side] += from_left[kind, pair, REACH1 : REACH1 + side].astype(f32) * left_on
            pooled[side : own_pool + 8] += from_right[kind, pair, REACH1 : REACH1 + side + 8].astype(f32) * right_on
            here, following = pooled[0:own_pool], pooled[1 : own_pool + 1]
            weight = [pool[5 * kind + tap : 5 * kind + tap + 1, lanes] for tap in range(5)]
            rows_held[pl.ds(0, own_pool, stride=4), :] = weight[2] * here
            rows_held[pl.ds(1, own_pool, stride=4), :] = weight[3] * here
            rows_held[pl.ds(2, own_pool, stride=4), :] = weight[4] * here + weight[0] * following
            rows_held[pl.ds(3, own_pool, stride=4), :] = weight[1] * following
            lanes = slice(wide + pair * BLOCK, wide + (pair + 1) * BLOCK)
            if kind:
                value_sum[:, lanes] = col_sum(rows_held[...])
            grads[kind, :, lanes] = rows_held[...].astype(bf16)
    wait_weights()
    total = attn_grad[...] + dot(query_grad[REACH1 : REACH1 + ROWS], weights[0])
    total = total + dot(grads[0], weights[1])
    low[1] = (total + dot(grads[1], weights[2])).astype(bf16)
    low[0] = block_low[...]


def input_grad_of(place, query_grad, near_own, pool_own, from_left, from_right, attn_grad, pool, block_low, pieces):
    return pl.pallas_call(
        input_grad_kernel,
        out_shape=(struct((2, ROWS, D), bf16), struct((1, D), f32)),
        grid=(1,),
        in_specs=[SM, *wholes((query_grad, near_own, pool_own, from_left, from_right, attn_grad, pool, block_low))] + [HB] * 5,
        out_specs=(whole((2, ROWS, D)), whole((1, D))),
        scratch_shapes=[
            pltpu.VMEM((ROWS // 4 + 8, BLOCK), f32),
            pltpu.VMEM((ROWS, BLOCK), f32),
            pltpu.VMEM((2, ROWS, D), bf16),
            pltpu.VMEM((3, D, D), bf16),
            pltpu.SemaphoreType.DMA((9,)),
        ],
        compiler_params=params(),
        name="input_grad",
    )(place, query_grad, near_own, pool_own, from_left, from_right, attn_grad, pool, block_low, *pieces)


def place_kernel(at, own, mine, other, block_out, input_grad):
    step = pl.program_id(0)
    for k, piece in enumerate((own, mine, other)):

        @pl.when(step == k)
        def _(piece=piece):
            block_out[...] = piece[0].astype(f32)
            input_grad[...] = piece[1].astype(f32)


def place_rows(at, *pieces):
    chunk = pl.BlockSpec((ROWS, D), lambda i, at: (at[i], 0))
    return pl.pallas_call(
        place_kernel,
        out_shape=(struct((4 * ROWS, D), f32),) * 2,
        grid_spec=pltpu.PrefetchScalarGridSpec(
            num_scalar_prefetch=1,
            grid=(3,),
            in_specs=[whole((2, ROWS, D))] * 3,
            out_specs=(chunk, chunk),
        ),
        compiler_params=params(56),
        name="place_rows",
    )(at, *pieces)


def place_last_kernel(at, piece, block_held, input_held, block_out, input_grad):
    block_out[...] = piece[0].astype(f32)
    input_grad[...] = piece[1].astype(f32)


def place_last(at, piece, block_out, input_grad):
    rows = ROWS // 2
    chunk = pl.BlockSpec((rows, D), lambda i, at: (at[3] * 2 + i, 0))
    return pl.pallas_call(
        place_last_kernel,
        out_shape=(struct((4 * ROWS, D), f32),) * 2,
        grid_spec=pltpu.PrefetchScalarGridSpec(
            num_scalar_prefetch=1,
            grid=(2,),
            in_specs=[pl.BlockSpec((2, rows, D), lambda i, at: (0, i, 0)), HB, HB],
            out_specs=(chunk, chunk),
        ),
        input_output_aliases={2: 0, 3: 1},
        compiler_params=params(56),
        name="place_last",
    )(at, piece, block_out, input_grad)


def slices_kernel(
    at, qkv, out_weight, in_weight, ff_out_weight,
    qkv_slice, out_slice, in_slice, ff_out_slice,
    qkv_held, out_held, in_held, ff_out_held, sems,
):
    first, shift = pl.multiple_of(at[0], BLOCK), at[1]
    lanes = pl.ds(first, 2 * BLOCK)
    copies = [
        pltpu.make_async_copy(in_weight.at[:, lanes], in_held, sems.at[0]),
        pltpu.make_async_copy(ff_out_weight.at[:, lanes], ff_out_held, sems.at[1]),
        pltpu.make_async_copy(out_weight.at[:, lanes], out_held, sems.at[2]),
        pltpu.make_async_copy(qkv.at[:, :, lanes], qkv_held, sems.at[3]),
    ]
    for copy in copies:
        copy.start()
    width = in_slice.shape[0]

    def moved(value):
        return pltpu.roll(value, shift, 1)[:, 0:BLOCK]

    for copy, held, target in ((copies[0], in_held, in_slice), (copies[1], ff_out_held, ff_out_slice)):
        copy.wait()
        target[...] = jnp.transpose(moved(held[...]))[0:width]
    copies[2].wait()
    out_slice[...] = moved(out_held[...])[:, 0:width]
    copies[3].wait()
    for c in range(3):
        qkv_slice[c] = jnp.transpose(moved(qkv_held[c]))[0:width]


def own_slices(offset, width, qkv_weight, out_weight, in_weight, ff_out_weight):
    local = qkv_weight.shape[2]
    first = jnp.minimum(offset // BLOCK * BLOCK, D - 2 * BLOCK)
    shift = (2 * BLOCK - (offset - first)) % (2 * BLOCK)
    shapes = (
        struct((3, width, local), f32),
        struct((local, width), f32),
        struct((width, D), f32),
        struct((width, D), f32),
    )
    return pl.pallas_call(
        slices_kernel,
        out_shape=shapes,
        grid=(1,),
        in_specs=[SM] + [HB] * 4,
        out_specs=tuple(wholes(shapes)),
        scratch_shapes=[
            pltpu.VMEM((3, local, 2 * BLOCK), f32),
            pltpu.VMEM((local, 2 * BLOCK), f32),
            pltpu.VMEM((D, 2 * BLOCK), f32),
            pltpu.VMEM((D, 2 * BLOCK), f32),
            pltpu.SemaphoreType.DMA((4,)),
        ],
        compiler_params=params(56),
        name="own_slices",
    )(
        jnp.stack([first, shift]).astype(jnp.int32),
        qkv_weight.transpose(0, 2, 1),
        out_weight,
        in_weight,
        ff_out_weight,
    )


def square_sum(value):
    return jnp.sum(value * value)


def pack_kernel(place, query_sum, value_sum, first_sums, second_sums, bias_sum, bias_rest, pool_sum, attn, hidden, packed):
    packed[...] = jnp.zeros_like(packed)
    for pair in range(2 * PAIRS):
        packed[0:1, pair * BLOCK : (pair + 1) * BLOCK] = query_sum[pair]
    packed[1:2] = value_sum[...]
    packed[2:3] = first_sums[0:1]
    packed[3:4] = second_sums[0:1]
    packed[4:6] = first_sums[1:3]
    packed[6:8] = second_sums[1:3]
    for at in range(2):
        packed[pl.ds(8 + place[at], 1), :] = bias_sum[at]
        packed[pl.ds(8 + place[2 + at], 1), :] = bias_rest[at]
    lane = lax.broadcasted_iota(jnp.int32, (1, BLOCK), 1)
    wide = lax.broadcasted_iota(jnp.int32, (1, PAIRS * BLOCK), 1)
    for tap in range(10):
        row = jnp.zeros((1, BLOCK), f32)
        taps = pool_sum[tap : tap + 1, :]
        for head in range(HEADS // 2):
            mine = (wide >= head * HEAD) & (wide < (head + 1) * HEAD)
            row = row + jnp.where(lane == head, jnp.sum(jnp.where(mine, taps, 0.0), axis=1, keepdims=True), 0.0)
        at = 12 + tap // 5
        packed[at : at + 1, (tap % 5) * BLOCK : (tap % 5 + 1) * BLOCK] = row
    first = square_sum(attn[...])
    second = square_sum(hidden[...])
    packed[14:15, 0:BLOCK] = jnp.where(lane == 0, first, jnp.where(lane == 1, second, 0.0))


def pack(*operands):
    return pl.pallas_call(
        pack_kernel,
        out_shape=struct((16, D), f32),
        grid=(1,),
        in_specs=[SM, *wholes(operands[1:])],
        out_specs=whole((16, D)),
        compiler_params=params(8),
        name="pack",
    )(*operands)


def update(weight, grad, moments, decay, clip, step, moments_new, at, flat=False):
    clipped = clip * grad
    first_moment = beta_first * moments[0] + (1.0 - beta_first) * clipped
    second_moment = beta_second * moments[1] + (1.0 - beta_second) * clipped * clipped
    corrected_first = first_moment * (1.0 / (1.0 - beta_first**adam_step))
    corrected_second = second_moment * (1.0 / (1.0 - beta_second**adam_step))
    result = corrected_first / (jnp.sqrt(corrected_second) + adam_eps)
    step[at] = result + decay * weight if decay else result
    if flat:
        moments_new[0:1, at[1]] = first_moment
        moments_new[1:2, at[1]] = second_moment
    else:
        moments_new[(0, *at)] = first_moment
        moments_new[(1, *at)] = second_moment


def finish_kernel(
    place, packed, attn, hidden,
    qkv_weight, out_weight, in_weight, ff_out_weight,
    qkv_moments, out_moments, in_moments, ff_out_moments, vector_moments, bias_moments, pool_moments,
    qkv_grad, qkv_step, qkv_new, out_grad, out_step, out_new, in_grad, in_step, in_new,
    ff_out_grad, ff_out_step, ff_out_new, vector_grad, vector_step, vector_new,
    bias_grad, bias_step, bias_new, pool_grad, pool_step, pool_new, clip_out, norms,
    held,
):
    lane = lax.broadcasted_iota(jnp.int32, (1, BLOCK), 1)
    squares = packed[14:15, 0:BLOCK]
    small = square_sum(packed[0:12])
    pooled = square_sum(packed[12:14])
    squares = jnp.where(lane == 2, small, jnp.where(lane == 3, pooled, squares))
    squares = jnp.where(lane < 4, squares, 0.0)
    total = jnp.sqrt(jnp.sum(squares, axis=1, keepdims=True))
    count = 4 * D * D + 2 * FF * D + 8 * D + FF + 10 * (HEADS // 2)
    clip = jnp.minimum(1.0, max_rms * math.sqrt(count) / (total + 1e-06))
    norms[...] = jnp.sqrt(squares)[:, 0:4]
    clip_out[...] = clip

    width = attn.shape[1]
    even = place[0] % 2 == 0
    held[...] = jnp.zeros_like(held)
    everything = (slice(None), slice(None))
    for c in range(4):
        whole_part = attn[0, :, c * BLOCK : (c + 1) * BLOCK]
        tile = attn[0, :, (4 + c // 2) * BLOCK : (5 + c // 2) * BLOCK]
        moved = pltpu.roll(tile, HEAD, 1)
        low, high = (tile, moved) if c % 2 == 0 else (moved, tile)
        straight = jnp.concatenate([whole_part, low], axis=1)
        turned = pltpu.roll(jnp.concatenate([whole_part, high], axis=1), HEAD, 1)
        both = jnp.where(even, straight, turned)
        local = qkv_grad.shape[2]
        if c < 3:
            grad = both[:, 0:local]
            qkv_grad[c] = grad
            moments = (qkv_moments[0, c], qkv_moments[1, c])
            update(qkv_weight[c], grad, moments, decay_rate, clip, qkv_step, qkv_new, (c,))
        else:
            held[0:width] = both
            grad = jnp.transpose(held[...])[0:local, 0:width]
            out_grad[...] = grad
            update(out_weight[...], grad, out_moments, decay_rate, clip, out_step, out_new, everything)
    for at, weight, moments, grad_ref, step, new in (
        (1, in_weight, in_moments, in_grad, in_step, in_new),
        (0, ff_out_weight, ff_out_moments, ff_out_grad, ff_out_step, ff_out_new),
    ):
        grad_ref[...] = hidden[at]
        update(weight[...], hidden[at], moments, decay_rate, clip, step, new, everything)
    vector_grad[...] = packed[0:8]
    update(None, packed[0:8], vector_moments, 0.0, clip, vector_step, vector_new, everything)
    for at in range(4):
        row = packed[8 + at : 9 + at]
        lanes = slice(at * D, (at + 1) * D)
        bias_grad[:, lanes] = row
        here = (slice(None), lanes)
        update(None, row, (bias_moments[0:1, lanes], bias_moments[1:2, lanes]), 0.0, clip, bias_step, bias_new, here, True)
    heads = HEADS // 2
    for tap in range(5):
        grad = packed[12:14, tap * BLOCK : tap * BLOCK + heads]
        pool_grad[tap] = grad
        update(None, grad, (pool_moments[0, tap], pool_moments[1, tap]), 0.0, clip, pool_step, pool_new, (tap,))


def finish(*operands):
    width = operands[2].shape[1]
    local = operands[4].shape[2]

    def three(*shape):
        return [struct(shape, f32), struct(shape, f32), struct((2, *shape), f32)]

    shapes = (
        three(3, width, local)
        + three(local, width)
        + three(width, D)
        + three(width, D)
        + three(8, D)
        + [struct((1, FF), f32), struct((1, FF), f32), struct((2, FF), f32)]
        + three(5, 2, HEADS // 2)
        + [struct((1, 1), f32), struct((1, 4), f32)]
    )
    return pl.pallas_call(
        finish_kernel,
        out_shape=tuple(shapes),
        grid=(1,),
        in_specs=[SM, *wholes(operands[1:])],
        out_specs=tuple(wholes(shapes)),
        scratch_shapes=[pltpu.VMEM((BLOCK, 2 * BLOCK), f32)],
        compiler_params=params(56),
        name="finish",
    )(*operands)


def cross_shards(own, mine, core):
    half = own.shape[0] // 2
    part = lax.dynamic_slice_in_dim(mine, core * half, half, 0)
    near_diag = lax.ppermute(part, PLACE, CROSS)
    other = lax.ppermute(mine, "seq", SWAP)
    far_diag = lax.ppermute(near_diag, "seq", SWAP)
    return (own, mine, other, near_diag, far_diag)


def after(value, *done):
    return lax.optimization_barrier((value, *done))[0]


def rows_by_dp(value, dp):
    n, rows, cols = value.shape
    return value.reshape(n * dp, rows // dp, cols)


class DpSum:
    def __init__(self, dp, dp_index, *groups):
        self.dp, self.dp_index, self.step = dp, dp_index, 1
        self.groups = [[(rows_by_dp(array, dp), slot * dp, 0) for array, slot in terms] for terms in groups]

    def blocks(self, targets):
        return [
            [(array, (first + (targets >> shift)).astype(jnp.int32)) for array, first, shift in terms]
            for terms in self.groups
        ]

    def send(self):
        step = self.step
        targets = jnp.arange(self.dp // (2 * step)) * (2 * step) + (self.dp_index % (2 * step) ^ step)
        return add_blocks(bf16, *self.blocks(targets), mib=56)

    def move(self, value):
        step = self.step
        got = lax.ppermute(value, "dp", [(i, i ^ step) for i in range(self.dp)])
        blocks = self.dp // (2 * step)
        for group, terms in enumerate(self.groups):
            terms.append((got, group * blocks, (2 * step).bit_length() - 1))
        self.step = 2 * step
        return got

    def done(self):
        return self.step >= self.dp

    def result(self):
        return add_blocks(f32, *self.blocks(self.dp_index + jnp.zeros((1,), jnp.int32)), mib=56)


def sum_everywhere(value, dp, between, beside):
    steps = [("lvl", 4, 1), ("lvl", 4, 2), ("seq", 2, 1)] + [("dp", dp, 1 << k) for k in range(dp.bit_length() - 1)]
    result = None
    for number, (axis, size, step) in enumerate(steps):
        got = lax.ppermute(value, axis, [(i, i ^ step) for i in range(size)])
        if number == 3:
            got = after(got, beside)
        value = value + got
        if (axis, step) == ("lvl", 2):
            result = between(value)
    return (value, result)


def on_device(
    tokens,
    cotangent,
    lengths,
    qkv_weight,
    out_weight,
    ffn_in_weight,
    ffn_out_weight,
    vectors,
    ffn_bias,
    pool_kernel,
    qkv_moments,
    out_moments,
    ffn_in_moments,
    ffn_out_moments,
    vector_moments,
    bias_moments,
    pool_moments,
):
    dp = lax.axis_size("dp")
    dp_index = lax.axis_index("dp")
    core = lax.axis_index("seq")
    level = lax.axis_index("lvl")
    length = lengths[0]
    count = tokens.shape[1]
    size = count // 4
    seq_len = 2 * count
    half = HEADS // 2
    along = jnp.where(core == 0, 1, 2)
    slots = [level, level ^ along, level ^ (3 - along), level ^ 3]

    def chunk_of(owner):
        order = owner ^ (owner >> 1)
        return jnp.where(core == 0, order, 3 - order)

    chunk = chunk_of(level)
    base = core * count + chunk * size
    width = D // (2 * dp)

    local = qkv_weight.shape[2]
    attn_own = jnp.concatenate(
        [bfloat(qkv_weight).transpose(0, 2, 1).reshape(3 * local, D), bfloat(out_weight)], axis=0
    )
    hidden = ffn_in_weight.shape[0]
    bias = jnp.stack([lax.dynamic_slice_in_dim(ffn_bias, s * hidden, hidden) for s in slots]).reshape(4, 1, D)
    edge = jnp.where(core == 0, tokens[0, count - HALO :], tokens[0, :HALO])
    pool_lanes = jnp.repeat(pool_kernel.reshape(10, half), HEAD, axis=1)
    place = jnp.stack([*slots, core, base, length, seq_len, chunk]).astype(jnp.int32)
    row = jnp.arange(D)
    side, rest = (row // (D // 2), row % (D // 2))
    feature = (rest // width) * (2 * width) + jnp.where(side == 0, core, 1 - core) * width + rest % width
    order = (feature[:, None] == row[None, :]).astype(bf16)
    chunks = jnp.stack([chunk_of(s) for s in slots]).astype(jnp.int32)

    def index(*at):
        return jnp.stack([jnp.asarray(a) for a in at]).astype(jnp.int32)

    attn_mine = lax.ppermute(attn_own, PLACE, MINE)
    edge = lax.ppermute(after(edge, attn_own), "seq", SWAP)
    in_own = bfloat(ffn_in_weight)
    out_own = bfloat(ffn_out_weight)
    weight_slices = own_slices(
        (dp_index * 2 + core) * width, width, qkv_weight, out_weight, ffn_in_weight, ffn_out_weight
    )
    attn_mine = after(attn_mine, weight_slices, edge, in_own, out_own, order, pool_lanes, place, bias)
    part = lax.dynamic_slice_in_dim(attn_mine, core * (D // 2), D // 2, 0)
    attn_near = lax.ppermute(part, PLACE, CROSS)
    attn_other = lax.ppermute(attn_mine, "seq", SWAP)
    extended, inputs, incoming, near_mask, far_mask = prepare(place, edge, after(tokens, part), cotangent)
    attn_near = after(attn_near, extended)
    attn_far = lax.ppermute(attn_near, "seq", SWAP)
    attn_pieces = [
        p.reshape(-1, local, D) for p in (attn_own, attn_mine, attn_other, attn_near, attn_far)
    ]
    in_mine = lax.ppermute(after(in_own, attn_near), PLACE, MINE)
    out_all, *kept = project(place, extended, attn_pieces, vectors, pool_lanes)
    query, near_keys, near_values, far_keys, far_values, pool_keys, pool_values = kept
    in_mine = after(in_mine, query)
    part = lax.dynamic_slice_in_dim(in_mine, core * (D // 2), D // 2, 0)
    in_near = lax.ppermute(part, PLACE, CROSS)
    in_other = lax.ppermute(in_mine, "seq", SWAP)
    out_mine = lax.ppermute(after(out_own, part), PLACE, MINE)
    mixed, log_total = attend_forward(
        after(query, part), near_keys, near_values, pool_keys, pool_values, near_mask, far_mask
    )
    in_near = after(in_near, mixed)
    in_far = lax.ppermute(in_near, "seq", SWAP)
    normed, inverse, first_low, act, slope = feed_forward(mixed, out_all, inputs, vectors, bias, (in_own, in_mine))
    out_mine = after(out_mine, first_low)
    part = lax.dynamic_slice_in_dim(out_mine, core * (D // 2), D // 2, 0)
    out_near = lax.ppermute(part, PLACE, CROSS)
    out_other = lax.ppermute(out_mine, "seq", SWAP)
    act_rest, slope_rest = feed_forward_rest(
        place, after(first_low, part), bias, (after(in_other, first_low), in_near, after(in_far, first_low))
    )
    out_near = after(out_near, act_rest)
    out_far = lax.ppermute(out_near, "seq", SWAP)
    in_pieces = (in_own, in_mine, in_other, in_near, in_far)
    out_pieces = (out_own, out_mine, out_other, out_near, out_far)
    block_low, branch_low, second, second_sums = branch_of(
        place, act, act_rest, normed, incoming, vectors, out_pieces
    )

    out_grad, grad_sent = ffn_grad(order, branch_low, act, act_rest)
    out_got = lax.ppermute(grad_sent, "seq", SWAP)
    pre_low, bias_sum, partial = feed_back(
        slope, after(branch_low, out_grad), second, in_pieces[:2], out_pieces[:2]
    )
    out_got = after(out_got, partial)
    out_send = add_blocks(bf16, [(out_grad, index(1, 3)), (out_got, index(2, 3))])
    out_first = lax.ppermute(out_send, PLACE, MINE)
    pre_rest, bias_rest, attn_low, attn_grad, heads_grad, first_sums = feed_back_rest(
        place, slope_rest, after(branch_low, out_send), partial, normed, inverse, vectors, out_all,
        in_pieces[2:], out_pieces[2:],
    )
    turned = turn_rows(order, after(extended, attn_low))
    out_first = after(out_first, turned)
    out_pass = add_blocks(bf16, [(out_grad, index(2)), (out_got, index(1)), (out_first, index(1))])
    out_second = lax.ppermute(out_pass, PLACE, CROSS)
    in_grad, grad_sent = ffn_grad(order, after(first_low, out_pass), pre_low, pre_rest)
    in_got = lax.ppermute(grad_sent, "seq", SWAP)
    in_send = add_blocks(bf16, [(in_grad, index(1, 3)), (in_got, index(2, 3))])
    in_first = lax.ppermute(in_send, PLACE, MINE)

    (query_grad, near_low, far_low, near_own, pool_own, to_left, to_right, query_sum, pool_sum) = attend_backward(
        after(heads_grad, in_send), *kept, near_mask, far_mask, log_total, pool_lanes
    )
    from_right = lax.ppermute(to_left, PLACE, LEFTWARD)
    from_left = lax.ppermute(to_right, PLACE, RIGHTWARD)
    in_first, out_second = after(in_first, query_grad), after(out_second, query_grad)
    in_pass = add_blocks(bf16, [(in_grad, index(2)), (in_got, index(1)), (in_first, index(1))])
    in_second = lax.ppermute(in_pass, PLACE, CROSS)
    grad_parts = (order, turned, attn_low, mixed, after(query_grad, in_pass, out_second), near_low, far_low)
    grad_sent = attn_weight_grad(1, *grad_parts)
    attn_got = lax.ppermute(grad_sent, "seq", SWAP)
    query_grad = after(query_grad, grad_sent)
    attn_wide = attn_weight_grad(0, *grad_parts[:4], query_grad, near_low, far_low)
    attn_got = after(attn_got, attn_wide, in_second, from_left, from_right)
    attn_at = index(slots[1], slots[3])
    attn_send = add_blocks(bf16, [(attn_wide, attn_at), (attn_got, attn_at)])
    attn_first = lax.ppermute(attn_send, PLACE, MINE)

    out_second, in_second = after(out_second, attn_send), after(in_second, attn_send)
    ffn_sum = DpSum(
        dp,
        dp_index,
        [(out_grad, 0), (out_got, 0), (out_first, 0), (out_second, 0)],
        [(in_grad, 0), (in_got, 0), (in_first, 0), (in_second, 0)],
    )
    ffn_part = ffn_sum.send()
    ffn_moved = ffn_sum.move(ffn_part)
    both_low, value_sum = input_grad_of(
        place, after(query_grad, ffn_part), near_own, pool_own, from_left, from_right, attn_grad, pool_lanes, block_low,
        attn_pieces,
    )
    attn_first = after(attn_first, both_low)
    attn_at = index(slots[2])
    attn_pass = add_blocks(bf16, [(attn_wide, attn_at), (attn_got, attn_at), (attn_first, index(1))], mib=56)
    attn_second = lax.ppermute(attn_pass, PLACE, CROSS)
    while not ffn_sum.done():
        ffn_part = ffn_sum.send()
        ffn_moved = ffn_sum.move(after(ffn_part, attn_pass))
    attn_second = after(attn_second, ffn_part)
    attn_sum = DpSum(
        dp, dp_index, [(attn_wide, slots[0]), (attn_got, slots[0]), (attn_first, 0), (attn_second, 0)]
    )
    attn_part = attn_sum.send()
    attn_moved = attn_sum.move(attn_part)
    both_mine = lax.ppermute(after(both_low, attn_part), PLACE, MINE)
    both_other = lax.ppermute(after(both_low, attn_part), PLACE, CROSS)
    attn_sum.groups[0][-1] = (after(attn_moved, ffn_moved), *attn_sum.groups[0][-1][1:])
    while not attn_sum.done():
        attn_part = attn_sum.send()
        attn_moved = attn_sum.move(attn_part)
    ffn_sum.groups = [[(after(terms[0][0], attn_part), *terms[0][1:]), *terms[1:]] for terms in ffn_sum.groups]
    ffn_shard = ffn_sum.result()
    attn_moved = after(attn_moved, ffn_shard)
    attn_sum.groups[0][-1] = (attn_moved, *attn_sum.groups[0][-1][1:])
    attn_shard = attn_sum.result()
    block_out, input_grad = place_rows(chunks, both_low, both_mine, both_other)

    packed = pack(
        place, query_sum, value_sum, first_sums, second_sums, bias_sum, bias_rest, pool_sum, attn_shard, ffn_shard
    )
    packed, diag_low = sum_everywhere(packed, dp, lambda value: after(both_mine, both_other, value), block_out)
    both_diag = lax.ppermute(diag_low, PLACE, CROSS)
    results = finish(
        place, packed, attn_shard, ffn_shard, *weight_slices,
        qkv_moments, out_moments, ffn_in_moments.transpose(0, 2, 1), ffn_out_moments.transpose(0, 2, 1), vector_moments,
        bias_moments, pool_moments.transpose(0, 2, 1, 3),
    )
    qkv_out, out_out, in_out, ff_out_out, vector_out = [results[3 * i : 3 * i + 3] for i in range(5)]
    block_out, input_grad = place_last(chunks, both_diag, block_out, input_grad)
    *_, bias_grad, bias_step, bias_new, pool_grad, pool_step, pool_new, clip, norms = results
    return (
        block_out[None],
        input_grad[None],
        *qkv_out,
        *out_out,
        *[value.swapaxes(-1, -2) for value in (*in_out, *ff_out_out)],
        *vector_out,
        bias_grad.reshape(FF),
        bias_step.reshape(FF),
        bias_new,
        pool_grad.transpose(1, 0, 2),
        pool_step.transpose(1, 0, 2),
        pool_new.transpose(0, 2, 1, 3),
        clip.reshape(()),
        norms.reshape(4),
    )


def solution(mesh):
    in_specs = (
        P("dp", "seq", None),
        P("dp", "seq", None),
        P("dp"),
        P(None, None, "lvl"),
        P("lvl", None),
        P("lvl", None),
        P("lvl", None),
        P(),
        P(),
        P(),
        P(None, None, ("dp", "seq"), "lvl"),
        P(None, "lvl", ("dp", "seq")),
        P(None, "lvl", ("dp", "seq")),
        P(None, "lvl", ("dp", "seq")),
        P(),
        P(),
        P(),
    )
    out_specs = (
        P("dp", "seq", None),
        P("dp", "seq", None),
        P(None, ("dp", "seq"), "lvl"),
        P(None, ("dp", "seq"), "lvl"),
        P(None, None, ("dp", "seq"), "lvl"),
        P("lvl", ("dp", "seq")),
        P("lvl", ("dp", "seq")),
        P(None, "lvl", ("dp", "seq")),
        P("lvl", ("dp", "seq")),
        P("lvl", ("dp", "seq")),
        P(None, "lvl", ("dp", "seq")),
        P("lvl", ("dp", "seq")),
        P("lvl", ("dp", "seq")),
        P(None, "lvl", ("dp", "seq")),
        P(),
        P(),
        P(),
        P(),
        P(),
        P(),
        P(),
        P(),
        P(),
        P(),
        P(),
    )
    return jax.shard_map(
        on_device, mesh=mesh, in_specs=in_specs, out_specs=out_specs, check_vma=False
    )
```

```python
import functools
import math

import jax
import jax.numpy as jnp
from jax import lax
from jax.experimental import pallas as pl
from jax.experimental.pallas import tpu as pltpu
from jax.sharding import PartitionSpec as P

D = 768
HEADS = 12
HEAD = 64
FF = 3072
REACH1 = 64
REACH2 = 256
HALO = 320
ROWS = 512
EXT = ROWS + 2 * HALO
NEAR = ROWS + 2 * REACH1
NEAR0 = HALO - REACH1
FAR0 = 48
FAR = 1056
POOLED = 256
TAP0 = 14
BLOCK = 128
BLOCKS = ROWS // BLOCK
PAIRS = HEADS // 4

norm_eps = 1e-05
beta_first = 0.9
beta_second = 0.999
adam_eps = 1e-08
decay_rate = 0.01
adam_step = 10.0
max_rms = 1.0
masked_score = -1e30
score_scale = 1.0 / math.sqrt(HEAD)

f32 = jnp.float32
bf16 = jnp.bfloat16
SWAP = [(0, 1), (1, 0)]
MINE = [(i, i ^ 1) for i in range(4)] + [(4 + i, 4 + (i ^ 2)) for i in range(4)]
CROSS = [(i, i ^ 2) for i in range(4)] + [(4 + i, 4 + (i ^ 1)) for i in range(4)]
PATH = [0, 1, 3, 2, 6, 7, 5, 4]
RIGHTWARD = list(zip(PATH, PATH[1:] + PATH[:1]))
LEFTWARD = [(b, a) for a, b in RIGHTWARD]
PLACE = ("seq", "lvl")

SM = pl.BlockSpec(memory_space=pltpu.SMEM)
HB = pl.BlockSpec(memory_space=pltpu.HBM)


def bfloat(value):
    return value.astype(bf16)


def params(mib=56):
    return pltpu.CompilerParams(vmem_limit_bytes=mib * 1024 * 1024)


def struct(shape, dtype):
    return jax.ShapeDtypeStruct(shape, dtype)


def dot(a, b):
    return jnp.dot(a, b, preferred_element_type=f32)


def dot_nt(a, b):
    return lax.dot_general(a, b, (((1,), (1,)), ((), ())), preferred_element_type=f32)


def turn(value):
    return jnp.transpose(value.astype(f32)).astype(bf16)


def row_mean(value):
    return jnp.mean(value, axis=-1, keepdims=True)


def col_sum(value):
    return jnp.sum(value, axis=0, keepdims=True)


def whole(shape):
    return pl.BlockSpec(shape, lambda *_: (0,) * len(shape), pipeline_mode=pl.Buffered(1))


def wholes(operands):
    return [whole(operand.shape) for operand in operands]


def copy_when(condition, source, target, sem):
    @pl.when(condition)
    def _():
        pltpu.make_async_copy(source, target, sem).start()


def wait_when(condition, target, sem):
    @pl.when(condition)
    def _():
        pltpu.make_async_copy(target, target, sem).wait()


def fetch_attention(place, pieces, weights, out_weight, sems):
    own, mine, other, near_diag, far_diag = pieces
    core = place[4]
    local = own.shape[1]
    copies = []

    def rows_of(owner):
        return pl.ds(pl.multiple_of(owner * local, 64), local)

    for at, piece in enumerate((own, mine, other)):
        rows = rows_of(place[at])
        copies.append(pltpu.make_async_copy(piece.at[pl.ds(0, 3)], weights.at[:, rows], sems.at[at]))
        if out_weight is not None:
            copies.append(pltpu.make_async_copy(piece.at[3], out_weight.at[rows], sems.at[3 + at]))
    for copy in copies:
        copy.start()
    rows = rows_of(place[3])
    targets = [weights.at[pl.ds(0, 2), rows], weights.at[2, rows]]
    if out_weight is not None:
        targets.append(out_weight.at[rows])
    for condition, low, high in ((core == 0, near_diag, far_diag), (core != 0, far_diag, near_diag)):
        for at, source in enumerate((low, high.at[0], high.at[1])[: len(targets)]):
            copy_when(condition, source, targets[at], sems.at[6 + at])

    def wait():
        for copy in copies:
            copy.wait()
        for at, target in enumerate(targets):
            pltpu.make_async_copy(target, target, sems.at[6 + at]).wait()

    return wait


def prepare_kernel(place, edge, tokens, cotangent, low, inputs, incoming, near_mask, far_mask, x, sems):
    core, base, length, seq_len, chunk = [place[i] for i in range(4, 9)]
    first = pl.multiple_of(chunk * ROWS, ROWS)
    left, right = x.at[pl.ds(0, HALO)], x.at[pl.ds(HALO + ROWS, HALO)]
    middle = pltpu.make_async_copy(tokens.at[0, pl.ds(first, ROWS)], inputs, sems.at[0])
    upper = pltpu.make_async_copy(cotangent.at[0, pl.ds(first, ROWS)], incoming, sems.at[3])
    middle.start()
    upper.start()
    starts, ends = chunk == 0, chunk == 3
    left_at = pl.multiple_of(jnp.maximum(first - HALO, 0), 64)
    right_at = pl.multiple_of(jnp.minimum(first + ROWS, 4 * ROWS - HALO), 64)
    copy_when(jnp.logical_not(starts), tokens.at[0, pl.ds(left_at, HALO)], left, sems.at[1])
    copy_when(jnp.logical_and(starts, core == 1), edge, left, sems.at[1])
    copy_when(jnp.logical_not(ends), tokens.at[0, pl.ds(right_at, HALO)], right, sems.at[2])
    copy_when(jnp.logical_and(ends, core == 0), edge, right, sems.at[2])
    no_left = jnp.logical_and(starts, core == 0)
    no_right = jnp.logical_and(ends, core == 1)

    @pl.when(no_left)
    def _():
        x[0:HALO] = jnp.zeros((HALO, D), f32)

    @pl.when(no_right)
    def _():
        x[HALO + ROWS : EXT] = jnp.zeros((HALO, D), f32)

    key_at = lax.broadcasted_iota(jnp.int32, (2 * BLOCK, BLOCK), 0)
    row_at = lax.broadcasted_iota(jnp.int32, (2 * BLOCK, BLOCK), 1)

    def bias(rows, cols, reach):
        same = jnp.where(rows < length, 1, 0) == jnp.where(cols < length, 1, 0)
        seen = (jnp.abs(rows - cols) <= reach) & same & (cols >= 0) & (cols < seq_len)
        return jnp.where(seen, 0.0, masked_score)

    for block in range(BLOCKS):
        rows = base + block * BLOCK + row_at
        near_mask[block] = bias(rows, base + block * BLOCK - REACH1 + key_at, REACH1)
        far_mask[block] = bias(rows, base - REACH2 + 4 * key_at, REACH2)

    middle.wait()
    upper.wait()
    wait_when(jnp.logical_not(no_left), left, sems.at[1])
    wait_when(jnp.logical_not(no_right), right, sems.at[2])
    low[0:HALO] = x[0:HALO].astype(bf16)
    low[HALO : HALO + ROWS] = inputs[...].astype(bf16)
    low[HALO + ROWS : EXT] = x[HALO + ROWS : EXT].astype(bf16)


def prepare(place, edge, tokens, cotangent):
    shapes = (
        struct((EXT, D), bf16),
        struct((ROWS, D), f32),
        struct((ROWS, D), f32),
        struct((BLOCKS, 2 * BLOCK, BLOCK), f32),
        struct((BLOCKS, 2 * BLOCK, BLOCK), f32),
    )
    return pl.pallas_call(
        prepare_kernel,
        out_shape=shapes,
        grid=(1,),
        in_specs=[SM] + [HB] * 3,
        out_specs=tuple(wholes(shapes)),
        scratch_shapes=[pltpu.VMEM((EXT, D), f32), pltpu.SemaphoreType.DMA((4,))],
        compiler_params=params(56),
        name="prepare",
    )(place, edge, tokens, cotangent)


def project_kernel(
    place, low, own, mine, other, near_diag, far_diag, vectors, pool,
    out_weight, query, near_keys, near_values, far_keys, far_values, pool_keys, pool_values,
    weights, key_rows, value_rows, sems,
):
    base, seq_len = place[5], place[7]
    fetch_attention(place, (own, mine, other, near_diag, far_diag), weights, out_weight, sems)()
    wide = PAIRS * BLOCK
    lane = lax.broadcasted_iota(jnp.int32, (ROWS, BLOCK), 1)
    projected = (dot_nt(low[HALO : HALO + ROWS], weights[0]) + vectors[0:1]).astype(bf16).astype(f32) * score_scale
    put_heads(query, projected, lane)

    def inside(rows, start):
        index = start + lax.broadcasted_iota(jnp.int32, (rows, BLOCK), 0)
        return (index >= 0) & (index < seq_len)

    near_inside = inside(NEAR, base - REACH1)
    far_inside = inside(FAR, base - HALO + FAR0)
    for c, near_ref, far_ref, rows_ref in ((1, near_keys, far_keys, key_rows), (2, near_values, far_values, value_rows)):
        near = dot_nt(low[NEAR0 : NEAR0 + NEAR], weights[c, 0:wide])
        far = dot_nt(low[FAR0 : FAR0 + FAR], weights[c, wide:D])
        if c == 2:
            near = near + vectors[1:2, 0:wide]
            far = far + vectors[1:2, wide:D]
        for pair in range(PAIRS):
            lanes = slice(pair * BLOCK, (pair + 1) * BLOCK)
            near_ref[pair] = jnp.where(near_inside, near[:, lanes], 0.0).astype(bf16)
            part = jnp.where(far_inside, far[:, lanes], 0.0).astype(bf16)
            far_ref[pair] = part
            rows_ref[pair] = part.astype(f32)
    for at, rows_ref, pooled_ref in ((0, key_rows, pool_keys), (5, value_rows, pool_values)):
        for pair in range(PAIRS):
            lanes = slice(pair * BLOCK, (pair + 1) * BLOCK)
            total = None
            for tap in range(5):
                part = pool[at + tap : at + tap + 1, lanes] * rows_ref[pair, pl.ds(TAP0 + tap, POOLED, stride=4), :]
                total = part if total is None else total + part
            pooled_ref[pair] = total.astype(bf16)


def put_heads(target, value, lane):
    for pair in range(2 * PAIRS):
        part = value[:, pair * BLOCK : (pair + 1) * BLOCK]
        first = jnp.where(lane < HEAD, part, 0.0).astype(bf16)
        second = jnp.where(lane >= HEAD, part, 0.0).astype(bf16)
        for block in range(BLOCKS):
            rows = slice(block * BLOCK, (block + 1) * BLOCK)
            target[pair, block, 0:BLOCK] = first[rows]
            target[pair, block, BLOCK : 2 * BLOCK] = second[rows]


def project(place, low, pieces, vectors, pool):
    shapes = (
        struct((D, D), bf16),
        struct((2 * PAIRS, BLOCKS, 2 * BLOCK, BLOCK), bf16),
        struct((PAIRS, NEAR, BLOCK), bf16),
        struct((PAIRS, NEAR, BLOCK), bf16),
        struct((PAIRS, FAR, BLOCK), bf16),
        struct((PAIRS, FAR, BLOCK), bf16),
        struct((PAIRS, POOLED, BLOCK), bf16),
        struct((PAIRS, POOLED, BLOCK), bf16),
    )
    return pl.pallas_call(
        project_kernel,
        out_shape=shapes,
        grid=(1,),
        in_specs=[SM, whole((EXT, D))] + [HB] * 5 + wholes((vectors, pool)),
        out_specs=tuple(wholes(shapes)),
        scratch_shapes=[
            pltpu.VMEM((3, D, D), bf16),
            pltpu.VMEM((PAIRS, FAR, BLOCK), f32),
            pltpu.VMEM((PAIRS, FAR, BLOCK), f32),
            pltpu.SemaphoreType.DMA((9,)),
        ],
        compiler_params=params(19),
        name="project",
    )(place, low, *pieces, vectors, pool)


def attend_forward_kernel(
    query, near_keys, near_values, pool_keys, pool_values, near_mask, far_mask,
    mixed, log_total,
):
    def attend(keys, turned, pair, block, mask):
        scores = dot_nt(keys, query[pair, block])
        parts = []
        for e in range(2):
            lanes = slice(e * BLOCK, (e + 1) * BLOCK)
            masked = scores[:, lanes] + mask[block]
            top = jnp.max(masked, axis=0, keepdims=True)
            raised = jnp.exp(masked - top)
            total = jnp.sum(raised, axis=0, keepdims=True)
            log_total[pair, block, :, lanes] = top + jnp.log(total)
            parts.append((raised * (1.0 / total)).astype(bf16))
        both = dot(turned, jnp.concatenate(parts, axis=1))
        output = jnp.concatenate([both[0:HEAD, 0:BLOCK], both[HEAD:BLOCK, BLOCK : 2 * BLOCK]], axis=0)
        lanes = pl.ds(pl.multiple_of(pair * BLOCK, BLOCK), BLOCK)
        mixed[block * BLOCK : (block + 1) * BLOCK, lanes] = turn(output)

    def near_pair(pair, carry):
        turned = turn(near_values[pair])
        for block in range(BLOCKS):
            window = slice(block * BLOCK, (block + 2) * BLOCK)
            attend(near_keys[pair, window], turned[:, window], pair, block, near_mask)
        return carry

    def far_pair(pair, carry):
        turned = turn(pool_values[pair])
        for block in range(BLOCKS):
            attend(pool_keys[pair], turned, PAIRS + pair, block, far_mask)
        return carry

    lax.fori_loop(0, PAIRS, near_pair, 0)
    lax.fori_loop(0, PAIRS, far_pair, 0)


def attend_forward(*operands):
    shapes = (struct((ROWS, D), bf16), struct((2 * PAIRS, BLOCKS, 1, 2 * BLOCK), f32))
    return pl.pallas_call(
        attend_forward_kernel,
        out_shape=shapes,
        grid=(1,),
        in_specs=wholes(operands),
        out_specs=tuple(wholes(shapes)),
        compiler_params=params(10),
        name="attend_forward",
    )(*operands)


def attend_backward_kernel(
    grad, query, near_keys, near_values, far_keys, far_values, pool_keys, pool_values, near_mask, far_mask, log_total,
    pool,
    query_grad, near_low, far_low, near_own, pool_own, to_left, to_right, query_sum, pool_sum,
    near_total, pool_total, far_rows, shifted,
):
    near_total[...] = jnp.zeros_like(near_total)
    pool_total[...] = jnp.zeros_like(pool_total)
    query_grad[0:REACH1] = jnp.zeros((REACH1, D), bf16)
    query_grad[NEAR - REACH1 : NEAR] = jnp.zeros((REACH1, D), bf16)

    def back(keys, values, turned, pair, block, mask):
        part = grad[pair, block]
        asked = query[pair, block]
        scores = dot_nt(keys, asked)
        chance_grads = dot_nt(values, part)
        chances = []
        score_grads = []
        for e in range(2):
            lanes = slice(e * BLOCK, (e + 1) * BLOCK)
            chance = jnp.exp(scores[:, lanes] + mask[block] - log_total[pair, block, :, lanes])
            chance_grad = chance_grads[:, lanes]
            mean = jnp.sum(chance * chance_grad, axis=0, keepdims=True)
            score_grads.append((chance * (chance_grad - mean)).astype(bf16))
            chances.append(chance.astype(bf16))
        score_grad = jnp.concatenate(score_grads, axis=1)
        both = dot(turned, score_grad)
        output = jnp.concatenate([both[0:HEAD, 0:BLOCK], both[HEAD:BLOCK, BLOCK : 2 * BLOCK]], axis=0)
        output = jnp.transpose(output) * score_scale
        lanes = pl.ds(pl.multiple_of(pair * BLOCK, BLOCK), BLOCK)
        query_grad[REACH1 + block * BLOCK : REACH1 + (block + 1) * BLOCK, lanes] = output.astype(bf16)
        return (col_sum(output), dot(score_grad, asked), dot(jnp.concatenate(chances, axis=1), part))

    def near_pair(pair, carry):
        turned = turn(near_keys[pair])
        sums = jnp.zeros((1, BLOCK), f32)
        for block in range(BLOCKS):
            window = slice(block * BLOCK, (block + 2) * BLOCK)
            part, keys, values = back(
                near_keys[pair, window], near_values[pair, window], turned[:, window], pair, block, near_mask
            )
            near_total[0, pair, window] += keys
            near_total[1, pair, window] += values
            sums = sums + part
        query_sum[pair] = sums
        return carry

    def far_pair(pair, carry):
        turned = turn(pool_keys[pair])
        sums = jnp.zeros((1, BLOCK), f32)
        for block in range(BLOCKS):
            part, keys, values = back(pool_keys[pair], pool_values[pair], turned, PAIRS + pair, block, far_mask)
            pool_total[0, pair] += keys
            pool_total[1, pair] += values
            sums = sums + part
        query_sum[PAIRS + pair] = sums
        return carry

    lax.fori_loop(0, PAIRS, near_pair, 0)
    lax.fori_loop(0, PAIRS, far_pair, 0)

    side = REACH2 // 4
    own_pool = ROWS // 4
    for kind in range(2):
        near_low[kind] = near_total[kind].astype(bf16)
        near_own[kind] = near_total[kind, :, REACH1 : REACH1 + ROWS]
        pool_own[kind] = pool_total[kind, :, side : side + own_pool + 8]
        to_left[kind, :, 0:REACH1] = near_total[kind, :, 0:REACH1].astype(bf16)
        to_left[kind, :, REACH1 : REACH1 + side + 16] = pool_total[kind, :, 0 : side + 16].astype(bf16)
        to_right[kind, :, 0:REACH1] = near_total[kind, :, NEAR - REACH1 : NEAR].astype(bf16)
        to_right[kind, :, REACH1 : REACH1 + side] = pool_total[kind, :, side + own_pool :].astype(bf16)

    for kind, rows_ref in ((0, far_keys), (1, far_values)):
        for pair in range(PAIRS):
            lanes = slice(pair * BLOCK, (pair + 1) * BLOCK)
            far_rows[0:FAR] = rows_ref[pair].astype(f32)
            pooled = pool_total[kind, pair]
            for tap in range(5):
                pool_sum[5 * kind + tap : 5 * kind + tap + 1, lanes] = col_sum(
                    pooled * far_rows[pl.ds(TAP0 + tap, POOLED, stride=4), :]
                )
            shifted[0:8] = jnp.zeros((8, BLOCK), f32)
            shifted[8 : 8 + POOLED] = pooled
            weight = [pool[5 * kind + tap : 5 * kind + tap + 1, lanes] for tap in range(5)]
            first = FAR0 + TAP0
            far_rows[0 : first + 2] = jnp.zeros((first + 2, BLOCK), f32)
            far_rows[EXT - 72 : EXT] = jnp.zeros((72, BLOCK), f32)
            far_rows[pl.ds(first, POOLED, stride=4), :] = weight[0] * pooled + weight[4] * shifted[7 : 7 + POOLED]
            for tap in range(1, 4):
                far_rows[pl.ds(first + tap, POOLED, stride=4), :] = weight[tap] * pooled
            far_rows[first + 4 * POOLED : first + 4 * POOLED + 1] = weight[4] * pooled[POOLED - 1 : POOLED]
            far_low[kind, pair] = far_rows[...].astype(bf16)


def attend_backward(*operands):
    side = REACH2 // 4
    shapes = (
        struct((NEAR, D), bf16),
        struct((2, PAIRS, NEAR, BLOCK), bf16),
        struct((2, PAIRS, EXT, BLOCK), bf16),
        struct((2, PAIRS, ROWS, BLOCK), f32),
        struct((2, PAIRS, ROWS // 4 + 8, BLOCK), f32),
        struct((2, PAIRS, REACH1 + side + 16, BLOCK), bf16),
        struct((2, PAIRS, REACH1 + side, BLOCK), bf16),
        struct((2 * PAIRS, 1, BLOCK), f32),
        struct((10, PAIRS * BLOCK), f32),
    )
    return pl.pallas_call(
        attend_backward_kernel,
        out_shape=shapes,
        grid=(1,),
        in_specs=wholes(operands),
        out_specs=tuple(wholes(shapes)),
        scratch_shapes=[
            pltpu.VMEM((2, PAIRS, NEAR, BLOCK), f32),
            pltpu.VMEM((2, PAIRS, POOLED, BLOCK), f32),
            pltpu.VMEM((EXT, BLOCK), f32),
            pltpu.VMEM((POOLED + 8, BLOCK), f32),
        ],
        compiler_params=params(19),
        name="attend_backward",
    )(*operands)


def fetch_hidden(place, pieces, held, sems):
    own, mine, other, near_diag, far_diag = pieces
    core = place[4]
    half = D // 2
    copies = [pltpu.make_async_copy(piece, held.at[at], sems.at[at]) for at, piece in enumerate((own, mine, other))]
    for at, (piece, where) in enumerate(((near_diag, core), (far_diag, 1 - core))):
        target = held.at[3, pl.ds(pl.multiple_of(where * half, half), half)]
        copies.append(pltpu.make_async_copy(piece, target, sems.at[3 + at]))
    for copy in copies:
        copy.start()


def wait_hidden(j, held, sems):
    @pl.when(j < 3)
    def _():
        pltpu.make_async_copy(held.at[j], held.at[j], sems.at[j]).wait()

    @pl.when(j == 3)
    def _():
        for at in range(2):
            target = held.at[3, pl.ds(at * (D // 2), D // 2)]
            pltpu.make_async_copy(target, target, sems.at[3 + at]).wait()


def gelu_block(first_low, held, bias, act, slope, j):
    for block in range(BLOCKS):
        rows = slice(block * BLOCK, (block + 1) * BLOCK)
        pre = dot_nt(first_low[rows], held) + bias
        gate = 0.5 + 0.5 * lax.erf(pre * math.sqrt(0.5))
        act[0, rows] = (pre * gate).astype(bf16)
        slope[0, rows] = gate + pre * (jnp.exp(-0.5 * pre * pre) * (1.0 / math.sqrt(2.0 * math.pi)))


def feed_forward_kernel(
    mixed, out_weight, inputs, vectors, bias, own, mine,
    normed, inverse, first_low, act, slope,
    held, total, sems,
):
    j = pl.program_id(0)

    @pl.when(j == 0)
    def _():
        copies = [pltpu.make_async_copy(piece, held.at[at], sems.at[at]) for at, piece in enumerate((own, mine))]
        for copy in copies:
            copy.start()
        total[...] = dot(mixed[...], out_weight[...])

        def rows_step(i, carry):
            rows = pl.ds(pl.multiple_of(i * BLOCK, BLOCK), BLOCK)
            value = inputs[rows] + total[rows] + vectors[2:3]
            centered = value - row_mean(value)
            inv = lax.rsqrt(row_mean(centered * centered) + norm_eps)
            z = centered * inv
            normed[rows] = z
            inverse[rows] = inv
            first_low[rows] = (z * vectors[4:5] + vectors[5:6]).astype(bf16)
            return carry

        lax.fori_loop(0, BLOCKS, rows_step, 0)

    pltpu.make_async_copy(held.at[j], held.at[j], sems.at[j]).wait()
    gelu_block(first_low, held[j], bias[j], act, slope, j)


def feed_forward(mixed, out_weight, inputs, vectors, bias, pieces):
    shapes = (
        struct((ROWS, D), f32),
        struct((ROWS, 1), f32),
        struct((ROWS, D), bf16),
        struct((2, ROWS, D), bf16),
        struct((2, ROWS, D), f32),
    )
    block = pl.BlockSpec((1, ROWS, D), lambda j: (j, 0, 0))
    return pl.pallas_call(
        feed_forward_kernel,
        out_shape=shapes,
        grid=(2,),
        in_specs=wholes((mixed, out_weight, inputs, vectors, bias)) + [HB] * 2,
        out_specs=(*wholes(shapes[:3]), block, block),
        scratch_shapes=[
            pltpu.VMEM((2, D, D), bf16),
            pltpu.VMEM((ROWS, D), f32),
            pltpu.SemaphoreType.DMA((2,)),
        ],
        compiler_params=params(17),
        name="feed_forward",
    )(mixed, out_weight, inputs, vectors, bias, *pieces)


def fetch_rest(place, pieces, held, sems):
    other, near_diag, far_diag = pieces
    half = D // 2
    core = place[4]
    pltpu.make_async_copy(other, held.at[0], sems.at[0]).start()
    for at, (piece, where) in enumerate(((near_diag, core), (far_diag, 1 - core))):
        target = held.at[1, pl.ds(pl.multiple_of(where * half, half), half)]
        pltpu.make_async_copy(piece, target, sems.at[1 + at]).start()


def wait_rest(j, held, sems):
    @pl.when(j == 0)
    def _():
        pltpu.make_async_copy(held.at[0], held.at[0], sems.at[0]).wait()

    @pl.when(j == 1)
    def _():
        for at in range(2):
            target = held.at[1, pl.ds(at * (D // 2), D // 2)]
            pltpu.make_async_copy(target, target, sems.at[1 + at]).wait()


def feed_forward_rest_kernel(
    place, first_low, bias, other, near_diag, far_diag,
    act, slope,
    held, sems,
):
    j = pl.program_id(0)

    @pl.when(j == 0)
    def _():
        fetch_rest(place, (other, near_diag, far_diag), held, sems)

    wait_rest(j, held, sems)
    gelu_block(first_low, held[j], bias[2 + j], act, slope, j)


def feed_forward_rest(place, first_low, bias, pieces):
    block = pl.BlockSpec((1, ROWS, D), lambda j: (j, 0, 0))
    return pl.pallas_call(
        feed_forward_rest_kernel,
        out_shape=(struct((2, ROWS, D), bf16), struct((2, ROWS, D), f32)),
        grid=(2,),
        in_specs=[SM, *wholes((first_low, bias))] + [HB] * 3,
        out_specs=(block, block),
        scratch_shapes=[pltpu.VMEM((2, D, D), bf16), pltpu.SemaphoreType.DMA((3,))],
        compiler_params=params(14),
        name="feed_forward_rest",
    )(place, first_low, bias, *pieces)


def two_halves(rows, cols):
    return [
        pl.BlockSpec((1, rows, cols), lambda j: (jnp.minimum(j, 1), 0, 0)),
        pl.BlockSpec((1, rows, cols), lambda j: (jnp.maximum(j - 2, 0), 0, 0)),
    ]


def with_half(j, first, second, use):
    @pl.when(j < 2)
    def _():
        use(first)

    @pl.when(j >= 2)
    def _():
        use(second)


def branch_kernel(
    place, act, act_rest, normed, incoming, vectors, own, mine, other, near_diag, far_diag,
    block_low, branch_low, second, sums,
    held, total, sems,
):
    j = pl.program_id(0)

    @pl.when(j == 0)
    def _():
        fetch_hidden(place, (own, mine, other, near_diag, far_diag), held, sems)
        sums[...] = jnp.zeros_like(sums)
        total[...] = jnp.zeros_like(total)

    wait_hidden(j, held, sems)

    def add(part):
        total[...] += dot(part[0], held[j])

    with_half(j, act, act_rest, add)

    @pl.when(j == 3)
    def _():

        def second_step(i, carry):
            rows = pl.ds(pl.multiple_of(i * BLOCK, BLOCK), BLOCK)
            first = normed[rows] * vectors[4:5] + vectors[5:6]
            value = first + total[rows] + vectors[3:4]
            centered = value - row_mean(value)
            inv = lax.rsqrt(row_mean(centered * centered) + norm_eps)
            z = centered * inv
            block_low[rows] = (z * vectors[6:7] + vectors[7:8]).astype(bf16)
            upper = incoming[rows]
            scaled = upper * vectors[6:7]
            grad = inv * (scaled - row_mean(scaled) - z * row_mean(scaled * z))
            second[rows] = grad
            branch_low[rows] = grad.astype(bf16)
            sums[0:1] += col_sum(grad)
            sums[1:2] += col_sum(upper * z)
            sums[2:3] += col_sum(upper)
            return carry

        lax.fori_loop(0, BLOCKS, second_step, 0)


def branch_of(place, act, act_rest, normed, incoming, vectors, pieces):
    shapes = (
        struct((ROWS, D), bf16),
        struct((ROWS, D), bf16),
        struct((ROWS, D), f32),
        struct((8, D), f32),
    )
    return pl.pallas_call(
        branch_kernel,
        out_shape=shapes,
        grid=(4,),
        in_specs=[SM, *two_halves(ROWS, D), *wholes((normed, incoming, vectors))] + [HB] * 5,
        out_specs=tuple(wholes(shapes)),
        scratch_shapes=[
            pltpu.VMEM((4, D, D), bf16),
            pltpu.VMEM((ROWS, D), f32),
            pltpu.SemaphoreType.DMA((5,)),
        ],
        compiler_params=params(17),
        name="branch",
    )(place, act, act_rest, normed, incoming, vectors, *pieces)


def hidden_back(j, slope, branch_low, in_held, out_held, pre_low, bias_sum, total):
    pre_grad = dot_nt(branch_low[...], out_held[j]) * slope[0]
    pre_low[0] = pre_grad.astype(bf16)
    bias_sum[0] = col_sum(pre_grad)
    total[...] += dot(pre_low[0], in_held[j])


def feed_back_kernel(
    slope, branch_low, second, in_own, in_mine, out_own, out_mine,
    pre_low, bias_sum, total,
    in_held, out_held, sems,
):
    j = pl.program_id(0)

    @pl.when(j == 0)
    def _():
        for at, (piece, target) in enumerate(
            ((out_own, out_held.at[0]), (in_own, in_held.at[0]), (out_mine, out_held.at[1]), (in_mine, in_held.at[1]))
        ):
            pltpu.make_async_copy(piece, target, sems.at[at]).start()
        total[...] = second[...]

    for held, at in ((out_held, 0), (in_held, 1)):
        pltpu.make_async_copy(held.at[j], held.at[j], sems.at[2 * j + at]).wait()
    hidden_back(j, slope, branch_low, in_held, out_held, pre_low, bias_sum, total)


def feed_back(slope, branch_low, second, in_pieces, out_pieces):
    shapes = (struct((2, ROWS, D), bf16), struct((2, 1, D), f32), struct((ROWS, D), f32))
    block = pl.BlockSpec((1, ROWS, D), lambda j: (j, 0, 0))
    return pl.pallas_call(
        feed_back_kernel,
        out_shape=shapes,
        grid=(2,),
        in_specs=[block, *wholes((branch_low, second))] + [HB] * 4,
        out_specs=(block, pl.BlockSpec((1, 1, D), lambda j: (j, 0, 0)), whole((ROWS, D))),
        scratch_shapes=[
            pltpu.VMEM((2, D, D), bf16),
            pltpu.VMEM((2, D, D), bf16),
            pltpu.SemaphoreType.DMA((4,)),
        ],
        compiler_params=params(16),
        name="feed_back",
    )(slope, branch_low, second, *in_pieces, *out_pieces)


def feed_back_rest_kernel(
    place, slope, branch_low, partial, normed, inverse, vectors, out_weight,
    in_other, in_near, in_far, out_other, out_near, out_far,
    pre_low, bias_sum, attn_low, attn_grad, heads_grad, sums,
    in_held, out_held, total, in_sems, out_sems,
):
    j = pl.program_id(0)

    @pl.when(j == 0)
    def _():
        fetch_rest(place, (out_other, out_near, out_far), out_held, out_sems)
        fetch_rest(place, (in_other, in_near, in_far), in_held, in_sems)
        sums[...] = jnp.zeros_like(sums)
        total[...] = partial[...]

    wait_rest(j, out_held, out_sems)
    wait_rest(j, in_held, in_sems)
    hidden_back(j, slope, branch_low, in_held, out_held, pre_low, bias_sum, total)

    @pl.when(j == 1)
    def _():
        def first_step(i, carry):
            rows = pl.ds(pl.multiple_of(i * BLOCK, BLOCK), BLOCK)
            z = normed[rows]
            first_grad = total[rows]
            scaled = first_grad * vectors[4:5]
            grad = inverse[rows] * (scaled - row_mean(scaled) - z * row_mean(scaled * z))
            attn_grad[rows] = grad
            attn_low[rows] = grad.astype(bf16)
            sums[0:1] += col_sum(grad)
            sums[1:2] += col_sum(first_grad * z)
            sums[2:3] += col_sum(first_grad)
            return carry

        lax.fori_loop(0, BLOCKS, first_step, 0)
        total[...] = dot_nt(attn_low[...], out_weight[...])
        put_heads(heads_grad, total, lax.broadcasted_iota(jnp.int32, (ROWS, BLOCK), 1))


def feed_back_rest(place, slope, branch_low, partial, normed, inverse, vectors, out_weight, in_pieces, out_pieces):
    shapes = (
        struct((2, ROWS, D), bf16),
        struct((2, 1, D), f32),
        struct((ROWS, D), bf16),
        struct((ROWS, D), f32),
        struct((2 * PAIRS, BLOCKS, 2 * BLOCK, BLOCK), bf16),
        struct((8, D), f32),
    )
    block = pl.BlockSpec((1, ROWS, D), lambda j: (j, 0, 0))
    return pl.pallas_call(
        feed_back_rest_kernel,
        out_shape=shapes,
        grid=(2,),
        in_specs=[SM, block, *wholes((branch_low, partial, normed, inverse, vectors, out_weight))] + [HB] * 6,
        out_specs=(block, pl.BlockSpec((1, 1, D), lambda j: (j, 0, 0)), *wholes(shapes[2:])),
        scratch_shapes=[
            pltpu.VMEM((2, D, D), bf16),
            pltpu.VMEM((2, D, D), bf16),
            pltpu.VMEM((ROWS, D), f32),
            pltpu.SemaphoreType.DMA((3,)),
            pltpu.SemaphoreType.DMA((3,)),
        ],
        compiler_params=params(22),
        name="feed_back_rest",
    )(place, slope, branch_low, partial, normed, inverse, vectors, out_weight, *in_pieces, *out_pieces)


def ffn_grad_kernel(order, rows, *refs):
    cols, (own, sent, turned) = refs[:-3], refs[-3:]
    j = pl.program_id(0)

    @pl.when(j == 0)
    def _():
        turned[...] = dot_nt(order[...], rows[...]).astype(bf16)

    def product(part):
        result = dot(turned[...], part[0]).astype(bf16)
        own[0] = result[: D // 2]
        sent[0] = result[D // 2 :]

    if len(cols) == 1:
        product(cols[0])
    else:
        with_half(j, *cols, product)


def ffn_grad(order, rows, *cols):
    slots = 2 * len(cols)
    block = pl.BlockSpec((1, D // 2, D), lambda j: (j, 0, 0))
    one = [pl.BlockSpec((1, ROWS, D), lambda j: (j, 0, 0))]
    return pl.pallas_call(
        ffn_grad_kernel,
        out_shape=(struct((slots, D // 2, D), bf16),) * 2,
        grid=(slots,),
        in_specs=wholes((order, rows)) + (one if len(cols) == 1 else two_halves(ROWS, D)),
        out_specs=(block, block),
        scratch_shapes=[pltpu.VMEM((D, ROWS), bf16)],
        compiler_params=params(12),
        name="ffn_grad",
    )(order, rows, *cols)


def turn_kernel(order, x, turned):
    turned[...] = dot_nt(order[...], x[...]).astype(bf16)


def turn_rows(order, x):
    return pl.pallas_call(
        turn_kernel,
        out_shape=struct((D, EXT), bf16),
        grid=(1,),
        in_specs=wholes((order, x)),
        out_specs=whole((D, EXT)),
        compiler_params=params(12),
        name="turn_rows",
    )(order, x)


def attn_weight_grad_kernel(order, turned, attn_low, mixed, query_grad, near_low, far_low, target, held):
    near_x = turned[:, NEAR0 : NEAR0 + NEAR]
    held[0] = dot(near_x, query_grad[...])
    for kind in range(2):
        near = jnp.concatenate([near_low[kind, pair] for pair in range(PAIRS)], axis=1)
        far = jnp.concatenate([far_low[kind, pair] for pair in range(PAIRS)], axis=1)
        held[1 + kind, :, 0 : D // 2] = dot(near_x, near)
        held[1 + kind, :, D // 2 : D] = dot(turned[...], far)
    held[3] = dot(dot_nt(order[...], attn_low[...]).astype(bf16), mixed[...])

    rows = D // 8
    lane = lax.broadcasted_iota(jnp.int32, (rows, BLOCK), 1)

    def step(i, carry):
        here = pl.ds(pl.multiple_of(i * rows, rows), rows)
        for pair in range(2):
            tiles = [
                [held[c, here, (3 * pair + t) * BLOCK : (3 * pair + t + 1) * BLOCK] for t in range(3)] for c in range(4)
            ]
            for odd in range(2):
                parts = [tiles[c][2 * odd] for c in range(4)]
                for c in (0, 2):
                    a, b = (tiles[c][1], tiles[c + 1][1])
                    if odd:
                        parts.append(jnp.where(lane < HEAD, pltpu.roll(a, HEAD, 1), b))
                    else:
                        parts.append(jnp.where(lane < HEAD, a, pltpu.roll(b, HEAD, 1)))
                for t, part in enumerate(parts):
                    target[2 * pair + odd, here, t * BLOCK : (t + 1) * BLOCK] = part.astype(bf16)
        return carry

    lax.fori_loop(0, 4, step, 0)


def attn_weight_grad(half, order, turned, attn_low, mixed, query_grad, near_low, far_low):
    return pl.pallas_call(
        attn_weight_grad_kernel,
        out_shape=struct((4, D // 2, D), bf16),
        grid=(1,),
        in_specs=[
            pl.BlockSpec((D // 2, D), lambda i: (half, 0)),
            pl.BlockSpec((D // 2, EXT), lambda i: (half, 0)),
        ]
        + [whole(a.shape) for a in (attn_low, mixed, query_grad, near_low, far_low)],
        out_specs=whole((4, D // 2, D)),
        scratch_shapes=[pltpu.VMEM((4, D // 2, D), f32)],
        compiler_params=params(19),
        name="attn_weight_grad",
    )(order, turned, attn_low, mixed, query_grad, near_low, far_low)


def add_kernel(groups, steps, *refs):
    count = sum(groups)
    operands, target = refs[count : 2 * count], refs[2 * count]
    step = pl.program_id(0)
    at = 0
    for group, terms in enumerate(groups):
        mine = operands[at : at + terms]
        at += terms

        @pl.when((step >= group * steps) & (step < (group + 1) * steps))
        def _(mine=mine):
            total = mine[0][...].astype(f32)
            for operand in mine[1:]:
                total = total + operand[...].astype(f32)
            target[...] = total.astype(target.dtype)


def add_blocks(dtype, *groups, mib=16):
    steps = groups[0][0][1].shape[0]
    rows, cols = groups[0][0][0].shape[1:]
    block = (1, rows, cols)
    terms = [(array, at, group) for group, members in enumerate(groups) for array, at in members]
    count = len(terms)
    total = steps * len(groups)

    def spec(k, group):
        return pl.BlockSpec(block, lambda i, *at: (at[k][jnp.clip(i - group * steps, 0, steps - 1)], 0, 0))

    return pl.pallas_call(
        functools.partial(add_kernel, [len(members) for members in groups], steps),
        out_shape=struct((total, rows, cols), dtype),
        grid_spec=pltpu.PrefetchScalarGridSpec(
            num_scalar_prefetch=count,
            grid=(total,),
            in_specs=[spec(k, group) for k, (_, _, group) in enumerate(terms)],
            out_specs=pl.BlockSpec(block, lambda i, *at: (i, 0, 0)),
        ),
        compiler_params=params(mib),
        name="add_blocks",
    )(*[at for _, at, _ in terms], *[array for array, _, _ in terms])


def input_grad_kernel(
    place, query_grad, near_own, pool_own, from_left, from_right, attn_grad, pool, block_low,
    own, mine, other, near_diag, far_diag,
    low, value_sum,
    pooled, rows_held, grads, weights, sems,
):
    wait_weights = fetch_attention(place, (own, mine, other, near_diag, far_diag), weights, None, sems)
    left_on = jnp.where(place[5] > 0, 1.0, 0.0)
    right_on = jnp.where(place[5] + ROWS < place[7], 1.0, 0.0)
    side = REACH2 // 4
    own_pool = ROWS // 4
    wide = PAIRS * BLOCK
    for kind in range(2):
        for pair in range(PAIRS):
            lanes = slice(pair * BLOCK, (pair + 1) * BLOCK)
            rows_held[...] = near_own[kind, pair]
            rows_held[0:REACH1] += from_left[kind, pair, 0:REACH1].astype(f32) * left_on
            rows_held[ROWS - REACH1 : ROWS] += from_right[kind, pair, 0:REACH1].astype(f32) * right_on
            if kind:
                value_sum[:, lanes] = col_sum(rows_held[...])
            grads[kind, :, lanes] = rows_held[...].astype(bf16)

            pooled[...] = pool_own[kind, pair]
            pooled[0:side] += from_left[kind, pair, REACH1 : REACH1 + side].astype(f32) * left_on
            arrived = from_right[kind, pair, REACH1 : REACH1 + side + 16].astype(f32) * right_on
            pooled[side : own_pool + 8] += arrived[0 : side + 8]
            here, following = pooled[0:own_pool], pooled[1 : own_pool + 1]
            weight = [pool[5 * kind + tap : 5 * kind + tap + 1, lanes] for tap in range(5)]
            rows_held[pl.ds(0, own_pool, stride=4), :] = weight[2] * here
            rows_held[pl.ds(1, own_pool, stride=4), :] = weight[3] * here
            rows_held[pl.ds(2, own_pool, stride=4), :] = weight[4] * here + weight[0] * following
            rows_held[pl.ds(3, own_pool, stride=4), :] = weight[1] * following
            lanes = slice(wide + pair * BLOCK, wide + (pair + 1) * BLOCK)
            if kind:
                value_sum[:, lanes] = col_sum(rows_held[...])
            grads[kind, :, lanes] = rows_held[...].astype(bf16)
    wait_weights()
    total = attn_grad[...] + dot(query_grad[REACH1 : REACH1 + ROWS], weights[0])
    total = total + dot(grads[0], weights[1])
    low[1] = (total + dot(grads[1], weights[2])).astype(bf16)
    low[0] = block_low[...]


def input_grad_of(place, query_grad, near_own, pool_own, from_left, from_right, attn_grad, pool, block_low, pieces):
    return pl.pallas_call(
        input_grad_kernel,
        out_shape=(struct((2, ROWS, D), bf16), struct((1, D), f32)),
        grid=(1,),
        in_specs=[SM, *wholes((query_grad, near_own, pool_own, from_left, from_right, attn_grad, pool, block_low))] + [HB] * 5,
        out_specs=(whole((2, ROWS, D)), whole((1, D))),
        scratch_shapes=[
            pltpu.VMEM((ROWS // 4 + 8, BLOCK), f32),
            pltpu.VMEM((ROWS, BLOCK), f32),
            pltpu.VMEM((2, ROWS, D), bf16),
            pltpu.VMEM((3, D, D), bf16),
            pltpu.SemaphoreType.DMA((9,)),
        ],
        compiler_params=params(),
        name="input_grad",
    )(place, query_grad, near_own, pool_own, from_left, from_right, attn_grad, pool, block_low, *pieces)


def place_kernel(at, own, mine, other, block_out, input_grad):
    step = pl.program_id(0)
    for k, piece in enumerate((own, mine, other)):

        @pl.when(step == k)
        def _(piece=piece):
            block_out[...] = piece[0].astype(f32)
            input_grad[...] = piece[1].astype(f32)


def place_rows(at, *pieces):
    chunk = pl.BlockSpec((ROWS, D), lambda i, at: (at[i], 0))
    return pl.pallas_call(
        place_kernel,
        out_shape=(struct((4 * ROWS, D), f32),) * 2,
        grid_spec=pltpu.PrefetchScalarGridSpec(
            num_scalar_prefetch=1,
            grid=(3,),
            in_specs=[whole((2, ROWS, D))] * 3,
            out_specs=(chunk, chunk),
        ),
        compiler_params=params(56),
        name="place_rows",
    )(at, *pieces)


def place_last_kernel(at, piece, block_held, input_held, block_out, input_grad):
    block_out[...] = piece[0].astype(f32)
    input_grad[...] = piece[1].astype(f32)


def place_last(at, piece, block_out, input_grad):
    rows = ROWS // 2
    chunk = pl.BlockSpec((rows, D), lambda i, at: (at[3] * 2 + i, 0))
    return pl.pallas_call(
        place_last_kernel,
        out_shape=(struct((4 * ROWS, D), f32),) * 2,
        grid_spec=pltpu.PrefetchScalarGridSpec(
            num_scalar_prefetch=1,
            grid=(2,),
            in_specs=[pl.BlockSpec((2, rows, D), lambda i, at: (0, i, 0)), HB, HB],
            out_specs=(chunk, chunk),
        ),
        input_output_aliases={2: 0, 3: 1},
        compiler_params=params(56),
        name="place_last",
    )(at, piece, block_out, input_grad)


def slices_kernel(
    at, qkv, out_weight, in_weight, ff_out_weight,
    qkv_slice, out_slice, in_slice, ff_out_slice,
    qkv_held, out_held, in_held, ff_out_held, sems,
):
    first, shift = pl.multiple_of(at[0], BLOCK), at[1]
    lanes = pl.ds(first, 2 * BLOCK)
    copies = [
        pltpu.make_async_copy(in_weight.at[:, lanes], in_held, sems.at[0]),
        pltpu.make_async_copy(ff_out_weight.at[:, lanes], ff_out_held, sems.at[1]),
        pltpu.make_async_copy(out_weight.at[:, lanes], out_held, sems.at[2]),
        pltpu.make_async_copy(qkv.at[:, :, lanes], qkv_held, sems.at[3]),
    ]
    for copy in copies:
        copy.start()
    width = in_slice.shape[0]

    def moved(value):
        return pltpu.roll(value, shift, 1)[:, 0:BLOCK]

    for copy, held, target in ((copies[0], in_held, in_slice), (copies[1], ff_out_held, ff_out_slice)):
        copy.wait()
        target[...] = jnp.transpose(moved(held[...]))[0:width]
    copies[2].wait()
    out_slice[...] = moved(out_held[...])[:, 0:width]
    copies[3].wait()
    for c in range(3):
        qkv_slice[c] = jnp.transpose(moved(qkv_held[c]))[0:width]


def own_slices(offset, width, qkv_weight, out_weight, in_weight, ff_out_weight):
    local = qkv_weight.shape[2]
    first = jnp.minimum(offset // BLOCK * BLOCK, D - 2 * BLOCK)
    shift = (2 * BLOCK - (offset - first)) % (2 * BLOCK)
    shapes = (
        struct((3, width, local), f32),
        struct((local, width), f32),
        struct((width, D), f32),
        struct((width, D), f32),
    )
    return pl.pallas_call(
        slices_kernel,
        out_shape=shapes,
        grid=(1,),
        in_specs=[SM] + [HB] * 4,
        out_specs=tuple(wholes(shapes)),
        scratch_shapes=[
            pltpu.VMEM((3, local, 2 * BLOCK), f32),
            pltpu.VMEM((local, 2 * BLOCK), f32),
            pltpu.VMEM((D, 2 * BLOCK), f32),
            pltpu.VMEM((D, 2 * BLOCK), f32),
            pltpu.SemaphoreType.DMA((4,)),
        ],
        compiler_params=params(56),
        name="own_slices",
    )(
        jnp.stack([first, shift]).astype(jnp.int32),
        qkv_weight.transpose(0, 2, 1),
        out_weight,
        in_weight,
        ff_out_weight,
    )


def square_sum(value):
    return jnp.sum(value * value)


def pack_kernel(place, query_sum, value_sum, first_sums, second_sums, bias_sum, bias_rest, pool_sum, attn, hidden, packed):
    packed[...] = jnp.zeros_like(packed)
    for pair in range(2 * PAIRS):
        packed[0:1, pair * BLOCK : (pair + 1) * BLOCK] = query_sum[pair]
    packed[1:2] = value_sum[...]
    packed[2:3] = first_sums[0:1]
    packed[3:4] = second_sums[0:1]
    packed[4:6] = first_sums[1:3]
    packed[6:8] = second_sums[1:3]
    for at in range(2):
        packed[pl.ds(8 + place[at], 1), :] = bias_sum[at]
        packed[pl.ds(8 + place[2 + at], 1), :] = bias_rest[at]
    lane = lax.broadcasted_iota(jnp.int32, (1, BLOCK), 1)
    wide = lax.broadcasted_iota(jnp.int32, (1, PAIRS * BLOCK), 1)
    for tap in range(10):
        row = jnp.zeros((1, BLOCK), f32)
        taps = pool_sum[tap : tap + 1, :]
        for head in range(HEADS // 2):
            mine = (wide >= head * HEAD) & (wide < (head + 1) * HEAD)
            row = row + jnp.where(lane == head, jnp.sum(jnp.where(mine, taps, 0.0), axis=1, keepdims=True), 0.0)
        at = 12 + tap // 5
        packed[at : at + 1, (tap % 5) * BLOCK : (tap % 5 + 1) * BLOCK] = row
    first = square_sum(attn[...])
    second = square_sum(hidden[...])
    packed[14:15, 0:BLOCK] = jnp.where(lane == 0, first, jnp.where(lane == 1, second, 0.0))


def pack(*operands):
    return pl.pallas_call(
        pack_kernel,
        out_shape=struct((16, D), f32),
        grid=(1,),
        in_specs=[SM, *wholes(operands[1:])],
        out_specs=whole((16, D)),
        compiler_params=params(8),
        name="pack",
    )(*operands)


def update(weight, grad, moments, decay, clip, step, moments_new, at, flat=False):
    clipped = clip * grad
    first_moment = beta_first * moments[0] + (1.0 - beta_first) * clipped
    second_moment = beta_second * moments[1] + (1.0 - beta_second) * clipped * clipped
    corrected_first = first_moment * (1.0 / (1.0 - beta_first**adam_step))
    corrected_second = second_moment * (1.0 / (1.0 - beta_second**adam_step))
    result = corrected_first / (jnp.sqrt(corrected_second) + adam_eps)
    step[at] = result + decay * weight if decay else result
    if flat:
        moments_new[0:1, at[1]] = first_moment
        moments_new[1:2, at[1]] = second_moment
    else:
        moments_new[(0, *at)] = first_moment
        moments_new[(1, *at)] = second_moment


def finish_kernel(
    place, packed, attn, hidden,
    qkv_weight, out_weight, in_weight, ff_out_weight,
    qkv_moments, out_moments, in_moments, ff_out_moments, vector_moments, bias_moments, pool_moments,
    qkv_grad, qkv_step, qkv_new, out_grad, out_step, out_new, in_grad, in_step, in_new,
    ff_out_grad, ff_out_step, ff_out_new, vector_grad, vector_step, vector_new,
    bias_grad, bias_step, bias_new, pool_grad, pool_step, pool_new, clip_out, norms,
    held,
):
    lane = lax.broadcasted_iota(jnp.int32, (1, BLOCK), 1)
    squares = packed[14:15, 0:BLOCK]
    small = square_sum(packed[0:12])
    pooled = square_sum(packed[12:14])
    squares = jnp.where(lane == 2, small, jnp.where(lane == 3, pooled, squares))
    squares = jnp.where(lane < 4, squares, 0.0)
    total = jnp.sqrt(jnp.sum(squares, axis=1, keepdims=True))
    count = 4 * D * D + 2 * FF * D + 8 * D + FF + 10 * (HEADS // 2)
    clip = jnp.minimum(1.0, max_rms * math.sqrt(count) / (total + 1e-06))
    norms[...] = jnp.sqrt(squares)[:, 0:4]
    clip_out[...] = clip

    width = attn.shape[1]
    even = place[0] % 2 == 0
    held[...] = jnp.zeros_like(held)
    everything = (slice(None), slice(None))
    for c in range(4):
        whole_part = attn[0, :, c * BLOCK : (c + 1) * BLOCK]
        tile = attn[0, :, (4 + c // 2) * BLOCK : (5 + c // 2) * BLOCK]
        moved = pltpu.roll(tile, HEAD, 1)
        low, high = (tile, moved) if c % 2 == 0 else (moved, tile)
        straight = jnp.concatenate([whole_part, low], axis=1)
        turned = pltpu.roll(jnp.concatenate([whole_part, high], axis=1), HEAD, 1)
        both = jnp.where(even, straight, turned)
        local = qkv_grad.shape[2]
        if c < 3:
            grad = both[:, 0:local]
            qkv_grad[c] = grad
            moments = (qkv_moments[0, c], qkv_moments[1, c])
            update(qkv_weight[c], grad, moments, decay_rate, clip, qkv_step, qkv_new, (c,))
        else:
            held[0:width] = both
            grad = jnp.transpose(held[...])[0:local, 0:width]
            out_grad[...] = grad
            update(out_weight[...], grad, out_moments, decay_rate, clip, out_step, out_new, everything)
    for at, weight, moments, grad_ref, step, new in (
        (1, in_weight, in_moments, in_grad, in_step, in_new),
        (0, ff_out_weight, ff_out_moments, ff_out_grad, ff_out_step, ff_out_new),
    ):
        grad_ref[...] = hidden[at]
        update(weight[...], hidden[at], moments, decay_rate, clip, step, new, everything)
    vector_grad[...] = packed[0:8]
    update(None, packed[0:8], vector_moments, 0.0, clip, vector_step, vector_new, everything)
    for at in range(4):
        row = packed[8 + at : 9 + at]
        lanes = slice(at * D, (at + 1) * D)
        bias_grad[:, lanes] = row
        here = (slice(None), lanes)
        update(None, row, (bias_moments[0:1, lanes], bias_moments[1:2, lanes]), 0.0, clip, bias_step, bias_new, here, True)
    heads = HEADS // 2
    for tap in range(5):
        grad = packed[12:14, tap * BLOCK : tap * BLOCK + heads]
        pool_grad[tap] = grad
        update(None, grad, (pool_moments[0, tap], pool_moments[1, tap]), 0.0, clip, pool_step, pool_new, (tap,))


def finish(*operands):
    width = operands[2].shape[1]
    local = operands[4].shape[2]

    def three(*shape):
        return [struct(shape, f32), struct(shape, f32), struct((2, *shape), f32)]

    shapes = (
        three(3, width, local)
        + three(local, width)
        + three(width, D)
        + three(width, D)
        + three(8, D)
        + [struct((1, FF), f32), struct((1, FF), f32), struct((2, FF), f32)]
        + three(5, 2, HEADS // 2)
        + [struct((1, 1), f32), struct((1, 4), f32)]
    )
    return pl.pallas_call(
        finish_kernel,
        out_shape=tuple(shapes),
        grid=(1,),
        in_specs=[SM, *wholes(operands[1:])],
        out_specs=tuple(wholes(shapes)),
        scratch_shapes=[pltpu.VMEM((BLOCK, 2 * BLOCK), f32)],
        compiler_params=params(56),
        name="finish",
    )(*operands)


def cross_shards(own, mine, core):
    half = own.shape[0] // 2
    part = lax.dynamic_slice_in_dim(mine, core * half, half, 0)
    near_diag = lax.ppermute(part, PLACE, CROSS)
    other = lax.ppermute(mine, "seq", SWAP)
    far_diag = lax.ppermute(near_diag, "seq", SWAP)
    return (own, mine, other, near_diag, far_diag)


def after(value, *done):
    return lax.optimization_barrier((value, *done))[0]


def rows_by_dp(value, dp):
    n, rows, cols = value.shape
    return value.reshape(n * dp, rows // dp, cols)


class DpSum:
    def __init__(self, dp, dp_index, *groups):
        self.dp, self.dp_index, self.step = dp, dp_index, 1
        self.groups = [[(rows_by_dp(array, dp), slot * dp, 0) for array, slot in terms] for terms in groups]

    def blocks(self, targets):
        return [
            [(array, (first + (targets >> shift)).astype(jnp.int32)) for array, first, shift in terms]
            for terms in self.groups
        ]

    def send(self):
        step = self.step
        targets = jnp.arange(self.dp // (2 * step)) * (2 * step) + (self.dp_index % (2 * step) ^ step)
        return add_blocks(bf16, *self.blocks(targets), mib=56)

    def move(self, value):
        step = self.step
        got = lax.ppermute(value, "dp", [(i, i ^ step) for i in range(self.dp)])
        blocks = self.dp // (2 * step)
        for group, terms in enumerate(self.groups):
            terms.append((got, group * blocks, (2 * step).bit_length() - 1))
        self.step = 2 * step
        return got

    def done(self):
        return self.step >= self.dp

    def result(self):
        return add_blocks(f32, *self.blocks(self.dp_index + jnp.zeros((1,), jnp.int32)), mib=56)


def sum_everywhere(value, dp, between, beside):
    steps = [("lvl", 4, 1), ("lvl", 4, 2), ("seq", 2, 1)] + [("dp", dp, 1 << k) for k in range(dp.bit_length() - 1)]
    result = None
    for number, (axis, size, step) in enumerate(steps):
        got = lax.ppermute(value, axis, [(i, i ^ step) for i in range(size)])
        if number == 3:
            got = after(got, beside)
        value = value + got
        if (axis, step) == ("lvl", 2):
            result = between(value)
    return (value, result)


def on_device(
    tokens,
    cotangent,
    lengths,
    qkv_weight,
    out_weight,
    ffn_in_weight,
    ffn_out_weight,
    vectors,
    ffn_bias,
    pool_kernel,
    qkv_moments,
    out_moments,
    ffn_in_moments,
    ffn_out_moments,
    vector_moments,
    bias_moments,
    pool_moments,
):
    dp = lax.axis_size("dp")
    dp_index = lax.axis_index("dp")
    core = lax.axis_index("seq")
    level = lax.axis_index("lvl")
    length = lengths[0]
    count = tokens.shape[1]
    size = count // 4
    seq_len = 2 * count
    half = HEADS // 2
    along = jnp.where(core == 0, 1, 2)
    slots = [level, level ^ along, level ^ (3 - along), level ^ 3]

    def chunk_of(owner):
        order = owner ^ (owner >> 1)
        return jnp.where(core == 0, order, 3 - order)

    chunk = chunk_of(level)
    base = core * count + chunk * size
    width = D // (2 * dp)

    local = qkv_weight.shape[2]
    attn_own = jnp.concatenate(
        [bfloat(qkv_weight).transpose(0, 2, 1).reshape(3 * local, D), bfloat(out_weight)], axis=0
    )
    hidden = ffn_in_weight.shape[0]
    bias = jnp.stack([lax.dynamic_slice_in_dim(ffn_bias, s * hidden, hidden) for s in slots]).reshape(4, 1, D)
    edge = jnp.where(core == 0, tokens[0, count - HALO :], tokens[0, :HALO])
    pool_lanes = jnp.repeat(pool_kernel.reshape(10, half), HEAD, axis=1)
    place = jnp.stack([*slots, core, base, length, seq_len, chunk]).astype(jnp.int32)
    row = jnp.arange(D)
    side, rest = (row // (D // 2), row % (D // 2))
    feature = (rest // width) * (2 * width) + jnp.where(side == 0, core, 1 - core) * width + rest % width
    order = (feature[:, None] == row[None, :]).astype(bf16)
    chunks = jnp.stack([chunk_of(s) for s in slots]).astype(jnp.int32)

    def index(*at):
        return jnp.stack([jnp.asarray(a) for a in at]).astype(jnp.int32)

    attn_mine = lax.ppermute(attn_own, PLACE, MINE)
    edge = lax.ppermute(after(edge, attn_own), "seq", SWAP)
    in_own = bfloat(ffn_in_weight)
    out_own = bfloat(ffn_out_weight)
    weight_slices = own_slices(
        (dp_index * 2 + core) * width, width, qkv_weight, out_weight, ffn_in_weight, ffn_out_weight
    )
    attn_mine = after(attn_mine, weight_slices, edge, in_own, out_own, order, pool_lanes, place, bias)
    part = lax.dynamic_slice_in_dim(attn_mine, core * (D // 2), D // 2, 0)
    attn_near = lax.ppermute(part, PLACE, CROSS)
    attn_other = lax.ppermute(attn_mine, "seq", SWAP)
    extended, inputs, incoming, near_mask, far_mask = prepare(place, edge, after(tokens, part), cotangent)
    attn_near = after(attn_near, extended)
    attn_far = lax.ppermute(attn_near, "seq", SWAP)
    attn_pieces = [
        p.reshape(-1, local, D) for p in (attn_own, attn_mine, attn_other, attn_near, attn_far)
    ]
    in_mine = lax.ppermute(after(in_own, attn_near), PLACE, MINE)
    out_all, *kept = project(place, extended, attn_pieces, vectors, pool_lanes)
    query, near_keys, near_values, far_keys, far_values, pool_keys, pool_values = kept
    in_mine = after(in_mine, query)
    part = lax.dynamic_slice_in_dim(in_mine, core * (D // 2), D // 2, 0)
    in_near = lax.ppermute(part, PLACE, CROSS)
    in_other = lax.ppermute(in_mine, "seq", SWAP)
    out_mine = lax.ppermute(after(out_own, part), PLACE, MINE)
    mixed, log_total = attend_forward(
        after(query, part), near_keys, near_values, pool_keys, pool_values, near_mask, far_mask
    )
    in_near = after(in_near, mixed)
    in_far = lax.ppermute(in_near, "seq", SWAP)
    normed, inverse, first_low, act, slope = feed_forward(mixed, out_all, inputs, vectors, bias, (in_own, in_mine))
    out_mine = after(out_mine, first_low)
    part = lax.dynamic_slice_in_dim(out_mine, core * (D // 2), D // 2, 0)
    out_near = lax.ppermute(part, PLACE, CROSS)
    out_other = lax.ppermute(out_mine, "seq", SWAP)
    act_rest, slope_rest = feed_forward_rest(
        place, after(first_low, part), bias, (after(in_other, first_low), in_near, after(in_far, first_low))
    )
    out_near = after(out_near, act_rest)
    out_far = lax.ppermute(out_near, "seq", SWAP)
    in_pieces = (in_own, in_mine, in_other, in_near, in_far)
    out_pieces = (out_own, out_mine, out_other, out_near, out_far)
    block_low, branch_low, second, second_sums = branch_of(
        place, act, act_rest, normed, incoming, vectors, out_pieces
    )

    out_grad, grad_sent = ffn_grad(order, branch_low, act, act_rest)
    out_got = lax.ppermute(grad_sent, "seq", SWAP)
    pre_low, bias_sum, partial = feed_back(
        slope, after(branch_low, out_grad), second, in_pieces[:2], out_pieces[:2]
    )
    out_got = after(out_got, partial)
    out_send = add_blocks(bf16, [(out_grad, index(1, 3)), (out_got, index(2, 3))])
    out_first = lax.ppermute(out_send, PLACE, MINE)
    pre_rest, bias_rest, attn_low, attn_grad, heads_grad, first_sums = feed_back_rest(
        place, slope_rest, after(branch_low, out_send), partial, normed, inverse, vectors, out_all,
        in_pieces[2:], out_pieces[2:],
    )
    turned = turn_rows(order, after(extended, attn_low))
    in_early, early_sent = ffn_grad(order, after(first_low, turned), pre_low)
    out_first = after(out_first, in_early)
    out_pass = add_blocks(bf16, [(out_grad, index(2)), (out_got, index(1)), (out_first, index(1))])
    out_second = lax.ppermute(out_pass, PLACE, CROSS)
    in_late, late_sent = ffn_grad(order, after(first_low, out_pass), pre_rest)
    late_got = lax.ppermute(late_sent, "seq", SWAP)
    in_send = add_blocks(
        bf16, [(in_early, index(1)), (late_got, index(0))], [(in_late, index(1)), (late_got, index(1))]
    )
    in_first = lax.ppermute(in_send, PLACE, MINE)
    early_got = lax.ppermute(after(early_sent, in_send), "seq", SWAP)

    (query_grad, near_low, far_low, near_own, pool_own, to_left, to_right, query_sum, pool_sum) = attend_backward(
        after(heads_grad, in_send), *kept, near_mask, far_mask, log_total, pool_lanes
    )
    from_right = lax.ppermute(to_left, PLACE, LEFTWARD)
    from_left = lax.ppermute(to_right, PLACE, RIGHTWARD)
    in_first, out_second = after(in_first, query_grad), after(out_second, query_grad)
    early_got = after(early_got, query_grad)
    in_pass = add_blocks(bf16, [(in_late, index(0)), (early_got, index(1)), (in_first, index(1))])
    in_second = lax.ppermute(in_pass, PLACE, CROSS)
    grad_parts = (order, turned, attn_low, mixed, after(query_grad, in_pass, out_second), near_low, far_low)
    grad_sent = attn_weight_grad(1, *grad_parts)
    attn_got = lax.ppermute(grad_sent, "seq", SWAP)
    query_grad = after(query_grad, grad_sent)
    attn_wide = attn_weight_grad(0, *grad_parts[:4], query_grad, near_low, far_low)
    attn_got = after(attn_got, attn_wide, in_second, from_left, from_right)
    attn_at = index(slots[1], slots[3])
    attn_send = add_blocks(bf16, [(attn_wide, attn_at), (attn_got, attn_at)])
    attn_first = lax.ppermute(attn_send, PLACE, MINE)

    out_second, in_second = after(out_second, attn_send), after(in_second, attn_send)
    ffn_sum = DpSum(
        dp,
        dp_index,
        [(out_grad, 0), (out_got, 0), (out_first, 0), (out_second, 0)],
        [(in_early, 0), (early_got, 0), (in_first, 0), (in_second, 0)],
    )
    ffn_part = ffn_sum.send()
    ffn_moved = ffn_sum.move(ffn_part)
    both_low, value_sum = input_grad_of(
        place, after(query_grad, ffn_part), near_own, pool_own, from_left, from_right, attn_grad, pool_lanes, block_low,
        attn_pieces,
    )
    attn_first = after(attn_first, both_low)
    attn_at = index(slots[2])
    attn_pass = add_blocks(bf16, [(attn_wide, attn_at), (attn_got, attn_at), (attn_first, index(1))], mib=56)
    attn_second = lax.ppermute(attn_pass, PLACE, CROSS)
    while not ffn_sum.done():
        ffn_part = ffn_sum.send()
        ffn_moved = ffn_sum.move(after(ffn_part, attn_pass))
    attn_second = after(attn_second, ffn_part)
    attn_sum = DpSum(
        dp, dp_index, [(attn_wide, slots[0]), (attn_got, slots[0]), (attn_first, 0), (attn_second, 0)]
    )
    attn_part = attn_sum.send()
    attn_moved = attn_sum.move(attn_part)
    both_mine = lax.ppermute(after(both_low, attn_part), PLACE, MINE)
    both_other = lax.ppermute(after(both_low, attn_part), PLACE, CROSS)
    attn_sum.groups[0][-1] = (after(attn_moved, ffn_moved), *attn_sum.groups[0][-1][1:])
    while not attn_sum.done():
        attn_part = attn_sum.send()
        attn_moved = attn_sum.move(attn_part)
    ffn_sum.groups = [[(after(terms[0][0], attn_part), *terms[0][1:]), *terms[1:]] for terms in ffn_sum.groups]
    ffn_shard = ffn_sum.result()
    attn_moved = after(attn_moved, ffn_shard)
    attn_sum.groups[0][-1] = (attn_moved, *attn_sum.groups[0][-1][1:])
    attn_shard = attn_sum.result()
    block_out, input_grad = place_rows(chunks, both_low, both_mine, both_other)

    packed = pack(
        place, query_sum, value_sum, first_sums, second_sums, bias_sum, bias_rest, pool_sum, attn_shard, ffn_shard
    )
    packed, diag_low = sum_everywhere(packed, dp, lambda value: after(both_mine, both_other, value), block_out)
    both_diag = lax.ppermute(diag_low, PLACE, CROSS)
    results = finish(
        place, packed, attn_shard, ffn_shard, *weight_slices,
        qkv_moments, out_moments, ffn_in_moments.transpose(0, 2, 1), ffn_out_moments.transpose(0, 2, 1), vector_moments,
        bias_moments, pool_moments.transpose(0, 2, 1, 3),
    )
    qkv_out, out_out, in_out, ff_out_out, vector_out = [results[3 * i : 3 * i + 3] for i in range(5)]
    block_out, input_grad = place_last(chunks, both_diag, block_out, input_grad)
    *_, bias_grad, bias_step, bias_new, pool_grad, pool_step, pool_new, clip, norms = results
    return (
        block_out[None],
        input_grad[None],
        *qkv_out,
        *out_out,
        *[value.swapaxes(-1, -2) for value in (*in_out, *ff_out_out)],
        *vector_out,
        bias_grad.reshape(FF),
        bias_step.reshape(FF),
        bias_new,
        pool_grad.transpose(1, 0, 2),
        pool_step.transpose(1, 0, 2),
        pool_new.transpose(0, 2, 1, 3),
        clip.reshape(()),
        norms.reshape(4),
    )


def solution(mesh):
    in_specs = (
        P("dp", "seq", None),
        P("dp", "seq", None),
        P("dp"),
        P(None, None, "lvl"),
        P("lvl", None),
        P("lvl", None),
        P("lvl", None),
        P(),
        P(),
        P(),
        P(None, None, ("dp", "seq"), "lvl"),
        P(None, "lvl", ("dp", "seq")),
        P(None, "lvl", ("dp", "seq")),
        P(None, "lvl", ("dp", "seq")),
        P(),
        P(),
        P(),
    )
    out_specs = (
        P("dp", "seq", None),
        P("dp", "seq", None),
        P(None, ("dp", "seq"), "lvl"),
        P(None, ("dp", "seq"), "lvl"),
        P(None, None, ("dp", "seq"), "lvl"),
        P("lvl", ("dp", "seq")),
        P("lvl", ("dp", "seq")),
        P(None, "lvl", ("dp", "seq")),
        P("lvl", ("dp", "seq")),
        P("lvl", ("dp", "seq")),
        P(None, "lvl", ("dp", "seq")),
        P("lvl", ("dp", "seq")),
        P("lvl", ("dp", "seq")),
        P(None, "lvl", ("dp", "seq")),
        P(),
        P(),
        P(),
        P(),
        P(),
        P(),
        P(),
        P(),
        P(),
        P(),
        P(),
    )
    return jax.shard_map(
        on_device, mesh=mesh, in_specs=in_specs, out_specs=out_specs, check_vma=False
    )
```

```python
import functools
import math

import jax
import jax.numpy as jnp
from jax import lax
from jax.experimental import pallas as pl
from jax.experimental.pallas import tpu as pltpu
from jax.sharding import PartitionSpec as P

D = 768
HEADS = 12
HEAD = 64
FF = 3072
REACH1 = 64
REACH2 = 256
HALO = 320
ROWS = 512
EXT = ROWS + 2 * HALO
NEAR = ROWS + 2 * REACH1
NEAR0 = HALO - REACH1
FAR0 = 48
FAR = 1056
POOLED = 256
TAP0 = 14
BLOCK = 128
BLOCKS = ROWS // BLOCK
PAIRS = HEADS // 4

norm_eps = 1e-05
beta_first = 0.9
beta_second = 0.999
adam_eps = 1e-08
decay_rate = 0.01
adam_step = 10.0
max_rms = 1.0
masked_score = -1e30
score_scale = 1.0 / math.sqrt(HEAD)

f32 = jnp.float32
bf16 = jnp.bfloat16
SWAP = [(0, 1), (1, 0)]
MINE = [(i, i ^ 1) for i in range(4)] + [(4 + i, 4 + (i ^ 2)) for i in range(4)]
CROSS = [(i, i ^ 2) for i in range(4)] + [(4 + i, 4 + (i ^ 1)) for i in range(4)]
PATH = [0, 1, 3, 2, 6, 7, 5, 4]
RIGHTWARD = list(zip(PATH, PATH[1:] + PATH[:1]))
LEFTWARD = [(b, a) for a, b in RIGHTWARD]
PLACE = ("seq", "lvl")

SM = pl.BlockSpec(memory_space=pltpu.SMEM)
HB = pl.BlockSpec(memory_space=pltpu.HBM)


def bfloat(value):
    return value.astype(bf16)


def params(mib=56):
    return pltpu.CompilerParams(vmem_limit_bytes=mib * 1024 * 1024)


def struct(shape, dtype):
    return jax.ShapeDtypeStruct(shape, dtype)


def dot(a, b):
    return jnp.dot(a, b, preferred_element_type=f32)


def dot_nt(a, b):
    return lax.dot_general(a, b, (((1,), (1,)), ((), ())), preferred_element_type=f32)


def turn(value):
    return jnp.transpose(value.astype(f32)).astype(bf16)


def row_mean(value):
    return jnp.mean(value, axis=-1, keepdims=True)


def col_sum(value):
    return jnp.sum(value, axis=0, keepdims=True)


def whole(shape):
    return pl.BlockSpec(shape, lambda *_: (0,) * len(shape), pipeline_mode=pl.Buffered(1))


def wholes(operands):
    return [whole(operand.shape) for operand in operands]


def copy_when(condition, source, target, sem):
    @pl.when(condition)
    def _():
        pltpu.make_async_copy(source, target, sem).start()


def wait_when(condition, target, sem):
    @pl.when(condition)
    def _():
        pltpu.make_async_copy(target, target, sem).wait()


def fetch_attention(place, pieces, weights, out_weight, sems):
    own, mine, other, near_diag, far_diag = pieces
    core = place[4]
    local = own.shape[1]
    copies = []

    def rows_of(owner):
        return pl.ds(pl.multiple_of(owner * local, 64), local)

    for at, piece in enumerate((own, mine, other)):
        rows = rows_of(place[at])
        copies.append(pltpu.make_async_copy(piece.at[pl.ds(0, 3)], weights.at[:, rows], sems.at[at]))
        if out_weight is not None:
            copies.append(pltpu.make_async_copy(piece.at[3], out_weight.at[rows], sems.at[3 + at]))
    for copy in copies:
        copy.start()
    rows = rows_of(place[3])
    targets = [weights.at[pl.ds(0, 2), rows], weights.at[2, rows]]
    if out_weight is not None:
        targets.append(out_weight.at[rows])
    for condition, low, high in ((core == 0, near_diag, far_diag), (core != 0, far_diag, near_diag)):
        for at, source in enumerate((low, high.at[0], high.at[1])[: len(targets)]):
            copy_when(condition, source, targets[at], sems.at[6 + at])

    def wait():
        for copy in copies:
            copy.wait()
        for at, target in enumerate(targets):
            pltpu.make_async_copy(target, target, sems.at[6 + at]).wait()

    return wait


def prepare_kernel(place, edge, tokens, cotangent, low, inputs, incoming, near_mask, far_mask, x, sems):
    core, base, length, seq_len, chunk = [place[i] for i in range(4, 9)]
    first = pl.multiple_of(chunk * ROWS, ROWS)
    left, right = x.at[pl.ds(0, HALO)], x.at[pl.ds(HALO + ROWS, HALO)]
    middle = pltpu.make_async_copy(tokens.at[0, pl.ds(first, ROWS)], inputs, sems.at[0])
    upper = pltpu.make_async_copy(cotangent.at[0, pl.ds(first, ROWS)], incoming, sems.at[3])
    middle.start()
    upper.start()
    starts, ends = chunk == 0, chunk == 3
    left_at = pl.multiple_of(jnp.maximum(first - HALO, 0), 64)
    right_at = pl.multiple_of(jnp.minimum(first + ROWS, 4 * ROWS - HALO), 64)
    copy_when(jnp.logical_not(starts), tokens.at[0, pl.ds(left_at, HALO)], left, sems.at[1])
    copy_when(jnp.logical_and(starts, core == 1), edge, left, sems.at[1])
    copy_when(jnp.logical_not(ends), tokens.at[0, pl.ds(right_at, HALO)], right, sems.at[2])
    copy_when(jnp.logical_and(ends, core == 0), edge, right, sems.at[2])
    no_left = jnp.logical_and(starts, core == 0)
    no_right = jnp.logical_and(ends, core == 1)

    @pl.when(no_left)
    def _():
        x[0:HALO] = jnp.zeros((HALO, D), f32)

    @pl.when(no_right)
    def _():
        x[HALO + ROWS : EXT] = jnp.zeros((HALO, D), f32)

    key_at = lax.broadcasted_iota(jnp.int32, (2 * BLOCK, BLOCK), 0)
    row_at = lax.broadcasted_iota(jnp.int32, (2 * BLOCK, BLOCK), 1)

    def bias(rows, cols, reach):
        same = jnp.where(rows < length, 1, 0) == jnp.where(cols < length, 1, 0)
        seen = (jnp.abs(rows - cols) <= reach) & same & (cols >= 0) & (cols < seq_len)
        return jnp.where(seen, 0.0, masked_score)

    for block in range(BLOCKS):
        rows = base + block * BLOCK + row_at
        near_mask[block] = bias(rows, base + block * BLOCK - REACH1 + key_at, REACH1)
        far_mask[block] = bias(rows, base - REACH2 + 4 * key_at, REACH2)

    middle.wait()
    upper.wait()
    wait_when(jnp.logical_not(no_left), left, sems.at[1])
    wait_when(jnp.logical_not(no_right), right, sems.at[2])
    low[0:HALO] = x[0:HALO].astype(bf16)
    low[HALO : HALO + ROWS] = inputs[...].astype(bf16)
    low[HALO + ROWS : EXT] = x[HALO + ROWS : EXT].astype(bf16)


def prepare(place, edge, tokens, cotangent):
    shapes = (
        struct((EXT, D), bf16),
        struct((ROWS, D), f32),
        struct((ROWS, D), f32),
        struct((BLOCKS, 2 * BLOCK, BLOCK), f32),
        struct((BLOCKS, 2 * BLOCK, BLOCK), f32),
    )
    return pl.pallas_call(
        prepare_kernel,
        out_shape=shapes,
        grid=(1,),
        in_specs=[SM] + [HB] * 3,
        out_specs=tuple(wholes(shapes)),
        scratch_shapes=[pltpu.VMEM((EXT, D), f32), pltpu.SemaphoreType.DMA((4,))],
        compiler_params=params(56),
        name="prepare",
    )(place, edge, tokens, cotangent)


def project_kernel(
    place, low, own, mine, other, near_diag, far_diag, vectors, pool,
    out_weight, query, near_keys, near_values, far_keys, far_values, pool_keys, pool_values,
    weights, key_rows, value_rows, sems,
):
    base, seq_len = place[5], place[7]
    fetch_attention(place, (own, mine, other, near_diag, far_diag), weights, out_weight, sems)()
    wide = PAIRS * BLOCK
    lane = lax.broadcasted_iota(jnp.int32, (ROWS, BLOCK), 1)
    projected = (dot_nt(low[HALO : HALO + ROWS], weights[0]) + vectors[0:1]).astype(bf16).astype(f32) * score_scale
    put_heads(query, projected, lane)

    def inside(rows, start):
        index = start + lax.broadcasted_iota(jnp.int32, (rows, BLOCK), 0)
        return (index >= 0) & (index < seq_len)

    near_inside = inside(NEAR, base - REACH1)
    far_inside = inside(FAR, base - HALO + FAR0)
    for c, near_ref, far_ref, rows_ref in ((1, near_keys, far_keys, key_rows), (2, near_values, far_values, value_rows)):
        near = dot_nt(low[NEAR0 : NEAR0 + NEAR], weights[c, 0:wide])
        far = dot_nt(low[FAR0 : FAR0 + FAR], weights[c, wide:D])
        if c == 2:
            near = near + vectors[1:2, 0:wide]
            far = far + vectors[1:2, wide:D]
        for pair in range(PAIRS):
            lanes = slice(pair * BLOCK, (pair + 1) * BLOCK)
            near_ref[pair] = jnp.where(near_inside, near[:, lanes], 0.0).astype(bf16)
            part = jnp.where(far_inside, far[:, lanes], 0.0).astype(bf16)
            far_ref[pair] = part
            rows_ref[pair] = part.astype(f32)
    for at, rows_ref, pooled_ref in ((0, key_rows, pool_keys), (5, value_rows, pool_values)):
        for pair in range(PAIRS):
            lanes = slice(pair * BLOCK, (pair + 1) * BLOCK)
            total = None
            for tap in range(5):
                part = pool[at + tap : at + tap + 1, lanes] * rows_ref[pair, pl.ds(TAP0 + tap, POOLED, stride=4), :]
                total = part if total is None else total + part
            pooled_ref[pair] = total.astype(bf16)


def put_heads(target, value, lane):
    for pair in range(2 * PAIRS):
        part = value[:, pair * BLOCK : (pair + 1) * BLOCK]
        first = jnp.where(lane < HEAD, part, 0.0).astype(bf16)
        second = jnp.where(lane >= HEAD, part, 0.0).astype(bf16)
        for block in range(BLOCKS):
            rows = slice(block * BLOCK, (block + 1) * BLOCK)
            target[pair, block, 0:BLOCK] = first[rows]
            target[pair, block, BLOCK : 2 * BLOCK] = second[rows]


def project(place, low, pieces, vectors, pool):
    shapes = (
        struct((D, D), bf16),
        struct((2 * PAIRS, BLOCKS, 2 * BLOCK, BLOCK), bf16),
        struct((PAIRS, NEAR, BLOCK), bf16),
        struct((PAIRS, NEAR, BLOCK), bf16),
        struct((PAIRS, FAR, BLOCK), bf16),
        struct((PAIRS, FAR, BLOCK), bf16),
        struct((PAIRS, POOLED, BLOCK), bf16),
        struct((PAIRS, POOLED, BLOCK), bf16),
    )
    return pl.pallas_call(
        project_kernel,
        out_shape=shapes,
        grid=(1,),
        in_specs=[SM, whole((EXT, D))] + [HB] * 5 + wholes((vectors, pool)),
        out_specs=tuple(wholes(shapes)),
        scratch_shapes=[
            pltpu.VMEM((3, D, D), bf16),
            pltpu.VMEM((PAIRS, FAR, BLOCK), f32),
            pltpu.VMEM((PAIRS, FAR, BLOCK), f32),
            pltpu.SemaphoreType.DMA((9,)),
        ],
        compiler_params=params(19),
        name="project",
    )(place, low, *pieces, vectors, pool)


def attend_forward_kernel(
    query, near_keys, near_values, pool_keys, pool_values, near_mask, far_mask,
    mixed, log_total,
):
    def attend(keys, turned, pair, block, mask):
        scores = dot_nt(keys, query[pair, block])
        parts = []
        for e in range(2):
            lanes = slice(e * BLOCK, (e + 1) * BLOCK)
            masked = scores[:, lanes] + mask[block]
            top = jnp.max(masked, axis=0, keepdims=True)
            raised = jnp.exp(masked - top)
            total = jnp.sum(raised, axis=0, keepdims=True)
            log_total[pair, block, :, lanes] = top + jnp.log(total)
            parts.append((raised * (1.0 / total)).astype(bf16))
        both = dot(turned, jnp.concatenate(parts, axis=1))
        output = jnp.concatenate([both[0:HEAD, 0:BLOCK], both[HEAD:BLOCK, BLOCK : 2 * BLOCK]], axis=0)
        lanes = pl.ds(pl.multiple_of(pair * BLOCK, BLOCK), BLOCK)
        mixed[block * BLOCK : (block + 1) * BLOCK, lanes] = turn(output)

    def near_pair(pair, carry):
        turned = turn(near_values[pair])
        for block in range(BLOCKS):
            window = slice(block * BLOCK, (block + 2) * BLOCK)
            attend(near_keys[pair, window], turned[:, window], pair, block, near_mask)
        return carry

    def far_pair(pair, carry):
        turned = turn(pool_values[pair])
        for block in range(BLOCKS):
            attend(pool_keys[pair], turned, PAIRS + pair, block, far_mask)
        return carry

    lax.fori_loop(0, PAIRS, near_pair, 0)
    lax.fori_loop(0, PAIRS, far_pair, 0)


def attend_forward(*operands):
    shapes = (struct((ROWS, D), bf16), struct((2 * PAIRS, BLOCKS, 1, 2 * BLOCK), f32))
    return pl.pallas_call(
        attend_forward_kernel,
        out_shape=shapes,
        grid=(1,),
        in_specs=wholes(operands),
        out_specs=tuple(wholes(shapes)),
        compiler_params=params(10),
        name="attend_forward",
    )(*operands)


def attend_backward_kernel(
    grad, query, near_keys, near_values, far_keys, far_values, pool_keys, pool_values, near_mask, far_mask, log_total,
    pool,
    query_grad, near_low, far_low, near_own, pool_own, to_left, to_right, query_sum, pool_sum,
    near_total, pool_total, far_rows, shifted,
):
    near_total[...] = jnp.zeros_like(near_total)
    pool_total[...] = jnp.zeros_like(pool_total)
    query_grad[0:REACH1] = jnp.zeros((REACH1, D), bf16)
    query_grad[NEAR - REACH1 : NEAR] = jnp.zeros((REACH1, D), bf16)

    def back(keys, values, turned, pair, block, mask):
        part = grad[pair, block]
        asked = query[pair, block]
        scores = dot_nt(keys, asked)
        chance_grads = dot_nt(values, part)
        chances = []
        score_grads = []
        for e in range(2):
            lanes = slice(e * BLOCK, (e + 1) * BLOCK)
            chance = jnp.exp(scores[:, lanes] + mask[block] - log_total[pair, block, :, lanes])
            chance_grad = chance_grads[:, lanes]
            mean = jnp.sum(chance * chance_grad, axis=0, keepdims=True)
            score_grads.append((chance * (chance_grad - mean)).astype(bf16))
            chances.append(chance.astype(bf16))
        score_grad = jnp.concatenate(score_grads, axis=1)
        both = dot(turned, score_grad)
        output = jnp.concatenate([both[0:HEAD, 0:BLOCK], both[HEAD:BLOCK, BLOCK : 2 * BLOCK]], axis=0)
        output = jnp.transpose(output) * score_scale
        lanes = pl.ds(pl.multiple_of(pair * BLOCK, BLOCK), BLOCK)
        query_grad[REACH1 + block * BLOCK : REACH1 + (block + 1) * BLOCK, lanes] = output.astype(bf16)
        return (col_sum(output), dot(score_grad, asked), dot(jnp.concatenate(chances, axis=1), part))

    def near_pair(pair, carry):
        turned = turn(near_keys[pair])
        sums = jnp.zeros((1, BLOCK), f32)
        for block in range(BLOCKS):
            window = slice(block * BLOCK, (block + 2) * BLOCK)
            part, keys, values = back(
                near_keys[pair, window], near_values[pair, window], turned[:, window], pair, block, near_mask
            )
            near_total[0, pair, window] += keys
            near_total[1, pair, window] += values
            sums = sums + part
        query_sum[pair] = sums
        return carry

    def far_pair(pair, carry):
        turned = turn(pool_keys[pair])
        sums = jnp.zeros((1, BLOCK), f32)
        for block in range(BLOCKS):
            part, keys, values = back(pool_keys[pair], pool_values[pair], turned, PAIRS + pair, block, far_mask)
            pool_total[0, pair] += keys
            pool_total[1, pair] += values
            sums = sums + part
        query_sum[PAIRS + pair] = sums
        return carry

    lax.fori_loop(0, PAIRS, near_pair, 0)
    lax.fori_loop(0, PAIRS, far_pair, 0)

    side = REACH2 // 4
    own_pool = ROWS // 4
    for kind in range(2):
        near_low[kind] = near_total[kind].astype(bf16)
        near_own[kind] = near_total[kind, :, REACH1 : REACH1 + ROWS]
        pool_own[kind] = pool_total[kind, :, side : side + own_pool + 8]
        to_left[kind, :, 0:REACH1] = near_total[kind, :, 0:REACH1].astype(bf16)
        to_left[kind, :, REACH1 : REACH1 + side + 16] = pool_total[kind, :, 0 : side + 16].astype(bf16)
        to_right[kind, :, 0:REACH1] = near_total[kind, :, NEAR - REACH1 : NEAR].astype(bf16)
        to_right[kind, :, REACH1 : REACH1 + side] = pool_total[kind, :, side + own_pool :].astype(bf16)

    for kind, rows_ref in ((0, far_keys), (1, far_values)):
        for pair in range(PAIRS):
            lanes = slice(pair * BLOCK, (pair + 1) * BLOCK)
            far_rows[0:FAR] = rows_ref[pair].astype(f32)
            pooled = pool_total[kind, pair]
            for tap in range(5):
                pool_sum[5 * kind + tap : 5 * kind + tap + 1, lanes] = col_sum(
                    pooled * far_rows[pl.ds(TAP0 + tap, POOLED, stride=4), :]
                )
            shifted[0:8] = jnp.zeros((8, BLOCK), f32)
            shifted[8 : 8 + POOLED] = pooled
            weight = [pool[5 * kind + tap : 5 * kind + tap + 1, lanes] for tap in range(5)]
            first = FAR0 + TAP0
            far_rows[0 : first + 2] = jnp.zeros((first + 2, BLOCK), f32)
            far_rows[EXT - 72 : EXT] = jnp.zeros((72, BLOCK), f32)
            far_rows[pl.ds(first, POOLED, stride=4), :] = weight[0] * pooled + weight[4] * shifted[7 : 7 + POOLED]
            for tap in range(1, 4):
                far_rows[pl.ds(first + tap, POOLED, stride=4), :] = weight[tap] * pooled
            far_rows[first + 4 * POOLED : first + 4 * POOLED + 1] = weight[4] * pooled[POOLED - 1 : POOLED]
            far_low[kind, pair] = far_rows[...].astype(bf16)


def attend_backward(*operands):
    side = REACH2 // 4
    shapes = (
        struct((NEAR, D), bf16),
        struct((2, PAIRS, NEAR, BLOCK), bf16),
        struct((2, PAIRS, EXT, BLOCK), bf16),
        struct((2, PAIRS, ROWS, BLOCK), f32),
        struct((2, PAIRS, ROWS // 4 + 8, BLOCK), f32),
        struct((2, PAIRS, REACH1 + side + 16, BLOCK), bf16),
        struct((2, PAIRS, REACH1 + side, BLOCK), bf16),
        struct((2 * PAIRS, 1, BLOCK), f32),
        struct((10, PAIRS * BLOCK), f32),
    )
    return pl.pallas_call(
        attend_backward_kernel,
        out_shape=shapes,
        grid=(1,),
        in_specs=wholes(operands),
        out_specs=tuple(wholes(shapes)),
        scratch_shapes=[
            pltpu.VMEM((2, PAIRS, NEAR, BLOCK), f32),
            pltpu.VMEM((2, PAIRS, POOLED, BLOCK), f32),
            pltpu.VMEM((EXT, BLOCK), f32),
            pltpu.VMEM((POOLED + 8, BLOCK), f32),
        ],
        compiler_params=params(19),
        name="attend_backward",
    )(*operands)


def fetch_hidden(place, pieces, held, sems):
    own, mine, other, near_diag, far_diag = pieces
    core = place[4]
    half = D // 2
    copies = [pltpu.make_async_copy(piece, held.at[at], sems.at[at]) for at, piece in enumerate((own, mine, other))]
    for at, (piece, where) in enumerate(((near_diag, core), (far_diag, 1 - core))):
        target = held.at[3, pl.ds(pl.multiple_of(where * half, half), half)]
        copies.append(pltpu.make_async_copy(piece, target, sems.at[3 + at]))
    for copy in copies:
        copy.start()


def wait_hidden(j, held, sems):
    @pl.when(j < 3)
    def _():
        pltpu.make_async_copy(held.at[j], held.at[j], sems.at[j]).wait()

    @pl.when(j == 3)
    def _():
        for at in range(2):
            target = held.at[3, pl.ds(at * (D // 2), D // 2)]
            pltpu.make_async_copy(target, target, sems.at[3 + at]).wait()


def gelu_block(first_low, held, bias, act, slope, j):
    for block in range(BLOCKS):
        rows = slice(block * BLOCK, (block + 1) * BLOCK)
        pre = dot_nt(first_low[rows], held) + bias
        gate = 0.5 + 0.5 * lax.erf(pre * math.sqrt(0.5))
        act[0, rows] = (pre * gate).astype(bf16)
        slope[0, rows] = gate + pre * (jnp.exp(-0.5 * pre * pre) * (1.0 / math.sqrt(2.0 * math.pi)))


def feed_forward_kernel(
    mixed, out_weight, inputs, vectors, bias, own, mine,
    normed, inverse, first_low, act, slope,
    held, total, sems,
):
    j = pl.program_id(0)

    @pl.when(j == 0)
    def _():
        copies = [pltpu.make_async_copy(piece, held.at[at], sems.at[at]) for at, piece in enumerate((own, mine))]
        for copy in copies:
            copy.start()
        total[...] = dot(mixed[...], out_weight[...])

        def rows_step(i, carry):
            rows = pl.ds(pl.multiple_of(i * BLOCK, BLOCK), BLOCK)
            value = inputs[rows] + total[rows] + vectors[2:3]
            centered = value - row_mean(value)
            inv = lax.rsqrt(row_mean(centered * centered) + norm_eps)
            z = centered * inv
            normed[rows] = z
            inverse[rows] = inv
            first_low[rows] = (z * vectors[4:5] + vectors[5:6]).astype(bf16)
            return carry

        lax.fori_loop(0, BLOCKS, rows_step, 0)

    pltpu.make_async_copy(held.at[j], held.at[j], sems.at[j]).wait()
    gelu_block(first_low, held[j], bias[j], act, slope, j)


def feed_forward(mixed, out_weight, inputs, vectors, bias, pieces):
    shapes = (
        struct((ROWS, D), f32),
        struct((ROWS, 1), f32),
        struct((ROWS, D), bf16),
        struct((2, ROWS, D), bf16),
        struct((2, ROWS, D), f32),
    )
    block = pl.BlockSpec((1, ROWS, D), lambda j: (j, 0, 0))
    return pl.pallas_call(
        feed_forward_kernel,
        out_shape=shapes,
        grid=(2,),
        in_specs=wholes((mixed, out_weight, inputs, vectors, bias)) + [HB] * 2,
        out_specs=(*wholes(shapes[:3]), block, block),
        scratch_shapes=[
            pltpu.VMEM((2, D, D), bf16),
            pltpu.VMEM((ROWS, D), f32),
            pltpu.SemaphoreType.DMA((2,)),
        ],
        compiler_params=params(17),
        name="feed_forward",
    )(mixed, out_weight, inputs, vectors, bias, *pieces)


def fetch_rest(place, pieces, held, sems):
    other, near_diag, far_diag = pieces
    half = D // 2
    core = place[4]
    pltpu.make_async_copy(other, held.at[0], sems.at[0]).start()
    for at, (piece, where) in enumerate(((near_diag, core), (far_diag, 1 - core))):
        target = held.at[1, pl.ds(pl.multiple_of(where * half, half), half)]
        pltpu.make_async_copy(piece, target, sems.at[1 + at]).start()


def wait_rest(j, held, sems):
    @pl.when(j == 0)
    def _():
        pltpu.make_async_copy(held.at[0], held.at[0], sems.at[0]).wait()

    @pl.when(j == 1)
    def _():
        for at in range(2):
            target = held.at[1, pl.ds(at * (D // 2), D // 2)]
            pltpu.make_async_copy(target, target, sems.at[1 + at]).wait()


def feed_forward_rest_kernel(
    place, first_low, bias, other, near_diag, far_diag,
    act, slope,
    held, sems,
):
    j = pl.program_id(0)

    @pl.when(j == 0)
    def _():
        fetch_rest(place, (other, near_diag, far_diag), held, sems)

    wait_rest(j, held, sems)
    gelu_block(first_low, held[j], bias[2 + j], act, slope, j)


def feed_forward_rest(place, first_low, bias, pieces):
    block = pl.BlockSpec((1, ROWS, D), lambda j: (j, 0, 0))
    return pl.pallas_call(
        feed_forward_rest_kernel,
        out_shape=(struct((2, ROWS, D), bf16), struct((2, ROWS, D), f32)),
        grid=(2,),
        in_specs=[SM, *wholes((first_low, bias))] + [HB] * 3,
        out_specs=(block, block),
        scratch_shapes=[pltpu.VMEM((2, D, D), bf16), pltpu.SemaphoreType.DMA((3,))],
        compiler_params=params(14),
        name="feed_forward_rest",
    )(place, first_low, bias, *pieces)


def two_halves(rows, cols):
    return [
        pl.BlockSpec((1, rows, cols), lambda j: (jnp.minimum(j, 1), 0, 0)),
        pl.BlockSpec((1, rows, cols), lambda j: (jnp.maximum(j - 2, 0), 0, 0)),
    ]


def with_half(j, first, second, use):
    @pl.when(j < 2)
    def _():
        use(first)

    @pl.when(j >= 2)
    def _():
        use(second)


def branch_kernel(
    place, act, act_rest, normed, incoming, vectors, own, mine, other, near_diag, far_diag,
    block_low, branch_low, second, sums,
    held, total, sems,
):
    j = pl.program_id(0)

    @pl.when(j == 0)
    def _():
        fetch_hidden(place, (own, mine, other, near_diag, far_diag), held, sems)
        sums[...] = jnp.zeros_like(sums)
        total[...] = jnp.zeros_like(total)

    wait_hidden(j, held, sems)

    def add(part):
        total[...] += dot(part[0], held[j])

    with_half(j, act, act_rest, add)

    @pl.when(j == 3)
    def _():

        def second_step(i, carry):
            rows = pl.ds(pl.multiple_of(i * BLOCK, BLOCK), BLOCK)
            first = normed[rows] * vectors[4:5] + vectors[5:6]
            value = first + total[rows] + vectors[3:4]
            centered = value - row_mean(value)
            inv = lax.rsqrt(row_mean(centered * centered) + norm_eps)
            z = centered * inv
            block_low[rows] = (z * vectors[6:7] + vectors[7:8]).astype(bf16)
            upper = incoming[rows]
            scaled = upper * vectors[6:7]
            grad = inv * (scaled - row_mean(scaled) - z * row_mean(scaled * z))
            second[rows] = grad
            branch_low[rows] = grad.astype(bf16)
            sums[0:1] += col_sum(grad)
            sums[1:2] += col_sum(upper * z)
            sums[2:3] += col_sum(upper)
            return carry

        lax.fori_loop(0, BLOCKS, second_step, 0)


def branch_of(place, act, act_rest, normed, incoming, vectors, pieces):
    shapes = (
        struct((ROWS, D), bf16),
        struct((ROWS, D), bf16),
        struct((ROWS, D), f32),
        struct((8, D), f32),
    )
    return pl.pallas_call(
        branch_kernel,
        out_shape=shapes,
        grid=(4,),
        in_specs=[SM, *two_halves(ROWS, D), *wholes((normed, incoming, vectors))] + [HB] * 5,
        out_specs=tuple(wholes(shapes)),
        scratch_shapes=[
            pltpu.VMEM((4, D, D), bf16),
            pltpu.VMEM((ROWS, D), f32),
            pltpu.SemaphoreType.DMA((5,)),
        ],
        compiler_params=params(17),
        name="branch",
    )(place, act, act_rest, normed, incoming, vectors, *pieces)


def hidden_back(j, slope, branch_low, in_held, out_held, pre_low, bias_sum, total):
    pre_grad = dot_nt(branch_low[...], out_held[j]) * slope[0]
    pre_low[0] = pre_grad.astype(bf16)
    bias_sum[0] = col_sum(pre_grad)
    total[...] += dot(pre_low[0], in_held[j])


def feed_back_kernel(
    slope, branch_low, second, in_own, in_mine, out_own, out_mine,
    pre_low, bias_sum, total,
    in_held, out_held, sems,
):
    j = pl.program_id(0)

    @pl.when(j == 0)
    def _():
        for at, (piece, target) in enumerate(
            ((out_own, out_held.at[0]), (in_own, in_held.at[0]), (out_mine, out_held.at[1]), (in_mine, in_held.at[1]))
        ):
            pltpu.make_async_copy(piece, target, sems.at[at]).start()
        total[...] = second[...]

    for held, at in ((out_held, 0), (in_held, 1)):
        pltpu.make_async_copy(held.at[j], held.at[j], sems.at[2 * j + at]).wait()
    hidden_back(j, slope, branch_low, in_held, out_held, pre_low, bias_sum, total)


def feed_back(slope, branch_low, second, in_pieces, out_pieces):
    shapes = (struct((2, ROWS, D), bf16), struct((2, 1, D), f32), struct((ROWS, D), f32))
    block = pl.BlockSpec((1, ROWS, D), lambda j: (j, 0, 0))
    return pl.pallas_call(
        feed_back_kernel,
        out_shape=shapes,
        grid=(2,),
        in_specs=[block, *wholes((branch_low, second))] + [HB] * 4,
        out_specs=(block, pl.BlockSpec((1, 1, D), lambda j: (j, 0, 0)), whole((ROWS, D))),
        scratch_shapes=[
            pltpu.VMEM((2, D, D), bf16),
            pltpu.VMEM((2, D, D), bf16),
            pltpu.SemaphoreType.DMA((4,)),
        ],
        compiler_params=params(16),
        name="feed_back",
    )(slope, branch_low, second, *in_pieces, *out_pieces)


def feed_back_rest_kernel(
    place, slope, branch_low, partial, normed, inverse, vectors, out_weight,
    in_other, in_near, in_far, out_other, out_near, out_far,
    pre_low, bias_sum, attn_low, attn_grad, heads_grad, sums,
    in_held, out_held, total, in_sems, out_sems,
):
    j = pl.program_id(0)

    @pl.when(j == 0)
    def _():
        fetch_rest(place, (out_other, out_near, out_far), out_held, out_sems)
        fetch_rest(place, (in_other, in_near, in_far), in_held, in_sems)
        sums[...] = jnp.zeros_like(sums)
        total[...] = partial[...]

    wait_rest(j, out_held, out_sems)
    wait_rest(j, in_held, in_sems)
    hidden_back(j, slope, branch_low, in_held, out_held, pre_low, bias_sum, total)

    @pl.when(j == 1)
    def _():
        def first_step(i, carry):
            rows = pl.ds(pl.multiple_of(i * BLOCK, BLOCK), BLOCK)
            z = normed[rows]
            first_grad = total[rows]
            scaled = first_grad * vectors[4:5]
            grad = inverse[rows] * (scaled - row_mean(scaled) - z * row_mean(scaled * z))
            attn_grad[rows] = grad
            attn_low[rows] = grad.astype(bf16)
            sums[0:1] += col_sum(grad)
            sums[1:2] += col_sum(first_grad * z)
            sums[2:3] += col_sum(first_grad)
            return carry

        lax.fori_loop(0, BLOCKS, first_step, 0)
        total[...] = dot_nt(attn_low[...], out_weight[...])
        put_heads(heads_grad, total, lax.broadcasted_iota(jnp.int32, (ROWS, BLOCK), 1))


def feed_back_rest(place, slope, branch_low, partial, normed, inverse, vectors, out_weight, in_pieces, out_pieces):
    shapes = (
        struct((2, ROWS, D), bf16),
        struct((2, 1, D), f32),
        struct((ROWS, D), bf16),
        struct((ROWS, D), f32),
        struct((2 * PAIRS, BLOCKS, 2 * BLOCK, BLOCK), bf16),
        struct((8, D), f32),
    )
    block = pl.BlockSpec((1, ROWS, D), lambda j: (j, 0, 0))
    return pl.pallas_call(
        feed_back_rest_kernel,
        out_shape=shapes,
        grid=(2,),
        in_specs=[SM, block, *wholes((branch_low, partial, normed, inverse, vectors, out_weight))] + [HB] * 6,
        out_specs=(block, pl.BlockSpec((1, 1, D), lambda j: (j, 0, 0)), *wholes(shapes[2:])),
        scratch_shapes=[
            pltpu.VMEM((2, D, D), bf16),
            pltpu.VMEM((2, D, D), bf16),
            pltpu.VMEM((ROWS, D), f32),
            pltpu.SemaphoreType.DMA((3,)),
            pltpu.SemaphoreType.DMA((3,)),
        ],
        compiler_params=params(22),
        name="feed_back_rest",
    )(place, slope, branch_low, partial, normed, inverse, vectors, out_weight, *in_pieces, *out_pieces)


def ffn_grad_kernel(order, rows, *refs):
    cols, (own, sent, turned) = refs[:-3], refs[-3:]
    j = pl.program_id(0)

    @pl.when(j == 0)
    def _():
        turned[...] = dot_nt(order[...], rows[...]).astype(bf16)

    def product(part):
        result = dot(turned[...], part[0]).astype(bf16)
        own[0] = result[: D // 2]
        sent[0] = result[D // 2 :]

    if len(cols) == 1:
        product(cols[0])
    else:
        with_half(j, *cols, product)


def ffn_grad(order, rows, *cols):
    slots = 2 * len(cols)
    block = pl.BlockSpec((1, D // 2, D), lambda j: (j, 0, 0))
    one = [pl.BlockSpec((1, ROWS, D), lambda j: (j, 0, 0))]
    return pl.pallas_call(
        ffn_grad_kernel,
        out_shape=(struct((slots, D // 2, D), bf16),) * 2,
        grid=(slots,),
        in_specs=wholes((order, rows)) + (one if len(cols) == 1 else two_halves(ROWS, D)),
        out_specs=(block, block),
        scratch_shapes=[pltpu.VMEM((D, ROWS), bf16)],
        compiler_params=params(12),
        name="ffn_grad",
    )(order, rows, *cols)


def turn_kernel(order, x, turned):
    turned[...] = dot_nt(order[...], x[...]).astype(bf16)


def turn_rows(order, x):
    return pl.pallas_call(
        turn_kernel,
        out_shape=struct((D, EXT), bf16),
        grid=(1,),
        in_specs=wholes((order, x)),
        out_specs=whole((D, EXT)),
        compiler_params=params(12),
        name="turn_rows",
    )(order, x)


def attn_weight_grad_kernel(order, turned, attn_low, mixed, query_grad, near_low, far_low, target, held):
    near_x = turned[:, NEAR0 : NEAR0 + NEAR]
    held[0] = dot(near_x, query_grad[...])
    for kind in range(2):
        near = jnp.concatenate([near_low[kind, pair] for pair in range(PAIRS)], axis=1)
        far = jnp.concatenate([far_low[kind, pair] for pair in range(PAIRS)], axis=1)
        held[1 + kind, :, 0 : D // 2] = dot(near_x, near)
        held[1 + kind, :, D // 2 : D] = dot(turned[...], far)
    held[3] = dot(dot_nt(order[...], attn_low[...]).astype(bf16), mixed[...])

    rows = D // 8
    lane = lax.broadcasted_iota(jnp.int32, (rows, BLOCK), 1)

    def step(i, carry):
        here = pl.ds(pl.multiple_of(i * rows, rows), rows)
        for pair in range(2):
            tiles = [
                [held[c, here, (3 * pair + t) * BLOCK : (3 * pair + t + 1) * BLOCK] for t in range(3)] for c in range(4)
            ]
            for odd in range(2):
                parts = [tiles[c][2 * odd] for c in range(4)]
                for c in (0, 2):
                    a, b = (tiles[c][1], tiles[c + 1][1])
                    if odd:
                        parts.append(jnp.where(lane < HEAD, pltpu.roll(a, HEAD, 1), b))
                    else:
                        parts.append(jnp.where(lane < HEAD, a, pltpu.roll(b, HEAD, 1)))
                for t, part in enumerate(parts):
                    target[2 * pair + odd, here, t * BLOCK : (t + 1) * BLOCK] = part.astype(bf16)
        return carry

    lax.fori_loop(0, 4, step, 0)


def attn_weight_grad(half, order, turned, attn_low, mixed, query_grad, near_low, far_low):
    return pl.pallas_call(
        attn_weight_grad_kernel,
        out_shape=struct((4, D // 2, D), bf16),
        grid=(1,),
        in_specs=[
            pl.BlockSpec((D // 2, D), lambda i: (half, 0)),
            pl.BlockSpec((D // 2, EXT), lambda i: (half, 0)),
        ]
        + [whole(a.shape) for a in (attn_low, mixed, query_grad, near_low, far_low)],
        out_specs=whole((4, D // 2, D)),
        scratch_shapes=[pltpu.VMEM((4, D // 2, D), f32)],
        compiler_params=params(19),
        name="attn_weight_grad",
    )(order, turned, attn_low, mixed, query_grad, near_low, far_low)


def add_kernel(groups, steps, *refs):
    count = sum(groups)
    operands, target = refs[count : 2 * count], refs[2 * count]
    step = pl.program_id(0)
    at = 0
    for group, terms in enumerate(groups):
        mine = operands[at : at + terms]
        at += terms

        @pl.when((step >= group * steps) & (step < (group + 1) * steps))
        def _(mine=mine):
            total = mine[0][...].astype(f32)
            for operand in mine[1:]:
                total = total + operand[...].astype(f32)
            target[...] = total.astype(target.dtype)


def add_blocks(dtype, *groups, mib=16):
    steps = groups[0][0][1].shape[0]
    rows, cols = groups[0][0][0].shape[1:]
    block = (1, rows, cols)
    terms = [(array, at, group) for group, members in enumerate(groups) for array, at in members]
    count = len(terms)
    total = steps * len(groups)

    def spec(k, group):
        return pl.BlockSpec(block, lambda i, *at: (at[k][jnp.clip(i - group * steps, 0, steps - 1)], 0, 0))

    return pl.pallas_call(
        functools.partial(add_kernel, [len(members) for members in groups], steps),
        out_shape=struct((total, rows, cols), dtype),
        grid_spec=pltpu.PrefetchScalarGridSpec(
            num_scalar_prefetch=count,
            grid=(total,),
            in_specs=[spec(k, group) for k, (_, _, group) in enumerate(terms)],
            out_specs=pl.BlockSpec(block, lambda i, *at: (i, 0, 0)),
        ),
        compiler_params=params(mib),
        name="add_blocks",
    )(*[at for _, at, _ in terms], *[array for array, _, _ in terms])


def input_grad_kernel(
    place, query_grad, near_own, pool_own, from_left, from_right, attn_grad, pool, block_low,
    own, mine, other, near_diag, far_diag,
    low, value_sum,
    pooled, rows_held, grads, weights, sems,
):
    wait_weights = fetch_attention(place, (own, mine, other, near_diag, far_diag), weights, None, sems)
    left_on = jnp.where(place[5] > 0, 1.0, 0.0)
    right_on = jnp.where(place[5] + ROWS < place[7], 1.0, 0.0)
    side = REACH2 // 4
    own_pool = ROWS // 4
    wide = PAIRS * BLOCK
    for kind in range(2):
        for pair in range(PAIRS):
            lanes = slice(pair * BLOCK, (pair + 1) * BLOCK)
            rows_held[...] = near_own[kind, pair]
            rows_held[0:REACH1] += from_left[kind, pair, 0:REACH1].astype(f32) * left_on
            rows_held[ROWS - REACH1 : ROWS] += from_right[kind, pair, 0:REACH1].astype(f32) * right_on
            if kind:
                value_sum[:, lanes] = col_sum(rows_held[...])
            grads[kind, :, lanes] = rows_held[...].astype(bf16)

            pooled[...] = pool_own[kind, pair]
            pooled[0:side] += from_left[kind, pair, REACH1 : REACH1 + side].astype(f32) * left_on
            arrived = from_right[kind, pair, REACH1 : REACH1 + side + 16].astype(f32) * right_on
            pooled[side : own_pool + 8] += arrived[0 : side + 8]
            here, following = pooled[0:own_pool], pooled[1 : own_pool + 1]
            weight = [pool[5 * kind + tap : 5 * kind + tap + 1, lanes] for tap in range(5)]
            rows_held[pl.ds(0, own_pool, stride=4), :] = weight[2] * here
            rows_held[pl.ds(1, own_pool, stride=4), :] = weight[3] * here
            rows_held[pl.ds(2, own_pool, stride=4), :] = weight[4] * here + weight[0] * following
            rows_held[pl.ds(3, own_pool, stride=4), :] = weight[1] * following
            lanes = slice(wide + pair * BLOCK, wide + (pair + 1) * BLOCK)
            if kind:
                value_sum[:, lanes] = col_sum(rows_held[...])
            grads[kind, :, lanes] = rows_held[...].astype(bf16)
    wait_weights()
    total = attn_grad[...] + dot(query_grad[REACH1 : REACH1 + ROWS], weights[0])
    total = total + dot(grads[0], weights[1])
    low[1] = (total + dot(grads[1], weights[2])).astype(bf16)
    low[0] = block_low[...]


def input_grad_of(place, query_grad, near_own, pool_own, from_left, from_right, attn_grad, pool, block_low, pieces):
    return pl.pallas_call(
        input_grad_kernel,
        out_shape=(struct((2, ROWS, D), bf16), struct((1, D), f32)),
        grid=(1,),
        in_specs=[SM, *wholes((query_grad, near_own, pool_own, from_left, from_right, attn_grad, pool, block_low))] + [HB] * 5,
        out_specs=(whole((2, ROWS, D)), whole((1, D))),
        scratch_shapes=[
            pltpu.VMEM((ROWS // 4 + 8, BLOCK), f32),
            pltpu.VMEM((ROWS, BLOCK), f32),
            pltpu.VMEM((2, ROWS, D), bf16),
            pltpu.VMEM((3, D, D), bf16),
            pltpu.SemaphoreType.DMA((9,)),
        ],
        compiler_params=params(),
        name="input_grad",
    )(place, query_grad, near_own, pool_own, from_left, from_right, attn_grad, pool, block_low, *pieces)


def place_kernel(at, own, mine, other, block_out, input_grad):
    step = pl.program_id(0)
    for k, piece in enumerate((own, mine, other)):

        @pl.when(step == k)
        def _(piece=piece):
            block_out[...] = piece[0].astype(f32)
            input_grad[...] = piece[1].astype(f32)


def place_rows(at, *pieces):
    chunk = pl.BlockSpec((ROWS, D), lambda i, at: (at[i], 0))
    return pl.pallas_call(
        place_kernel,
        out_shape=(struct((4 * ROWS, D), f32),) * 2,
        grid_spec=pltpu.PrefetchScalarGridSpec(
            num_scalar_prefetch=1,
            grid=(3,),
            in_specs=[whole((2, ROWS, D))] * 3,
            out_specs=(chunk, chunk),
        ),
        compiler_params=params(56),
        name="place_rows",
    )(at, *pieces)


def place_last_kernel(at, piece, block_held, input_held, block_out, input_grad):
    block_out[...] = piece[0].astype(f32)
    input_grad[...] = piece[1].astype(f32)


def place_last(at, piece, block_out, input_grad):
    rows = ROWS // 2
    chunk = pl.BlockSpec((rows, D), lambda i, at: (at[3] * 2 + i, 0))
    return pl.pallas_call(
        place_last_kernel,
        out_shape=(struct((4 * ROWS, D), f32),) * 2,
        grid_spec=pltpu.PrefetchScalarGridSpec(
            num_scalar_prefetch=1,
            grid=(2,),
            in_specs=[pl.BlockSpec((2, rows, D), lambda i, at: (0, i, 0)), HB, HB],
            out_specs=(chunk, chunk),
        ),
        input_output_aliases={2: 0, 3: 1},
        compiler_params=params(56),
        name="place_last",
    )(at, piece, block_out, input_grad)


def slices_kernel(
    at, qkv, out_weight, in_weight, ff_out_weight,
    qkv_slice, out_slice, in_slice, ff_out_slice,
    qkv_held, out_held, in_held, ff_out_held, sems,
):
    first, shift = pl.multiple_of(at[0], BLOCK), at[1]
    lanes = pl.ds(first, 2 * BLOCK)
    copies = [
        pltpu.make_async_copy(in_weight.at[:, lanes], in_held, sems.at[0]),
        pltpu.make_async_copy(ff_out_weight.at[:, lanes], ff_out_held, sems.at[1]),
        pltpu.make_async_copy(out_weight.at[:, lanes], out_held, sems.at[2]),
        pltpu.make_async_copy(qkv.at[:, :, lanes], qkv_held, sems.at[3]),
    ]
    for copy in copies:
        copy.start()
    width = in_slice.shape[0]

    def moved(value):
        return pltpu.roll(value, shift, 1)[:, 0:BLOCK]

    for copy, held, target in ((copies[0], in_held, in_slice), (copies[1], ff_out_held, ff_out_slice)):
        copy.wait()
        target[...] = jnp.transpose(moved(held[...]))[0:width]
    copies[2].wait()
    out_slice[...] = moved(out_held[...])[:, 0:width]
    copies[3].wait()
    for c in range(3):
        qkv_slice[c] = jnp.transpose(moved(qkv_held[c]))[0:width]


def own_slices(offset, width, qkv_weight, out_weight, in_weight, ff_out_weight):
    local = qkv_weight.shape[2]
    first = jnp.minimum(offset // BLOCK * BLOCK, D - 2 * BLOCK)
    shift = (2 * BLOCK - (offset - first)) % (2 * BLOCK)
    shapes = (
        struct((3, width, local), f32),
        struct((local, width), f32),
        struct((width, D), f32),
        struct((width, D), f32),
    )
    return pl.pallas_call(
        slices_kernel,
        out_shape=shapes,
        grid=(1,),
        in_specs=[SM] + [HB] * 4,
        out_specs=tuple(wholes(shapes)),
        scratch_shapes=[
            pltpu.VMEM((3, local, 2 * BLOCK), f32),
            pltpu.VMEM((local, 2 * BLOCK), f32),
            pltpu.VMEM((D, 2 * BLOCK), f32),
            pltpu.VMEM((D, 2 * BLOCK), f32),
            pltpu.SemaphoreType.DMA((4,)),
        ],
        compiler_params=params(56),
        name="own_slices",
    )(
        jnp.stack([first, shift]).astype(jnp.int32),
        qkv_weight.transpose(0, 2, 1),
        out_weight,
        in_weight,
        ff_out_weight,
    )


def square_sum(value):
    return jnp.sum(value * value)


def pack_kernel(place, query_sum, value_sum, first_sums, second_sums, bias_sum, bias_rest, pool_sum, attn, hidden, packed):
    packed[...] = jnp.zeros_like(packed)
    for pair in range(2 * PAIRS):
        packed[0:1, pair * BLOCK : (pair + 1) * BLOCK] = query_sum[pair]
    packed[1:2] = value_sum[...]
    packed[2:3] = first_sums[0:1]
    packed[3:4] = second_sums[0:1]
    packed[4:6] = first_sums[1:3]
    packed[6:8] = second_sums[1:3]
    for at in range(2):
        packed[pl.ds(8 + place[at], 1), :] = bias_sum[at]
        packed[pl.ds(8 + place[2 + at], 1), :] = bias_rest[at]
    lane = lax.broadcasted_iota(jnp.int32, (1, BLOCK), 1)
    wide = lax.broadcasted_iota(jnp.int32, (1, PAIRS * BLOCK), 1)
    for tap in range(10):
        row = jnp.zeros((1, BLOCK), f32)
        taps = pool_sum[tap : tap + 1, :]
        for head in range(HEADS // 2):
            mine = (wide >= head * HEAD) & (wide < (head + 1) * HEAD)
            row = row + jnp.where(lane == head, jnp.sum(jnp.where(mine, taps, 0.0), axis=1, keepdims=True), 0.0)
        at = 12 + tap // 5
        packed[at : at + 1, (tap % 5) * BLOCK : (tap % 5 + 1) * BLOCK] = row
    first = square_sum(attn[...])
    second = square_sum(hidden[...])
    packed[14:15, 0:BLOCK] = jnp.where(lane == 0, first, jnp.where(lane == 1, second, 0.0))


def pack(*operands):
    return pl.pallas_call(
        pack_kernel,
        out_shape=struct((16, D), f32),
        grid=(1,),
        in_specs=[SM, *wholes(operands[1:])],
        out_specs=whole((16, D)),
        compiler_params=params(8),
        name="pack",
    )(*operands)


def update(weight, grad, moments, decay, clip, step, moments_new, at, flat=False):
    clipped = clip * grad
    first_moment = beta_first * moments[0] + (1.0 - beta_first) * clipped
    second_moment = beta_second * moments[1] + (1.0 - beta_second) * clipped * clipped
    corrected_first = first_moment * (1.0 / (1.0 - beta_first**adam_step))
    corrected_second = second_moment * (1.0 / (1.0 - beta_second**adam_step))
    result = corrected_first / (jnp.sqrt(corrected_second) + adam_eps)
    step[at] = result + decay * weight if decay else result
    if flat:
        moments_new[0:1, at[1]] = first_moment
        moments_new[1:2, at[1]] = second_moment
    else:
        moments_new[(0, *at)] = first_moment
        moments_new[(1, *at)] = second_moment


def finish_kernel(
    place, packed, attn, hidden,
    qkv_weight, out_weight, in_weight, ff_out_weight,
    qkv_moments, out_moments, in_moments, ff_out_moments, vector_moments, bias_moments, pool_moments,
    qkv_grad, qkv_step, qkv_new, out_grad, out_step, out_new, in_grad, in_step, in_new,
    ff_out_grad, ff_out_step, ff_out_new, vector_grad, vector_step, vector_new,
    bias_grad, bias_step, bias_new, pool_grad, pool_step, pool_new, clip_out, norms,
    held,
):
    lane = lax.broadcasted_iota(jnp.int32, (1, BLOCK), 1)
    squares = packed[14:15, 0:BLOCK]
    small = square_sum(packed[0:12])
    pooled = square_sum(packed[12:14])
    squares = jnp.where(lane == 2, small, jnp.where(lane == 3, pooled, squares))
    squares = jnp.where(lane < 4, squares, 0.0)
    total = jnp.sqrt(jnp.sum(squares, axis=1, keepdims=True))
    count = 4 * D * D + 2 * FF * D + 8 * D + FF + 10 * (HEADS // 2)
    clip = jnp.minimum(1.0, max_rms * math.sqrt(count) / (total + 1e-06))
    norms[...] = jnp.sqrt(squares)[:, 0:4]
    clip_out[...] = clip

    width = attn.shape[1]
    even = place[0] % 2 == 0
    held[...] = jnp.zeros_like(held)
    everything = (slice(None), slice(None))
    for c in range(4):
        whole_part = attn[0, :, c * BLOCK : (c + 1) * BLOCK]
        tile = attn[0, :, (4 + c // 2) * BLOCK : (5 + c // 2) * BLOCK]
        moved = pltpu.roll(tile, HEAD, 1)
        low, high = (tile, moved) if c % 2 == 0 else (moved, tile)
        straight = jnp.concatenate([whole_part, low], axis=1)
        turned = pltpu.roll(jnp.concatenate([whole_part, high], axis=1), HEAD, 1)
        both = jnp.where(even, straight, turned)
        local = qkv_grad.shape[2]
        if c < 3:
            grad = both[:, 0:local]
            qkv_grad[c] = grad
            moments = (qkv_moments[0, c], qkv_moments[1, c])
            update(qkv_weight[c], grad, moments, decay_rate, clip, qkv_step, qkv_new, (c,))
        else:
            held[0:width] = both
            grad = jnp.transpose(held[...])[0:local, 0:width]
            out_grad[...] = grad
            update(out_weight[...], grad, out_moments, decay_rate, clip, out_step, out_new, everything)
    for at, weight, moments, grad_ref, step, new in (
        (1, in_weight, in_moments, in_grad, in_step, in_new),
        (0, ff_out_weight, ff_out_moments, ff_out_grad, ff_out_step, ff_out_new),
    ):
        grad_ref[...] = hidden[at]
        update(weight[...], hidden[at], moments, decay_rate, clip, step, new, everything)
    vector_grad[...] = packed[0:8]
    update(None, packed[0:8], vector_moments, 0.0, clip, vector_step, vector_new, everything)
    for at in range(4):
        row = packed[8 + at : 9 + at]
        lanes = slice(at * D, (at + 1) * D)
        bias_grad[:, lanes] = row
        here = (slice(None), lanes)
        update(None, row, (bias_moments[0:1, lanes], bias_moments[1:2, lanes]), 0.0, clip, bias_step, bias_new, here, True)
    heads = HEADS // 2
    for tap in range(5):
        grad = packed[12:14, tap * BLOCK : tap * BLOCK + heads]
        pool_grad[tap] = grad
        update(None, grad, (pool_moments[0, tap], pool_moments[1, tap]), 0.0, clip, pool_step, pool_new, (tap,))


def finish(*operands):
    width = operands[2].shape[1]
    local = operands[4].shape[2]

    def three(*shape):
        return [struct(shape, f32), struct(shape, f32), struct((2, *shape), f32)]

    shapes = (
        three(3, width, local)
        + three(local, width)
        + three(width, D)
        + three(width, D)
        + three(8, D)
        + [struct((1, FF), f32), struct((1, FF), f32), struct((2, FF), f32)]
        + three(5, 2, HEADS // 2)
        + [struct((1, 1), f32), struct((1, 4), f32)]
    )
    return pl.pallas_call(
        finish_kernel,
        out_shape=tuple(shapes),
        grid=(1,),
        in_specs=[SM, *wholes(operands[1:])],
        out_specs=tuple(wholes(shapes)),
        scratch_shapes=[pltpu.VMEM((BLOCK, 2 * BLOCK), f32)],
        compiler_params=params(56),
        name="finish",
    )(*operands)


def cross_shards(own, mine, core):
    half = own.shape[0] // 2
    part = lax.dynamic_slice_in_dim(mine, core * half, half, 0)
    near_diag = lax.ppermute(part, PLACE, CROSS)
    other = lax.ppermute(mine, "seq", SWAP)
    far_diag = lax.ppermute(near_diag, "seq", SWAP)
    return (own, mine, other, near_diag, far_diag)


def after(value, *done):
    return lax.optimization_barrier((value, *done))[0]


def rows_by_dp(value, dp):
    n, rows, cols = value.shape
    return value.reshape(n * dp, rows // dp, cols)


class DpSum:
    def __init__(self, dp, dp_index, *groups):
        self.dp, self.dp_index, self.step = dp, dp_index, 1
        self.groups = [[(rows_by_dp(array, dp), slot * dp, 0) for array, slot in terms] for terms in groups]

    def blocks(self, targets):
        return [
            [(array, (first + (targets >> shift)).astype(jnp.int32)) for array, first, shift in terms]
            for terms in self.groups
        ]

    def send(self):
        step = self.step
        targets = jnp.arange(self.dp // (2 * step)) * (2 * step) + (self.dp_index % (2 * step) ^ step)
        return add_blocks(bf16, *self.blocks(targets), mib=56)

    def move(self, value):
        step = self.step
        got = lax.ppermute(value, "dp", [(i, i ^ step) for i in range(self.dp)])
        blocks = self.dp // (2 * step)
        for group, terms in enumerate(self.groups):
            terms.append((got, group * blocks, (2 * step).bit_length() - 1))
        self.step = 2 * step
        return got

    def done(self):
        return self.step >= self.dp

    def result(self):
        return add_blocks(f32, *self.blocks(self.dp_index + jnp.zeros((1,), jnp.int32)), mib=56)


def sum_everywhere(value, dp, between, beside):
    def moved(value, axis, size, step):
        return lax.ppermute(value, axis, [(i, i ^ step) for i in range(size)])

    def four(value, axis, size, step, extra=None):
        got = [moved(value, axis, size, k * step) for k in (1, 2, 3)]
        if extra is not None:
            got[2] = after(got[2], extra)
        return (value + got[0]) + (got[1] + got[2])

    value = four(value, "lvl", 4, 1)
    result = between(value)
    value = value + moved(value, "seq", 2, 1)
    step = 1
    while step < dp:
        extra = beside if step == 1 else None
        if step * 4 <= dp:
            value = four(value, "dp", dp, step, extra)
            step *= 4
        else:
            got = moved(value, "dp", dp, step)
            value = value + (got if extra is None else after(got, extra))
            step *= 2
    return (value, result)


def on_device(
    tokens,
    cotangent,
    lengths,
    qkv_weight,
    out_weight,
    ffn_in_weight,
    ffn_out_weight,
    vectors,
    ffn_bias,
    pool_kernel,
    qkv_moments,
    out_moments,
    ffn_in_moments,
    ffn_out_moments,
    vector_moments,
    bias_moments,
    pool_moments,
):
    dp = lax.axis_size("dp")
    dp_index = lax.axis_index("dp")
    core = lax.axis_index("seq")
    level = lax.axis_index("lvl")
    length = lengths[0]
    count = tokens.shape[1]
    size = count // 4
    seq_len = 2 * count
    half = HEADS // 2
    along = jnp.where(core == 0, 1, 2)
    slots = [level, level ^ along, level ^ (3 - along), level ^ 3]

    def chunk_of(owner):
        order = owner ^ (owner >> 1)
        return jnp.where(core == 0, order, 3 - order)

    chunk = chunk_of(level)
    base = core * count + chunk * size
    width = D // (2 * dp)

    local = qkv_weight.shape[2]
    attn_own = jnp.concatenate(
        [bfloat(qkv_weight).transpose(0, 2, 1).reshape(3 * local, D), bfloat(out_weight)], axis=0
    )
    hidden = ffn_in_weight.shape[0]
    bias = jnp.stack([lax.dynamic_slice_in_dim(ffn_bias, s * hidden, hidden) for s in slots]).reshape(4, 1, D)
    edge = jnp.where(core == 0, tokens[0, count - HALO :], tokens[0, :HALO])
    pool_lanes = jnp.repeat(pool_kernel.reshape(10, half), HEAD, axis=1)
    place = jnp.stack([*slots, core, base, length, seq_len, chunk]).astype(jnp.int32)
    row = jnp.arange(D)
    side, rest = (row // (D // 2), row % (D // 2))
    feature = (rest // width) * (2 * width) + jnp.where(side == 0, core, 1 - core) * width + rest % width
    order = (feature[:, None] == row[None, :]).astype(bf16)
    chunks = jnp.stack([chunk_of(s) for s in slots]).astype(jnp.int32)

    def index(*at):
        return jnp.stack([jnp.asarray(a) for a in at]).astype(jnp.int32)

    attn_mine = lax.ppermute(attn_own, PLACE, MINE)
    edge = lax.ppermute(after(edge, attn_own), "seq", SWAP)
    in_own = bfloat(ffn_in_weight)
    out_own = bfloat(ffn_out_weight)
    weight_slices = own_slices(
        (dp_index * 2 + core) * width, width, qkv_weight, out_weight, ffn_in_weight, ffn_out_weight
    )
    attn_mine = after(attn_mine, weight_slices, edge, in_own, out_own, order, pool_lanes, place, bias)
    part = lax.dynamic_slice_in_dim(attn_mine, core * (D // 2), D // 2, 0)
    attn_near = lax.ppermute(part, PLACE, CROSS)
    attn_other = lax.ppermute(attn_mine, "seq", SWAP)
    extended, inputs, incoming, near_mask, far_mask = prepare(place, edge, after(tokens, part), cotangent)
    attn_near = after(attn_near, extended)
    attn_far = lax.ppermute(attn_near, "seq", SWAP)
    attn_pieces = [
        p.reshape(-1, local, D) for p in (attn_own, attn_mine, attn_other, attn_near, attn_far)
    ]
    in_mine = lax.ppermute(after(in_own, attn_near), PLACE, MINE)
    out_all, *kept = project(place, extended, attn_pieces, vectors, pool_lanes)
    query, near_keys, near_values, far_keys, far_values, pool_keys, pool_values = kept
    in_mine = after(in_mine, query)
    part = lax.dynamic_slice_in_dim(in_mine, core * (D // 2), D // 2, 0)
    in_near = lax.ppermute(part, PLACE, CROSS)
    in_other = lax.ppermute(in_mine, "seq", SWAP)
    out_mine = lax.ppermute(after(out_own, part), PLACE, MINE)
    mixed, log_total = attend_forward(
        after(query, part), near_keys, near_values, pool_keys, pool_values, near_mask, far_mask
    )
    in_near = after(in_near, mixed)
    in_far = lax.ppermute(in_near, "seq", SWAP)
    normed, inverse, first_low, act, slope = feed_forward(mixed, out_all, inputs, vectors, bias, (in_own, in_mine))
    out_mine = after(out_mine, first_low)
    part = lax.dynamic_slice_in_dim(out_mine, core * (D // 2), D // 2, 0)
    out_near = lax.ppermute(part, PLACE, CROSS)
    out_other = lax.ppermute(out_mine, "seq", SWAP)
    act_rest, slope_rest = feed_forward_rest(
        place, after(first_low, part), bias, (after(in_other, first_low), in_near, after(in_far, first_low))
    )
    out_near = after(out_near, act_rest)
    out_far = lax.ppermute(out_near, "seq", SWAP)
    in_pieces = (in_own, in_mine, in_other, in_near, in_far)
    out_pieces = (out_own, out_mine, out_other, out_near, out_far)
    block_low, branch_low, second, second_sums = branch_of(
        place, act, act_rest, normed, incoming, vectors, out_pieces
    )

    out_grad, grad_sent = ffn_grad(order, branch_low, act, act_rest)
    out_got = lax.ppermute(grad_sent, "seq", SWAP)
    pre_low, bias_sum, partial = feed_back(
        slope, after(branch_low, out_grad), second, in_pieces[:2], out_pieces[:2]
    )
    out_got = after(out_got, partial)
    out_send = add_blocks(bf16, [(out_grad, index(1, 3)), (out_got, index(2, 3))])
    out_first = lax.ppermute(out_send, PLACE, MINE)
    pre_rest, bias_rest, attn_low, attn_grad, heads_grad, first_sums = feed_back_rest(
        place, slope_rest, after(branch_low, out_send), partial, normed, inverse, vectors, out_all,
        in_pieces[2:], out_pieces[2:],
    )
    turned = turn_rows(order, after(extended, attn_low))
    in_early, early_sent = ffn_grad(order, after(first_low, turned), pre_low)
    out_first = after(out_first, in_early)
    out_pass = add_blocks(bf16, [(out_grad, index(2)), (out_got, index(1)), (out_first, index(1))])
    out_second = lax.ppermute(out_pass, PLACE, CROSS)
    in_late, late_sent = ffn_grad(order, after(first_low, out_pass), pre_rest)
    late_got = lax.ppermute(late_sent, "seq", SWAP)
    in_send = add_blocks(
        bf16, [(in_early, index(1)), (late_got, index(0))], [(in_late, index(1)), (late_got, index(1))]
    )
    in_first = lax.ppermute(in_send, PLACE, MINE)
    early_got = lax.ppermute(after(early_sent, in_send), "seq", SWAP)

    (query_grad, near_low, far_low, near_own, pool_own, to_left, to_right, query_sum, pool_sum) = attend_backward(
        after(heads_grad, in_send), *kept, near_mask, far_mask, log_total, pool_lanes
    )
    from_right = lax.ppermute(to_left, PLACE, LEFTWARD)
    from_left = lax.ppermute(to_right, PLACE, RIGHTWARD)
    in_first, out_second = after(in_first, query_grad), after(out_second, query_grad)
    early_got = after(early_got, query_grad)
    in_pass = add_blocks(bf16, [(in_late, index(0)), (early_got, index(1)), (in_first, index(1))])
    in_second = lax.ppermute(in_pass, PLACE, CROSS)
    grad_parts = (order, turned, attn_low, mixed, after(query_grad, in_pass, out_second), near_low, far_low)
    grad_sent = attn_weight_grad(1, *grad_parts)
    attn_got = lax.ppermute(grad_sent, "seq", SWAP)
    query_grad = after(query_grad, grad_sent)
    attn_wide = attn_weight_grad(0, *grad_parts[:4], query_grad, near_low, far_low)
    attn_got = after(attn_got, attn_wide, in_second, from_left, from_right)
    attn_at = index(slots[1], slots[3])
    attn_send = add_blocks(bf16, [(attn_wide, attn_at), (attn_got, attn_at)])
    attn_first = lax.ppermute(attn_send, PLACE, MINE)

    out_second, in_second = after(out_second, attn_send), after(in_second, attn_send)
    ffn_sum = DpSum(
        dp,
        dp_index,
        [(out_grad, 0), (out_got, 0), (out_first, 0), (out_second, 0)],
        [(in_early, 0), (early_got, 0), (in_first, 0), (in_second, 0)],
    )
    ffn_part = ffn_sum.send()
    ffn_moved = ffn_sum.move(ffn_part)
    both_low, value_sum = input_grad_of(
        place, after(query_grad, ffn_part), near_own, pool_own, from_left, from_right, attn_grad, pool_lanes, block_low,
        attn_pieces,
    )
    attn_first = after(attn_first, both_low)
    attn_at = index(slots[2])
    attn_pass = add_blocks(bf16, [(attn_wide, attn_at), (attn_got, attn_at), (attn_first, index(1))], mib=56)
    attn_second = lax.ppermute(attn_pass, PLACE, CROSS)
    while not ffn_sum.done():
        ffn_part = ffn_sum.send()
        ffn_moved = ffn_sum.move(after(ffn_part, attn_pass))
    attn_second = after(attn_second, ffn_part)
    attn_sum = DpSum(
        dp, dp_index, [(attn_wide, slots[0]), (attn_got, slots[0]), (attn_first, 0), (attn_second, 0)]
    )
    attn_part = attn_sum.send()
    attn_moved = attn_sum.move(attn_part)
    both_mine = lax.ppermute(after(both_low, attn_part), PLACE, MINE)
    both_other = lax.ppermute(after(both_low, attn_part), PLACE, CROSS)
    attn_sum.groups[0][-1] = (after(attn_moved, ffn_moved), *attn_sum.groups[0][-1][1:])
    while not attn_sum.done():
        attn_part = attn_sum.send()
        attn_moved = attn_sum.move(attn_part)
    ffn_sum.groups = [[(after(terms[0][0], attn_part), *terms[0][1:]), *terms[1:]] for terms in ffn_sum.groups]
    ffn_shard = ffn_sum.result()
    attn_moved = after(attn_moved, ffn_shard)
    attn_sum.groups[0][-1] = (attn_moved, *attn_sum.groups[0][-1][1:])
    attn_shard = attn_sum.result()
    block_out, input_grad = place_rows(chunks, both_low, both_mine, both_other)

    packed = pack(
        place, query_sum, value_sum, first_sums, second_sums, bias_sum, bias_rest, pool_sum, attn_shard, ffn_shard
    )
    packed, diag_low = sum_everywhere(packed, dp, lambda value: after(both_mine, both_other, value), block_out)
    both_diag = lax.ppermute(diag_low, PLACE, CROSS)
    results = finish(
        place, packed, attn_shard, ffn_shard, *weight_slices,
        qkv_moments, out_moments, ffn_in_moments.transpose(0, 2, 1), ffn_out_moments.transpose(0, 2, 1), vector_moments,
        bias_moments, pool_moments.transpose(0, 2, 1, 3),
    )
    qkv_out, out_out, in_out, ff_out_out, vector_out = [results[3 * i : 3 * i + 3] for i in range(5)]
    block_out, input_grad = place_last(chunks, both_diag, block_out, input_grad)
    *_, bias_grad, bias_step, bias_new, pool_grad, pool_step, pool_new, clip, norms = results
    return (
        block_out[None],
        input_grad[None],
        *qkv_out,
        *out_out,
        *[value.swapaxes(-1, -2) for value in (*in_out, *ff_out_out)],
        *vector_out,
        bias_grad.reshape(FF),
        bias_step.reshape(FF),
        bias_new,
        pool_grad.transpose(1, 0, 2),
        pool_step.transpose(1, 0, 2),
        pool_new.transpose(0, 2, 1, 3),
        clip.reshape(()),
        norms.reshape(4),
    )


def solution(mesh):
    in_specs = (
        P("dp", "seq", None),
        P("dp", "seq", None),
        P("dp"),
        P(None, None, "lvl"),
        P("lvl", None),
        P("lvl", None),
        P("lvl", None),
        P(),
        P(),
        P(),
        P(None, None, ("dp", "seq"), "lvl"),
        P(None, "lvl", ("dp", "seq")),
        P(None, "lvl", ("dp", "seq")),
        P(None, "lvl", ("dp", "seq")),
        P(),
        P(),
        P(),
    )
    out_specs = (
        P("dp", "seq", None),
        P("dp", "seq", None),
        P(None, ("dp", "seq"), "lvl"),
        P(None, ("dp", "seq"), "lvl"),
        P(None, None, ("dp", "seq"), "lvl"),
        P("lvl", ("dp", "seq")),
        P("lvl", ("dp", "seq")),
        P(None, "lvl", ("dp", "seq")),
        P("lvl", ("dp", "seq")),
        P("lvl", ("dp", "seq")),
        P(None, "lvl", ("dp", "seq")),
        P("lvl", ("dp", "seq")),
        P("lvl", ("dp", "seq")),
        P(None, "lvl", ("dp", "seq")),
        P(),
        P(),
        P(),
        P(),
        P(),
        P(),
        P(),
        P(),
        P(),
        P(),
        P(),
    )
    return jax.shard_map(
        on_device, mesh=mesh, in_specs=in_specs, out_specs=out_specs, check_vma=False
    )
```

```python
import functools
import math

import jax
import jax.numpy as jnp
from jax import lax
from jax.experimental import pallas as pl
from jax.experimental.pallas import tpu as pltpu
from jax.sharding import PartitionSpec as P

D = 768
HEADS = 12
HEAD = 64
FF = 3072
REACH1 = 64
REACH2 = 256
HALO = 320
ROWS = 512
EXT = ROWS + 2 * HALO
NEAR = ROWS + 2 * REACH1
NEAR0 = HALO - REACH1
FAR0 = 48
FAR = 1056
POOLED = 256
TAP0 = 14
BLOCK = 128
BLOCKS = ROWS // BLOCK
PAIRS = HEADS // 4

norm_eps = 1e-05
beta_first = 0.9
beta_second = 0.999
adam_eps = 1e-08
decay_rate = 0.01
adam_step = 10.0
max_rms = 1.0
masked_score = -1e30
score_scale = 1.0 / math.sqrt(HEAD)

f32 = jnp.float32
bf16 = jnp.bfloat16
SWAP = [(0, 1), (1, 0)]
MINE = [(i, i ^ 1) for i in range(4)] + [(4 + i, 4 + (i ^ 2)) for i in range(4)]
CROSS = [(i, i ^ 2) for i in range(4)] + [(4 + i, 4 + (i ^ 1)) for i in range(4)]
PATH = [0, 1, 3, 2, 6, 7, 5, 4]
RIGHTWARD = list(zip(PATH, PATH[1:] + PATH[:1]))
LEFTWARD = [(b, a) for a, b in RIGHTWARD]
PLACE = ("seq", "lvl")

SM = pl.BlockSpec(memory_space=pltpu.SMEM)
HB = pl.BlockSpec(memory_space=pltpu.HBM)


def bfloat(value):
    return value.astype(bf16)


def params(mib=56):
    return pltpu.CompilerParams(vmem_limit_bytes=mib * 1024 * 1024)


def struct(shape, dtype):
    return jax.ShapeDtypeStruct(shape, dtype)


def dot(a, b):
    return jnp.dot(a, b, preferred_element_type=f32)


def dot_nt(a, b):
    return lax.dot_general(a, b, (((1,), (1,)), ((), ())), preferred_element_type=f32)


def turn(value):
    return jnp.transpose(value.astype(f32)).astype(bf16)


def row_mean(value):
    return jnp.mean(value, axis=-1, keepdims=True)


def col_sum(value):
    return jnp.sum(value, axis=0, keepdims=True)


def whole(shape):
    return pl.BlockSpec(shape, lambda *_: (0,) * len(shape), pipeline_mode=pl.Buffered(1))


def wholes(operands):
    return [whole(operand.shape) for operand in operands]


def copy_when(condition, source, target, sem):
    @pl.when(condition)
    def _():
        pltpu.make_async_copy(source, target, sem).start()


def wait_when(condition, target, sem):
    @pl.when(condition)
    def _():
        pltpu.make_async_copy(target, target, sem).wait()


def fetch_attention(place, pieces, weights, out_weight, sems):
    own, mine, other, near_diag, far_diag = pieces
    core = place[4]
    local = own.shape[1]
    copies = []

    def rows_of(owner):
        return pl.ds(pl.multiple_of(owner * local, 64), local)

    for at, piece in enumerate((own, mine, other)):
        rows = rows_of(place[at])
        copies.append(pltpu.make_async_copy(piece.at[pl.ds(0, 3)], weights.at[:, rows], sems.at[at]))
        if out_weight is not None:
            copies.append(pltpu.make_async_copy(piece.at[3], out_weight.at[rows], sems.at[3 + at]))
    for copy in copies:
        copy.start()
    rows = rows_of(place[3])
    targets = [weights.at[pl.ds(0, 2), rows], weights.at[2, rows]]
    if out_weight is not None:
        targets.append(out_weight.at[rows])
    for condition, low, high in ((core == 0, near_diag, far_diag), (core != 0, far_diag, near_diag)):
        for at, source in enumerate((low, high.at[0], high.at[1])[: len(targets)]):
            copy_when(condition, source, targets[at], sems.at[6 + at])

    def wait():
        for copy in copies:
            copy.wait()
        for at, target in enumerate(targets):
            pltpu.make_async_copy(target, target, sems.at[6 + at]).wait()

    return wait


def prepare_kernel(place, edge, tokens, cotangent, low, inputs, incoming, near_mask, far_mask, x, sems):
    core, base, length, seq_len, chunk = [place[i] for i in range(4, 9)]
    first = pl.multiple_of(chunk * ROWS, ROWS)
    left, right = x.at[pl.ds(0, HALO)], x.at[pl.ds(HALO + ROWS, HALO)]
    middle = pltpu.make_async_copy(tokens.at[0, pl.ds(first, ROWS)], inputs, sems.at[0])
    upper = pltpu.make_async_copy(cotangent.at[0, pl.ds(first, ROWS)], incoming, sems.at[3])
    middle.start()
    upper.start()
    starts, ends = chunk == 0, chunk == 3
    left_at = pl.multiple_of(jnp.maximum(first - HALO, 0), 64)
    right_at = pl.multiple_of(jnp.minimum(first + ROWS, 4 * ROWS - HALO), 64)
    copy_when(jnp.logical_not(starts), tokens.at[0, pl.ds(left_at, HALO)], left, sems.at[1])
    copy_when(jnp.logical_and(starts, core == 1), edge, left, sems.at[1])
    copy_when(jnp.logical_not(ends), tokens.at[0, pl.ds(right_at, HALO)], right, sems.at[2])
    copy_when(jnp.logical_and(ends, core == 0), edge, right, sems.at[2])
    no_left = jnp.logical_and(starts, core == 0)
    no_right = jnp.logical_and(ends, core == 1)

    @pl.when(no_left)
    def _():
        x[0:HALO] = jnp.zeros((HALO, D), f32)

    @pl.when(no_right)
    def _():
        x[HALO + ROWS : EXT] = jnp.zeros((HALO, D), f32)

    key_at = lax.broadcasted_iota(jnp.int32, (2 * BLOCK, BLOCK), 0)
    row_at = lax.broadcasted_iota(jnp.int32, (2 * BLOCK, BLOCK), 1)

    def bias(rows, cols, reach):
        same = jnp.where(rows < length, 1, 0) == jnp.where(cols < length, 1, 0)
        seen = (jnp.abs(rows - cols) <= reach) & same & (cols >= 0) & (cols < seq_len)
        return jnp.where(seen, 0.0, masked_score)

    for block in range(BLOCKS):
        rows = base + block * BLOCK + row_at
        near_mask[block] = bias(rows, base + block * BLOCK - REACH1 + key_at, REACH1)
        far_mask[block] = bias(rows, base - REACH2 + 4 * key_at, REACH2)

    middle.wait()
    upper.wait()
    wait_when(jnp.logical_not(no_left), left, sems.at[1])
    wait_when(jnp.logical_not(no_right), right, sems.at[2])
    low[0:HALO] = x[0:HALO].astype(bf16)
    low[HALO : HALO + ROWS] = inputs[...].astype(bf16)
    low[HALO + ROWS : EXT] = x[HALO + ROWS : EXT].astype(bf16)


def prepare(place, edge, tokens, cotangent):
    shapes = (
        struct((EXT, D), bf16),
        struct((ROWS, D), f32),
        struct((ROWS, D), f32),
        struct((BLOCKS, 2 * BLOCK, BLOCK), f32),
        struct((BLOCKS, 2 * BLOCK, BLOCK), f32),
    )
    return pl.pallas_call(
        prepare_kernel,
        out_shape=shapes,
        grid=(1,),
        in_specs=[SM] + [HB] * 3,
        out_specs=tuple(wholes(shapes)),
        scratch_shapes=[pltpu.VMEM((EXT, D), f32), pltpu.SemaphoreType.DMA((4,))],
        compiler_params=params(56),
        name="prepare",
    )(place, edge, tokens, cotangent)


def project_kernel(
    place, low, own, mine, other, near_diag, far_diag, vectors, pool,
    out_weight, query, near_keys, near_values, far_keys, far_values, pool_keys, pool_values,
    weights, key_rows, value_rows, sems,
):
    base, seq_len = place[5], place[7]
    fetch_attention(place, (own, mine, other, near_diag, far_diag), weights, out_weight, sems)()
    wide = PAIRS * BLOCK
    lane = lax.broadcasted_iota(jnp.int32, (ROWS, BLOCK), 1)
    projected = (dot_nt(low[HALO : HALO + ROWS], weights[0]) + vectors[0:1]).astype(bf16).astype(f32) * score_scale
    put_heads(query, projected, lane)

    def inside(rows, start):
        index = start + lax.broadcasted_iota(jnp.int32, (rows, BLOCK), 0)
        return (index >= 0) & (index < seq_len)

    near_inside = inside(NEAR, base - REACH1)
    far_inside = inside(FAR, base - HALO + FAR0)
    for c, near_ref, far_ref, rows_ref in ((1, near_keys, far_keys, key_rows), (2, near_values, far_values, value_rows)):
        near = dot_nt(low[NEAR0 : NEAR0 + NEAR], weights[c, 0:wide])
        far = dot_nt(low[FAR0 : FAR0 + FAR], weights[c, wide:D])
        if c == 2:
            near = near + vectors[1:2, 0:wide]
            far = far + vectors[1:2, wide:D]
        for pair in range(PAIRS):
            lanes = slice(pair * BLOCK, (pair + 1) * BLOCK)
            near_ref[pair] = jnp.where(near_inside, near[:, lanes], 0.0).astype(bf16)
            part = jnp.where(far_inside, far[:, lanes], 0.0).astype(bf16)
            far_ref[pair] = part
            rows_ref[pair] = part.astype(f32)
    for at, rows_ref, pooled_ref in ((0, key_rows, pool_keys), (5, value_rows, pool_values)):
        for pair in range(PAIRS):
            lanes = slice(pair * BLOCK, (pair + 1) * BLOCK)
            total = None
            for tap in range(5):
                part = pool[at + tap : at + tap + 1, lanes] * rows_ref[pair, pl.ds(TAP0 + tap, POOLED, stride=4), :]
                total = part if total is None else total + part
            pooled_ref[pair] = total.astype(bf16)


def put_heads(target, value, lane):
    for pair in range(2 * PAIRS):
        part = value[:, pair * BLOCK : (pair + 1) * BLOCK]
        first = jnp.where(lane < HEAD, part, 0.0).astype(bf16)
        second = jnp.where(lane >= HEAD, part, 0.0).astype(bf16)
        for block in range(BLOCKS):
            rows = slice(block * BLOCK, (block + 1) * BLOCK)
            target[pair, block, 0:BLOCK] = first[rows]
            target[pair, block, BLOCK : 2 * BLOCK] = second[rows]


def project(place, low, pieces, vectors, pool):
    shapes = (
        struct((D, D), bf16),
        struct((2 * PAIRS, BLOCKS, 2 * BLOCK, BLOCK), bf16),
        struct((PAIRS, NEAR, BLOCK), bf16),
        struct((PAIRS, NEAR, BLOCK), bf16),
        struct((PAIRS, FAR, BLOCK), bf16),
        struct((PAIRS, FAR, BLOCK), bf16),
        struct((PAIRS, POOLED, BLOCK), bf16),
        struct((PAIRS, POOLED, BLOCK), bf16),
    )
    return pl.pallas_call(
        project_kernel,
        out_shape=shapes,
        grid=(1,),
        in_specs=[SM, whole((EXT, D))] + [HB] * 5 + wholes((vectors, pool)),
        out_specs=tuple(wholes(shapes)),
        scratch_shapes=[
            pltpu.VMEM((3, D, D), bf16),
            pltpu.VMEM((PAIRS, FAR, BLOCK), f32),
            pltpu.VMEM((PAIRS, FAR, BLOCK), f32),
            pltpu.SemaphoreType.DMA((9,)),
        ],
        compiler_params=params(19),
        name="project",
    )(place, low, *pieces, vectors, pool)


def attend_forward_kernel(
    query, near_keys, near_values, pool_keys, pool_values, near_mask, far_mask,
    mixed, log_total,
):
    def attend(keys, turned, pair, block, mask):
        scores = dot_nt(keys, query[pair, block])
        parts = []
        for e in range(2):
            lanes = slice(e * BLOCK, (e + 1) * BLOCK)
            masked = scores[:, lanes] + mask[block]
            top = jnp.max(masked, axis=0, keepdims=True)
            raised = jnp.exp(masked - top)
            total = jnp.sum(raised, axis=0, keepdims=True)
            log_total[pair, block, :, lanes] = top + jnp.log(total)
            parts.append((raised * (1.0 / total)).astype(bf16))
        both = dot(turned, jnp.concatenate(parts, axis=1))
        output = jnp.concatenate([both[0:HEAD, 0:BLOCK], both[HEAD:BLOCK, BLOCK : 2 * BLOCK]], axis=0)
        lanes = pl.ds(pl.multiple_of(pair * BLOCK, BLOCK), BLOCK)
        mixed[block * BLOCK : (block + 1) * BLOCK, lanes] = turn(output)

    def near_pair(pair, carry):
        turned = turn(near_values[pair])
        for block in range(BLOCKS):
            window = slice(block * BLOCK, (block + 2) * BLOCK)
            attend(near_keys[pair, window], turned[:, window], pair, block, near_mask)
        return carry

    def far_pair(pair, carry):
        turned = turn(pool_values[pair])
        for block in range(BLOCKS):
            attend(pool_keys[pair], turned, PAIRS + pair, block, far_mask)
        return carry

    lax.fori_loop(0, PAIRS, near_pair, 0)
    lax.fori_loop(0, PAIRS, far_pair, 0)


def attend_forward(*operands):
    shapes = (struct((ROWS, D), bf16), struct((2 * PAIRS, BLOCKS, 1, 2 * BLOCK), f32))
    return pl.pallas_call(
        attend_forward_kernel,
        out_shape=shapes,
        grid=(1,),
        in_specs=wholes(operands),
        out_specs=tuple(wholes(shapes)),
        compiler_params=params(10),
        name="attend_forward",
    )(*operands)


def attend_backward_kernel(
    grad, query, near_keys, near_values, far_keys, far_values, pool_keys, pool_values, near_mask, far_mask, log_total,
    pool,
    query_grad, near_low, far_low, near_own, pool_own, to_left, to_right, query_sum, pool_sum,
    near_total, pool_total, far_rows, shifted,
):
    near_total[...] = jnp.zeros_like(near_total)
    pool_total[...] = jnp.zeros_like(pool_total)
    query_grad[0:REACH1] = jnp.zeros((REACH1, D), bf16)
    query_grad[NEAR - REACH1 : NEAR] = jnp.zeros((REACH1, D), bf16)

    def back(keys, values, turned, pair, block, mask):
        part = grad[pair, block]
        asked = query[pair, block]
        scores = dot_nt(keys, asked)
        chance_grads = dot_nt(values, part)
        chances = []
        score_grads = []
        for e in range(2):
            lanes = slice(e * BLOCK, (e + 1) * BLOCK)
            chance = jnp.exp(scores[:, lanes] + mask[block] - log_total[pair, block, :, lanes])
            chance_grad = chance_grads[:, lanes]
            mean = jnp.sum(chance * chance_grad, axis=0, keepdims=True)
            score_grads.append((chance * (chance_grad - mean)).astype(bf16))
            chances.append(chance.astype(bf16))
        score_grad = jnp.concatenate(score_grads, axis=1)
        both = dot(turned, score_grad)
        output = jnp.concatenate([both[0:HEAD, 0:BLOCK], both[HEAD:BLOCK, BLOCK : 2 * BLOCK]], axis=0)
        output = jnp.transpose(output) * score_scale
        lanes = pl.ds(pl.multiple_of(pair * BLOCK, BLOCK), BLOCK)
        query_grad[REACH1 + block * BLOCK : REACH1 + (block + 1) * BLOCK, lanes] = output.astype(bf16)
        return (col_sum(output), dot(score_grad, asked), dot(jnp.concatenate(chances, axis=1), part))

    def near_pair(pair, carry):
        turned = turn(near_keys[pair])
        sums = jnp.zeros((1, BLOCK), f32)
        for block in range(BLOCKS):
            window = slice(block * BLOCK, (block + 2) * BLOCK)
            part, keys, values = back(
                near_keys[pair, window], near_values[pair, window], turned[:, window], pair, block, near_mask
            )
            near_total[0, pair, window] += keys
            near_total[1, pair, window] += values
            sums = sums + part
        query_sum[pair] = sums
        return carry

    def far_pair(pair, carry):
        turned = turn(pool_keys[pair])
        sums = jnp.zeros((1, BLOCK), f32)
        for block in range(BLOCKS):
            part, keys, values = back(pool_keys[pair], pool_values[pair], turned, PAIRS + pair, block, far_mask)
            pool_total[0, pair] += keys
            pool_total[1, pair] += values
            sums = sums + part
        query_sum[PAIRS + pair] = sums
        return carry

    lax.fori_loop(0, PAIRS, near_pair, 0)
    lax.fori_loop(0, PAIRS, far_pair, 0)

    side = REACH2 // 4
    own_pool = ROWS // 4
    for kind in range(2):
        near_low[kind] = near_total[kind].astype(bf16)
        near_own[kind] = near_total[kind, :, REACH1 : REACH1 + ROWS]
        pool_own[kind] = pool_total[kind, :, side : side + own_pool + 8]
        to_left[kind, :, 0:REACH1] = near_total[kind, :, 0:REACH1].astype(bf16)
        to_left[kind, :, REACH1 : REACH1 + side + 16] = pool_total[kind, :, 0 : side + 16].astype(bf16)
        to_right[kind, :, 0:REACH1] = near_total[kind, :, NEAR - REACH1 : NEAR].astype(bf16)
        to_right[kind, :, REACH1 : REACH1 + side] = pool_total[kind, :, side + own_pool :].astype(bf16)

    for kind, rows_ref in ((0, far_keys), (1, far_values)):
        for pair in range(PAIRS):
            lanes = slice(pair * BLOCK, (pair + 1) * BLOCK)
            far_rows[0:FAR] = rows_ref[pair].astype(f32)
            pooled = pool_total[kind, pair]
            for tap in range(5):
                pool_sum[5 * kind + tap : 5 * kind + tap + 1, lanes] = col_sum(
                    pooled * far_rows[pl.ds(TAP0 + tap, POOLED, stride=4), :]
                )
            shifted[0:8] = jnp.zeros((8, BLOCK), f32)
            shifted[8 : 8 + POOLED] = pooled
            weight = [pool[5 * kind + tap : 5 * kind + tap + 1, lanes] for tap in range(5)]
            first = FAR0 + TAP0
            far_rows[0 : first + 2] = jnp.zeros((first + 2, BLOCK), f32)
            far_rows[EXT - 72 : EXT] = jnp.zeros((72, BLOCK), f32)
            far_rows[pl.ds(first, POOLED, stride=4), :] = weight[0] * pooled + weight[4] * shifted[7 : 7 + POOLED]
            for tap in range(1, 4):
                far_rows[pl.ds(first + tap, POOLED, stride=4), :] = weight[tap] * pooled
            far_rows[first + 4 * POOLED : first + 4 * POOLED + 1] = weight[4] * pooled[POOLED - 1 : POOLED]
            far_low[kind, pair] = far_rows[...].astype(bf16)


def attend_backward(*operands):
    side = REACH2 // 4
    shapes = (
        struct((NEAR, D), bf16),
        struct((2, PAIRS, NEAR, BLOCK), bf16),
        struct((2, PAIRS, EXT, BLOCK), bf16),
        struct((2, PAIRS, ROWS, BLOCK), f32),
        struct((2, PAIRS, ROWS // 4 + 8, BLOCK), f32),
        struct((2, PAIRS, REACH1 + side + 16, BLOCK), bf16),
        struct((2, PAIRS, REACH1 + side, BLOCK), bf16),
        struct((2 * PAIRS, 1, BLOCK), f32),
        struct((10, PAIRS * BLOCK), f32),
    )
    return pl.pallas_call(
        attend_backward_kernel,
        out_shape=shapes,
        grid=(1,),
        in_specs=wholes(operands),
        out_specs=tuple(wholes(shapes)),
        scratch_shapes=[
            pltpu.VMEM((2, PAIRS, NEAR, BLOCK), f32),
            pltpu.VMEM((2, PAIRS, POOLED, BLOCK), f32),
            pltpu.VMEM((EXT, BLOCK), f32),
            pltpu.VMEM((POOLED + 8, BLOCK), f32),
        ],
        compiler_params=params(19),
        name="attend_backward",
    )(*operands)


def fetch_hidden(place, pieces, held, sems):
    own, mine, other, near_diag, far_diag = pieces
    core = place[4]
    half = D // 2
    copies = [pltpu.make_async_copy(piece, held.at[at], sems.at[at]) for at, piece in enumerate((own, mine, other))]
    for at, (piece, where) in enumerate(((near_diag, core), (far_diag, 1 - core))):
        target = held.at[3, pl.ds(pl.multiple_of(where * half, half), half)]
        copies.append(pltpu.make_async_copy(piece, target, sems.at[3 + at]))
    for copy in copies:
        copy.start()


def wait_hidden(j, held, sems):
    @pl.when(j < 3)
    def _():
        pltpu.make_async_copy(held.at[j], held.at[j], sems.at[j]).wait()

    @pl.when(j == 3)
    def _():
        for at in range(2):
            target = held.at[3, pl.ds(at * (D // 2), D // 2)]
            pltpu.make_async_copy(target, target, sems.at[3 + at]).wait()


def gelu_block(first_low, held, bias, act, slope, j):
    for block in range(BLOCKS):
        rows = slice(block * BLOCK, (block + 1) * BLOCK)
        pre = dot_nt(first_low[rows], held) + bias
        gate = 0.5 + 0.5 * lax.erf(pre * math.sqrt(0.5))
        act[0, rows] = (pre * gate).astype(bf16)
        slope[0, rows] = gate + pre * (jnp.exp(-0.5 * pre * pre) * (1.0 / math.sqrt(2.0 * math.pi)))


def feed_forward_kernel(
    mixed, out_weight, inputs, vectors, bias, own, mine,
    normed, inverse, first_low, act, slope,
    held, total, sems,
):
    j = pl.program_id(0)

    @pl.when(j == 0)
    def _():
        copies = [pltpu.make_async_copy(piece, held.at[at], sems.at[at]) for at, piece in enumerate((own, mine))]
        for copy in copies:
            copy.start()
        total[...] = dot(mixed[...], out_weight[...])

        def rows_step(i, carry):
            rows = pl.ds(pl.multiple_of(i * BLOCK, BLOCK), BLOCK)
            value = inputs[rows] + total[rows] + vectors[2:3]
            centered = value - row_mean(value)
            inv = lax.rsqrt(row_mean(centered * centered) + norm_eps)
            z = centered * inv
            normed[rows] = z
            inverse[rows] = inv
            first_low[rows] = (z * vectors[4:5] + vectors[5:6]).astype(bf16)
            return carry

        lax.fori_loop(0, BLOCKS, rows_step, 0)

    pltpu.make_async_copy(held.at[j], held.at[j], sems.at[j]).wait()
    gelu_block(first_low, held[j], bias[j], act, slope, j)


def feed_forward(mixed, out_weight, inputs, vectors, bias, pieces):
    shapes = (
        struct((ROWS, D), f32),
        struct((ROWS, 1), f32),
        struct((ROWS, D), bf16),
        struct((2, ROWS, D), bf16),
        struct((2, ROWS, D), f32),
    )
    block = pl.BlockSpec((1, ROWS, D), lambda j: (j, 0, 0))
    return pl.pallas_call(
        feed_forward_kernel,
        out_shape=shapes,
        grid=(2,),
        in_specs=wholes((mixed, out_weight, inputs, vectors, bias)) + [HB] * 2,
        out_specs=(*wholes(shapes[:3]), block, block),
        scratch_shapes=[
            pltpu.VMEM((2, D, D), bf16),
            pltpu.VMEM((ROWS, D), f32),
            pltpu.SemaphoreType.DMA((2,)),
        ],
        compiler_params=params(17),
        name="feed_forward",
    )(mixed, out_weight, inputs, vectors, bias, *pieces)


def fetch_rest(place, pieces, held, sems):
    other, near_diag, far_diag = pieces
    half = D // 2
    core = place[4]
    pltpu.make_async_copy(other, held.at[0], sems.at[0]).start()
    for at, (piece, where) in enumerate(((near_diag, core), (far_diag, 1 - core))):
        target = held.at[1, pl.ds(pl.multiple_of(where * half, half), half)]
        pltpu.make_async_copy(piece, target, sems.at[1 + at]).start()


def wait_rest(j, held, sems):
    @pl.when(j == 0)
    def _():
        pltpu.make_async_copy(held.at[0], held.at[0], sems.at[0]).wait()

    @pl.when(j == 1)
    def _():
        for at in range(2):
            target = held.at[1, pl.ds(at * (D // 2), D // 2)]
            pltpu.make_async_copy(target, target, sems.at[1 + at]).wait()


def feed_forward_rest_kernel(
    place, first_low, bias, other, near_diag, far_diag,
    act, slope,
    held, sems,
):
    j = pl.program_id(0)

    @pl.when(j == 0)
    def _():
        fetch_rest(place, (other, near_diag, far_diag), held, sems)

    wait_rest(j, held, sems)
    gelu_block(first_low, held[j], bias[2 + j], act, slope, j)


def feed_forward_rest(place, first_low, bias, pieces):
    block = pl.BlockSpec((1, ROWS, D), lambda j: (j, 0, 0))
    return pl.pallas_call(
        feed_forward_rest_kernel,
        out_shape=(struct((2, ROWS, D), bf16), struct((2, ROWS, D), f32)),
        grid=(2,),
        in_specs=[SM, *wholes((first_low, bias))] + [HB] * 3,
        out_specs=(block, block),
        scratch_shapes=[pltpu.VMEM((2, D, D), bf16), pltpu.SemaphoreType.DMA((3,))],
        compiler_params=params(14),
        name="feed_forward_rest",
    )(place, first_low, bias, *pieces)


def two_halves(rows, cols):
    return [
        pl.BlockSpec((1, rows, cols), lambda j: (jnp.minimum(j, 1), 0, 0)),
        pl.BlockSpec((1, rows, cols), lambda j: (jnp.maximum(j - 2, 0), 0, 0)),
    ]


def with_half(j, first, second, use):
    @pl.when(j < 2)
    def _():
        use(first)

    @pl.when(j >= 2)
    def _():
        use(second)


def branch_kernel(
    place, act, act_rest, normed, incoming, vectors, own, mine, other, near_diag, far_diag,
    block_low, branch_low, second, sums,
    held, total, sems,
):
    j = pl.program_id(0)

    @pl.when(j == 0)
    def _():
        fetch_hidden(place, (own, mine, other, near_diag, far_diag), held, sems)
        sums[...] = jnp.zeros_like(sums)
        total[...] = jnp.zeros_like(total)

    wait_hidden(j, held, sems)

    def add(part):
        total[...] += dot(part[0], held[j])

    with_half(j, act, act_rest, add)

    @pl.when(j == 3)
    def _():

        def second_step(i, carry):
            rows = pl.ds(pl.multiple_of(i * BLOCK, BLOCK), BLOCK)
            first = normed[rows] * vectors[4:5] + vectors[5:6]
            value = first + total[rows] + vectors[3:4]
            centered = value - row_mean(value)
            inv = lax.rsqrt(row_mean(centered * centered) + norm_eps)
            z = centered * inv
            block_low[rows] = (z * vectors[6:7] + vectors[7:8]).astype(bf16)
            upper = incoming[rows]
            scaled = upper * vectors[6:7]
            grad = inv * (scaled - row_mean(scaled) - z * row_mean(scaled * z))
            second[rows] = grad
            branch_low[rows] = grad.astype(bf16)
            sums[0:1] += col_sum(grad)
            sums[1:2] += col_sum(upper * z)
            sums[2:3] += col_sum(upper)
            return carry

        lax.fori_loop(0, BLOCKS, second_step, 0)


def branch_of(place, act, act_rest, normed, incoming, vectors, pieces):
    shapes = (
        struct((ROWS, D), bf16),
        struct((ROWS, D), bf16),
        struct((ROWS, D), f32),
        struct((8, D), f32),
    )
    return pl.pallas_call(
        branch_kernel,
        out_shape=shapes,
        grid=(4,),
        in_specs=[SM, *two_halves(ROWS, D), *wholes((normed, incoming, vectors))] + [HB] * 5,
        out_specs=tuple(wholes(shapes)),
        scratch_shapes=[
            pltpu.VMEM((4, D, D), bf16),
            pltpu.VMEM((ROWS, D), f32),
            pltpu.SemaphoreType.DMA((5,)),
        ],
        compiler_params=params(17),
        name="branch",
    )(place, act, act_rest, normed, incoming, vectors, *pieces)


def hidden_back(j, slope, branch_low, in_held, out_held, pre_low, bias_sum, total):
    pre_grad = dot_nt(branch_low[...], out_held[j]) * slope[0]
    pre_low[0] = pre_grad.astype(bf16)
    bias_sum[0] = col_sum(pre_grad)
    total[...] += dot(pre_low[0], in_held[j])


def feed_back_kernel(
    slope, branch_low, second, in_own, in_mine, out_own, out_mine,
    pre_low, bias_sum, total,
    in_held, out_held, sems,
):
    j = pl.program_id(0)

    @pl.when(j == 0)
    def _():
        for at, (piece, target) in enumerate(
            ((out_own, out_held.at[0]), (in_own, in_held.at[0]), (out_mine, out_held.at[1]), (in_mine, in_held.at[1]))
        ):
            pltpu.make_async_copy(piece, target, sems.at[at]).start()
        total[...] = second[...]

    for held, at in ((out_held, 0), (in_held, 1)):
        pltpu.make_async_copy(held.at[j], held.at[j], sems.at[2 * j + at]).wait()
    hidden_back(j, slope, branch_low, in_held, out_held, pre_low, bias_sum, total)


def feed_back(slope, branch_low, second, in_pieces, out_pieces):
    shapes = (struct((2, ROWS, D), bf16), struct((2, 1, D), f32), struct((ROWS, D), f32))
    block = pl.BlockSpec((1, ROWS, D), lambda j: (j, 0, 0))
    return pl.pallas_call(
        feed_back_kernel,
        out_shape=shapes,
        grid=(2,),
        in_specs=[block, *wholes((branch_low, second))] + [HB] * 4,
        out_specs=(block, pl.BlockSpec((1, 1, D), lambda j: (j, 0, 0)), whole((ROWS, D))),
        scratch_shapes=[
            pltpu.VMEM((2, D, D), bf16),
            pltpu.VMEM((2, D, D), bf16),
            pltpu.SemaphoreType.DMA((4,)),
        ],
        compiler_params=params(16),
        name="feed_back",
    )(slope, branch_low, second, *in_pieces, *out_pieces)


def feed_back_rest_kernel(
    place, slope, branch_low, partial, normed, inverse, vectors, out_weight,
    in_other, in_near, in_far, out_other, out_near, out_far,
    pre_low, bias_sum, attn_low, attn_grad, heads_grad, sums,
    in_held, out_held, total, in_sems, out_sems,
):
    j = pl.program_id(0)

    @pl.when(j == 0)
    def _():
        fetch_rest(place, (out_other, out_near, out_far), out_held, out_sems)
        fetch_rest(place, (in_other, in_near, in_far), in_held, in_sems)
        sums[...] = jnp.zeros_like(sums)
        total[...] = partial[...]

    wait_rest(j, out_held, out_sems)
    wait_rest(j, in_held, in_sems)
    hidden_back(j, slope, branch_low, in_held, out_held, pre_low, bias_sum, total)

    @pl.when(j == 1)
    def _():
        def first_step(i, carry):
            rows = pl.ds(pl.multiple_of(i * BLOCK, BLOCK), BLOCK)
            z = normed[rows]
            first_grad = total[rows]
            scaled = first_grad * vectors[4:5]
            grad = inverse[rows] * (scaled - row_mean(scaled) - z * row_mean(scaled * z))
            attn_grad[rows] = grad
            attn_low[rows] = grad.astype(bf16)
            sums[0:1] += col_sum(grad)
            sums[1:2] += col_sum(first_grad * z)
            sums[2:3] += col_sum(first_grad)
            return carry

        lax.fori_loop(0, BLOCKS, first_step, 0)
        total[...] = dot_nt(attn_low[...], out_weight[...])
        put_heads(heads_grad, total, lax.broadcasted_iota(jnp.int32, (ROWS, BLOCK), 1))


def feed_back_rest(place, slope, branch_low, partial, normed, inverse, vectors, out_weight, in_pieces, out_pieces):
    shapes = (
        struct((2, ROWS, D), bf16),
        struct((2, 1, D), f32),
        struct((ROWS, D), bf16),
        struct((ROWS, D), f32),
        struct((2 * PAIRS, BLOCKS, 2 * BLOCK, BLOCK), bf16),
        struct((8, D), f32),
    )
    block = pl.BlockSpec((1, ROWS, D), lambda j: (j, 0, 0))
    return pl.pallas_call(
        feed_back_rest_kernel,
        out_shape=shapes,
        grid=(2,),
        in_specs=[SM, block, *wholes((branch_low, partial, normed, inverse, vectors, out_weight))] + [HB] * 6,
        out_specs=(block, pl.BlockSpec((1, 1, D), lambda j: (j, 0, 0)), *wholes(shapes[2:])),
        scratch_shapes=[
            pltpu.VMEM((2, D, D), bf16),
            pltpu.VMEM((2, D, D), bf16),
            pltpu.VMEM((ROWS, D), f32),
            pltpu.SemaphoreType.DMA((3,)),
            pltpu.SemaphoreType.DMA((3,)),
        ],
        compiler_params=params(22),
        name="feed_back_rest",
    )(place, slope, branch_low, partial, normed, inverse, vectors, out_weight, *in_pieces, *out_pieces)


def ffn_grad_kernel(order, rows, *refs):
    cols, (own, sent, turned) = refs[:-3], refs[-3:]
    j = pl.program_id(0)

    @pl.when(j == 0)
    def _():
        turned[...] = dot_nt(order[...], rows[...]).astype(bf16)

    def product(part):
        result = dot(turned[...], part[0]).astype(bf16)
        own[0] = result[: D // 2]
        sent[0] = result[D // 2 :]

    if len(cols) == 1:
        product(cols[0])
    else:
        with_half(j, *cols, product)


def ffn_grad(order, rows, *cols):
    slots = 2 * len(cols)
    block = pl.BlockSpec((1, D // 2, D), lambda j: (j, 0, 0))
    one = [pl.BlockSpec((1, ROWS, D), lambda j: (j, 0, 0))]
    return pl.pallas_call(
        ffn_grad_kernel,
        out_shape=(struct((slots, D // 2, D), bf16),) * 2,
        grid=(slots,),
        in_specs=wholes((order, rows)) + (one if len(cols) == 1 else two_halves(ROWS, D)),
        out_specs=(block, block),
        scratch_shapes=[pltpu.VMEM((D, ROWS), bf16)],
        compiler_params=params(12),
        name="ffn_grad",
    )(order, rows, *cols)


def turn_kernel(order, x, turned):
    turned[...] = dot_nt(order[...], x[...]).astype(bf16)


def turn_rows(order, x):
    return pl.pallas_call(
        turn_kernel,
        out_shape=struct((D, EXT), bf16),
        grid=(1,),
        in_specs=wholes((order, x)),
        out_specs=whole((D, EXT)),
        compiler_params=params(12),
        name="turn_rows",
    )(order, x)


def attn_weight_grad_kernel(order, turned, attn_low, mixed, query_grad, near_low, far_low, target, held):
    near_x = turned[:, NEAR0 : NEAR0 + NEAR]
    held[0] = dot(near_x, query_grad[...])
    for kind in range(2):
        near = jnp.concatenate([near_low[kind, pair] for pair in range(PAIRS)], axis=1)
        far = jnp.concatenate([far_low[kind, pair] for pair in range(PAIRS)], axis=1)
        held[1 + kind, :, 0 : D // 2] = dot(near_x, near)
        held[1 + kind, :, D // 2 : D] = dot(turned[...], far)
    held[3] = dot(dot_nt(order[...], attn_low[...]).astype(bf16), mixed[...])

    rows = D // 8
    lane = lax.broadcasted_iota(jnp.int32, (rows, BLOCK), 1)

    def step(i, carry):
        here = pl.ds(pl.multiple_of(i * rows, rows), rows)
        for pair in range(2):
            tiles = [
                [held[c, here, (3 * pair + t) * BLOCK : (3 * pair + t + 1) * BLOCK] for t in range(3)] for c in range(4)
            ]
            for odd in range(2):
                parts = [tiles[c][2 * odd] for c in range(4)]
                for c in (0, 2):
                    a, b = (tiles[c][1], tiles[c + 1][1])
                    if odd:
                        parts.append(jnp.where(lane < HEAD, pltpu.roll(a, HEAD, 1), b))
                    else:
                        parts.append(jnp.where(lane < HEAD, a, pltpu.roll(b, HEAD, 1)))
                for t, part in enumerate(parts):
                    target[2 * pair + odd, here, t * BLOCK : (t + 1) * BLOCK] = part.astype(bf16)
        return carry

    lax.fori_loop(0, 4, step, 0)


def attn_weight_grad(half, order, turned, attn_low, mixed, query_grad, near_low, far_low):
    return pl.pallas_call(
        attn_weight_grad_kernel,
        out_shape=struct((4, D // 2, D), bf16),
        grid=(1,),
        in_specs=[
            pl.BlockSpec((D // 2, D), lambda i: (half, 0)),
            pl.BlockSpec((D // 2, EXT), lambda i: (half, 0)),
        ]
        + [whole(a.shape) for a in (attn_low, mixed, query_grad, near_low, far_low)],
        out_specs=whole((4, D // 2, D)),
        scratch_shapes=[pltpu.VMEM((4, D // 2, D), f32)],
        compiler_params=params(19),
        name="attn_weight_grad",
    )(order, turned, attn_low, mixed, query_grad, near_low, far_low)


def add_kernel(groups, steps, *refs):
    count = sum(groups)
    operands, target = refs[count : 2 * count], refs[2 * count]
    step = pl.program_id(0)
    at = 0
    for group, terms in enumerate(groups):
        mine = operands[at : at + terms]
        at += terms

        @pl.when((step >= group * steps) & (step < (group + 1) * steps))
        def _(mine=mine):
            total = mine[0][...].astype(f32)
            for operand in mine[1:]:
                total = total + operand[...].astype(f32)
            target[...] = total.astype(target.dtype)


def add_blocks(dtype, *groups, mib=16, fused=False):
    steps = groups[0][0][1].shape[0]
    if fused:
        parts = [lax.dynamic_index_in_dim(array, at[0], 0).astype(f32) for array, at in groups[0]]
        return sum(parts[1:], parts[0]).astype(dtype)
    rows, cols = groups[0][0][0].shape[1:]
    block = (1, rows, cols)
    terms = [(array, at, group) for group, members in enumerate(groups) for array, at in members]
    count = len(terms)
    total = steps * len(groups)

    def spec(k, group):
        return pl.BlockSpec(block, lambda i, *at: (at[k][jnp.clip(i - group * steps, 0, steps - 1)], 0, 0))

    return pl.pallas_call(
        functools.partial(add_kernel, [len(members) for members in groups], steps),
        out_shape=struct((total, rows, cols), dtype),
        grid_spec=pltpu.PrefetchScalarGridSpec(
            num_scalar_prefetch=count,
            grid=(total,),
            in_specs=[spec(k, group) for k, (_, _, group) in enumerate(terms)],
            out_specs=pl.BlockSpec(block, lambda i, *at: (i, 0, 0)),
        ),
        compiler_params=params(mib),
        name="add_blocks",
    )(*[at for _, at, _ in terms], *[array for array, _, _ in terms])


def input_grad_kernel(
    place, query_grad, near_own, pool_own, from_left, from_right, attn_grad, pool, block_low,
    own, mine, other, near_diag, far_diag,
    low, value_sum,
    pooled, rows_held, grads, weights, sems,
):
    wait_weights = fetch_attention(place, (own, mine, other, near_diag, far_diag), weights, None, sems)
    left_on = jnp.where(place[5] > 0, 1.0, 0.0)
    right_on = jnp.where(place[5] + ROWS < place[7], 1.0, 0.0)
    side = REACH2 // 4
    own_pool = ROWS // 4
    wide = PAIRS * BLOCK
    for kind in range(2):
        for pair in range(PAIRS):
            lanes = slice(pair * BLOCK, (pair + 1) * BLOCK)
            rows_held[...] = near_own[kind, pair]
            rows_held[0:REACH1] += from_left[kind, pair, 0:REACH1].astype(f32) * left_on
            rows_held[ROWS - REACH1 : ROWS] += from_right[kind, pair, 0:REACH1].astype(f32) * right_on
            if kind:
                value_sum[:, lanes] = col_sum(rows_held[...])
            grads[kind, :, lanes] = rows_held[...].astype(bf16)

            pooled[...] = pool_own[kind, pair]
            pooled[0:side] += from_left[kind, pair, REACH1 : REACH1 + side].astype(f32) * left_on
            arrived = from_right[kind, pair, REACH1 : REACH1 + side + 16].astype(f32) * right_on
            pooled[side : own_pool + 8] += arrived[0 : side + 8]
            here, following = pooled[0:own_pool], pooled[1 : own_pool + 1]
            weight = [pool[5 * kind + tap : 5 * kind + tap + 1, lanes] for tap in range(5)]
            rows_held[pl.ds(0, own_pool, stride=4), :] = weight[2] * here
            rows_held[pl.ds(1, own_pool, stride=4), :] = weight[3] * here
            rows_held[pl.ds(2, own_pool, stride=4), :] = weight[4] * here + weight[0] * following
            rows_held[pl.ds(3, own_pool, stride=4), :] = weight[1] * following
            lanes = slice(wide + pair * BLOCK, wide + (pair + 1) * BLOCK)
            if kind:
                value_sum[:, lanes] = col_sum(rows_held[...])
            grads[kind, :, lanes] = rows_held[...].astype(bf16)
    wait_weights()
    total = attn_grad[...] + dot(query_grad[REACH1 : REACH1 + ROWS], weights[0])
    total = total + dot(grads[0], weights[1])
    low[1] = (total + dot(grads[1], weights[2])).astype(bf16)
    low[0] = block_low[...]


def input_grad_of(place, query_grad, near_own, pool_own, from_left, from_right, attn_grad, pool, block_low, pieces):
    return pl.pallas_call(
        input_grad_kernel,
        out_shape=(struct((2, ROWS, D), bf16), struct((1, D), f32)),
        grid=(1,),
        in_specs=[SM, *wholes((query_grad, near_own, pool_own, from_left, from_right, attn_grad, pool, block_low))] + [HB] * 5,
        out_specs=(whole((2, ROWS, D)), whole((1, D))),
        scratch_shapes=[
            pltpu.VMEM((ROWS // 4 + 8, BLOCK), f32),
            pltpu.VMEM((ROWS, BLOCK), f32),
            pltpu.VMEM((2, ROWS, D), bf16),
            pltpu.VMEM((3, D, D), bf16),
            pltpu.SemaphoreType.DMA((9,)),
        ],
        compiler_params=params(),
        name="input_grad",
    )(place, query_grad, near_own, pool_own, from_left, from_right, attn_grad, pool, block_low, *pieces)


def place_kernel(at, own, mine, other, block_out, input_grad):
    step = pl.program_id(0)
    for k, piece in enumerate((own, mine, other)):

        @pl.when(step == k)
        def _(piece=piece):
            block_out[...] = piece[0].astype(f32)
            input_grad[...] = piece[1].astype(f32)


def place_rows(at, *pieces):
    chunk = pl.BlockSpec((ROWS, D), lambda i, at: (at[i], 0))
    return pl.pallas_call(
        place_kernel,
        out_shape=(struct((4 * ROWS, D), f32),) * 2,
        grid_spec=pltpu.PrefetchScalarGridSpec(
            num_scalar_prefetch=1,
            grid=(3,),
            in_specs=[whole((2, ROWS, D))] * 3,
            out_specs=(chunk, chunk),
        ),
        compiler_params=params(56),
        name="place_rows",
    )(at, *pieces)


def place_last_kernel(at, piece, block_held, input_held, block_out, input_grad):
    block_out[...] = piece[0].astype(f32)
    input_grad[...] = piece[1].astype(f32)


def place_last(at, piece, block_out, input_grad):
    rows = ROWS // 2
    chunk = pl.BlockSpec((rows, D), lambda i, at: (at[3] * 2 + i, 0))
    return pl.pallas_call(
        place_last_kernel,
        out_shape=(struct((4 * ROWS, D), f32),) * 2,
        grid_spec=pltpu.PrefetchScalarGridSpec(
            num_scalar_prefetch=1,
            grid=(2,),
            in_specs=[pl.BlockSpec((2, rows, D), lambda i, at: (0, i, 0)), HB, HB],
            out_specs=(chunk, chunk),
        ),
        input_output_aliases={2: 0, 3: 1},
        compiler_params=params(56),
        name="place_last",
    )(at, piece, block_out, input_grad)


def slices_kernel(
    at, qkv, out_weight, in_weight, ff_out_weight,
    qkv_slice, out_slice, in_slice, ff_out_slice,
    qkv_held, out_held, in_held, ff_out_held, sems,
):
    first, shift = pl.multiple_of(at[0], BLOCK), at[1]
    lanes = pl.ds(first, 2 * BLOCK)
    copies = [
        pltpu.make_async_copy(in_weight.at[:, lanes], in_held, sems.at[0]),
        pltpu.make_async_copy(ff_out_weight.at[:, lanes], ff_out_held, sems.at[1]),
        pltpu.make_async_copy(out_weight.at[:, lanes], out_held, sems.at[2]),
        pltpu.make_async_copy(qkv.at[:, :, lanes], qkv_held, sems.at[3]),
    ]
    for copy in copies:
        copy.start()
    width = in_slice.shape[0]

    def moved(value):
        return pltpu.roll(value, shift, 1)[:, 0:BLOCK]

    for copy, held, target in ((copies[0], in_held, in_slice), (copies[1], ff_out_held, ff_out_slice)):
        copy.wait()
        target[...] = jnp.transpose(moved(held[...]))[0:width]
    copies[2].wait()
    out_slice[...] = moved(out_held[...])[:, 0:width]
    copies[3].wait()
    for c in range(3):
        qkv_slice[c] = jnp.transpose(moved(qkv_held[c]))[0:width]


def own_slices(offset, width, qkv_weight, out_weight, in_weight, ff_out_weight):
    local = qkv_weight.shape[2]
    first = jnp.minimum(offset // BLOCK * BLOCK, D - 2 * BLOCK)
    shift = (2 * BLOCK - (offset - first)) % (2 * BLOCK)
    shapes = (
        struct((3, width, local), f32),
        struct((local, width), f32),
        struct((width, D), f32),
        struct((width, D), f32),
    )
    return pl.pallas_call(
        slices_kernel,
        out_shape=shapes,
        grid=(1,),
        in_specs=[SM] + [HB] * 4,
        out_specs=tuple(wholes(shapes)),
        scratch_shapes=[
            pltpu.VMEM((3, local, 2 * BLOCK), f32),
            pltpu.VMEM((local, 2 * BLOCK), f32),
            pltpu.VMEM((D, 2 * BLOCK), f32),
            pltpu.VMEM((D, 2 * BLOCK), f32),
            pltpu.SemaphoreType.DMA((4,)),
        ],
        compiler_params=params(56),
        name="own_slices",
    )(
        jnp.stack([first, shift]).astype(jnp.int32),
        qkv_weight.transpose(0, 2, 1),
        out_weight,
        in_weight,
        ff_out_weight,
    )


def square_sum(value):
    return jnp.sum(value * value)


def pack_kernel(place, query_sum, value_sum, first_sums, second_sums, bias_sum, bias_rest, pool_sum, attn, hidden, packed):
    packed[...] = jnp.zeros_like(packed)
    for pair in range(2 * PAIRS):
        packed[0:1, pair * BLOCK : (pair + 1) * BLOCK] = query_sum[pair]
    packed[1:2] = value_sum[...]
    packed[2:3] = first_sums[0:1]
    packed[3:4] = second_sums[0:1]
    packed[4:6] = first_sums[1:3]
    packed[6:8] = second_sums[1:3]
    for at in range(2):
        packed[pl.ds(8 + place[at], 1), :] = bias_sum[at]
        packed[pl.ds(8 + place[2 + at], 1), :] = bias_rest[at]
    lane = lax.broadcasted_iota(jnp.int32, (1, BLOCK), 1)
    wide = lax.broadcasted_iota(jnp.int32, (1, PAIRS * BLOCK), 1)
    for tap in range(10):
        row = jnp.zeros((1, BLOCK), f32)
        taps = pool_sum[tap : tap + 1, :]
        for head in range(HEADS // 2):
            mine = (wide >= head * HEAD) & (wide < (head + 1) * HEAD)
            row = row + jnp.where(lane == head, jnp.sum(jnp.where(mine, taps, 0.0), axis=1, keepdims=True), 0.0)
        at = 12 + tap // 5
        packed[at : at + 1, (tap % 5) * BLOCK : (tap % 5 + 1) * BLOCK] = row
    first = square_sum(attn[...])
    second = square_sum(hidden[...])
    packed[14:15, 0:BLOCK] = jnp.where(lane == 0, first, jnp.where(lane == 1, second, 0.0))


def pack(*operands):
    return pl.pallas_call(
        pack_kernel,
        out_shape=struct((16, D), f32),
        grid=(1,),
        in_specs=[SM, *wholes(operands[1:])],
        out_specs=whole((16, D)),
        compiler_params=params(8),
        name="pack",
    )(*operands)


def update(weight, grad, moments, decay, clip, step, moments_new, at, flat=False):
    clipped = clip * grad
    first_moment = beta_first * moments[0] + (1.0 - beta_first) * clipped
    second_moment = beta_second * moments[1] + (1.0 - beta_second) * clipped * clipped
    corrected_first = first_moment * (1.0 / (1.0 - beta_first**adam_step))
    corrected_second = second_moment * (1.0 / (1.0 - beta_second**adam_step))
    result = corrected_first / (jnp.sqrt(corrected_second) + adam_eps)
    step[at] = result + decay * weight if decay else result
    if flat:
        moments_new[0:1, at[1]] = first_moment
        moments_new[1:2, at[1]] = second_moment
    else:
        moments_new[(0, *at)] = first_moment
        moments_new[(1, *at)] = second_moment


def finish_kernel(
    place, packed, attn, hidden,
    qkv_weight, out_weight, in_weight, ff_out_weight,
    qkv_moments, out_moments, in_moments, ff_out_moments, vector_moments, bias_moments, pool_moments,
    qkv_grad, qkv_step, qkv_new, out_grad, out_step, out_new, in_grad, in_step, in_new,
    ff_out_grad, ff_out_step, ff_out_new, vector_grad, vector_step, vector_new,
    bias_grad, bias_step, bias_new, pool_grad, pool_step, pool_new, clip_out, norms,
    held,
):
    lane = lax.broadcasted_iota(jnp.int32, (1, BLOCK), 1)
    squares = packed[14:15, 0:BLOCK]
    small = square_sum(packed[0:12])
    pooled = square_sum(packed[12:14])
    squares = jnp.where(lane == 2, small, jnp.where(lane == 3, pooled, squares))
    squares = jnp.where(lane < 4, squares, 0.0)
    total = jnp.sqrt(jnp.sum(squares, axis=1, keepdims=True))
    count = 4 * D * D + 2 * FF * D + 8 * D + FF + 10 * (HEADS // 2)
    clip = jnp.minimum(1.0, max_rms * math.sqrt(count) / (total + 1e-06))
    norms[...] = jnp.sqrt(squares)[:, 0:4]
    clip_out[...] = clip

    width = attn.shape[1]
    even = place[0] % 2 == 0
    held[...] = jnp.zeros_like(held)
    everything = (slice(None), slice(None))
    for c in range(4):
        whole_part = attn[0, :, c * BLOCK : (c + 1) * BLOCK]
        tile = attn[0, :, (4 + c // 2) * BLOCK : (5 + c // 2) * BLOCK]
        moved = pltpu.roll(tile, HEAD, 1)
        low, high = (tile, moved) if c % 2 == 0 else (moved, tile)
        straight = jnp.concatenate([whole_part, low], axis=1)
        turned = pltpu.roll(jnp.concatenate([whole_part, high], axis=1), HEAD, 1)
        both = jnp.where(even, straight, turned)
        local = qkv_grad.shape[2]
        if c < 3:
            grad = both[:, 0:local]
            qkv_grad[c] = grad
            moments = (qkv_moments[0, c], qkv_moments[1, c])
            update(qkv_weight[c], grad, moments, decay_rate, clip, qkv_step, qkv_new, (c,))
        else:
            held[0:width] = both
            grad = jnp.transpose(held[...])[0:local, 0:width]
            out_grad[...] = grad
            update(out_weight[...], grad, out_moments, decay_rate, clip, out_step, out_new, everything)
    for at, weight, moments, grad_ref, step, new in (
        (1, in_weight, in_moments, in_grad, in_step, in_new),
        (0, ff_out_weight, ff_out_moments, ff_out_grad, ff_out_step, ff_out_new),
    ):
        grad_ref[...] = hidden[at]
        update(weight[...], hidden[at], moments, decay_rate, clip, step, new, everything)
    vector_grad[...] = packed[0:8]
    update(None, packed[0:8], vector_moments, 0.0, clip, vector_step, vector_new, everything)
    for at in range(4):
        row = packed[8 + at : 9 + at]
        lanes = slice(at * D, (at + 1) * D)
        bias_grad[:, lanes] = row
        here = (slice(None), lanes)
        update(None, row, (bias_moments[0:1, lanes], bias_moments[1:2, lanes]), 0.0, clip, bias_step, bias_new, here, True)
    heads = HEADS // 2
    for tap in range(5):
        grad = packed[12:14, tap * BLOCK : tap * BLOCK + heads]
        pool_grad[tap] = grad
        update(None, grad, (pool_moments[0, tap], pool_moments[1, tap]), 0.0, clip, pool_step, pool_new, (tap,))


def finish(*operands):
    width = operands[2].shape[1]
    local = operands[4].shape[2]

    def three(*shape):
        return [struct(shape, f32), struct(shape, f32), struct((2, *shape), f32)]

    shapes = (
        three(3, width, local)
        + three(local, width)
        + three(width, D)
        + three(width, D)
        + three(8, D)
        + [struct((1, FF), f32), struct((1, FF), f32), struct((2, FF), f32)]
        + three(5, 2, HEADS // 2)
        + [struct((1, 1), f32), struct((1, 4), f32)]
    )
    return pl.pallas_call(
        finish_kernel,
        out_shape=tuple(shapes),
        grid=(1,),
        in_specs=[SM, *wholes(operands[1:])],
        out_specs=tuple(wholes(shapes)),
        scratch_shapes=[pltpu.VMEM((BLOCK, 2 * BLOCK), f32)],
        compiler_params=params(56),
        name="finish",
    )(*operands)


def cross_shards(own, mine, core):
    half = own.shape[0] // 2
    part = lax.dynamic_slice_in_dim(mine, core * half, half, 0)
    near_diag = lax.ppermute(part, PLACE, CROSS)
    other = lax.ppermute(mine, "seq", SWAP)
    far_diag = lax.ppermute(near_diag, "seq", SWAP)
    return (own, mine, other, near_diag, far_diag)


def after(value, *done):
    return lax.optimization_barrier((value, *done))[0]


def rows_by_dp(value, dp):
    n, rows, cols = value.shape
    return value.reshape(n * dp, rows // dp, cols)


class DpSum:
    def __init__(self, dp, dp_index, *groups):
        self.dp, self.dp_index, self.step = dp, dp_index, 1
        self.groups = [[(rows_by_dp(array, dp), slot * dp, 0) for array, slot in terms] for terms in groups]

    def blocks(self, targets):
        return [
            [(array, (first + (targets >> shift)).astype(jnp.int32)) for array, first, shift in terms]
            for terms in self.groups
        ]

    def send(self):
        step = self.step
        targets = jnp.arange(self.dp // (2 * step)) * (2 * step) + (self.dp_index % (2 * step) ^ step)
        fused = len(self.groups) == 1 and targets.shape[0] == 1
        return add_blocks(bf16, *self.blocks(targets), mib=56, fused=fused)

    def move(self, value):
        step = self.step
        got = lax.ppermute(value, "dp", [(i, i ^ step) for i in range(self.dp)])
        blocks = self.dp // (2 * step)
        for group, terms in enumerate(self.groups):
            terms.append((got, group * blocks, (2 * step).bit_length() - 1))
        self.step = 2 * step
        return got

    def done(self):
        return self.step >= self.dp

    def result(self):
        return add_blocks(f32, *self.blocks(self.dp_index + jnp.zeros((1,), jnp.int32)), mib=56, fused=len(self.groups) == 1)


def sum_everywhere(value, dp, between, beside):
    def moved(value, axis, size, step):
        return lax.ppermute(value, axis, [(i, i ^ step) for i in range(size)])

    def four(value, axis, size, step, extra=None):
        got = [moved(value, axis, size, k * step) for k in (1, 2, 3)]
        if extra is not None:
            got[2] = after(got[2], extra)
        return (value + got[0]) + (got[1] + got[2])

    value = four(value, "lvl", 4, 1)
    result = between(value)
    value = value + moved(value, "seq", 2, 1)
    step = 1
    while step < dp:
        extra = beside if step == 1 else None
        if step * 4 <= dp:
            value = four(value, "dp", dp, step, extra)
            step *= 4
        else:
            got = moved(value, "dp", dp, step)
            value = value + (got if extra is None else after(got, extra))
            step *= 2
    return (value, result)


def on_device(
    tokens,
    cotangent,
    lengths,
    qkv_weight,
    out_weight,
    ffn_in_weight,
    ffn_out_weight,
    vectors,
    ffn_bias,
    pool_kernel,
    qkv_moments,
    out_moments,
    ffn_in_moments,
    ffn_out_moments,
    vector_moments,
    bias_moments,
    pool_moments,
):
    dp = lax.axis_size("dp")
    dp_index = lax.axis_index("dp")
    core = lax.axis_index("seq")
    level = lax.axis_index("lvl")
    length = lengths[0]
    count = tokens.shape[1]
    size = count // 4
    seq_len = 2 * count
    half = HEADS // 2
    along = jnp.where(core == 0, 1, 2)
    slots = [level, level ^ along, level ^ (3 - along), level ^ 3]

    def chunk_of(owner):
        order = owner ^ (owner >> 1)
        return jnp.where(core == 0, order, 3 - order)

    chunk = chunk_of(level)
    base = core * count + chunk * size
    width = D // (2 * dp)

    local = qkv_weight.shape[2]
    attn_own = jnp.concatenate(
        [bfloat(qkv_weight).transpose(0, 2, 1).reshape(3 * local, D), bfloat(out_weight)], axis=0
    )
    hidden = ffn_in_weight.shape[0]
    bias = jnp.stack([lax.dynamic_slice_in_dim(ffn_bias, s * hidden, hidden) for s in slots]).reshape(4, 1, D)
    edge = jnp.where(core == 0, tokens[0, count - HALO :], tokens[0, :HALO])
    pool_lanes = jnp.repeat(pool_kernel.reshape(10, half), HEAD, axis=1)
    place = jnp.stack([*slots, core, base, length, seq_len, chunk]).astype(jnp.int32)
    row = jnp.arange(D)
    side, rest = (row // (D // 2), row % (D // 2))
    feature = (rest // width) * (2 * width) + jnp.where(side == 0, core, 1 - core) * width + rest % width
    order = (feature[:, None] == row[None, :]).astype(bf16)
    chunks = jnp.stack([chunk_of(s) for s in slots]).astype(jnp.int32)

    def index(*at):
        return jnp.stack([jnp.asarray(a) for a in at]).astype(jnp.int32)

    attn_mine = lax.ppermute(attn_own, PLACE, MINE)
    edge = lax.ppermute(after(edge, attn_own), "seq", SWAP)
    in_own = bfloat(ffn_in_weight)
    out_own = bfloat(ffn_out_weight)
    weight_slices = own_slices(
        (dp_index * 2 + core) * width, width, qkv_weight, out_weight, ffn_in_weight, ffn_out_weight
    )
    attn_mine = after(attn_mine, weight_slices, edge, in_own, out_own, order, pool_lanes, place, bias)
    part = lax.dynamic_slice_in_dim(attn_mine, core * (D // 2), D // 2, 0)
    attn_near = lax.ppermute(part, PLACE, CROSS)
    attn_other = lax.ppermute(attn_mine, "seq", SWAP)
    extended, inputs, incoming, near_mask, far_mask = prepare(place, edge, after(tokens, part), cotangent)
    attn_near = after(attn_near, extended)
    attn_far = lax.ppermute(attn_near, "seq", SWAP)
    attn_pieces = [
        p.reshape(-1, local, D) for p in (attn_own, attn_mine, attn_other, attn_near, attn_far)
    ]
    in_mine = lax.ppermute(after(in_own, attn_near), PLACE, MINE)
    out_all, *kept = project(place, extended, attn_pieces, vectors, pool_lanes)
    query, near_keys, near_values, far_keys, far_values, pool_keys, pool_values = kept
    in_mine = after(in_mine, query)
    part = lax.dynamic_slice_in_dim(in_mine, core * (D // 2), D // 2, 0)
    in_near = lax.ppermute(part, PLACE, CROSS)
    in_other = lax.ppermute(in_mine, "seq", SWAP)
    out_mine = lax.ppermute(after(out_own, part), PLACE, MINE)
    mixed, log_total = attend_forward(
        after(query, part), near_keys, near_values, pool_keys, pool_values, near_mask, far_mask
    )
    in_near = after(in_near, mixed)
    in_far = lax.ppermute(in_near, "seq", SWAP)
    normed, inverse, first_low, act, slope = feed_forward(mixed, out_all, inputs, vectors, bias, (in_own, in_mine))
    out_mine = after(out_mine, first_low)
    part = lax.dynamic_slice_in_dim(out_mine, core * (D // 2), D // 2, 0)
    out_near = lax.ppermute(part, PLACE, CROSS)
    out_other = lax.ppermute(out_mine, "seq", SWAP)
    act_rest, slope_rest = feed_forward_rest(
        place, after(first_low, part), bias, (after(in_other, first_low), in_near, after(in_far, first_low))
    )
    out_near = after(out_near, act_rest)
    out_far = lax.ppermute(out_near, "seq", SWAP)
    in_pieces = (in_own, in_mine, in_other, in_near, in_far)
    out_pieces = (out_own, out_mine, out_other, out_near, out_far)
    block_low, branch_low, second, second_sums = branch_of(
        place, act, act_rest, normed, incoming, vectors, out_pieces
    )

    out_grad, grad_sent = ffn_grad(order, branch_low, act, act_rest)
    out_got = lax.ppermute(grad_sent, "seq", SWAP)
    pre_low, bias_sum, partial = feed_back(
        slope, after(branch_low, out_grad), second, in_pieces[:2], out_pieces[:2]
    )
    out_got = after(out_got, partial)
    out_send = add_blocks(bf16, [(out_grad, index(1, 3)), (out_got, index(2, 3))])
    out_first = lax.ppermute(out_send, PLACE, MINE)
    pre_rest, bias_rest, attn_low, attn_grad, heads_grad, first_sums = feed_back_rest(
        place, slope_rest, after(branch_low, out_send), partial, normed, inverse, vectors, out_all,
        in_pieces[2:], out_pieces[2:],
    )
    turned = turn_rows(order, after(extended, attn_low))
    in_early, early_sent = ffn_grad(order, after(first_low, turned), pre_low)
    out_first = after(out_first, in_early)
    out_pass = add_blocks(bf16, [(out_grad, index(2)), (out_got, index(1)), (out_first, index(1))])
    out_second = lax.ppermute(out_pass, PLACE, CROSS)
    in_late, late_sent = ffn_grad(order, after(first_low, out_pass), pre_rest)
    late_got = lax.ppermute(late_sent, "seq", SWAP)
    in_send = add_blocks(
        bf16, [(in_early, index(1)), (late_got, index(0))], [(in_late, index(1)), (late_got, index(1))]
    )
    in_first = lax.ppermute(in_send, PLACE, MINE)
    early_got = lax.ppermute(after(early_sent, in_send), "seq", SWAP)

    (query_grad, near_low, far_low, near_own, pool_own, to_left, to_right, query_sum, pool_sum) = attend_backward(
        after(heads_grad, in_send), *kept, near_mask, far_mask, log_total, pool_lanes
    )
    from_right = lax.ppermute(to_left, PLACE, LEFTWARD)
    from_left = lax.ppermute(to_right, PLACE, RIGHTWARD)
    in_first, out_second = after(in_first, query_grad), after(out_second, query_grad)
    early_got = after(early_got, query_grad)
    in_pass = add_blocks(bf16, [(in_late, index(0)), (early_got, index(1)), (in_first, index(1))])
    in_second = lax.ppermute(in_pass, PLACE, CROSS)
    grad_parts = (order, turned, attn_low, mixed, after(query_grad, in_pass, out_second), near_low, far_low)
    grad_sent = attn_weight_grad(1, *grad_parts)
    attn_got = lax.ppermute(grad_sent, "seq", SWAP)
    query_grad = after(query_grad, grad_sent)
    attn_wide = attn_weight_grad(0, *grad_parts[:4], query_grad, near_low, far_low)
    attn_got = after(attn_got, attn_wide, in_second, from_left, from_right)
    attn_at = index(slots[1], slots[3])
    attn_send = add_blocks(bf16, [(attn_wide, attn_at), (attn_got, attn_at)])
    attn_first = lax.ppermute(attn_send, PLACE, MINE)

    out_second, in_second = after(out_second, attn_send), after(in_second, attn_send)
    ffn_sum = DpSum(
        dp,
        dp_index,
        [(out_grad, 0), (out_got, 0), (out_first, 0), (out_second, 0)],
        [(in_early, 0), (early_got, 0), (in_first, 0), (in_second, 0)],
    )
    ffn_part = ffn_sum.send()
    ffn_moved = ffn_sum.move(ffn_part)
    both_low, value_sum = input_grad_of(
        place, after(query_grad, ffn_part), near_own, pool_own, from_left, from_right, attn_grad, pool_lanes, block_low,
        attn_pieces,
    )
    attn_first = after(attn_first, both_low)
    attn_at = index(slots[2])
    attn_pass = add_blocks(bf16, [(attn_wide, attn_at), (attn_got, attn_at), (attn_first, index(1))], fused=True)
    attn_second = lax.ppermute(attn_pass, PLACE, CROSS)
    while not ffn_sum.done():
        ffn_part = ffn_sum.send()
        ffn_moved = ffn_sum.move(after(ffn_part, attn_pass))
    attn_second = after(attn_second, ffn_part)
    attn_sum = DpSum(
        dp, dp_index, [(attn_wide, slots[0]), (attn_got, slots[0]), (attn_first, 0), (attn_second, 0)]
    )
    attn_part = attn_sum.send()
    attn_moved = attn_sum.move(attn_part)
    both_mine = lax.ppermute(after(both_low, attn_part), PLACE, MINE)
    both_other = lax.ppermute(after(both_low, attn_part), PLACE, CROSS)
    attn_sum.groups[0][-1] = (after(attn_moved, ffn_moved), *attn_sum.groups[0][-1][1:])
    while not attn_sum.done():
        attn_part = attn_sum.send()
        attn_moved = attn_sum.move(attn_part)
    ffn_sum.groups = [[(after(terms[0][0], attn_part), *terms[0][1:]), *terms[1:]] for terms in ffn_sum.groups]
    ffn_shard = ffn_sum.result()
    attn_moved = after(attn_moved, ffn_shard)
    attn_sum.groups[0][-1] = (attn_moved, *attn_sum.groups[0][-1][1:])
    attn_shard = attn_sum.result()
    block_out, input_grad = place_rows(chunks, both_low, both_mine, both_other)

    packed = pack(
        place, query_sum, value_sum, first_sums, second_sums, bias_sum, bias_rest, pool_sum, attn_shard, ffn_shard
    )
    packed, diag_low = sum_everywhere(packed, dp, lambda value: after(both_mine, both_other, value), block_out)
    both_diag = lax.ppermute(diag_low, PLACE, CROSS)
    results = finish(
        place, packed, attn_shard, ffn_shard, *weight_slices,
        qkv_moments, out_moments, ffn_in_moments.transpose(0, 2, 1), ffn_out_moments.transpose(0, 2, 1), vector_moments,
        bias_moments, pool_moments.transpose(0, 2, 1, 3),
    )
    qkv_out, out_out, in_out, ff_out_out, vector_out = [results[3 * i : 3 * i + 3] for i in range(5)]
    block_out, input_grad = place_last(chunks, both_diag, block_out, input_grad)
    *_, bias_grad, bias_step, bias_new, pool_grad, pool_step, pool_new, clip, norms = results
    return (
        block_out[None],
        input_grad[None],
        *qkv_out,
        *out_out,
        *[value.swapaxes(-1, -2) for value in (*in_out, *ff_out_out)],
        *vector_out,
        bias_grad.reshape(FF),
        bias_step.reshape(FF),
        bias_new,
        pool_grad.transpose(1, 0, 2),
        pool_step.transpose(1, 0, 2),
        pool_new.transpose(0, 2, 1, 3),
        clip.reshape(()),
        norms.reshape(4),
    )


def solution(mesh):
    in_specs = (
        P("dp", "seq", None),
        P("dp", "seq", None),
        P("dp"),
        P(None, None, "lvl"),
        P("lvl", None),
        P("lvl", None),
        P("lvl", None),
        P(),
        P(),
        P(),
        P(None, None, ("dp", "seq"), "lvl"),
        P(None, "lvl", ("dp", "seq")),
        P(None, "lvl", ("dp", "seq")),
        P(None, "lvl", ("dp", "seq")),
        P(),
        P(),
        P(),
    )
    out_specs = (
        P("dp", "seq", None),
        P("dp", "seq", None),
        P(None, ("dp", "seq"), "lvl"),
        P(None, ("dp", "seq"), "lvl"),
        P(None, None, ("dp", "seq"), "lvl"),
        P("lvl", ("dp", "seq")),
        P("lvl", ("dp", "seq")),
        P(None, "lvl", ("dp", "seq")),
        P("lvl", ("dp", "seq")),
        P("lvl", ("dp", "seq")),
        P(None, "lvl", ("dp", "seq")),
        P("lvl", ("dp", "seq")),
        P("lvl", ("dp", "seq")),
        P(None, "lvl", ("dp", "seq")),
        P(),
        P(),
        P(),
        P(),
        P(),
        P(),
        P(),
        P(),
        P(),
        P(),
        P(),
    )
    return jax.shard_map(
        on_device, mesh=mesh, in_specs=in_specs, out_specs=out_specs, check_vma=False
    )
```
